32 devices in a mesh: sec: 2 (over y), rad: 4 (over z), ax: 4 (over x, core).
Axes of the slice: x: 2, y: 2, z: 4, core: 2. Of those that a mesh axis runs over, the one named last changes fastest.
Arguments:
- state: float32 [5, 8, 1024, 2048], P(None, 'ax', 'rad', 'sec'), may hold values from -1.6 to 4, as said below
- coarsen: int32 [16], replicated, may hold values from 1 to 16, as said below
Outputs:
- tendency: float32 [5, 8, 1024, 2048], P(None, 'ax', 'rad', 'sec')
The draws below stay inside these ranges and needn't reach their ends.
Inputs may be any that keep to these rules, and one draw needn't show every extreme that they name: `coarsen`: each entry is a power of two; cycle 0 takes 16 and cycle 16 - 1 takes 1. state[0] (density) lies in 0.6 to 1.4, the momenta in -1.6 to 1.6, state[4] (energy) in 2.5 to 4.0.
All inputs are finite; a program needn't handle non-finite values.
Results may differ from the reference program's by a relative error of at most 0.0003.
Values sent between devices are 32-bit elements; how exact they have to be, the bound alone decides.
No kernel may reach another device: no remote copies, remote signals or barrier semaphores. Data moves between devices by JAX's collectives and lax.ppermute only.
A program may use at most 256 MiB of HBM per device.

```python
import math
import jax
import jax.numpy as jnp
from jax import lax

NT = 2048
NR = 1024
R_NEAR = 16
FMAX = 16
NA = 8


def draw_state(key, part):
    subkeys = jax.random.split(key, 3)
    grid_shape = (NA, NR, NT)
    density = jax.random.uniform(subkeys[0], grid_shape, minval=0.6, maxval=1.4)
    momenta = jnp.clip(0.4 * jax.random.normal(subkeys[1], (3,) + grid_shape), -1.6, 1.6)
    energy = jax.random.uniform(subkeys[2], grid_shape, minval=2.5, maxval=4.0)
    return jnp.concatenate([density[None], momenta, energy[None]], axis=0).astype(jnp.float32)


def draw_coarsen(key, part):
    levels = jax.random.randint(key, (R_NEAR,), 0, FMAX.bit_length()).astype(jnp.int32)
    factors = jnp.left_shift(jnp.ones((R_NEAR,), jnp.int32), levels)
    factors = factors.at[0].set(FMAX).at[R_NEAR - 1].set(1)
    return factors.astype(jnp.int32)


def setup_inputs(seed: int = 0) -> dict:
    seeds = jax.random.split(jax.random.key(seed), 3)
    state = draw_state(jax.random.fold_in(seeds[2], 71), 0)
    coarsen = draw_coarsen(jax.random.fold_in(seeds[2], 71), 0)
    return dict(state=state, coarsen=coarsen)


GAMMA = 1.4
KAPPA = 1.44


def primitive(plane):
    density = plane[0]
    mom_ax = plane[1]
    mom_rad = plane[2]
    mom_az = plane[3]
    energy = plane[4]
    vel_ax = mom_ax / density
    vel_rad = mom_rad / density
    vel_az = mom_az / density
    pressure = (GAMMA - 1.0) * (energy - 0.5 * (mom_ax * vel_ax + mom_rad * vel_rad + mom_az * vel_az))
    return mom_ax, mom_rad, mom_az, energy, vel_ax, vel_rad, vel_az, pressure


def axial_flux(plane):
    mom_ax, mom_rad, mom_az, energy, vel_ax, vel_rad, vel_az, pressure = primitive(plane)
    return jnp.stack([mom_ax, mom_ax * vel_ax + pressure, mom_rad * vel_ax, mom_az * vel_ax, (energy + pressure) * vel_ax])


def reference(state, coarsen):
    dtheta = 2.0 * math.pi / NT
    radius = (jnp.arange(NR, dtype=jnp.float32) + 0.5)[:, None]

    def flux_at(index):
        clipped = jnp.clip(index, 0, NA - 1).astype(jnp.int32)
        plane = lax.dynamic_index_in_dim(state, clipped, axis=1, keepdims=False)
        valid = ((index >= 0) & (index < NA)).astype(jnp.float32)
        return axial_flux(plane) * valid

    def one_plane(index):
        plane = lax.dynamic_index_in_dim(state, index, axis=1, keepdims=False)
        mom_ax, mom_rad, mom_az, energy, vel_ax, vel_rad, vel_az, pressure = primitive(plane)
        flux_rad = jnp.stack([mom_rad, mom_ax * vel_rad, mom_rad * vel_rad + pressure, mom_az * vel_rad, (energy + pressure) * vel_rad]) * radius
        flux_az = jnp.stack([mom_az, mom_ax * vel_az, mom_rad * vel_az, mom_az * vel_az + pressure, (energy + pressure) * vel_az])
        result = -(flux_at(index + 1) - flux_at(index - 1)) * 0.5
        padded_rad = jnp.pad(flux_rad, ((0, 0), (1, 1), (0, 0)))
        result = result - (padded_rad[:, 2:] - padded_rad[:, :-2]) * 0.5 / radius
        result = result - (jnp.roll(flux_az, -1, axis=2) - jnp.roll(flux_az, 1, axis=2)) * 0.5 / (radius * dtheta)
        zero_part = jnp.zeros_like(pressure)
        source = jnp.stack([zero_part, zero_part, (pressure + mom_az * vel_az) / radius, -(mom_rad * vel_az) / radius, zero_part])
        return result + source

    tendency = lax.map(one_plane, jnp.arange(NA, dtype=jnp.int32))
    tendency = jnp.transpose(tendency, (1, 0, 2, 3))
    cycle_rows = []
    for cycle_index in range(R_NEAR):
        cycle_line = tendency[:, :, cycle_index, :]
        smoothed = jnp.zeros_like(cycle_line)
        for power in range(FMAX.bit_length()):
            factor = 2 ** power
            blocks = NT // factor
            coarse = cycle_line.reshape(5, NA, blocks, factor).sum(axis=-1) / factor
            stiffness = KAPPA / (factor * dtheta) ** 2
            wavenumber = jnp.arange(blocks // 2 + 1, dtype=jnp.float32)
            denominator = 1.0 + 4.0 * stiffness * jnp.sin(math.pi * wavenumber / blocks) ** 2
            solved = jnp.fft.irfft(jnp.fft.rfft(coarse, axis=-1) / denominator, n=blocks, axis=-1)
            expanded = jnp.repeat(solved, factor, axis=-1).astype(jnp.float32)
            smoothed = jnp.where(coarsen[cycle_index] == factor, expanded, smoothed)
        cycle_rows.append(smoothed)
    near_axis = jnp.stack(cycle_rows, axis=2)
    return jnp.concatenate([near_axis, tendency[:, :, R_NEAR:, :]], axis=2)
```

```python
import functools
import math

import jax
import jax.numpy as jnp
from jax import lax
from jax.experimental import pallas as pl
from jax.experimental.pallas import tpu as pltpu
from jax.sharding import PartitionSpec as P

R_NEAR = 16
FMAX = 16

GAMMA = 1.4
KAPPA = 1.44

FIELDS = 5
PLANES = 2
ROWS = 16
LANES = 128
VMEM_LIMIT = 40 * 1024 * 1024

COL_LOG = 32
COL_GAIN = 33

PARITY, OUTER, FIRST, LAST, BASE, PLANE = range(6)


def primitives(fields):
    density, mom_ax, mom_rad, mom_az, energy = fields
    inverse = 1.0 / density
    vel_ax = mom_ax * inverse
    vel_rad = mom_rad * inverse
    vel_az = mom_az * inverse
    pressure = (GAMMA - 1.0) * (
        energy - 0.5 * (mom_ax * vel_ax + mom_rad * vel_rad + mom_az * vel_az)
    )
    return vel_ax, vel_rad, vel_az, pressure


def flux(fields, velocity, pressure, along):
    _, mom_ax, mom_rad, mom_az, energy = fields
    out = [fields[along], mom_ax * velocity, mom_rad * velocity, mom_az * velocity]
    out[along] = out[along] + pressure
    return out + [(energy + pressure) * velocity]


def stencil(flags, first_row, fields, above, below, edges, inner, outer, dtheta):
    rows, cells = fields[0][0].shape
    row = lax.broadcasted_iota(jnp.int32, (rows, 1), 0)
    lane = lax.broadcasted_iota(jnp.int32, (rows, cells), 1)
    sub = lax.broadcasted_iota(jnp.int32, (rows, cells), 0)
    start = flags[BASE] + first_row
    radius = (start + row).astype(jnp.float32) + 0.5
    inv_radius = 1.0 / radius
    half_inv = 0.5 * inv_radius
    half_arc = 0.5 / (radius * dtheta)
    radius_above = jnp.maximum(start - 1, 0).astype(jnp.float32) + 0.5
    radius_below = (start + rows).astype(jnp.float32) + 0.5
    radius_above = jnp.where((flags[FIRST] == 1) & (first_row == 0), 0.0, radius_above)
    out = []
    axial = []
    for plane in range(PLANES):
        mine = fields[plane]
        vel_ax, vel_rad, vel_az, pressure = primitives(mine)
        axial.append(flux(mine, vel_ax, pressure, 1))
        flux_rad = [g * radius for g in flux(mine, vel_rad, pressure, 2)]
        _, vel, _, press = primitives(above[plane])
        flux_above = [g * radius_above for g in flux(above[plane], vel, press, 2)]
        _, vel, _, press = primitives(below[plane][0])
        flux_below = [g * radius_below * below[plane][1] for g in flux(below[plane][0], vel, press, 2)]
        flux_az = flux(mine, vel_az, pressure, 3)
        _, _, vel, press = primitives(edges[plane][0])
        flux_left = flux(edges[plane][0], vel, press, 3)
        _, _, vel, press = primitives(edges[plane][1])
        flux_right = flux(edges[plane][1], vel, press, 3)
        result = []
        for f in range(FIELDS):
            up = jnp.where(sub == 0, flux_above[f], pltpu.roll(flux_rad[f], 1, 0))
            down = jnp.where(sub == rows - 1, flux_below[f], pltpu.roll(flux_rad[f], rows - 1, 0))
            left = jnp.where(lane == 0, flux_left[f], pltpu.roll(flux_az[f], 1, 1))
            right = jnp.where(lane == cells - 1, flux_right[f], pltpu.roll(flux_az[f], cells - 1, 1))
            result.append((up - down) * half_inv + (left - right) * half_arc)
        result[2] = result[2] + (pressure + mine[3] * vel_az) * inv_radius
        result[3] = result[3] - (mine[2] * vel_az) * inv_radius
        out.append(result)
    vel, _, _, press = primitives(inner)
    flux_inner = flux(inner, vel, press, 1)
    odd = flags[PARITY].astype(jnp.float32)
    low = [g * odd for g in flux_inner]
    high = [g * (1.0 - odd) for g in flux_inner]
    if outer is not None:
        flux_outer = outer_flux(flags, outer)
        low = [a + g * (1.0 - odd) for a, g in zip(low, flux_outer)]
        high = [a + g * odd for a, g in zip(high, flux_outer)]
    for f in range(FIELDS):
        out[0][f] = out[0][f] - 0.5 * (axial[1][f] - low[f])
        out[1][f] = out[1][f] - 0.5 * (high[f] - axial[0][f])
    return out


def outer_flux(flags, outer):
    present = flags[OUTER] == 1
    outer = [jnp.where(present, outer[0], 1.0)] + [jnp.where(present, g, 0.0) for g in outer[1:]]
    vel, _, _, press = primitives(outer)
    return flux(outer, vel, press, 1)


def edge_columns(edge_ref):
    edges = []
    for plane in range(PLANES):
        sides = []
        for side in range(2):
            at = [(side * FIELDS + f) * PLANES + plane for f in range(FIELDS)]
            sides.append([edge_ref[:, c : c + 1] for c in at])
        edges.append(sides)
    return edges


def bulk_kernel(dtheta, blocks, flags, state, before, after, halo_low, halo_high, inner, edge, out):
    block = pl.program_id(0) + 1
    last = block == blocks - 1
    fields = [[state[f, p] for f in range(FIELDS)] for p in range(PLANES)]
    above = [[before[f, p, 7:8, :] for f in range(FIELDS)] for p in range(PLANES)]
    keep = jnp.where((flags[LAST] == 1) & last, 0.0, 1.0)
    present = jnp.logical_not((flags[LAST] == 1) & last)
    below = []
    for p in range(PLANES):
        rows = []
        for f in range(FIELDS):
            k = f * PLANES + p
            value = jnp.where(last, halo_high[k : k + 1, :], after[f, p, 0:1, :])
            rows.append(jnp.where(present, value, 1.0))
        below.append((rows, keep))
    inner_fields = [inner[f] for f in range(FIELDS)]
    result = stencil(
        flags, block * ROWS, fields, above, below, edge_columns(edge), inner_fields, None, dtheta
    )
    for p in range(PLANES):
        for f in range(FIELDS):
            out[f, p] = result[p][f]


def near_kernel(dtheta, flags, state, after, halo_low, inner, outer, edge, table, rhs, local, carry):
    cells = state.shape[-1]
    steps = int(math.log2(cells))
    fields = [[state[f, p] for f in range(FIELDS)] for p in range(PLANES)]
    present = flags[FIRST] == 0
    above = []
    for p in range(PLANES):
        at = [f * PLANES + p for f in range(FIELDS)]
        above.append([jnp.where(present, halo_low[k : k + 1, :], 1.0) for k in at])
    below = [([after[f, p, 0:1, :] for f in range(FIELDS)], 1.0) for p in range(PLANES)]
    inner_fields = [inner[f] for f in range(FIELDS)]
    outer_fields = [outer[f] for f in range(FIELDS)]
    result = stencil(
        flags, 0, fields, above, below, edge_columns(edge), inner_fields, outer_fields, dtheta
    )
    for p in range(PLANES):
        for f in range(FIELDS):
            rhs[f * PLANES + p] = result[p][f]
    lane = lax.broadcasted_iota(jnp.int32, (R_NEAR, cells), 1)
    column = lax.broadcasted_iota(jnp.int32, (R_NEAR, LANES), 1)
    coefs = [table[:, k : k + 1] for k in range(steps)]

    def line(k, ends):
        mean = rhs[k]
        for level in range(FMAX.bit_length() - 1):
            width = 1 << level
            partner = jnp.where(
                (lane & width) == 0,
                pltpu.roll(mean, cells - width, 1),
                pltpu.roll(mean, width, 1),
            )
            mean = jnp.where(table[:, level : level + 1] == 0.0, 0.5 * (mean + partner), mean)
        ahead = mean
        behind = mean
        for step in range(steps):
            width = 1 << step
            moved = jnp.where(lane >= width, pltpu.roll(ahead, width, 1), 0.0)
            ahead = ahead + coefs[step] * moved
            moved = jnp.where(lane < cells - width, pltpu.roll(behind, cells - width, 1), 0.0)
            behind = behind + coefs[step] * moved
        local[k] = ahead + behind - mean
        ends = jnp.where(column == k, ahead[:, cells - 1 : cells], ends)
        return jnp.where(column == k + FIELDS * PLANES, behind[:, 0:1], ends)

    ends = lax.fori_loop(0, FIELDS * PLANES, line, jnp.zeros((R_NEAR, LANES), jnp.float32))
    carry[...] = ends


def finish_kernel(flags, factor, rhs, local, carry, table, held, out):
    cells = out.shape[-1]
    lane = lax.broadcasted_iota(jnp.int32, (R_NEAR, cells), 1).astype(jnp.float32)
    width = factor[:, 0:1].astype(jnp.float32)
    block = jnp.floor((lane + 0.5) / width)
    count = cells / width
    log_ratio = table[:, COL_LOG : COL_LOG + 1]
    gain = table[:, COL_GAIN : COL_GAIN + 1]
    from_left = jnp.exp(log_ratio * (block + 1.0))
    from_right = jnp.exp(log_ratio * (count - block))
    near = flags[FIRST] == 1
    for f in range(FIELDS):
        for p in range(PLANES):
            k = f * PLANES + p
            j = k + FIELDS * PLANES
            smooth = gain * (
                local[k] + from_left * carry[:, k : k + 1] + from_right * carry[:, j : j + 1]
            )
            out[f, p] = jnp.where(near, smooth, rhs[k])


def outer_kernel(flags, outer, held, out):
    values = outer_flux(flags, [outer[f] for f in range(FIELDS)])
    sign = jnp.where(flags[PARITY] == 1, -0.5, 0.5)
    for f in range(FIELDS):
        out[f, 0] = held[f, 0] + sign * values[f]


def cost(flops, nbytes):
    return pl.CostEstimate(flops=flops, bytes_accessed=nbytes, transcendentals=0)


def bulk(flags, state, halo_low, halo_high, inner, edge, dtheta):
    _, _, rows, cells = state.shape
    blocks = rows // ROWS
    eights = ROWS // 8
    size = state.size * 4
    return pl.pallas_call(
        functools.partial(bulk_kernel, dtheta, blocks),
        grid_spec=pltpu.PrefetchScalarGridSpec(
            num_scalar_prefetch=1,
            grid=(blocks - 1,),
            in_specs=[
                pl.BlockSpec((FIELDS, PLANES, ROWS, cells), lambda i, s: (0, 0, i + 1, 0)),
                pl.BlockSpec(
                    (FIELDS, PLANES, 8, cells), lambda i, s: (0, 0, (i + 1) * eights - 1, 0)
                ),
                pl.BlockSpec(
                    (FIELDS, PLANES, 8, cells),
                    lambda i, s: (0, 0, jnp.minimum((i + 2) * eights, rows // 8 - 1), 0),
                ),
                pl.BlockSpec((FIELDS * PLANES, cells), lambda i, s: (0, 0)),
                pl.BlockSpec((FIELDS * PLANES, cells), lambda i, s: (0, 0)),
                pl.BlockSpec((FIELDS, ROWS, cells), lambda i, s: (0, i + 1, 0)),
                pl.BlockSpec((ROWS, LANES), lambda i, s: (i + 1, 0)),
            ],
            out_specs=pl.BlockSpec((FIELDS, PLANES, ROWS, cells), lambda i, s: (0, 0, i + 1, 0)),
        ),
        out_shape=jax.ShapeDtypeStruct(state.shape, jnp.float32),
        compiler_params=pltpu.CompilerParams(vmem_limit_bytes=VMEM_LIMIT),
        cost_estimate=cost(state.size * 40, size * 3),
        name="bulk",
    )(flags, state, state, state, halo_low, halo_high, inner, edge)


def near(flags, state, halo_low, inner, outer, edge, table, dtheta):
    _, _, rows, cells = state.shape
    lines = FIELDS * PLANES
    whole = lambda *shape: pl.BlockSpec(shape, lambda i, s: (0,) * len(shape))
    out = jax.ShapeDtypeStruct((lines, R_NEAR, cells), jnp.float32)
    return pl.pallas_call(
        functools.partial(near_kernel, dtheta),
        grid_spec=pltpu.PrefetchScalarGridSpec(
            num_scalar_prefetch=1,
            grid=(1,),
            in_specs=[
                whole(FIELDS, PLANES, R_NEAR, cells),
                pl.BlockSpec((FIELDS, PLANES, 8, cells), lambda i, s: (0, 0, R_NEAR // 8, 0)),
                whole(lines, cells),
                whole(FIELDS, R_NEAR, cells),
                whole(FIELDS, R_NEAR, cells),
                whole(R_NEAR, LANES),
                whole(R_NEAR, LANES),
            ],
            out_specs=[
                whole(lines, R_NEAR, cells),
                whole(lines, R_NEAR, cells),
                whole(R_NEAR, LANES),
            ],
        ),
        out_shape=[out, out, jax.ShapeDtypeStruct((R_NEAR, LANES), jnp.float32)],
        compiler_params=pltpu.CompilerParams(vmem_limit_bytes=VMEM_LIMIT),
        cost_estimate=cost(lines * R_NEAR * cells * 200, lines * R_NEAR * cells * 20),
        name="near",
    )(flags, state, state, halo_low, inner, outer, edge, table)


def finish(flags, factor, rhs, local, carry, table, held):
    lines, _, cells = rhs.shape
    whole = lambda *shape: pl.BlockSpec(shape, lambda i, s: (0,) * len(shape))
    return pl.pallas_call(
        finish_kernel,
        grid_spec=pltpu.PrefetchScalarGridSpec(
            num_scalar_prefetch=1,
            grid=(1,),
            in_specs=[
                whole(R_NEAR, LANES),
                whole(lines, R_NEAR, cells),
                whole(lines, R_NEAR, cells),
                whole(R_NEAR, LANES),
                whole(R_NEAR, LANES),
                pl.BlockSpec(memory_space=pl.ANY),
            ],
            out_specs=whole(FIELDS, PLANES, R_NEAR, cells),
        ),
        out_shape=jax.ShapeDtypeStruct(held.shape, jnp.float32),
        input_output_aliases={6: 0},
        compiler_params=pltpu.CompilerParams(vmem_limit_bytes=VMEM_LIMIT),
        cost_estimate=cost(lines * R_NEAR * cells * 10, lines * R_NEAR * cells * 12),
        name="finish",
    )(flags, factor, rhs, local, carry, table, held)


def add_outer(flags, outer, first, held):
    _, count, cells = outer.shape
    at = first // ROWS
    place = pl.BlockSpec((FIELDS, 1, ROWS, cells), lambda i, s: (0, s[PLANE], i + at, 0))
    return pl.pallas_call(
        outer_kernel,
        grid_spec=pltpu.PrefetchScalarGridSpec(
            num_scalar_prefetch=1,
            grid=(count // ROWS,),
            in_specs=[pl.BlockSpec((FIELDS, ROWS, cells), lambda i, s: (0, i, 0)), place],
            out_specs=place,
        ),
        out_shape=jax.ShapeDtypeStruct(held.shape, jnp.float32),
        input_output_aliases={2: 0},
        compiler_params=pltpu.CompilerParams(vmem_limit_bytes=VMEM_LIMIT),
        cost_estimate=cost(outer.size * 6, outer.size * 12),
        name="add_outer",
    )(flags, outer, held)


def chunk_bounds(rows):
    units = rows // ROWS
    cuts = {1, units}
    for share in (0.4, 0.8):
        cuts.add(max(1, min(units, round(1 + share * (units - 1)))))
    return [0] + [c * ROWS for c in sorted(cuts)]


def smoothing_table(coarsen, cells, total_cells, dtheta):
    factor = coarsen.astype(jnp.float32)[:, None]
    stiffness = KAPPA / (factor * dtheta) ** 2
    inverse_half = 0.5 / stiffness
    one_minus = jnp.sqrt(inverse_half * (2.0 + inverse_half)) - inverse_half
    log_ratio = jnp.log1p(-one_minus)
    gain = (1.0 - one_minus) / (stiffness * one_minus * (2.0 - one_minus))
    closing = 1.0 / -jnp.expm1((total_cells / factor) * log_ratio)
    across = jnp.exp((cells / factor) * log_ratio)
    column = jnp.arange(LANES, dtype=jnp.int32)[None, :]
    width = jnp.left_shift(1, jnp.minimum(column, 20)).astype(jnp.float32)
    table = jnp.where(width >= factor, jnp.exp(log_ratio * (width / factor)), 0.0)
    table = jnp.where(column == COL_LOG, log_ratio, table)
    table = jnp.where(column == COL_GAIN, gain, table)
    return table, closing, across


def ring(value, axis, shift):
    size = lax.axis_size(axis)
    return lax.ppermute(value, axis, [(i, (i + shift) % size) for i in range(size)])


def body(state, coarsen):
    fields, planes, rows, cells = state.shape
    sec_count = lax.axis_size("sec")
    rad_count = lax.axis_size("rad")
    ax_count = lax.axis_size("ax")
    assert fields == FIELDS and planes == PLANES and ax_count % 2 == 0
    rad_index = lax.axis_index("rad")
    ax_index = lax.axis_index("ax")
    total_cells = cells * sec_count
    dtheta = 2.0 * math.pi / total_cells
    odd = ax_index % 2
    outer_pairs = []
    for i in range(1, ax_count - 1, 2):
        outer_pairs += [(i, i + 1), (i + 1, i)]
    inner_pairs = []
    for i in range(0, ax_count, 2):
        inner_pairs += [(i, i + 1), (i + 1, i)]
    flags = jnp.stack(
        [
            odd,
            ((ax_index > 0) & (ax_index < ax_count - 1)).astype(jnp.int32),
            (rad_index == 0).astype(jnp.int32),
            (rad_index == rad_count - 1).astype(jnp.int32),
            rad_index * rows,
            odd,
        ]
    ).astype(jnp.int32)

    bounds = chunk_bounds(rows)
    outer = []
    for first, end in zip(bounds[:-1], bounds[1:]):
        part = lax.dynamic_slice(
            state, (0, odd, first, 0), (FIELDS, 1, end - first, cells)
        ).reshape(FIELDS, end - first, cells)
        outer.append(lax.ppermute(part, "ax", outer_pairs))
    part = lax.dynamic_slice(state, (0, 1 - odd, 0, 0), (FIELDS, 1, rows, cells))
    inner = lax.ppermute(part.reshape(FIELDS, rows, cells), "ax", inner_pairs)

    lines = FIELDS * PLANES
    up = [(i, i + 1) for i in range(rad_count - 1)]
    down = [(i + 1, i) for i in range(rad_count - 1)]
    halo_low = lax.ppermute(state[:, :, rows - 1, :].reshape(lines, cells), "rad", up)
    halo_high = lax.ppermute(state[:, :, 0, :].reshape(lines, cells), "rad", down)

    first_column = state[:, :, :, 0].reshape(lines, rows)
    last_column = state[:, :, :, cells - 1].reshape(lines, rows)
    if sec_count == 2:
        edge = ring(jnp.concatenate([last_column, first_column], axis=0), "sec", 1)
    else:
        edge = jnp.concatenate([ring(last_column, "sec", 1), ring(first_column, "sec", -1)], axis=0)
    edge = jnp.pad(edge.T, ((0, 0), (0, LANES - 2 * lines)), constant_values=1.0)

    table, closing, across = smoothing_table(coarsen, cells, total_cells, dtheta)
    factor = jnp.broadcast_to(coarsen[:, None], (R_NEAR, LANES))

    rhs, local, ends = near(flags, state, halo_low, inner, outer[0], edge, table, dtheta)
    arrived = [ends] + [ring(ends, "sec", k) for k in range(1, sec_count)] + [ends]
    from_left = jnp.arange(LANES)[None, :] < lines
    carry = jnp.zeros_like(ends)
    for k in range(sec_count, 0, -1):
        carry = carry * across + jnp.where(from_left, arrived[k], arrived[sec_count - k])
    carry = carry * closing

    out = bulk(flags, state, halo_low, halo_high, inner, edge, dtheta)
    for k in range(1, len(outer) - 1):
        out = add_outer(flags, outer[k], bounds[k], out)
    out = finish(flags, factor, rhs, local, carry, table, out)
    return add_outer(flags, outer[-1], bounds[-2], out)


def solution(mesh):
    return jax.shard_map(
        body,
        mesh=mesh,
        in_specs=(P(None, "ax", "rad", "sec"), P()),
        out_specs=P(None, "ax", "rad", "sec"),
        check_vma=False,
    )
```

```python
import functools
import math

import jax
import jax.numpy as jnp
from jax import lax
from jax.experimental import pallas as pl
from jax.experimental.pallas import tpu as pltpu
from jax.sharding import PartitionSpec as P

R_NEAR = 16
FMAX = 16

GAMMA = 1.4
KAPPA = 1.44

FIELDS = 5
PLANES = 2
LINES = FIELDS * PLANES
EIGHT = 8
LANES = 128
VMEM_LIMIT = 28 * 1024 * 1024

COL_LOG = 32
COL_GAIN = 33

ODD, OUTER, FIRST, LAST, BASE = range(5)


def plane_of(odd, q):
    return odd if q else 1 - odd


def primitives(fields):
    density, mom_ax, mom_rad, mom_az, energy = fields
    inverse = 1.0 / density
    vel_ax = mom_ax * inverse
    vel_rad = mom_rad * inverse
    vel_az = mom_az * inverse
    pressure = (GAMMA - 1.0) * (
        energy - 0.5 * (mom_ax * vel_ax + mom_rad * vel_rad + mom_az * vel_az)
    )
    return vel_ax, vel_rad, vel_az, pressure


def flux(fields, velocity, pressure, along):
    _, mom_ax, mom_rad, mom_az, energy = fields
    out = [fields[along], mom_ax * velocity, mom_rad * velocity, mom_az * velocity]
    out[along] = out[along] + pressure
    return out + [(energy + pressure) * velocity]


def flux_along(fields, along):
    velocities = primitives(fields)
    return flux(fields, velocities[along - 1], velocities[3], along)


def outer_flux(flags, outer):
    present = flags[OUTER] == 1
    outer = [jnp.where(present, outer[0], 1.0)] + [jnp.where(present, g, 0.0) for g in outer[1:]]
    return flux_along(outer, 1)


def stencil(flags, first_row, rows, dtheta, load, above, below, edge, inner, outer, store):
    strips = rows // EIGHT
    cells = load(0, 0, 0).shape[-1]
    row = lax.broadcasted_iota(jnp.int32, (EIGHT, 1), 0)
    sub = lax.broadcasted_iota(jnp.int32, (EIGHT, cells), 0)
    lane = lax.broadcasted_iota(jnp.int32, (EIGHT, LANES), 1)
    start = flags[BASE] + first_row
    axial_sign = jnp.where(flags[ODD] == 1, 0.5, -0.5)
    no_above = (flags[FIRST] == 1) & (first_row == 0)
    radius_above = jnp.where(no_above, 0.0, (start - 1).astype(jnp.float32) + 0.5)
    radius_below = (start + rows).astype(jnp.float32) + 0.5
    radii = [(start + EIGHT * t + row).astype(jnp.float32) + 0.5 for t in range(strips)]

    flux_above = []
    flux_below = []
    for q in range(PLANES):
        values = [above(f, q) for f in range(FIELDS)]
        values[0] = jnp.where(no_above, 1.0, values[0])
        flux_above.append([g * radius_above for g in flux_along(values, 2)])
        values, present = below(q)
        flux_below.append([g * (radius_below * present) for g in flux_along(values, 2)])

    def parts(t):
        axial, radial, azimuthal, source = [], [], [], []
        for q in range(PLANES):
            fields = [load(f, q, EIGHT * t) for f in range(FIELDS)]
            vel_ax, vel_rad, vel_az, pressure = primitives(fields)
            axial.append(flux(fields, vel_ax, pressure, 1))
            radial.append([g * radii[t] for g in flux(fields, vel_rad, pressure, 2)])
            azimuthal.append(flux(fields, vel_az, pressure, 3))
            source.append((pressure + fields[3] * vel_az, fields[2] * vel_az))
        return axial, radial, azimuthal, source

    last = None
    current = parts(0)
    for t in range(strips):
        following = parts(t + 1) if t + 1 < strips else None
        axial, radial, azimuthal, source = current
        half_inv = 0.5 / radii[t]
        inner_flux = flux_along([inner(f, EIGHT * t) for f in range(FIELDS)], 1)
        beside = [[a - b for a, b in zip(inner_flux, axial[1])], axial[0]]
        if outer is not None:
            far = outer_flux(flags, [outer(f, EIGHT * t) for f in range(FIELDS)])
            beside[1] = [a - b for a, b in zip(axial[0], far)]
        for q in range(PLANES):
            sides = []
            for side in range(2):
                at = [side * LINES + f * PLANES + q for f in range(FIELDS)]
                sides.append(flux_along([edge(c, EIGHT * t) for c in at], 3))
            for f in range(FIELDS):
                here = radial[q][f]
                before = flux_above[q][f] if last is None else pltpu.roll(last[1][q][f], 1, 0)
                after = (
                    flux_below[q][f]
                    if following is None
                    else pltpu.roll(following[1][q][f], EIGHT - 1, 0)
                )
                up = jnp.where(sub == 0, before, pltpu.roll(here, 1, 0))
                down = jnp.where(sub == EIGHT - 1, after, pltpu.roll(here, EIGHT - 1, 0))
                round_ = azimuthal[q][f]
                left = pltpu.roll(round_, 1, 1)
                left = jnp.concatenate(
                    [jnp.where(lane == 0, sides[0][f], left[:, :LANES]), left[:, LANES:]], axis=1
                )
                right = pltpu.roll(round_, cells - 1, 1)
                end = cells - LANES
                right = jnp.concatenate(
                    [right[:, :end], jnp.where(lane == LANES - 1, sides[1][f], right[:, end:])],
                    axis=1,
                )
                total = (up - down) + (left - right) * (1.0 / dtheta)
                if f == 2:
                    total = total + 2.0 * source[q][0]
                if f == 3:
                    total = total - 2.0 * source[q][1]
                store(f, q, EIGHT * t, total * half_inv + axial_sign * beside[q][f])
        last, current = current, following


def bulk_kernel(dtheta, rows, first, total_rows, fused, part, flags, state, before, after, low, high, inner, edge, *rest):
    rest = list(rest)
    outer = rest.pop(0) if fused else None
    token, held = rest.pop(0), rest.pop(0)
    hbm = rest.pop(0)
    out = rest.pop(0)
    odd = flags[ODD]
    step = pl.program_id(0)
    if part is not None:
        sent, sem = rest
        copy = pltpu.make_async_copy(hbm.at[:, lax.axis_index("ax") % 2, part[0] : part[1], :], sent, sem)
        pl.when(step == 0)(copy.start)
    first_row = first + step * rows
    at_end = first_row + rows == total_rows
    present = jnp.logical_not((flags[LAST] == 1) & at_end)

    def load(f, q, r):
        return state[f, plane_of(odd, q), r : r + EIGHT, :]

    def above(f, q):
        return before[f, plane_of(odd, q), EIGHT - 1 : EIGHT, :]

    def below(q):
        rows_ = []
        for f in range(FIELDS):
            k = f * PLANES + q
            value = jnp.where(at_end, high[k : k + 1, :], after[f, plane_of(odd, q), 0:1, :])
            rows_.append(jnp.where(present, value, 1.0))
        return rows_, jnp.where(present, 1.0, 0.0)

    def store(f, q, r, value):
        out[f, plane_of(odd, q), r : r + EIGHT, :] = value

    stencil(
        flags,
        first_row,
        rows,
        dtheta,
        load,
        above,
        below,
        lambda c, r: edge[r : r + EIGHT, c : c + 1],
        lambda f, r: inner[f, r : r + EIGHT, :],
        None if outer is None else lambda f, r: outer[f, r : r + EIGHT, :],
        store,
    )
    if part is not None:
        pl.when(step == pl.num_programs(0) - 1)(copy.wait)


def near_kernel(
    dtheta, total_rows, flags, state, after, low, high, inner, outer, edge, factor, table, token, rhs, local, carry
):
    cells = state.shape[-1]
    odd = flags[ODD]
    at_end = total_rows == R_NEAR
    present = jnp.logical_not((flags[LAST] == 1) & at_end)

    def below(q):
        rows_ = []
        for f in range(FIELDS):
            k = f * PLANES + q
            value = high[k : k + 1, :] if at_end else after[f, plane_of(odd, q), 0:1, :]
            rows_.append(jnp.where(present, value, 1.0))
        return rows_, jnp.where(present, 1.0, 0.0)

    def store(f, q, r, value):
        rhs[f * PLANES + q, r : r + EIGHT, :] = value

    stencil(
        flags,
        0,
        R_NEAR,
        dtheta,
        lambda f, q, r: state[f, plane_of(odd, q), r : r + EIGHT, :],
        lambda f, q: low[f * PLANES + q : f * PLANES + q + 1, :],
        below,
        lambda c, r: edge[r : r + EIGHT, c : c + 1],
        lambda f, r: inner[f, r : r + EIGHT, :],
        lambda f, r: outer[f, r : r + EIGHT, :],
        store,
    )

    pieces = cells // LANES
    steps = LANES.bit_length() - 1
    lane = lax.broadcasted_iota(jnp.int32, (R_NEAR, LANES), 1)
    width = factor[...]
    ahead_coef = []
    behind_coef = []
    for k in range(steps):
        coef = jnp.broadcast_to(table[:, k : k + 1], (R_NEAR, LANES))
        ahead_coef.append(jnp.where(lane >= (1 << k), coef, 0.0))
        behind_coef.append(jnp.where(lane < LANES - (1 << k), coef, 0.0))
    log_ratio = table[:, COL_LOG : COL_LOG + 1]
    block = jnp.floor((lane.astype(jnp.float32) + 0.5) / width)
    ahead_entry = jnp.exp(log_ratio * (block + 1.0))
    behind_entry = jnp.exp(log_ratio * (LANES / width - block))
    across = jnp.exp(log_ratio * (LANES / width))

    def line(k, ends):
        ahead = []
        behind = []
        means = []
        for b in range(pieces):
            mean = rhs[k, :, b * LANES : (b + 1) * LANES]
            for level in range(FMAX.bit_length() - 1):
                size = 1 << level
                partner = jnp.where(
                    (lane & size) == 0, pltpu.roll(mean, LANES - size, 1), pltpu.roll(mean, size, 1)
                )
                mean = jnp.where(width > size, 0.5 * (mean + partner), mean)
            up = mean
            down = mean
            for step in range(steps):
                up = up + ahead_coef[step] * pltpu.roll(up, 1 << step, 1)
                down = down + behind_coef[step] * pltpu.roll(down, LANES - (1 << step), 1)
            means.append(mean)
            ahead.append(up)
            behind.append(down)
        enter = jnp.zeros((R_NEAR, LANES), jnp.float32)
        for b in range(pieces):
            leave = jnp.broadcast_to(ahead[b][:, LANES - 1 : LANES], (R_NEAR, LANES))
            ahead[b] = ahead[b] + ahead_entry * enter
            enter = leave + across * enter
        ends = jnp.where(lane == k, enter, ends)
        enter = jnp.zeros((R_NEAR, LANES), jnp.float32)
        for b in reversed(range(pieces)):
            leave = jnp.broadcast_to(behind[b][:, 0:1], (R_NEAR, LANES))
            behind[b] = behind[b] + behind_entry * enter
            enter = leave + across * enter
        for b in range(pieces):
            local[k, :, b * LANES : (b + 1) * LANES] = ahead[b] + behind[b] - means[b]
        return jnp.where(lane == k + LINES, enter, ends)

    carry[...] = lax.fori_loop(
        0, LINES, line, jnp.zeros((R_NEAR, LANES), jnp.float32)
    )


def finish_kernel(flags, factor, rhs, local, carry, table, held, out):
    cells = out.shape[-1]
    lane = lax.broadcasted_iota(jnp.int32, (R_NEAR, cells), 1).astype(jnp.float32)
    width = factor[:, 0:1]
    block = jnp.floor((lane + 0.5) / width)
    count = cells / width
    log_ratio = table[:, COL_LOG : COL_LOG + 1]
    gain = table[:, COL_GAIN : COL_GAIN + 1]
    from_left = jnp.exp(log_ratio * (block + 1.0))
    from_right = jnp.exp(log_ratio * (count - block))
    near = flags[FIRST] == 1
    for f in range(FIELDS):
        for q in range(PLANES):
            k = f * PLANES + q
            j = k + LINES
            smooth = gain * (
                local[k] + from_left * carry[:, k : k + 1] + from_right * carry[:, j : j + 1]
            )
            out[f, plane_of(flags[ODD], q)] = jnp.where(near, smooth, rhs[k])


def outer_kernel(flags, outer, held, out):
    sign = jnp.where(flags[ODD] == 1, -0.5, 0.5)
    for r in range(0, outer.shape[1], EIGHT):
        values = outer_flux(flags, [outer[f, r : r + EIGHT, :] for f in range(FIELDS)])
        for f in range(FIELDS):
            out[f, 0, r : r + EIGHT, :] = held[f, 0, r : r + EIGHT, :] + sign * values[f]


def pack_edges_kernel(count, state, part, low, high, edge, left, right, top, bottom, sems):
    _, _, rows, cells = state.shape
    odd = lax.axis_index("ax") % 2
    copies = [
        pltpu.make_async_copy(state.at[:, odd, 0:count, :], part, sems.at[0]),
        pltpu.make_async_copy(state.at[:, :, :, cells - LANES : cells], left, sems.at[1]),
        pltpu.make_async_copy(state.at[:, :, :, 0:LANES], right, sems.at[2]),
        pltpu.make_async_copy(state.at[:, :, rows - EIGHT : rows, :], top, sems.at[3]),
        pltpu.make_async_copy(state.at[:, :, 0:EIGHT, :], bottom, sems.at[4]),
    ]
    for copy in copies:
        copy.start()
    for copy in copies[1:]:
        copy.wait()
    lane = lax.broadcasted_iota(jnp.int32, (rows, LANES), 1)
    columns = jnp.ones((rows, LANES), jnp.float32)
    for f in range(FIELDS):
        for q in range(PLANES):
            k = f * PLANES + q
            p = plane_of(odd, q)
            low[k : k + 1, :] = top[f, p, EIGHT - 1 : EIGHT, :]
            high[k : k + 1, :] = bottom[f, p, 0:1, :]
            columns = jnp.where(lane == k, left[f, p, :, LANES - 1 : LANES], columns)
            columns = jnp.where(lane == k + LINES, right[f, p, :, 0:1], columns)
    edge[...] = columns
    copies[0].wait()


def pack_planes_kernel(part, state, token, side, *rest):
    odd = lax.axis_index("ax") % 2
    sems = rest[-1]
    copies = [pltpu.make_async_copy(state.at[:, 1 - odd, :, :], side, sems.at[0])]
    if part is not None:
        source = state.at[:, odd, part[0] : part[1], :]
        copies.insert(0, pltpu.make_async_copy(source, rest[0], sems.at[1]))
    for copy in copies:
        copy.start()
    for copy in copies:
        copy.wait()


ANY = pl.BlockSpec(memory_space=pl.ANY)
PARAMS = pltpu.CompilerParams(vmem_limit_bytes=VMEM_LIMIT)


def whole(*shape):
    return pl.BlockSpec(shape, lambda i, s: (0,) * len(shape))


def rows_from(shape, axis, first, step):
    def place(i, s):
        row = (first // EIGHT + i * (step // EIGHT)) * EIGHT
        return tuple(row if d == axis else 0 for d in range(len(shape)))

    return pl.BlockSpec(tuple(pl.Element(n) for n in shape), place)


def in_hbm(value):
    return pltpu.with_memory_space_constraint(value, pltpu.HBM)


def cost(flops, nbytes):
    return pl.CostEstimate(flops=flops, bytes_accessed=nbytes, transcendentals=0)


def pack_edges(state, count):
    fields, planes, rows, cells = state.shape
    vmem = pl.BlockSpec(memory_space=pltpu.VMEM)
    row = jax.ShapeDtypeStruct((LINES, cells), jnp.float32)
    return pl.pallas_call(
        functools.partial(pack_edges_kernel, count),
        in_specs=[ANY],
        out_specs=[ANY, vmem, vmem, vmem],
        out_shape=[
            pltpu.VMEM((fields, count, cells), jnp.float32),
            row,
            row,
            jax.ShapeDtypeStruct((rows, LANES), jnp.float32),
        ],
        scratch_shapes=[
            pltpu.VMEM((fields, planes, rows, LANES), jnp.float32),
            pltpu.VMEM((fields, planes, rows, LANES), jnp.float32),
            pltpu.VMEM((fields, planes, EIGHT, cells), jnp.float32),
            pltpu.VMEM((fields, planes, EIGHT, cells), jnp.float32),
            pltpu.SemaphoreType.DMA((5,)),
        ],
        compiler_params=PARAMS,
        cost_estimate=cost(0, fields * count * cells * 8),
        name="pack_edges",
    )(in_hbm(state))


def pack_planes(state, part, token):
    fields, _, rows, cells = state.shape
    shapes = [pltpu.VMEM((fields, rows, cells), jnp.float32)]
    if part is not None:
        shapes.append(pltpu.VMEM((fields, part[1] - part[0], cells), jnp.float32))
    out = pl.pallas_call(
        functools.partial(pack_planes_kernel, part),
        in_specs=[ANY, ANY],
        out_specs=[ANY] * len(shapes),
        out_shape=shapes,
        scratch_shapes=[pltpu.SemaphoreType.DMA((2,))],
        compiler_params=PARAMS,
        cost_estimate=cost(0, sum(math.prod(x.shape) for x in shapes) * 8),
        name="pack_planes",
    )(in_hbm(state), token)
    return out if part is not None else (out[0], None)


def bulk(flags, state, low, high, inner, edge, dtheta, span, rows, token, held, outer=None, part=None):
    fields, planes, total_rows, cells = state.shape
    first, end = span
    fused = outer is not None
    tail = total_rows // EIGHT - 1
    eights = rows // EIGHT
    at = first // EIGHT
    row_block = (fields, planes, EIGHT, cells)
    in_specs = [
        rows_from((fields, planes, rows, cells), 2, first, rows),
        pl.BlockSpec(row_block, lambda i, s: (0, 0, at + i * eights - 1, 0)),
        pl.BlockSpec(row_block, lambda i, s: (0, 0, jnp.minimum(at + (i + 1) * eights, tail), 0)),
        whole(LINES, cells),
        whole(LINES, cells),
        rows_from((fields, rows, cells), 1, first, rows),
        rows_from((rows, LANES), 0, first, rows),
    ]
    state = in_hbm(state)
    operands = [state, state, state, low, high, inner, edge]
    if fused:
        in_specs.append(rows_from((fields, rows, cells), 1, first, rows))
        operands.append(outer)
    in_specs += [ANY, ANY, ANY]
    operands += [token, state if held is None else held, state]
    out_specs = [rows_from((fields, planes, rows, cells), 2, first, rows)]
    out_shape = [pltpu.HBM(state.shape, jnp.float32)]
    scratch = []
    if part is not None:
        out_specs.append(ANY)
        out_shape.append(pltpu.VMEM((fields, part[1] - part[0], cells), jnp.float32))
        scratch.append(pltpu.SemaphoreType.DMA)
    size = fields * planes * (end - first) * cells
    out = pl.pallas_call(
        functools.partial(bulk_kernel, dtheta, rows, first, total_rows, fused, part),
        grid_spec=pltpu.PrefetchScalarGridSpec(
            num_scalar_prefetch=1,
            grid=((end - first) // rows,),
            in_specs=in_specs,
            out_specs=out_specs,
            scratch_shapes=scratch,
        ),
        out_shape=out_shape,
        input_output_aliases={} if held is None else {len(operands) - 1: 0},
        compiler_params=PARAMS,
        cost_estimate=cost(size * 60, size * 24),
        name="bulk",
    )(flags, *operands)
    return out if part is not None else (out[0], None)


def near(flags, state, low, high, inner, outer, edge, factor, table, dtheta, token):
    fields, planes, rows, cells = state.shape
    out = jax.ShapeDtypeStruct((LINES, R_NEAR, cells), jnp.float32)
    tail = min(R_NEAR // EIGHT, rows // EIGHT - 1)
    state = in_hbm(state)
    return pl.pallas_call(
        functools.partial(near_kernel, dtheta, rows),
        grid_spec=pltpu.PrefetchScalarGridSpec(
            num_scalar_prefetch=1,
            grid=(1,),
            in_specs=[
                whole(fields, planes, R_NEAR, cells),
                pl.BlockSpec((fields, planes, EIGHT, cells), lambda i, s: (0, 0, tail, 0)),
                whole(LINES, cells),
                whole(LINES, cells),
                whole(fields, R_NEAR, cells),
                whole(fields, R_NEAR, cells),
                whole(R_NEAR, LANES),
                whole(R_NEAR, LANES),
                whole(R_NEAR, LANES),
                ANY,
            ],
            out_specs=[
                whole(LINES, R_NEAR, cells),
                whole(LINES, R_NEAR, cells),
                whole(R_NEAR, LANES),
            ],
        ),
        out_shape=[out, out, jax.ShapeDtypeStruct((R_NEAR, LANES), jnp.float32)],
        compiler_params=PARAMS,
        cost_estimate=cost(LINES * R_NEAR * cells * 200, LINES * R_NEAR * cells * 80),
        name="near",
    )(flags, state, state, low, high, inner, outer, edge, factor, table, token)


def finish(flags, factor, rhs, local, carry, table, held):
    _, _, cells = rhs.shape
    return pl.pallas_call(
        finish_kernel,
        grid_spec=pltpu.PrefetchScalarGridSpec(
            num_scalar_prefetch=1,
            grid=(1,),
            in_specs=[
                whole(R_NEAR, LANES),
                whole(LINES, R_NEAR, cells),
                whole(LINES, R_NEAR, cells),
                whole(R_NEAR, LANES),
                whole(R_NEAR, LANES),
                ANY,
            ],
            out_specs=whole(FIELDS, PLANES, R_NEAR, cells),
        ),
        out_shape=pltpu.HBM(held.shape, jnp.float32),
        input_output_aliases={6: 0},
        compiler_params=PARAMS,
        cost_estimate=cost(LINES * R_NEAR * cells * 10, LINES * R_NEAR * cells * 20),
        name="finish",
    )(flags, factor, rhs, local, carry, table, held)


def add_outer(flags, outer, span, rows, held):
    fields, _, cells = outer.shape
    first, end = span
    place = pl.BlockSpec(
        tuple(pl.Element(n) for n in (fields, 1, rows, cells)),
        lambda i, s: (0, s[ODD], (first // EIGHT + i * (rows // EIGHT)) * EIGHT, 0),
    )
    return pl.pallas_call(
        outer_kernel,
        grid_spec=pltpu.PrefetchScalarGridSpec(
            num_scalar_prefetch=1,
            grid=((end - first) // rows,),
            in_specs=[rows_from((fields, rows, cells), 1, 0, rows), place],
            out_specs=place,
        ),
        out_shape=pltpu.HBM(held.shape, jnp.float32),
        input_output_aliases={2: 0},
        compiler_params=PARAMS,
        cost_estimate=cost(outer.size * 6, outer.size * 16),
        name="add_outer",
    )(flags, outer, held)


def chunks(rows):
    size = 48 if (rows - R_NEAR) % 48 == 0 else EIGHT
    blocks = (rows - R_NEAR) // size
    cuts = sorted({1, 1 + (blocks - 1) // 2, blocks - (blocks - 1) // 4, blocks})
    ends = [R_NEAR + c * size for c in cuts]
    return size, list(zip([0] + ends[:-1], ends))


def smoothing_table(coarsen, cells, total_cells, dtheta):
    factor = coarsen.astype(jnp.float32)[:, None]
    stiffness = KAPPA / (factor * dtheta) ** 2
    inverse_half = 0.5 / stiffness
    one_minus = jnp.sqrt(inverse_half * (2.0 + inverse_half)) - inverse_half
    log_ratio = jnp.log1p(-one_minus)
    gain = (1.0 - one_minus) / (stiffness * one_minus * (2.0 - one_minus))
    closing = 1.0 / -jnp.expm1((total_cells / factor) * log_ratio)
    across = jnp.exp((cells / factor) * log_ratio)
    column = jnp.arange(LANES, dtype=jnp.int32)[None, :]
    width = jnp.left_shift(1, jnp.minimum(column, 20)).astype(jnp.float32)
    table = jnp.where(width >= factor, jnp.exp(log_ratio * (width / factor)), 0.0)
    table = jnp.where(column == COL_LOG, log_ratio, table)
    table = jnp.where(column == COL_GAIN, gain, table)
    return table, closing, across


def ring(value, axis, shift):
    size = lax.axis_size(axis)
    return lax.ppermute(value, axis, [(i, (i + shift) % size) for i in range(size)])


def body(state, coarsen):
    fields, planes, rows, cells = state.shape
    sec_count = lax.axis_size("sec")
    rad_count = lax.axis_size("rad")
    ax_count = lax.axis_size("ax")
    assert fields == FIELDS and planes == PLANES and ax_count % 2 == 0
    rad_index = lax.axis_index("rad")
    ax_index = lax.axis_index("ax")
    total_cells = cells * sec_count
    dtheta = 2.0 * math.pi / total_cells
    outer_pairs = []
    for i in range(1, ax_count - 1, 2):
        outer_pairs += [(i, i + 1), (i + 1, i)]
    inner_pairs = []
    for i in range(0, ax_count, 2):
        inner_pairs += [(i, i + 1), (i + 1, i)]
    up = [(i, i + 1) for i in range(rad_count - 1)]
    down = [(i + 1, i) for i in range(rad_count - 1)]
    flags = jnp.stack(
        [
            ax_index % 2,
            ((ax_index > 0) & (ax_index < ax_count - 1)).astype(jnp.int32),
            (rad_index == 0).astype(jnp.int32),
            (rad_index == rad_count - 1).astype(jnp.int32),
            rad_index * rows,
        ]
    ).astype(jnp.int32)
    size, spans = chunks(rows)
    count = len(spans)

    part, low, high, columns = pack_edges(state, spans[0][1])
    outer = [lax.ppermute(part, "ax", outer_pairs)]
    low = lax.ppermute(low, "rad", up)
    high = lax.ppermute(high, "rad", down)
    if sec_count == 2:
        edge = ring(columns, "sec", 1)
    else:
        from_left = jnp.arange(LANES)[None, :] < LINES
        edge = jnp.where(from_left, ring(columns, "sec", 1), ring(columns, "sec", -1))
    side, part = pack_planes(state, spans[1] if count > 1 else None, part)
    inner = lax.ppermute(side, "ax", inner_pairs)
    if count > 1:
        outer.append(lax.ppermute(part, "ax", outer_pairs))

    table, closing, across = smoothing_table(coarsen, cells, total_cells, dtheta)
    factor = jnp.broadcast_to(coarsen.astype(jnp.float32)[:, None], (R_NEAR, LANES))

    given = (flags, state, low, high, inner, edge, dtheta)
    out = None
    token = side
    if count > 1:
        out, part = bulk(*given, spans[1], size, token, None, part=spans[2] if count > 2 else None)
        if part is not None:
            outer.append(lax.ppermute(part, "ax", outer_pairs))
            token = part
    rhs, local, ends = near(
        flags, state, low, high, inner, outer[0], edge, factor, table, dtheta, token
    )
    arrived = [ends] + [ring(ends, "sec", k) for k in range(1, sec_count)] + [ends]
    from_left = jnp.arange(LANES)[None, :] < LINES
    carry = jnp.zeros_like(ends)
    for k in range(sec_count, 0, -1):
        carry = carry * across + jnp.where(from_left, arrived[k], arrived[sec_count - k])
    carry = carry * closing

    first_span = (R_NEAR, spans[0][1])
    part = spans[3] if count > 3 else None
    out, part = bulk(*given, first_span, size, ends, out, outer=outer[0], part=part)
    if part is not None:
        outer.append(lax.ppermute(part, "ax", outer_pairs))
    if count > 2:
        out, _ = bulk(*given, (spans[2][0], rows), size, ends, out)
    out = finish(flags, factor, rhs, local, carry, table, out)
    for k in range(1, count):
        out = add_outer(flags, outer[k], spans[k], size, out)
    return out


def solution(mesh):
    return jax.shard_map(
        body,
        mesh=mesh,
        in_specs=(P(None, "ax", "rad", "sec"), P()),
        out_specs=P(None, "ax", "rad", "sec"),
        check_vma=False,
    )
```

```python
import functools
import math

import jax
import jax.numpy as jnp
from jax import lax
from jax.experimental import pallas as pl
from jax.experimental.pallas import tpu as pltpu
from jax.sharding import PartitionSpec as P

R_NEAR = 16
FMAX = 16

GAMMA = 1.4
KAPPA = 1.44

FIELDS = 5
PLANES = 2
LINES = FIELDS * PLANES
EIGHT = 8
LANES = 128
VMEM_LIMIT = 28 * 1024 * 1024

COL_LOG = 32
COL_GAIN = 33

ODD, OUTER, FIRST, LAST, BASE = range(5)


def plane_of(odd, q):
    return odd if q else 1 - odd


def primitives(fields):
    density, mom_ax, mom_rad, mom_az, energy = fields
    inverse = 1.0 / density
    vel_ax = mom_ax * inverse
    vel_rad = mom_rad * inverse
    vel_az = mom_az * inverse
    pressure = (GAMMA - 1.0) * (
        energy - 0.5 * (mom_ax * vel_ax + mom_rad * vel_rad + mom_az * vel_az)
    )
    return vel_ax, vel_rad, vel_az, pressure


def flux(fields, velocity, pressure, along):
    _, mom_ax, mom_rad, mom_az, energy = fields
    out = [fields[along], mom_ax * velocity, mom_rad * velocity, mom_az * velocity]
    out[along] = out[along] + pressure
    return out + [(energy + pressure) * velocity]


def flux_along(fields, along):
    velocities = primitives(fields)
    return flux(fields, velocities[along - 1], velocities[3], along)


def outer_flux(flags, outer):
    present = flags[OUTER] == 1
    outer = [jnp.where(present, outer[0], 1.0)] + [jnp.where(present, g, 0.0) for g in outer[1:]]
    return flux_along(outer, 1)


def stencil(flags, first_row, rows, dtheta, load, above, below, edge, inner, outer, place, scratch):
    strips = rows // EIGHT
    pieces = scratch.shape[2]
    row = lax.broadcasted_iota(jnp.int32, (EIGHT, 1), 0)
    lane = lax.broadcasted_iota(jnp.int32, (EIGHT, LANES), 1)
    start = flags[BASE] + first_row
    axial_sign = jnp.where(flags[ODD] == 1, 0.5, -0.5)
    no_above = (flags[FIRST] == 1) & (first_row == 0)
    radius_above = jnp.where(no_above, 0.0, (start - 1).astype(jnp.float32) + 0.5)
    radius_below = (start + rows).astype(jnp.float32) + 0.5
    at = [slice(b * LANES, (b + 1) * LANES) for b in range(pieces)]

    for q in range(PLANES):
        for b in range(pieces):
            values = [above(f, q, at[b]) for f in range(FIELDS)]
            values[0] = jnp.where(no_above, 1.0, values[0])
            flux_above = flux_along(values, 2)
            values, present = below(q, at[b])
            flux_below = flux_along(values, 2)
            for f in range(FIELDS):
                scratch[q, f, b, EIGHT - 1 : EIGHT, :] = flux_above[f] * radius_above
                scratch[q, f, b, EIGHT + rows : EIGHT + rows + 1, :] = flux_below[f] * (
                    radius_below * present
                )

    def across(t, carry):
        r = pl.multiple_of(EIGHT * t, EIGHT)
        radius = (start + r + row).astype(jnp.float32) + 0.5
        half_inv = 0.5 / radius
        half_arc = half_inv * (1.0 / dtheta)
        side = []
        for q in range(PLANES):
            columns = [[(s * FIELDS + f) * PLANES + q for f in range(FIELDS)] for s in range(2)]
            side.append([flux_along([edge(c, r) for c in cs], 3) for cs in columns])

        def piece(b):
            fields = [[load(f, q, r, at[b]) for f in range(FIELDS)] for q in range(PLANES)]
            base, left, right = [], [], []
            axial = []
            for q in range(PLANES):
                vel_ax, vel_rad, vel_az, pressure = primitives(fields[q])
                axial.append(flux(fields[q], vel_ax, pressure, 1))
                radial = flux(fields[q], vel_rad, pressure, 2)
                for f in range(FIELDS):
                    scratch[q, f, b, pl.ds(r + EIGHT, EIGHT), :] = radial[f] * radius
                azimuthal = flux(fields[q], vel_az, pressure, 3)
                left.append([pltpu.roll(g, 1, 1) for g in azimuthal])
                right.append([pltpu.roll(g, LANES - 1, 1) for g in azimuthal])
                source = (pressure + fields[q][3] * vel_az) * (2.0 * half_inv)
                swirl = (fields[q][2] * vel_az) * (2.0 * half_inv)
                base.append([None, None, source, -swirl, None])
            inner_flux = flux_along([inner(f, r, at[b]) for f in range(FIELDS)], 1)
            beside = [[x - y for x, y in zip(inner_flux, axial[1])], axial[0]]
            if outer is not None:
                far = outer_flux(flags, [outer(f, r, at[b]) for f in range(FIELDS)])
                beside[1] = [x - y for x, y in zip(axial[0], far)]
            for q in range(PLANES):
                for f in range(FIELDS):
                    value = axial_sign * beside[q][f]
                    base[q][f] = value if base[q][f] is None else base[q][f] + value
            return base, left, right

        before = [side[q][0] for q in range(PLANES)]
        here = piece(0)
        for b in range(pieces):
            following = piece(b + 1) if b + 1 < pieces else None
            base, left, right = here
            for q in range(PLANES):
                for f in range(FIELDS):
                    after = side[q][1][f] if following is None else following[2][q][f]
                    ahead = jnp.where(lane == LANES - 1, after, right[q][f])
                    behind = jnp.where(lane == 0, before[q][f], left[q][f])
                    place(f, q, r)[:, at[b]] = base[q][f] + (behind - ahead) * half_arc
            before, here = left, following
        return carry

    lax.fori_loop(0, strips, across, 0)

    def along(t, carry):
        r = pl.multiple_of(EIGHT * t, EIGHT)
        radius = (start + r + row).astype(jnp.float32) + 0.5
        half_inv = 0.5 / radius
        for q in range(PLANES):
            for f in range(FIELDS):
                out = place(f, q, r)
                for b in range(pieces):
                    up = scratch[q, f, b, pl.ds(r + EIGHT - 1, EIGHT), :]
                    down = scratch[q, f, b, pl.ds(r + EIGHT + 1, EIGHT), :]
                    out[:, at[b]] = out[:, at[b]] + (up - down) * half_inv
        return carry

    lax.fori_loop(0, strips, along, 0)


def bulk_kernel(
    dtheta, rows, first, total_rows, flags, state, before, after, low, high, inner, edge, outer, token, held, out, scratch
):
    odd = flags[ODD]
    step = pl.program_id(0)
    first_row = first + step * rows
    at_end = first_row + rows == total_rows
    present = jnp.logical_not((flags[LAST] == 1) & at_end)

    def load(f, q, r, at):
        return state[f, plane_of(odd, q), pl.ds(r, EIGHT), at]

    def above(f, q, at):
        return before[f, plane_of(odd, q), EIGHT - 1 : EIGHT, at]

    def below(q, at):
        values = []
        for f in range(FIELDS):
            k = f * PLANES + q
            value = jnp.where(at_end, high[k : k + 1, at], after[f, plane_of(odd, q), 0:1, at])
            values.append(jnp.where(present, value, 1.0))
        return values, jnp.where(present, 1.0, 0.0)

    stencil(
        flags,
        first_row,
        rows,
        dtheta,
        load,
        above,
        below,
        lambda c, r: edge[pl.ds(r, EIGHT), c : c + 1],
        lambda f, r, at: inner[f, pl.ds(r, EIGHT), at],
        lambda f, r, at: outer[f, pl.ds(r, EIGHT), at],
        lambda f, q, r: out.at[f, plane_of(odd, q), pl.ds(r, EIGHT), :],
        scratch,
    )


def near_kernel(
    dtheta,
    total_rows,
    part_first,
    flags,
    state,
    after,
    low,
    high,
    inner,
    outer,
    edge,
    factor,
    table,
    token,
    hbm,
    rhs,
    local,
    carry,
    *rest,
):
    cells = state.shape[-1]
    odd = flags[ODD]
    at_end = total_rows == R_NEAR
    present = jnp.logical_not((flags[LAST] == 1) & at_end)
    part = rest[0] if len(rest) > 1 else None
    scratch = rest[-1 if part is None else -2]
    if part is not None:
        source = hbm.at[:, lax.axis_index("ax") % 2, part_first : part_first + part.shape[1], :]
        copy = pltpu.make_async_copy(source, part, rest[-1])
        copy.start()

    def below(q, at):
        values = []
        for f in range(FIELDS):
            k = f * PLANES + q
            value = high[k : k + 1, at] if at_end else after[f, plane_of(odd, q), 0:1, at]
            values.append(jnp.where(present, value, 1.0))
        return values, jnp.where(present, 1.0, 0.0)

    stencil(
        flags,
        0,
        R_NEAR,
        dtheta,
        lambda f, q, r, at: state[f, plane_of(odd, q), pl.ds(r, EIGHT), at],
        lambda f, q, at: low[f * PLANES + q : f * PLANES + q + 1, at],
        below,
        lambda c, r: edge[pl.ds(r, EIGHT), c : c + 1],
        lambda f, r, at: inner[f, pl.ds(r, EIGHT), at],
        lambda f, r, at: outer[f, pl.ds(r, EIGHT), at],
        lambda f, q, r: rhs.at[f * PLANES + q, pl.ds(r, EIGHT), :],
        scratch,
    )

    pieces = cells // LANES
    steps = LANES.bit_length() - 1
    lane = lax.broadcasted_iota(jnp.int32, (R_NEAR, LANES), 1)
    width = factor[...]
    ahead_coef = []
    behind_coef = []
    for k in range(steps):
        coef = jnp.broadcast_to(table[:, k : k + 1], (R_NEAR, LANES))
        ahead_coef.append(jnp.where(lane >= (1 << k), coef, 0.0))
        behind_coef.append(jnp.where(lane < LANES - (1 << k), coef, 0.0))
    log_ratio = table[:, COL_LOG : COL_LOG + 1]
    block = jnp.floor((lane.astype(jnp.float32) + 0.5) / width)
    ahead_entry = jnp.exp(log_ratio * (block + 1.0))
    behind_entry = jnp.exp(log_ratio * (LANES / width - block))
    across = jnp.exp(log_ratio * (LANES / width))

    def line(k, ends):
        ahead = []
        behind = []
        means = []
        for b in range(pieces):
            mean = rhs[k, :, b * LANES : (b + 1) * LANES]
            for level in range(FMAX.bit_length() - 1):
                size = 1 << level
                partner = jnp.where(
                    (lane & size) == 0, pltpu.roll(mean, LANES - size, 1), pltpu.roll(mean, size, 1)
                )
                mean = jnp.where(width > size, 0.5 * (mean + partner), mean)
            up = mean
            down = mean
            for step in range(steps):
                up = up + ahead_coef[step] * pltpu.roll(up, 1 << step, 1)
                down = down + behind_coef[step] * pltpu.roll(down, LANES - (1 << step), 1)
            means.append(mean)
            ahead.append(up)
            behind.append(down)
        enter = jnp.zeros((R_NEAR, LANES), jnp.float32)
        for b in range(pieces):
            leave = jnp.broadcast_to(ahead[b][:, LANES - 1 : LANES], (R_NEAR, LANES))
            ahead[b] = ahead[b] + ahead_entry * enter
            enter = leave + across * enter
        ends = jnp.where(lane == k, enter, ends)
        enter = jnp.zeros((R_NEAR, LANES), jnp.float32)
        for b in reversed(range(pieces)):
            leave = jnp.broadcast_to(behind[b][:, 0:1], (R_NEAR, LANES))
            behind[b] = behind[b] + behind_entry * enter
            enter = leave + across * enter
        for b in range(pieces):
            local[k, :, b * LANES : (b + 1) * LANES] = ahead[b] + behind[b] - means[b]
        return jnp.where(lane == k + LINES, enter, ends)

    carry[...] = lax.fori_loop(
        0, LINES, line, jnp.zeros((R_NEAR, LANES), jnp.float32)
    )
    if part is not None:
        copy.wait()


def finish_kernel(flags, factor, rhs, local, carry, table, held, out):
    cells = out.shape[-1]
    lane = lax.broadcasted_iota(jnp.int32, (R_NEAR, cells), 1).astype(jnp.float32)
    width = factor[:, 0:1]
    block = jnp.floor((lane + 0.5) / width)
    count = cells / width
    log_ratio = table[:, COL_LOG : COL_LOG + 1]
    gain = table[:, COL_GAIN : COL_GAIN + 1]
    from_left = jnp.exp(log_ratio * (block + 1.0))
    from_right = jnp.exp(log_ratio * (count - block))
    near = flags[FIRST] == 1
    for f in range(FIELDS):
        for q in range(PLANES):
            k = f * PLANES + q
            j = k + LINES
            smooth = gain * (
                local[k] + from_left * carry[:, k : k + 1] + from_right * carry[:, j : j + 1]
            )
            out[f, plane_of(flags[ODD], q)] = jnp.where(near, smooth, rhs[k])


def pack_first_kernel(count, state, part, low, high, top, bottom, sems):
    _, _, rows, _ = state.shape
    odd = lax.axis_index("ax") % 2
    copies = [
        pltpu.make_async_copy(state.at[:, odd, 0:count, :], part, sems.at[0]),
        pltpu.make_async_copy(state.at[:, :, rows - EIGHT : rows, :], top, sems.at[1]),
        pltpu.make_async_copy(state.at[:, :, 0:EIGHT, :], bottom, sems.at[2]),
    ]
    for copy in copies:
        copy.start()
    for copy in copies[1:]:
        copy.wait()
    for f in range(FIELDS):
        for q in range(PLANES):
            k = f * PLANES + q
            p = plane_of(odd, q)
            low[k : k + 1, :] = top[f, p, EIGHT - 1 : EIGHT, :]
            high[k : k + 1, :] = bottom[f, p, 0:1, :]
    copies[0].wait()


def pack_edges_kernel(state, token, edge, side, left, right, sems):
    _, _, rows, cells = state.shape
    odd = lax.axis_index("ax") % 2
    copies = [
        pltpu.make_async_copy(state.at[:, :, :, cells - LANES : cells], left, sems.at[0]),
        pltpu.make_async_copy(state.at[:, :, :, 0:LANES], right, sems.at[1]),
        pltpu.make_async_copy(state.at[:, 1 - odd, 0:R_NEAR, :], side, sems.at[2]),
    ]
    for copy in copies:
        copy.start()
    for copy in copies[:2]:
        copy.wait()
    lane = lax.broadcasted_iota(jnp.int32, (rows, LANES), 1)
    columns = jnp.ones((rows, LANES), jnp.float32)
    for f in range(FIELDS):
        for q in range(PLANES):
            k = f * PLANES + q
            p = plane_of(odd, q)
            columns = jnp.where(lane == k, left[f, p, :, LANES - 1 : LANES], columns)
            columns = jnp.where(lane == k + LINES, right[f, p, :, 0:1], columns)
    edge[...] = columns
    copies[2].wait()


def pack_rest_kernel(parts, state, token, *rest):
    odd = lax.axis_index("ax") % 2
    sems = rest[-1]
    copies = []
    for k, (q, first, last) in enumerate(parts):
        source = state.at[:, plane_of(odd, q), first:last, :]
        copies.append(pltpu.make_async_copy(source, rest[k], sems.at[k]))
    for copy in copies:
        copy.start()
    for copy in copies:
        copy.wait()


ANY = pl.BlockSpec(memory_space=pl.ANY)
PARAMS = pltpu.CompilerParams(vmem_limit_bytes=VMEM_LIMIT)


def whole(*shape):
    return pl.BlockSpec(shape, lambda i, s: (0,) * len(shape))


def rows_from(shape, axis, first, step):
    def place(i, s):
        row = (first // EIGHT + i * (step // EIGHT)) * EIGHT
        return tuple(row if d == axis else 0 for d in range(len(shape)))

    return pl.BlockSpec(tuple(pl.Element(n) for n in shape), place)


def in_hbm(value):
    return pltpu.with_memory_space_constraint(value, pltpu.HBM)


def cost(flops, nbytes):
    return pl.CostEstimate(flops=flops, bytes_accessed=nbytes, transcendentals=0)


def pack_first(state, count):
    fields, planes, _, cells = state.shape
    vmem = pl.BlockSpec(memory_space=pltpu.VMEM)
    row = jax.ShapeDtypeStruct((LINES, cells), jnp.float32)
    rows = pltpu.VMEM((fields, planes, EIGHT, cells), jnp.float32)
    return pl.pallas_call(
        functools.partial(pack_first_kernel, count),
        in_specs=[ANY],
        out_specs=[vmem, vmem, vmem],
        out_shape=[jax.ShapeDtypeStruct((fields, count, cells), jnp.float32), row, row],
        scratch_shapes=[rows, rows, pltpu.SemaphoreType.DMA((3,))],
        compiler_params=PARAMS,
        cost_estimate=cost(0, fields * count * cells * 8),
        name="pack_first",
    )(in_hbm(state))


def pack_edges(state, token):
    fields, planes, rows, cells = state.shape
    vmem = pl.BlockSpec(memory_space=pltpu.VMEM)
    tiles = pltpu.VMEM((fields, planes, rows, LANES), jnp.float32)
    return pl.pallas_call(
        pack_edges_kernel,
        in_specs=[ANY, ANY],
        out_specs=[vmem, vmem],
        out_shape=[
            jax.ShapeDtypeStruct((rows, LANES), jnp.float32),
            jax.ShapeDtypeStruct((fields, R_NEAR, cells), jnp.float32),
        ],
        scratch_shapes=[tiles, tiles, pltpu.SemaphoreType.DMA((3,))],
        compiler_params=PARAMS,
        cost_estimate=cost(0, fields * planes * rows * LANES * 16),
        name="pack_edges",
    )(in_hbm(state), token)


def pack_rest(state, parts, token):
    fields, _, _, cells = state.shape
    shapes = [jax.ShapeDtypeStruct((fields, last - first, cells), jnp.float32) for _, first, last in parts]
    return pl.pallas_call(
        functools.partial(pack_rest_kernel, parts),
        in_specs=[ANY, ANY],
        out_specs=[pl.BlockSpec(memory_space=pltpu.VMEM)] * len(shapes),
        out_shape=shapes,
        scratch_shapes=[pltpu.SemaphoreType.DMA((len(parts),))],
        compiler_params=PARAMS,
        cost_estimate=cost(0, sum(math.prod(x.shape) for x in shapes) * 8),
        name="pack_rest",
    )(in_hbm(state), token)


def flux_scratch(rows, cells):
    return pltpu.VMEM((PLANES, FIELDS, cells // LANES, rows + 2 * EIGHT, LANES), jnp.float32)


def bulk(flags, state, low, high, inner, edge, dtheta, outer, span, first, rows, token, held):
    fields, planes, total_rows, cells = state.shape
    end = span[1]
    tail = total_rows // EIGHT - 1
    eights = rows // EIGHT
    at = first // EIGHT
    row_block = (fields, planes, EIGHT, cells)
    in_specs = [
        rows_from((fields, planes, rows, cells), 2, first, rows),
        pl.BlockSpec(row_block, lambda i, s: (0, 0, at + i * eights - 1, 0)),
        pl.BlockSpec(row_block, lambda i, s: (0, 0, jnp.minimum(at + (i + 1) * eights, tail), 0)),
        whole(LINES, cells),
        whole(LINES, cells),
        rows_from((fields, rows, cells), 1, 0, rows),
        rows_from((rows, LANES), 0, first, rows),
        rows_from((fields, rows, cells), 1, first - span[0], rows),
        ANY,
        ANY,
    ]
    state = in_hbm(state)
    operands = [state, state, state, low, high, inner, edge, outer]
    operands += [token, state if held is None else held]
    size = fields * planes * (end - first) * cells
    return pl.pallas_call(
        functools.partial(bulk_kernel, dtheta, rows, first, total_rows),
        grid_spec=pltpu.PrefetchScalarGridSpec(
            num_scalar_prefetch=1,
            grid=((end - first) // rows,),
            in_specs=in_specs,
            out_specs=rows_from((fields, planes, rows, cells), 2, first, rows),
            scratch_shapes=[flux_scratch(rows, cells)],
        ),
        out_shape=pltpu.HBM(state.shape, jnp.float32),
        input_output_aliases={} if held is None else {len(operands): 0},
        compiler_params=PARAMS,
        cost_estimate=cost(size * 60, size * 60),
        name="bulk",
    )(flags, *operands)


def near(flags, state, low, high, inner, edge, dtheta, outer, factor, table, token, part=None):
    fields, planes, rows, cells = state.shape
    out = jax.ShapeDtypeStruct((LINES, R_NEAR, cells), jnp.float32)
    tail = min(R_NEAR // EIGHT, rows // EIGHT - 1)
    state = in_hbm(state)
    out_specs = [whole(LINES, R_NEAR, cells), whole(LINES, R_NEAR, cells), whole(R_NEAR, LANES)]
    out_shape = [out, out, jax.ShapeDtypeStruct((R_NEAR, LANES), jnp.float32)]
    scratch = [flux_scratch(R_NEAR, cells)]
    if part is not None:
        out_specs.append(whole(fields, part[1] - part[0], cells))
        out_shape.append(jax.ShapeDtypeStruct((fields, part[1] - part[0], cells), jnp.float32))
        scratch.append(pltpu.SemaphoreType.DMA)
    result = pl.pallas_call(
        functools.partial(near_kernel, dtheta, rows, part[0] if part else 0),
        grid_spec=pltpu.PrefetchScalarGridSpec(
            num_scalar_prefetch=1,
            grid=(1,),
            in_specs=[
                whole(fields, planes, R_NEAR, cells),
                pl.BlockSpec((fields, planes, EIGHT, cells), lambda i, s: (0, 0, tail, 0)),
                whole(LINES, cells),
                whole(LINES, cells),
                whole(fields, R_NEAR, cells),
                whole(fields, R_NEAR, cells),
                whole(R_NEAR, LANES),
                whole(R_NEAR, LANES),
                whole(R_NEAR, LANES),
                ANY,
                ANY,
            ],
            out_specs=out_specs,
            scratch_shapes=scratch,
        ),
        out_shape=out_shape,
        compiler_params=PARAMS,
        cost_estimate=cost(LINES * R_NEAR * cells * 200, LINES * R_NEAR * cells * 250),
        name="near",
    )(flags, state, state, low, high, inner, outer, edge, factor, table, token, state)
    return result if part is not None else (*result, None)


def finish(flags, factor, rhs, local, carry, table, held):
    _, _, cells = rhs.shape
    return pl.pallas_call(
        finish_kernel,
        grid_spec=pltpu.PrefetchScalarGridSpec(
            num_scalar_prefetch=1,
            grid=(1,),
            in_specs=[
                whole(R_NEAR, LANES),
                whole(LINES, R_NEAR, cells),
                whole(LINES, R_NEAR, cells),
                whole(R_NEAR, LANES),
                whole(R_NEAR, LANES),
                ANY,
            ],
            out_specs=whole(FIELDS, PLANES, R_NEAR, cells),
        ),
        out_shape=pltpu.HBM(held.shape, jnp.float32),
        input_output_aliases={6: 0},
        compiler_params=PARAMS,
        cost_estimate=cost(LINES * R_NEAR * cells * 10, LINES * R_NEAR * cells * 20),
        name="finish",
    )(flags, factor, rhs, local, carry, table, held)


def chunks(rows):
    size = 48 if (rows - R_NEAR) % 48 == 0 else EIGHT
    blocks = (rows - R_NEAR) // size
    cuts = sorted({-(-2 * blocks // 5), -(-4 * blocks // 5), blocks})
    ends = [R_NEAR + c * size for c in cuts]
    return size, list(zip([0] + ends[:-1], ends))


def smoothing_table(coarsen, cells, total_cells, dtheta):
    factor = coarsen.astype(jnp.float32)[:, None]
    stiffness = KAPPA / (factor * dtheta) ** 2
    inverse_half = 0.5 / stiffness
    one_minus = jnp.sqrt(inverse_half * (2.0 + inverse_half)) - inverse_half
    log_ratio = jnp.log1p(-one_minus)
    gain = (1.0 - one_minus) / (stiffness * one_minus * (2.0 - one_minus))
    closing = 1.0 / -jnp.expm1((total_cells / factor) * log_ratio)
    across = jnp.exp((cells / factor) * log_ratio)
    column = jnp.arange(LANES, dtype=jnp.int32)[None, :]
    width = jnp.left_shift(1, jnp.minimum(column, 20)).astype(jnp.float32)
    table = jnp.where(width >= factor, jnp.exp(log_ratio * (width / factor)), 0.0)
    table = jnp.where(column == COL_LOG, log_ratio, table)
    table = jnp.where(column == COL_GAIN, gain, table)
    return table, closing, across


def ring(value, axis, shift):
    size = lax.axis_size(axis)
    return lax.ppermute(value, axis, [(i, (i + shift) % size) for i in range(size)])


def body(state, coarsen):
    fields, planes, rows, cells = state.shape
    sec_count = lax.axis_size("sec")
    rad_count = lax.axis_size("rad")
    ax_count = lax.axis_size("ax")
    assert fields == FIELDS and planes == PLANES and ax_count % 2 == 0
    rad_index = lax.axis_index("rad")
    ax_index = lax.axis_index("ax")
    total_cells = cells * sec_count
    dtheta = 2.0 * math.pi / total_cells
    outer_pairs = []
    for i in range(1, ax_count - 1, 2):
        outer_pairs += [(i, i + 1), (i + 1, i)]
    inner_pairs = []
    for i in range(0, ax_count, 2):
        inner_pairs += [(i, i + 1), (i + 1, i)]
    up = [(i, i + 1) for i in range(rad_count - 1)]
    down = [(i + 1, i) for i in range(rad_count - 1)]
    flags = jnp.stack(
        [
            ax_index % 2,
            ((ax_index > 0) & (ax_index < ax_count - 1)).astype(jnp.int32),
            (rad_index == 0).astype(jnp.int32),
            (rad_index == rad_count - 1).astype(jnp.int32),
            rad_index * rows,
        ]
    ).astype(jnp.int32)
    size, spans = chunks(rows)
    count = len(spans)

    part, low, high = pack_first(state, spans[0][1])
    outer = [lax.ppermute(part, "ax", outer_pairs)]
    columns, side = pack_edges(state, high)
    low = lax.ppermute(low, "rad", up)
    high = lax.ppermute(high, "rad", down)
    inner = [lax.ppermute(side, "ax", inner_pairs)]
    wanted = [(0, R_NEAR, spans[0][1])] + [(0, *span) for span in spans[1:]]
    if count > 1:
        wanted.insert(1, (1, *spans[1]))
    parts = pack_rest(state, wanted, columns)
    for k, value in enumerate(parts):
        if wanted[k][0]:
            outer.append(lax.ppermute(value, "ax", outer_pairs))
        else:
            inner.append(lax.ppermute(value, "ax", inner_pairs))
    if sec_count == 2:
        edge = ring(columns, "sec", 1)
    else:
        from_left = jnp.arange(LANES)[None, :] < LINES
        edge = jnp.where(from_left, ring(columns, "sec", 1), ring(columns, "sec", -1))

    table, closing, across = smoothing_table(coarsen, cells, total_cells, dtheta)
    factor = jnp.broadcast_to(coarsen.astype(jnp.float32)[:, None], (R_NEAR, LANES))

    given = (flags, state, low, high)
    part = spans[2] if count > 2 else None
    rhs, local, ends, part = near(
        *given, inner[0], edge, dtheta, outer[0], factor, table, parts[0], part
    )
    if part is not None:
        outer.append(lax.ppermute(part, "ax", outer_pairs))
    arrived = [ends] + [ring(ends, "sec", k) for k in range(1, sec_count)] + [ends]
    from_left = jnp.arange(LANES)[None, :] < LINES
    carry = jnp.zeros_like(ends)
    for k in range(sec_count, 0, -1):
        carry = carry * across + jnp.where(from_left, arrived[k], arrived[sec_count - k])
    carry = carry * closing

    out = None
    for k in range(count):
        first = spans[k][0] if k else R_NEAR
        if k == count - 1 and k:
            out = finish(flags, factor, rhs, local, carry, table, out)
        out = bulk(*given, inner[k + 1], edge, dtheta, outer[k], spans[k], first, size, ends, out)
    return out if count > 1 else finish(flags, factor, rhs, local, carry, table, out)


def solution(mesh):
    return jax.shard_map(
        body,
        mesh=mesh,
        in_specs=(P(None, "ax", "rad", "sec"), P()),
        out_specs=P(None, "ax", "rad", "sec"),
        check_vma=False,
    )
```

```python
import functools
import math

import jax
import jax.numpy as jnp
import numpy as np
from jax import lax
from jax.experimental import pallas as pl
from jax.experimental.pallas import tpu as pltpu
from jax.sharding import PartitionSpec as P

R_NEAR = 16
FMAX = 16

GAMMA = 1.4
KAPPA = 1.44

FIELDS = 5
PLANES = 2
LINES = FIELDS * PLANES
EIGHT = 8
LANES = 128
VMEM_LIMIT = 28 * 1024 * 1024

COL_LOG = 32
COL_GAIN = 33

ODD, OUTER, FIRST, LAST, BASE = range(5)


def plane_of(odd, q):
    return odd if q else 1 - odd


def reciprocal(x):
    y = pl.reciprocal(x, approx=True)
    y = y * (2.0 - x * y)
    return y * (2.0 - x * y)


def fluxes(fields, want):
    density, energy = fields[0], fields[4]
    momentum = fields[1:4]
    inverse = reciprocal(density)
    velocity = [m * inverse for m in momentum]
    square = {}
    for i in range(3):
        for j in range(i, 3):
            if i == j or i + 1 in want or j + 1 in want or (i, j) == (1, 2):
                square[i, j] = square[j, i] = momentum[i] * velocity[j]
    pressure = (GAMMA - 1.0) * (energy - 0.5 * (square[0, 0] + square[1, 1] + square[2, 2]))
    enthalpy = energy + pressure
    out = {}
    for d in want:
        k = d - 1
        flow = [square[i, k] + pressure if i == k else square[i, k] for i in range(3)]
        out[d] = [momentum[k]] + flow + [enthalpy * velocity[k]]
    return out, (pressure, square[2, 2], square[1, 2])


def flux_along(fields, along):
    return fluxes(fields, (along,))[0][along]


def outer_flux(flags, outer):
    present = flags[OUTER] == 1
    outer = [jnp.where(present, outer[0], 1.0)] + [jnp.where(present, g, 0.0) for g in outer[1:]]
    return flux_along(outer, 1)


def stencil(flags, first_row, rows, dtheta, load, above, below, edge, inner, outer, place, scratch):
    strips = rows // EIGHT
    pieces = scratch.shape[2]
    row = lax.broadcasted_iota(jnp.int32, (EIGHT, 1), 0)
    lane = lax.broadcasted_iota(jnp.int32, (EIGHT, LANES), 1)
    start = flags[BASE] + first_row
    axial_sign = jnp.where(flags[ODD] == 1, 0.5, -0.5)
    no_above = (flags[FIRST] == 1) & (first_row == 0)
    radius_above = jnp.where(no_above, 0.0, (start - 1).astype(jnp.float32) + 0.5)
    radius_below = (start + rows).astype(jnp.float32) + 0.5
    at = [slice(b * LANES, (b + 1) * LANES) for b in range(pieces)]

    for q in range(PLANES):
        for b in range(pieces):
            values = [above(f, q, at[b]) for f in range(FIELDS)]
            values[0] = jnp.where(no_above, 1.0, values[0])
            flux_above = flux_along(values, 2)
            values, present = below(q, at[b])
            flux_below = flux_along(values, 2)
            for f in range(FIELDS):
                scratch[q, f, b, EIGHT - 1 : EIGHT, :] = flux_above[f] * radius_above
                scratch[q, f, b, EIGHT + rows : EIGHT + rows + 1, :] = flux_below[f] * (
                    radius_below * present
                )

    def across(t, carry):
        r = pl.multiple_of(EIGHT * t, EIGHT)
        radius = (start + r + row).astype(jnp.float32) + 0.5
        inv_radius = 1.0 / radius
        half_arc = inv_radius * (0.5 / dtheta)
        beyond = [edge(r)] + [pltpu.roll(edge(r), LANES - 4 * f, 1) for f in range(1, FIELDS)]
        beyond = flux_along(beyond, 3)
        side = [[beyond, beyond]]
        side.append([[pltpu.roll(g, shift, 1) for g in beyond] for shift in (LANES - 1, 1)])

        def piece(b):
            fields = [[load(f, q, r, at[b]) for f in range(FIELDS)] for q in range(PLANES)]
            base, left, right = [], [], []
            axial = []
            for q in range(PLANES):
                flow, (pressure, twist, swirl) = fluxes(fields[q], (1, 2, 3))
                axial.append(flow[1])
                for f in range(FIELDS):
                    scratch[q, f, b, pl.ds(r + EIGHT, EIGHT), :] = flow[2][f] * radius
                left.append([pltpu.roll(g, 1, 1) for g in flow[3]])
                right.append([pltpu.roll(g, LANES - 1, 1) for g in flow[3]])
                source = (pressure + twist) * inv_radius
                base.append([None, None, source, swirl * -inv_radius, None])
            inner_flux = flux_along([inner(f, r, at[b]) for f in range(FIELDS)], 1)
            beside = [[x - y for x, y in zip(inner_flux, axial[1])], axial[0]]
            if outer is not None:
                far = outer_flux(flags, [outer(f, r, at[b]) for f in range(FIELDS)])
                beside[1] = [x - y for x, y in zip(axial[0], far)]
            for q in range(PLANES):
                for f in range(FIELDS):
                    value = axial_sign * beside[q][f]
                    base[q][f] = value if base[q][f] is None else base[q][f] + value
            return base, left, right

        before = [side[q][0] for q in range(PLANES)]
        here = piece(0)
        for b in range(pieces):
            following = piece(b + 1) if b + 1 < pieces else None
            base, left, right = here
            for q in range(PLANES):
                for f in range(FIELDS):
                    after = side[q][1][f] if following is None else following[2][q][f]
                    ahead = jnp.where(lane == LANES - 1, after, right[q][f])
                    behind = jnp.where(lane == 0, before[q][f], left[q][f])
                    place(f, q, r)[:, at[b]] = base[q][f] + (behind - ahead) * half_arc
            before, here = left, following
        return carry

    lax.fori_loop(0, strips, across, 0)

    def along(t, carry):
        r = pl.multiple_of(EIGHT * t, EIGHT)
        radius = (start + r + row).astype(jnp.float32) + 0.5
        half_inv = 0.5 / radius
        for q in range(PLANES):
            for f in range(FIELDS):
                out = place(f, q, r)
                for b in range(pieces):
                    up = scratch[q, f, b, pl.ds(r + EIGHT - 1, EIGHT), :]
                    down = scratch[q, f, b, pl.ds(r + EIGHT + 1, EIGHT), :]
                    out[:, at[b]] = out[:, at[b]] + (up - down) * half_inv
        return carry

    lax.fori_loop(0, strips, along, 0)


def bulk_kernel(
    dtheta, rows, first, total_rows, flags, state, before, after, low, high, inner, edge, outer, token, held, out, scratch
):
    odd = flags[ODD]
    step = pl.program_id(0)
    first_row = first + step * rows
    at_end = first_row + rows == total_rows
    present = jnp.logical_not((flags[LAST] == 1) & at_end)

    def load(f, q, r, at):
        return state[f, plane_of(odd, q), pl.ds(r, EIGHT), at]

    def above(f, q, at):
        return before[f, plane_of(odd, q), EIGHT - 1 : EIGHT, at]

    def below(q, at):
        values = []
        for f in range(FIELDS):
            k = f * PLANES + q
            value = jnp.where(at_end, high[k : k + 1, at], after[f, plane_of(odd, q), 0:1, at])
            values.append(jnp.where(present, value, 1.0))
        return values, jnp.where(present, 1.0, 0.0)

    stencil(
        flags,
        first_row,
        rows,
        dtheta,
        load,
        above,
        below,
        lambda r: edge[pl.ds(r, EIGHT), :],
        lambda f, r, at: inner[f, pl.ds(r, EIGHT), at],
        lambda f, r, at: outer[f, pl.ds(r, EIGHT), at],
        lambda f, q, r: out.at[f, plane_of(odd, q), pl.ds(r, EIGHT), :],
        scratch,
    )


def near_kernel(
    dtheta,
    total_rows,
    part_first,
    flags,
    state,
    after,
    low,
    high,
    inner,
    outer,
    edge,
    factor,
    table,
    solve,
    token,
    hbm,
    rhs,
    local,
    carry,
    *rest,
):
    cells = state.shape[-1]
    odd = flags[ODD]
    at_end = total_rows == R_NEAR
    present = jnp.logical_not((flags[LAST] == 1) & at_end)
    part = rest[0] if len(rest) > 1 else None
    scratch = rest[-1 if part is None else -2]
    if part is not None:
        source = hbm.at[:, lax.axis_index("ax") % 2, part_first : part_first + part.shape[1], :]
        copy = pltpu.make_async_copy(source, part, rest[-1])
        copy.start()

    def below(q, at):
        values = []
        for f in range(FIELDS):
            k = f * PLANES + q
            value = high[k : k + 1, at] if at_end else after[f, plane_of(odd, q), 0:1, at]
            values.append(jnp.where(present, value, 1.0))
        return values, jnp.where(present, 1.0, 0.0)

    stencil(
        flags,
        0,
        R_NEAR,
        dtheta,
        lambda f, q, r, at: state[f, plane_of(odd, q), pl.ds(r, EIGHT), at],
        lambda f, q, at: low[f * PLANES + q : f * PLANES + q + 1, at],
        below,
        lambda r: edge[pl.ds(r, EIGHT), :],
        lambda f, r, at: inner[f, pl.ds(r, EIGHT), at],
        lambda f, r, at: outer[f, pl.ds(r, EIGHT), at],
        lambda f, q, r: rhs.at[f * PLANES + q, pl.ds(r, EIGHT), :],
        scratch,
    )

    pieces = cells // LANES
    lane = lax.broadcasted_iota(jnp.int32, (R_NEAR, LANES), 1)
    width = factor[...]
    log_ratio = table[:, COL_LOG : COL_LOG + 1]
    block = jnp.floor((lane.astype(jnp.float32) + 0.5) / width)
    ahead_entry = jnp.exp(log_ratio * (block + 1.0))
    behind_entry = jnp.exp(log_ratio * (LANES / width - block))
    across = jnp.exp(log_ratio * (LANES / width))

    def line(k, ends):
        rows = jnp.concatenate([rhs[k, :, b * LANES : (b + 1) * LANES] for b in range(pieces)], axis=0)
        solved = jnp.dot(
            rows, solve[...], precision=lax.Precision.HIGHEST, preferred_element_type=jnp.float32
        )
        inside = []
        for b in range(pieces):
            mine = solved[b * R_NEAR : (b + 1) * R_NEAR]
            value = mine[:, :LANES]
            for level in range(1, FMAX.bit_length()):
                chosen = mine[:, level * LANES : (level + 1) * LANES]
                value = jnp.where(width == (1 << level), chosen, value)
            inside.append(value)
        total = list(inside)
        enter = jnp.zeros((R_NEAR, LANES), jnp.float32)
        for b in range(pieces):
            leave = jnp.broadcast_to(inside[b][:, LANES - 1 : LANES], (R_NEAR, LANES))
            total[b] = total[b] + ahead_entry * enter
            enter = leave + across * enter
        ends = jnp.where(lane == k, enter, ends)
        enter = jnp.zeros((R_NEAR, LANES), jnp.float32)
        for b in reversed(range(pieces)):
            leave = jnp.broadcast_to(inside[b][:, 0:1], (R_NEAR, LANES))
            total[b] = total[b] + behind_entry * enter
            enter = leave + across * enter
        for b in range(pieces):
            local[k, :, b * LANES : (b + 1) * LANES] = total[b]
        return jnp.where(lane == k + LINES, enter, ends)

    carry[...] = lax.fori_loop(
        0, LINES, line, jnp.zeros((R_NEAR, LANES), jnp.float32)
    )
    if part is not None:
        copy.wait()


def finish_kernel(flags, factor, rhs, local, carry, table, held, out):
    cells = out.shape[-1]
    lane = lax.broadcasted_iota(jnp.int32, (R_NEAR, cells), 1).astype(jnp.float32)
    width = factor[:, 0:1]
    block = jnp.floor((lane + 0.5) / width)
    count = cells / width
    log_ratio = table[:, COL_LOG : COL_LOG + 1]
    gain = table[:, COL_GAIN : COL_GAIN + 1]
    from_left = jnp.exp(log_ratio * (block + 1.0))
    from_right = jnp.exp(log_ratio * (count - block))
    near = flags[FIRST] == 1
    for f in range(FIELDS):
        for q in range(PLANES):
            k = f * PLANES + q
            j = k + LINES
            smooth = gain * (
                local[k] + from_left * carry[:, k : k + 1] + from_right * carry[:, j : j + 1]
            )
            out[f, plane_of(flags[ODD], q)] = jnp.where(near, smooth, rhs[k])


def pack_first_kernel(count, state, part, low, high, top, bottom, sems):
    _, _, rows, _ = state.shape
    odd = lax.axis_index("ax") % 2
    copies = [
        pltpu.make_async_copy(state.at[:, odd, 0:count, :], part, sems.at[0]),
        pltpu.make_async_copy(state.at[:, :, rows - EIGHT : rows, :], top, sems.at[1]),
        pltpu.make_async_copy(state.at[:, :, 0:EIGHT, :], bottom, sems.at[2]),
    ]
    for copy in copies:
        copy.start()
    for copy in copies[1:]:
        copy.wait()
    for f in range(FIELDS):
        for q in range(PLANES):
            k = f * PLANES + q
            p = plane_of(odd, q)
            low[k : k + 1, :] = top[f, p, EIGHT - 1 : EIGHT, :]
            high[k : k + 1, :] = bottom[f, p, 0:1, :]
    copies[0].wait()


def pack_edges_kernel(state, token, edge, side, left, right, sems):
    _, _, rows, cells = state.shape
    odd = lax.axis_index("ax") % 2
    copies = [
        pltpu.make_async_copy(state.at[:, :, :, cells - LANES : cells], left, sems.at[0]),
        pltpu.make_async_copy(state.at[:, :, :, 0:LANES], right, sems.at[1]),
        pltpu.make_async_copy(state.at[:, 1 - odd, 0:R_NEAR, :], side, sems.at[2]),
    ]
    for copy in copies:
        copy.start()
    for copy in copies[:2]:
        copy.wait()
    lane = lax.broadcasted_iota(jnp.int32, (rows, LANES), 1)
    columns = jnp.ones((rows, LANES), jnp.float32)
    for f in range(FIELDS):
        for q in range(PLANES):
            p = plane_of(odd, q)
            columns = jnp.where(lane == 4 * f + q, left[f, p, :, LANES - 1 : LANES], columns)
            columns = jnp.where(lane == (4 * f - 1 - q) % LANES, right[f, p, :, 0:1], columns)
    edge[...] = columns
    copies[2].wait()


def pack_rest_kernel(parts, tokens, state, *rest):
    rest = rest[tokens:]
    odd = lax.axis_index("ax") % 2
    sems = rest[-1]
    copies = []
    for k, (q, first, last) in enumerate(parts):
        source = state.at[:, plane_of(odd, q), first:last, :]
        copies.append(pltpu.make_async_copy(source, rest[k], sems.at[k]))
    for copy in copies:
        copy.start()
    for copy in copies:
        copy.wait()


ANY = pl.BlockSpec(memory_space=pl.ANY)
PARAMS = pltpu.CompilerParams(vmem_limit_bytes=VMEM_LIMIT)


def whole(*shape):
    return pl.BlockSpec(shape, lambda i, s: (0,) * len(shape))


def rows_from(shape, axis, first, step):
    def place(i, s):
        row = (first // EIGHT + i * (step // EIGHT)) * EIGHT
        return tuple(row if d == axis else 0 for d in range(len(shape)))

    return pl.BlockSpec(tuple(pl.Element(n) for n in shape), place)


def in_hbm(value):
    return pltpu.with_memory_space_constraint(value, pltpu.HBM)


def cost(flops, nbytes):
    return pl.CostEstimate(flops=flops, bytes_accessed=nbytes, transcendentals=0)


def pack_first(state, count):
    fields, planes, _, cells = state.shape
    vmem = pl.BlockSpec(memory_space=pltpu.VMEM)
    row = jax.ShapeDtypeStruct((LINES, cells), jnp.float32)
    rows = pltpu.VMEM((fields, planes, EIGHT, cells), jnp.float32)
    return pl.pallas_call(
        functools.partial(pack_first_kernel, count),
        in_specs=[ANY],
        out_specs=[vmem, vmem, vmem],
        out_shape=[jax.ShapeDtypeStruct((fields, count, cells), jnp.float32), row, row],
        scratch_shapes=[rows, rows, pltpu.SemaphoreType.DMA((3,))],
        compiler_params=PARAMS,
        cost_estimate=cost(0, fields * count * cells * 8),
        name="pack_first",
    )(in_hbm(state))


def pack_edges(state, token):
    fields, planes, rows, cells = state.shape
    vmem = pl.BlockSpec(memory_space=pltpu.VMEM)
    tiles = pltpu.VMEM((fields, planes, rows, LANES), jnp.float32)
    return pl.pallas_call(
        pack_edges_kernel,
        in_specs=[ANY, ANY],
        out_specs=[vmem, vmem],
        out_shape=[
            jax.ShapeDtypeStruct((rows, LANES), jnp.float32),
            jax.ShapeDtypeStruct((fields, R_NEAR, cells), jnp.float32),
        ],
        scratch_shapes=[tiles, tiles, pltpu.SemaphoreType.DMA((3,))],
        compiler_params=PARAMS,
        cost_estimate=cost(0, fields * planes * rows * LANES * 16),
        name="pack_edges",
    )(in_hbm(state), token)


def pack_rest(state, parts, *tokens):
    fields, _, _, cells = state.shape
    shapes = [jax.ShapeDtypeStruct((fields, last - first, cells), jnp.float32) for _, first, last in parts]
    return pl.pallas_call(
        functools.partial(pack_rest_kernel, parts, len(tokens)),
        in_specs=[ANY] * (1 + len(tokens)),
        out_specs=[pl.BlockSpec(memory_space=pltpu.VMEM)] * len(shapes),
        out_shape=shapes,
        scratch_shapes=[pltpu.SemaphoreType.DMA((len(parts),))],
        compiler_params=PARAMS,
        cost_estimate=cost(0, sum(math.prod(x.shape) for x in shapes) * 8),
        name="pack_rest",
    )(in_hbm(state), *tokens)


def flux_scratch(rows, cells):
    return pltpu.VMEM((PLANES, FIELDS, cells // LANES, rows + 2 * EIGHT, LANES), jnp.float32)


def bulk(flags, state, low, high, inner, edge, dtheta, outer, span, first, rows, token, held):
    fields, planes, total_rows, cells = state.shape
    end = span[1]
    tail = total_rows // EIGHT - 1
    eights = rows // EIGHT
    at = first // EIGHT
    row_block = (fields, planes, EIGHT, cells)
    in_specs = [
        rows_from((fields, planes, rows, cells), 2, first, rows),
        pl.BlockSpec(row_block, lambda i, s: (0, 0, at + i * eights - 1, 0)),
        pl.BlockSpec(row_block, lambda i, s: (0, 0, jnp.minimum(at + (i + 1) * eights, tail), 0)),
        whole(LINES, cells),
        whole(LINES, cells),
        rows_from((fields, rows, cells), 1, 0, rows),
        rows_from((rows, LANES), 0, first, rows),
        rows_from((fields, rows, cells), 1, first - span[0], rows),
        ANY,
        ANY,
    ]
    state = in_hbm(state)
    operands = [state, state, state, low, high, inner, edge, outer]
    operands += [token, state if held is None else held]
    size = fields * planes * (end - first) * cells
    return pl.pallas_call(
        functools.partial(bulk_kernel, dtheta, rows, first, total_rows),
        grid_spec=pltpu.PrefetchScalarGridSpec(
            num_scalar_prefetch=1,
            grid=((end - first) // rows,),
            in_specs=in_specs,
            out_specs=rows_from((fields, planes, rows, cells), 2, first, rows),
            scratch_shapes=[flux_scratch(rows, cells)],
        ),
        out_shape=pltpu.HBM(state.shape, jnp.float32),
        input_output_aliases={} if held is None else {len(operands): 0},
        compiler_params=PARAMS,
        cost_estimate=cost(size * 60, size * 60),
        name="bulk",
    )(flags, *operands)


def near(flags, state, low, high, inner, edge, dtheta, outer, factor, table, solve, token, part=None):
    fields, planes, rows, cells = state.shape
    out = jax.ShapeDtypeStruct((LINES, R_NEAR, cells), jnp.float32)
    tail = min(R_NEAR // EIGHT, rows // EIGHT - 1)
    state = in_hbm(state)
    out_specs = [whole(LINES, R_NEAR, cells), whole(LINES, R_NEAR, cells), whole(R_NEAR, LANES)]
    out_shape = [out, out, jax.ShapeDtypeStruct((R_NEAR, LANES), jnp.float32)]
    scratch = [flux_scratch(R_NEAR, cells)]
    if part is not None:
        out_specs.append(whole(fields, part[1] - part[0], cells))
        out_shape.append(jax.ShapeDtypeStruct((fields, part[1] - part[0], cells), jnp.float32))
        scratch.append(pltpu.SemaphoreType.DMA)
    result = pl.pallas_call(
        functools.partial(near_kernel, dtheta, rows, part[0] if part else 0),
        grid_spec=pltpu.PrefetchScalarGridSpec(
            num_scalar_prefetch=1,
            grid=(1,),
            in_specs=[
                whole(fields, planes, R_NEAR, cells),
                pl.BlockSpec((fields, planes, EIGHT, cells), lambda i, s: (0, 0, tail, 0)),
                whole(LINES, cells),
                whole(LINES, cells),
                whole(fields, R_NEAR, cells),
                whole(fields, R_NEAR, cells),
                whole(R_NEAR, LANES),
                whole(R_NEAR, LANES),
                whole(R_NEAR, LANES),
                whole(*solve.shape),
                ANY,
                ANY,
            ],
            out_specs=out_specs,
            scratch_shapes=scratch,
        ),
        out_shape=out_shape,
        compiler_params=PARAMS,
        cost_estimate=cost(LINES * R_NEAR * cells * 200, LINES * R_NEAR * cells * 250),
        name="near",
    )(flags, state, state, low, high, inner, outer, edge, factor, table, solve, token, state)
    return result if part is not None else (*result, None)


def finish(flags, factor, rhs, local, carry, table, held):
    _, _, cells = rhs.shape
    return pl.pallas_call(
        finish_kernel,
        grid_spec=pltpu.PrefetchScalarGridSpec(
            num_scalar_prefetch=1,
            grid=(1,),
            in_specs=[
                whole(R_NEAR, LANES),
                whole(LINES, R_NEAR, cells),
                whole(LINES, R_NEAR, cells),
                whole(R_NEAR, LANES),
                whole(R_NEAR, LANES),
                ANY,
            ],
            out_specs=whole(FIELDS, PLANES, R_NEAR, cells),
        ),
        out_shape=pltpu.HBM(held.shape, jnp.float32),
        input_output_aliases={6: 0},
        compiler_params=PARAMS,
        cost_estimate=cost(LINES * R_NEAR * cells * 10, LINES * R_NEAR * cells * 20),
        name="finish",
    )(flags, factor, rhs, local, carry, table, held)


def chunks(rows):
    size = 48 if (rows - R_NEAR) % 48 == 0 else EIGHT
    blocks = (rows - R_NEAR) // size
    cuts = sorted({-(-2 * blocks // 5), -(-4 * blocks // 5), blocks})
    ends = [R_NEAR + c * size for c in cuts]
    return size, list(zip([0] + ends[:-1], ends))


def smoothing_table(coarsen, cells, total_cells, dtheta):
    factor = coarsen.astype(jnp.float32)[:, None]
    stiffness = KAPPA / (factor * dtheta) ** 2
    inverse_half = 0.5 / stiffness
    one_minus = jnp.sqrt(inverse_half * (2.0 + inverse_half)) - inverse_half
    log_ratio = jnp.log1p(-one_minus)
    gain = (1.0 - one_minus) / (stiffness * one_minus * (2.0 - one_minus))
    closing = 1.0 / -jnp.expm1((total_cells / factor) * log_ratio)
    across = jnp.exp((cells / factor) * log_ratio)
    column = jnp.arange(LANES, dtype=jnp.int32)[None, :]
    width = jnp.left_shift(1, jnp.minimum(column, 20)).astype(jnp.float32)
    table = jnp.where(width >= factor, jnp.exp(log_ratio * (width / factor)), 0.0)
    table = jnp.where(column == COL_LOG, log_ratio, table)
    table = jnp.where(column == COL_GAIN, gain, table)
    return table, closing, across


def piece_tables(dtheta):
    tables = []
    for level in range(FMAX.bit_length()):
        width = 1 << level
        half = 0.5 * (width * dtheta) ** 2 / KAPPA
        ratio = 1.0 - (math.sqrt(half * (2.0 + half)) - half)
        block = np.arange(LANES) // width
        tables.append(ratio ** np.abs(block[:, None] - block[None, :]) / width)
    return jnp.asarray(np.concatenate(tables, axis=1), jnp.float32)


def ring(value, axis, shift):
    size = lax.axis_size(axis)
    return lax.ppermute(value, axis, [(i, (i + shift) % size) for i in range(size)])


def body(state, coarsen):
    fields, planes, rows, cells = state.shape
    sec_count = lax.axis_size("sec")
    rad_count = lax.axis_size("rad")
    ax_count = lax.axis_size("ax")
    assert fields == FIELDS and planes == PLANES and ax_count % 2 == 0
    rad_index = lax.axis_index("rad")
    ax_index = lax.axis_index("ax")
    total_cells = cells * sec_count
    dtheta = 2.0 * math.pi / total_cells
    outer_pairs = []
    for i in range(1, ax_count - 1, 2):
        outer_pairs += [(i, i + 1), (i + 1, i)]
    inner_pairs = []
    for i in range(0, ax_count, 2):
        inner_pairs += [(i, i + 1), (i + 1, i)]
    up = [(i, i + 1) for i in range(rad_count - 1)]
    down = [(i + 1, i) for i in range(rad_count - 1)]
    flags = jnp.stack(
        [
            ax_index % 2,
            ((ax_index > 0) & (ax_index < ax_count - 1)).astype(jnp.int32),
            (rad_index == 0).astype(jnp.int32),
            (rad_index == rad_count - 1).astype(jnp.int32),
            rad_index * rows,
        ]
    ).astype(jnp.int32)
    size, spans = chunks(rows)
    count = len(spans)

    part, low, high = pack_first(state, spans[0][1])
    outer = [lax.ppermute(part, "ax", outer_pairs)]
    columns, side = pack_edges(state, high)
    low = lax.ppermute(low, "rad", up)
    high = lax.ppermute(high, "rad", down)
    inner = [lax.ppermute(side, "ax", inner_pairs)]
    wanted = [(0, R_NEAR, spans[0][1])] + [(0, *span) for span in spans[1:]]
    if count > 1:
        wanted.insert(1, (1, *spans[1]))
    parts = pack_rest(state, wanted, columns, low, high)
    for k, value in enumerate(parts):
        if wanted[k][0]:
            outer.append(lax.ppermute(value, "ax", outer_pairs))
        else:
            inner.append(lax.ppermute(value, "ax", inner_pairs))
    if sec_count == 2:
        edge = ring(columns, "sec", 1)
    else:
        from_left = jnp.arange(LANES)[None, :] % 4 < 2
        edge = jnp.where(from_left, ring(columns, "sec", 1), ring(columns, "sec", -1))

    table, closing, across = smoothing_table(coarsen, cells, total_cells, dtheta)
    factor = jnp.broadcast_to(coarsen.astype(jnp.float32)[:, None], (R_NEAR, LANES))

    solve = piece_tables(dtheta)
    given = (flags, state, low, high)
    part = spans[2] if count > 2 else None
    rhs, local, ends, part = near(
        *given, inner[0], edge, dtheta, outer[0], factor, table, solve, parts[0], part
    )
    if part is not None:
        outer.append(lax.ppermute(part, "ax", outer_pairs))
    arrived = [ends] + [ring(ends, "sec", k) for k in range(1, sec_count)] + [ends]
    from_left = jnp.arange(LANES)[None, :] < LINES
    carry = jnp.zeros_like(ends)
    for k in range(sec_count, 0, -1):
        carry = carry * across + jnp.where(from_left, arrived[k], arrived[sec_count - k])
    carry = carry * closing

    out = None
    for k in range(count):
        first = spans[k][0] if k else R_NEAR
        if k == count - 1 and k:
            out = finish(flags, factor, rhs, local, carry, table, out)
        out = bulk(*given, inner[k + 1], edge, dtheta, outer[k], spans[k], first, size, ends, out)
    return out if count > 1 else finish(flags, factor, rhs, local, carry, table, out)


def solution(mesh):
    return jax.shard_map(
        body,
        mesh=mesh,
        in_specs=(P(None, "ax", "rad", "sec"), P()),
        out_specs=P(None, "ax", "rad", "sec"),
        check_vma=False,
    )
```

```python
import functools
import math

import jax
import jax.numpy as jnp
import numpy as np
from jax import lax
from jax.experimental import pallas as pl
from jax.experimental.pallas import tpu as pltpu
from jax.sharding import PartitionSpec as P

R_NEAR = 16
FMAX = 16

GAMMA = 1.4
KAPPA = 1.44

FIELDS = 5
PLANES = 2
LINES = FIELDS * PLANES
EIGHT = 8
LANES = 128
VMEM_LIMIT = 28 * 1024 * 1024

COL_LOG = 32
COL_GAIN = 33

ODD, OUTER, FIRST, LAST, BASE = range(5)


def plane_of(odd, q):
    return odd if q else 1 - odd


def reciprocal(x):
    y = pl.reciprocal(x, approx=True)
    y = y * (2.0 - x * y)
    return y * (2.0 - x * y)


def fluxes(fields, want):
    density, energy = fields[0], fields[4]
    momentum = fields[1:4]
    inverse = reciprocal(density)
    velocity = [m * inverse for m in momentum]
    square = {}
    for i in range(3):
        for j in range(i, 3):
            if i == j or i + 1 in want or j + 1 in want or (i, j) == (1, 2):
                square[i, j] = square[j, i] = momentum[i] * velocity[j]
    pressure = (GAMMA - 1.0) * (energy - 0.5 * (square[0, 0] + square[1, 1] + square[2, 2]))
    enthalpy = energy + pressure
    out = {}
    for d in want:
        k = d - 1
        flow = [square[i, k] + pressure if i == k else square[i, k] for i in range(3)]
        out[d] = [momentum[k]] + flow + [enthalpy * velocity[k]]
    return out, (pressure, square[2, 2], square[1, 2])


def flux_along(fields, along):
    return fluxes(fields, (along,))[0][along]


def outer_flux(flags, outer):
    present = flags[OUTER] == 1
    outer = [jnp.where(present, outer[0], 1.0)] + [jnp.where(present, g, 0.0) for g in outer[1:]]
    return flux_along(outer, 1)


def stencil(flags, first_row, rows, dtheta, load, above, below, edge, inner, outer, place, scratch):
    strips = rows // EIGHT
    pieces = scratch.shape[2]
    row = lax.broadcasted_iota(jnp.int32, (EIGHT, 1), 0)
    lane = lax.broadcasted_iota(jnp.int32, (EIGHT, LANES), 1)
    start = flags[BASE] + first_row
    axial_sign = jnp.where(flags[ODD] == 1, 0.5, -0.5)
    no_above = (flags[FIRST] == 1) & (first_row == 0)
    radius_above = jnp.where(no_above, 0.0, (start - 1).astype(jnp.float32) + 0.5)
    radius_below = (start + rows).astype(jnp.float32) + 0.5
    at = [slice(b * LANES, (b + 1) * LANES) for b in range(pieces)]

    for q in range(PLANES):
        for b in range(pieces):
            values = [above(f, q, at[b]) for f in range(FIELDS)]
            values[0] = jnp.where(no_above, 1.0, values[0])
            flux_above = flux_along(values, 2)
            values, present = below(q, at[b])
            flux_below = flux_along(values, 2)
            for f in range(FIELDS):
                scratch[q, f, b, EIGHT - 1 : EIGHT, :] = flux_above[f] * radius_above
                scratch[q, f, b, EIGHT + rows : EIGHT + rows + 1, :] = flux_below[f] * (
                    radius_below * present
                )

    def across(t, carry):
        r = pl.multiple_of(EIGHT * t, EIGHT)
        radius = (start + r + row).astype(jnp.float32) + 0.5
        inv_radius = 1.0 / radius
        half_arc = inv_radius * (0.5 / dtheta)
        beyond = [edge(r)] + [pltpu.roll(edge(r), LANES - 4 * f, 1) for f in range(1, FIELDS)]
        beyond = flux_along(beyond, 3)
        side = [[beyond, beyond]]
        side.append([[pltpu.roll(g, shift, 1) for g in beyond] for shift in (LANES - 1, 1)])

        def piece(b):
            fields = [[load(f, q, r, at[b]) for f in range(FIELDS)] for q in range(PLANES)]
            base, left, right = [], [], []
            axial = []
            for q in range(PLANES):
                flow, (pressure, twist, swirl) = fluxes(fields[q], (1, 2, 3))
                axial.append(flow[1])
                for f in range(FIELDS):
                    scratch[q, f, b, pl.ds(r + EIGHT, EIGHT), :] = flow[2][f] * radius
                left.append([pltpu.roll(g, 1, 1) for g in flow[3]])
                right.append([pltpu.roll(g, LANES - 1, 1) for g in flow[3]])
                source = (pressure + twist) * inv_radius
                base.append([None, None, source, swirl * -inv_radius, None])
            inner_flux = flux_along([inner(f, r, at[b]) for f in range(FIELDS)], 1)
            beside = [[x - y for x, y in zip(inner_flux, axial[1])], axial[0]]
            if outer is not None:
                far = outer_flux(flags, [outer(f, r, at[b]) for f in range(FIELDS)])
                beside[1] = [x - y for x, y in zip(axial[0], far)]
            for q in range(PLANES):
                for f in range(FIELDS):
                    value = axial_sign * beside[q][f]
                    base[q][f] = value if base[q][f] is None else base[q][f] + value
            return base, left, right

        before = [side[q][0] for q in range(PLANES)]
        here = piece(0)
        for b in range(pieces):
            following = piece(b + 1) if b + 1 < pieces else None
            base, left, right = here
            for q in range(PLANES):
                for f in range(FIELDS):
                    after = side[q][1][f] if following is None else following[2][q][f]
                    ahead = jnp.where(lane == LANES - 1, after, right[q][f])
                    behind = jnp.where(lane == 0, before[q][f], left[q][f])
                    place(f, q, r)[:, at[b]] = base[q][f] + (behind - ahead) * half_arc
            before, here = left, following
        return carry

    lax.fori_loop(0, strips, across, 0)

    def along(t, carry):
        r = pl.multiple_of(EIGHT * t, EIGHT)
        radius = (start + r + row).astype(jnp.float32) + 0.5
        half_inv = 0.5 / radius
        for q in range(PLANES):
            for f in range(FIELDS):
                out = place(f, q, r)
                for b in range(pieces):
                    up = scratch[q, f, b, pl.ds(r + EIGHT - 1, EIGHT), :]
                    down = scratch[q, f, b, pl.ds(r + EIGHT + 1, EIGHT), :]
                    out[:, at[b]] = out[:, at[b]] + (up - down) * half_inv
        return carry

    lax.fori_loop(0, strips, along, 0)


def bulk_kernel(dtheta, rows, first, total_rows, fused, flags, state, before, after, low, high, inner, edge, *rest):
    rest = list(rest)
    outer = rest.pop(0) if fused else None
    _, _, out, scratch = rest
    odd = flags[ODD]
    step = pl.program_id(0)
    first_row = first + step * rows
    at_end = first_row + rows == total_rows
    present = jnp.logical_not((flags[LAST] == 1) & at_end)

    def load(f, q, r, at):
        return state[f, plane_of(odd, q), pl.ds(r, EIGHT), at]

    def above(f, q, at):
        return before[f, plane_of(odd, q), EIGHT - 1 : EIGHT, at]

    def below(q, at):
        values = []
        for f in range(FIELDS):
            k = f * PLANES + q
            value = jnp.where(at_end, high[k : k + 1, at], after[f, plane_of(odd, q), 0:1, at])
            values.append(jnp.where(present, value, 1.0))
        return values, jnp.where(present, 1.0, 0.0)

    stencil(
        flags,
        first_row,
        rows,
        dtheta,
        load,
        above,
        below,
        lambda r: edge[pl.ds(r, EIGHT), :],
        lambda f, r, at: inner[f, pl.ds(r, EIGHT), at],
        None if outer is None else lambda f, r, at: outer[f, pl.ds(r, EIGHT), at],
        lambda f, q, r: out.at[f, plane_of(odd, q), pl.ds(r, EIGHT), :],
        scratch,
    )


def outer_kernel(flags, outer, held, out):
    sign = jnp.where(flags[ODD] == 1, -0.5, 0.5)

    def strip(t, carry):
        r = pl.multiple_of(EIGHT * t, EIGHT)
        at = pl.ds(r, EIGHT)
        values = outer_flux(flags, [outer[f, at, :] for f in range(FIELDS)])
        for f in range(FIELDS):
            out[f, 0, at, :] = held[f, 0, at, :] + sign * values[f]
        return carry

    lax.fori_loop(0, outer.shape[1] // EIGHT, strip, 0)


def near_kernel(
    dtheta,
    total_rows,
    flags,
    state,
    after,
    low,
    high,
    inner,
    outer,
    edge,
    factor,
    table,
    solve,
    token,
    rhs,
    local,
    carry,
    scratch,
):
    cells = state.shape[-1]
    odd = flags[ODD]
    at_end = total_rows == R_NEAR
    present = jnp.logical_not((flags[LAST] == 1) & at_end)

    def below(q, at):
        values = []
        for f in range(FIELDS):
            k = f * PLANES + q
            value = high[k : k + 1, at] if at_end else after[f, plane_of(odd, q), 0:1, at]
            values.append(jnp.where(present, value, 1.0))
        return values, jnp.where(present, 1.0, 0.0)

    stencil(
        flags,
        0,
        R_NEAR,
        dtheta,
        lambda f, q, r, at: state[f, plane_of(odd, q), pl.ds(r, EIGHT), at],
        lambda f, q, at: low[f * PLANES + q : f * PLANES + q + 1, at],
        below,
        lambda r: edge[pl.ds(r, EIGHT), :],
        lambda f, r, at: inner[f, pl.ds(r, EIGHT), at],
        lambda f, r, at: outer[f, pl.ds(r, EIGHT), at],
        lambda f, q, r: rhs.at[f * PLANES + q, pl.ds(r, EIGHT), :],
        scratch,
    )

    pieces = cells // LANES
    lane = lax.broadcasted_iota(jnp.int32, (R_NEAR, LANES), 1)
    width = factor[...]
    log_ratio = table[:, COL_LOG : COL_LOG + 1]
    block = jnp.floor((lane.astype(jnp.float32) + 0.5) / width)
    ahead_entry = jnp.exp(log_ratio * (block + 1.0))
    behind_entry = jnp.exp(log_ratio * (LANES / width - block))
    across = jnp.exp(log_ratio * (LANES / width))

    def line(k, ends):
        rows = jnp.concatenate([rhs[k, :, b * LANES : (b + 1) * LANES] for b in range(pieces)], axis=0)
        solved = jnp.dot(
            rows, solve[...], precision=lax.Precision.HIGHEST, preferred_element_type=jnp.float32
        )
        inside = []
        for b in range(pieces):
            mine = solved[b * R_NEAR : (b + 1) * R_NEAR]
            value = mine[:, :LANES]
            for level in range(1, FMAX.bit_length()):
                chosen = mine[:, level * LANES : (level + 1) * LANES]
                value = jnp.where(width == (1 << level), chosen, value)
            inside.append(value)
        total = list(inside)
        enter = jnp.zeros((R_NEAR, LANES), jnp.float32)
        for b in range(pieces):
            leave = jnp.broadcast_to(inside[b][:, LANES - 1 : LANES], (R_NEAR, LANES))
            total[b] = total[b] + ahead_entry * enter
            enter = leave + across * enter
        ends = jnp.where(lane == k, enter, ends)
        enter = jnp.zeros((R_NEAR, LANES), jnp.float32)
        for b in reversed(range(pieces)):
            leave = jnp.broadcast_to(inside[b][:, 0:1], (R_NEAR, LANES))
            total[b] = total[b] + behind_entry * enter
            enter = leave + across * enter
        for b in range(pieces):
            local[k, :, b * LANES : (b + 1) * LANES] = total[b]
        return jnp.where(lane == k + LINES, enter, ends)

    carry[...] = lax.fori_loop(
        0, LINES, line, jnp.zeros((R_NEAR, LANES), jnp.float32)
    )


def finish_kernel(flags, factor, rhs, local, carry, table, held, out):
    cells = out.shape[-1]
    lane = lax.broadcasted_iota(jnp.int32, (R_NEAR, cells), 1).astype(jnp.float32)
    width = factor[:, 0:1]
    block = jnp.floor((lane + 0.5) / width)
    count = cells / width
    log_ratio = table[:, COL_LOG : COL_LOG + 1]
    gain = table[:, COL_GAIN : COL_GAIN + 1]
    from_left = jnp.exp(log_ratio * (block + 1.0))
    from_right = jnp.exp(log_ratio * (count - block))
    near = flags[FIRST] == 1
    for f in range(FIELDS):
        for q in range(PLANES):
            k = f * PLANES + q
            j = k + LINES
            smooth = gain * (
                local[k] + from_left * carry[:, k : k + 1] + from_right * carry[:, j : j + 1]
            )
            out[f, plane_of(flags[ODD], q)] = jnp.where(near, smooth, rhs[k])


def pack_first_kernel(count, state, part, low, high, top, bottom, sems):
    _, _, rows, _ = state.shape
    odd = lax.axis_index("ax") % 2
    copies = [
        pltpu.make_async_copy(state.at[:, odd, 0:count, :], part, sems.at[0]),
        pltpu.make_async_copy(state.at[:, :, rows - EIGHT : rows, :], top, sems.at[1]),
        pltpu.make_async_copy(state.at[:, :, 0:EIGHT, :], bottom, sems.at[2]),
    ]
    for copy in copies:
        copy.start()
    for copy in copies[1:]:
        copy.wait()
    for f in range(FIELDS):
        for q in range(PLANES):
            k = f * PLANES + q
            p = plane_of(odd, q)
            low[k : k + 1, :] = top[f, p, EIGHT - 1 : EIGHT, :]
            high[k : k + 1, :] = bottom[f, p, 0:1, :]
    copies[0].wait()


def pack_edges_kernel(spans, state, token, edge, *rest):
    _, _, rows, cells = state.shape
    odd = lax.axis_index("ax") % 2
    left, right, sems = rest[-3:]
    copies = [
        pltpu.make_async_copy(state.at[:, :, :, cells - LANES : cells], left, sems.at[0]),
        pltpu.make_async_copy(state.at[:, :, :, 0:LANES], right, sems.at[1]),
    ]
    for k, (first, last) in enumerate(spans):
        source = state.at[:, odd, first:last, :]
        copies.append(pltpu.make_async_copy(source, rest[k], sems.at[2 + k]))
    for copy in copies:
        copy.start()
    for copy in copies[:2]:
        copy.wait()
    lane = lax.broadcasted_iota(jnp.int32, (rows, LANES), 1)
    columns = jnp.ones((rows, LANES), jnp.float32)
    for f in range(FIELDS):
        for q in range(PLANES):
            p = plane_of(odd, q)
            columns = jnp.where(lane == 4 * f + q, left[f, p, :, LANES - 1 : LANES], columns)
            columns = jnp.where(lane == (4 * f - 1 - q) % LANES, right[f, p, :, 0:1], columns)
    edge[...] = columns
    for copy in copies[2:]:
        copy.wait()


def pack_rest_kernel(parts, tokens, state, *rest):
    rest = rest[tokens:]
    odd = lax.axis_index("ax") % 2
    sems = rest[-1]
    copies = []
    for k, (first, last) in enumerate(parts):
        source = state.at[:, 1 - odd, first:last, :]
        copies.append(pltpu.make_async_copy(source, rest[k], sems.at[k]))
    for copy in copies:
        copy.start()
    for copy in copies:
        copy.wait()


ANY = pl.BlockSpec(memory_space=pl.ANY)
PARAMS = pltpu.CompilerParams(vmem_limit_bytes=VMEM_LIMIT)


def whole(*shape):
    return pl.BlockSpec(shape, lambda i, s: (0,) * len(shape))


def rows_from(shape, axis, first, step):
    def place(i, s):
        row = (first // EIGHT + i * (step // EIGHT)) * EIGHT
        return tuple(row if d == axis else 0 for d in range(len(shape)))

    return pl.BlockSpec(tuple(pl.Element(n) for n in shape), place)


def in_hbm(value):
    return pltpu.with_memory_space_constraint(value, pltpu.HBM)


def cost(flops, nbytes):
    return pl.CostEstimate(flops=flops, bytes_accessed=nbytes, transcendentals=0)


def pack_first(state, count):
    fields, planes, _, cells = state.shape
    vmem = pl.BlockSpec(memory_space=pltpu.VMEM)
    row = jax.ShapeDtypeStruct((LINES, cells), jnp.float32)
    rows = pltpu.VMEM((fields, planes, EIGHT, cells), jnp.float32)
    return pl.pallas_call(
        functools.partial(pack_first_kernel, count),
        in_specs=[ANY],
        out_specs=[vmem] * 3,
        out_shape=[jax.ShapeDtypeStruct((fields, count, cells), jnp.float32), row, row],
        scratch_shapes=[rows, rows, pltpu.SemaphoreType.DMA((3,))],
        compiler_params=PARAMS,
        cost_estimate=cost(0, fields * count * cells * 8),
        name="pack_first",
    )(in_hbm(state))


def pack_edges(state, spans, token):
    fields, planes, rows, cells = state.shape
    tiles = pltpu.VMEM((fields, planes, rows, LANES), jnp.float32)
    shapes = [jax.ShapeDtypeStruct((rows, LANES), jnp.float32)]
    shapes += [jax.ShapeDtypeStruct((fields, b - a, cells), jnp.float32) for a, b in spans]
    return pl.pallas_call(
        functools.partial(pack_edges_kernel, spans),
        in_specs=[ANY, ANY],
        out_specs=[pl.BlockSpec(memory_space=pltpu.VMEM)] * len(shapes),
        out_shape=shapes,
        scratch_shapes=[tiles, tiles, pltpu.SemaphoreType.DMA((2 + len(spans),))],
        compiler_params=PARAMS,
        cost_estimate=cost(0, fields * planes * rows * LANES * 16),
        name="pack_edges",
    )(in_hbm(state), token)


def pack_rest(state, parts, *tokens):
    fields, _, _, cells = state.shape
    shapes = [jax.ShapeDtypeStruct((fields, b - a, cells), jnp.float32) for a, b in parts]
    return pl.pallas_call(
        functools.partial(pack_rest_kernel, parts, len(tokens)),
        in_specs=[ANY] * (1 + len(tokens)),
        out_specs=[pl.BlockSpec(memory_space=pltpu.VMEM)] * len(shapes),
        out_shape=shapes,
        scratch_shapes=[pltpu.SemaphoreType.DMA((len(parts),))],
        compiler_params=PARAMS,
        cost_estimate=cost(0, sum(math.prod(x.shape) for x in shapes) * 8),
        name="pack_rest",
    )(in_hbm(state), *tokens)


def flux_scratch(rows, cells):
    return pltpu.VMEM((PLANES, FIELDS, cells // LANES, rows + 2 * EIGHT, LANES), jnp.float32)


def bulk(flags, state, low, high, inner, edge, dtheta, span, rows, token, held, outer=None, origin=0):
    fields, planes, total_rows, cells = state.shape
    first, end = span
    tail = total_rows // EIGHT - 1
    eights = rows // EIGHT
    at = first // EIGHT
    row_block = (fields, planes, EIGHT, cells)
    in_specs = [
        rows_from((fields, planes, rows, cells), 2, first, rows),
        pl.BlockSpec(row_block, lambda i, s: (0, 0, at + i * eights - 1, 0)),
        pl.BlockSpec(row_block, lambda i, s: (0, 0, jnp.minimum(at + (i + 1) * eights, tail), 0)),
        whole(LINES, cells),
        whole(LINES, cells),
        rows_from((fields, rows, cells), 1, 0, rows),
        rows_from((rows, LANES), 0, first, rows),
    ]
    state = in_hbm(state)
    operands = [state, state, state, low, high, inner, edge]
    if outer is not None:
        in_specs.append(rows_from((fields, rows, cells), 1, first - origin, rows))
        operands.append(outer)
    in_specs += [ANY, ANY]
    operands += [token, state if held is None else held]
    size = fields * planes * (end - first) * cells
    return pl.pallas_call(
        functools.partial(bulk_kernel, dtheta, rows, first, total_rows, outer is not None),
        grid_spec=pltpu.PrefetchScalarGridSpec(
            num_scalar_prefetch=1,
            grid=((end - first) // rows,),
            in_specs=in_specs,
            out_specs=rows_from((fields, planes, rows, cells), 2, first, rows),
            scratch_shapes=[flux_scratch(rows, cells)],
        ),
        out_shape=pltpu.HBM(state.shape, jnp.float32),
        input_output_aliases={} if held is None else {len(operands): 0},
        compiler_params=PARAMS,
        cost_estimate=cost(size * 60, size * 10),
        name="bulk",
    )(flags, *operands)


def add_outer(flags, outer, span, rows, held):
    fields, _, cells = outer.shape
    first, end = span
    place = pl.BlockSpec(
        tuple(pl.Element(n) for n in (fields, 1, rows, cells)),
        lambda i, s: (0, s[ODD], (first // EIGHT + i * (rows // EIGHT)) * EIGHT, 0),
    )
    return pl.pallas_call(
        outer_kernel,
        grid_spec=pltpu.PrefetchScalarGridSpec(
            num_scalar_prefetch=1,
            grid=((end - first) // rows,),
            in_specs=[rows_from((fields, rows, cells), 1, 0, rows), place],
            out_specs=place,
        ),
        out_shape=pltpu.HBM(held.shape, jnp.float32),
        input_output_aliases={2: 0},
        compiler_params=PARAMS,
        cost_estimate=cost(outer.size * 6, outer.size * 16),
        name="add_outer",
    )(flags, outer, held)


def near(flags, state, low, high, inner, edge, dtheta, outer, factor, table, solve, token):
    fields, planes, rows, cells = state.shape
    out = jax.ShapeDtypeStruct((LINES, R_NEAR, cells), jnp.float32)
    tail = min(R_NEAR // EIGHT, rows // EIGHT - 1)
    state = in_hbm(state)
    return pl.pallas_call(
        functools.partial(near_kernel, dtheta, rows),
        grid_spec=pltpu.PrefetchScalarGridSpec(
            num_scalar_prefetch=1,
            grid=(1,),
            in_specs=[
                whole(fields, planes, R_NEAR, cells),
                pl.BlockSpec((fields, planes, EIGHT, cells), lambda i, s: (0, 0, tail, 0)),
                whole(LINES, cells),
                whole(LINES, cells),
                whole(fields, R_NEAR, cells),
                whole(fields, R_NEAR, cells),
                whole(R_NEAR, LANES),
                whole(R_NEAR, LANES),
                whole(R_NEAR, LANES),
                whole(*solve.shape),
                ANY,
            ],
            out_specs=[
                whole(LINES, R_NEAR, cells),
                whole(LINES, R_NEAR, cells),
                whole(R_NEAR, LANES),
            ],
            scratch_shapes=[flux_scratch(R_NEAR, cells)],
        ),
        out_shape=[out, out, jax.ShapeDtypeStruct((R_NEAR, LANES), jnp.float32)],
        compiler_params=PARAMS,
        cost_estimate=cost(LINES * R_NEAR * cells * 200, LINES * R_NEAR * cells * 20),
        name="near",
    )(flags, state, state, low, high, inner, outer, edge, factor, table, solve, token)


def finish(flags, factor, rhs, local, carry, table, held):
    _, _, cells = rhs.shape
    return pl.pallas_call(
        finish_kernel,
        grid_spec=pltpu.PrefetchScalarGridSpec(
            num_scalar_prefetch=1,
            grid=(1,),
            in_specs=[
                whole(R_NEAR, LANES),
                whole(LINES, R_NEAR, cells),
                whole(LINES, R_NEAR, cells),
                whole(R_NEAR, LANES),
                whole(R_NEAR, LANES),
                ANY,
            ],
            out_specs=whole(FIELDS, PLANES, R_NEAR, cells),
        ),
        out_shape=pltpu.HBM(held.shape, jnp.float32),
        input_output_aliases={6: 0},
        compiler_params=PARAMS,
        cost_estimate=cost(LINES * R_NEAR * cells * 10, LINES * R_NEAR * cells * 20),
        name="finish",
    )(flags, factor, rhs, local, carry, table, held)


def chunks(rows):
    units = (rows - R_NEAR) // 16
    cuts = [3, 3 + (units - 6) // 2, units - 3, units] if units > 7 else [units]
    ends = [R_NEAR + 16 * c for c in cuts]
    return list(zip([R_NEAR] + ends[:-1], ends))


def smoothing_table(coarsen, cells, total_cells, dtheta):
    factor = coarsen.astype(jnp.float32)[:, None]
    stiffness = KAPPA / (factor * dtheta) ** 2
    inverse_half = 0.5 / stiffness
    one_minus = jnp.sqrt(inverse_half * (2.0 + inverse_half)) - inverse_half
    log_ratio = jnp.log1p(-one_minus)
    gain = (1.0 - one_minus) / (stiffness * one_minus * (2.0 - one_minus))
    closing = 1.0 / -jnp.expm1((total_cells / factor) * log_ratio)
    across = jnp.exp((cells / factor) * log_ratio)
    column = jnp.arange(LANES, dtype=jnp.int32)[None, :]
    width = jnp.left_shift(1, jnp.minimum(column, 20)).astype(jnp.float32)
    table = jnp.where(width >= factor, jnp.exp(log_ratio * (width / factor)), 0.0)
    table = jnp.where(column == COL_LOG, log_ratio, table)
    table = jnp.where(column == COL_GAIN, gain, table)
    return table, closing, across


def piece_tables(dtheta):
    tables = []
    for level in range(FMAX.bit_length()):
        width = 1 << level
        half = 0.5 * (width * dtheta) ** 2 / KAPPA
        ratio = 1.0 - (math.sqrt(half * (2.0 + half)) - half)
        block = np.arange(LANES) // width
        tables.append(ratio ** np.abs(block[:, None] - block[None, :]) / width)
    return jnp.asarray(np.concatenate(tables, axis=1), jnp.float32)


def ring(value, axis, shift):
    size = lax.axis_size(axis)
    return lax.ppermute(value, axis, [(i, (i + shift) % size) for i in range(size)])


def body(state, coarsen):
    fields, planes, rows, cells = state.shape
    sec_count = lax.axis_size("sec")
    rad_count = lax.axis_size("rad")
    ax_count = lax.axis_size("ax")
    assert fields == FIELDS and planes == PLANES and ax_count % 2 == 0
    rad_index = lax.axis_index("rad")
    ax_index = lax.axis_index("ax")
    total_cells = cells * sec_count
    dtheta = 2.0 * math.pi / total_cells
    outer_pairs = []
    for i in range(1, ax_count - 1, 2):
        outer_pairs += [(i, i + 1), (i + 1, i)]
    inner_pairs = []
    for i in range(0, ax_count, 2):
        inner_pairs += [(i, i + 1), (i + 1, i)]
    up = [(i, i + 1) for i in range(rad_count - 1)]
    down = [(i + 1, i) for i in range(rad_count - 1)]
    flags = jnp.stack(
        [
            ax_index % 2,
            ((ax_index > 0) & (ax_index < ax_count - 1)).astype(jnp.int32),
            (rad_index == 0).astype(jnp.int32),
            (rad_index == rad_count - 1).astype(jnp.int32),
            rad_index * rows,
        ]
    ).astype(jnp.int32)
    spans = chunks(rows)
    count = len(spans)

    part, low, high = pack_first(state, spans[0][1])
    outer = [lax.ppermute(part, "ax", outer_pairs)]
    columns, *rest = pack_edges(state, spans[1:], high)
    low = lax.ppermute(low, "rad", up)
    high = lax.ppermute(high, "rad", down)
    outer += [lax.ppermute(part, "ax", outer_pairs) for part in rest]
    if sec_count == 2:
        edge = ring(columns, "sec", 1)
    else:
        from_left = jnp.arange(LANES)[None, :] % 4 < 2
        edge = jnp.where(from_left, ring(columns, "sec", 1), ring(columns, "sec", -1))

    parts = pack_rest(state, [(0, R_NEAR)] + spans, low, high, edge)
    near_inner, *inner = [lax.ppermute(value, "ax", inner_pairs) for value in parts]

    table, closing, across = smoothing_table(coarsen, cells, total_cells, dtheta)
    factor = jnp.broadcast_to(coarsen.astype(jnp.float32)[:, None], (R_NEAR, LANES))
    solve = piece_tables(dtheta)
    rhs, local, ends = near(
        flags,
        state,
        low,
        high,
        near_inner,
        edge,
        dtheta,
        outer[0],
        factor,
        table,
        solve,
        parts[0],
    )
    arrived = [ends] + [ring(ends, "sec", k) for k in range(1, sec_count)] + [ends]
    from_left = jnp.arange(LANES)[None, :] < LINES
    carry = jnp.zeros_like(ends)
    for k in range(sec_count, 0, -1):
        carry = carry * across + jnp.where(from_left, arrived[k], arrived[sec_count - k])
    carry = carry * closing

    def pass_over(k, held, **more):
        span = spans[k]
        block = (span[1] - span[0]) // 2
        return bulk(flags, state, low, high, inner[k], edge, dtheta, span, block, ends, held, **more)

    out = pass_over(0, None, outer=outer[0])
    count = len(spans)
    for k in range(1, count - 1):
        if k == count - 2:
            out = pass_over(-1, out)
            out = finish(flags, factor, rhs, local, carry, table, out)
        out = pass_over(k, out, outer=outer[k], origin=spans[k][0])
    if count == 1:
        return finish(flags, factor, rhs, local, carry, table, out)
    return add_outer(flags, outer[-1], spans[-1], 24, out)


def solution(mesh):
    return jax.shard_map(
        body,
        mesh=mesh,
        in_specs=(P(None, "ax", "rad", "sec"), P()),
        out_specs=P(None, "ax", "rad", "sec"),
        check_vma=False,
    )
```

```python
import functools
import math

import jax
import jax.numpy as jnp
import numpy as np
from jax import lax
from jax.experimental import pallas as pl
from jax.experimental.pallas import tpu as pltpu
from jax.sharding import PartitionSpec as P

R_NEAR = 16
FMAX = 16

GAMMA = 1.4
KAPPA = 1.44

FIELDS = 5
PLANES = 2
LINES = FIELDS * PLANES
EIGHT = 8
LANES = 128
VMEM_LIMIT = 28 * 1024 * 1024

COL_LOG = 32
COL_GAIN = 33

ODD, OUTER, FIRST, LAST, BASE = range(5)


def plane_of(odd, q):
    return odd if q else 1 - odd


def reciprocal(x):
    y = pl.reciprocal(x, approx=True)
    y = y * (2.0 - x * y)
    return y * (2.0 - x * y)


def fluxes(fields, want):
    density, energy = fields[0], fields[4]
    momentum = fields[1:4]
    inverse = reciprocal(density)
    velocity = [m * inverse for m in momentum]
    square = {}
    for i in range(3):
        for j in range(i, 3):
            if i == j or i + 1 in want or j + 1 in want or (i, j) == (1, 2):
                square[i, j] = square[j, i] = momentum[i] * velocity[j]
    pressure = (GAMMA - 1.0) * (energy - 0.5 * (square[0, 0] + square[1, 1] + square[2, 2]))
    enthalpy = energy + pressure
    out = {}
    for d in want:
        k = d - 1
        flow = [square[i, k] + pressure if i == k else square[i, k] for i in range(3)]
        out[d] = [momentum[k]] + flow + [enthalpy * velocity[k]]
    return out, (pressure, square[2, 2], square[1, 2])


def flux_along(fields, along):
    return fluxes(fields, (along,))[0][along]


def outer_flux(flags, outer):
    present = flags[OUTER] == 1
    outer = [jnp.where(present, outer[0], 1.0)] + [jnp.where(present, g, 0.0) for g in outer[1:]]
    return flux_along(outer, 1)


def stencil(
    flags, first_row, rows, total_rows, dtheta, load, next_rows, edge, inner, outer, place, radial, azimuthal
):
    strips = rows // EIGHT
    pieces = radial.shape[2]
    row = lax.broadcasted_iota(jnp.int32, (EIGHT, 1), 0)
    lane = lax.broadcasted_iota(jnp.int32, (EIGHT, LANES), 1)
    start = flags[BASE] + first_row
    axial_sign = jnp.where(flags[ODD] == 1, 0.5, -0.5)
    above = jnp.where((flags[FIRST] == 1) & (first_row == 0), 0.0, (start - 1).astype(jnp.float32) + 0.5)
    end = first_row + rows == total_rows
    below = jnp.where((flags[LAST] == 1) & end, 0.0, (start + rows).astype(jnp.float32) + 0.5)
    scale = jnp.where(row >= EIGHT // 2, above, below)
    at = [slice(b * LANES, (b + 1) * LANES) for b in range(pieces)]

    for q in range(PLANES):
        for b in range(pieces):
            values = [next_rows(f, q, at[b]) for f in range(FIELDS)]
            values[0] = jnp.where(scale > 0.0, values[0], 1.0)
            flux_next = flux_along(values, 2)
            for f in range(FIELDS):
                radial[q, f, b, 0:EIGHT, :] = flux_next[f] * scale
                radial[q, f, b, EIGHT + rows : 2 * EIGHT + rows, :] = flux_next[f] * scale

    def inside(t, carry):
        r = pl.multiple_of(EIGHT * t, EIGHT)
        radius = (start + r + row).astype(jnp.float32) + 0.5
        inv_radius = 1.0 / radius
        for b in range(pieces):
            beside = flux_along([inner(f, r, at[b]) for f in range(FIELDS)], 1)
            axial, source = [], []
            for q in range(PLANES):
                fields = [load(f, q, r, at[b]) for f in range(FIELDS)]
                flow, (pressure, twist, swirl) = fluxes(fields, (1, 2, 3))
                axial.append(flow[1])
                for f in range(FIELDS):
                    radial[q, f, b, pl.ds(r + EIGHT, EIGHT), :] = flow[2][f] * radius
                    azimuthal[q, f, b, pl.ds(r, EIGHT), :] = flow[3][f]
                source.append(((pressure + twist) * inv_radius, swirl * -inv_radius))
            base = [[axial_sign * (x - y) for x, y in zip(beside, axial[1])]]
            if outer is None:
                base.append([axial_sign * x for x in axial[0]])
            else:
                far = outer_flux(flags, [outer(f, r, at[b]) for f in range(FIELDS)])
                base.append([axial_sign * (x - y) for x, y in zip(axial[0], far)])
            for q in range(PLANES):
                base[q][2] = base[q][2] + source[q][0]
                base[q][3] = base[q][3] + source[q][1]
                for f in range(FIELDS):
                    place(f, q, r)[:, at[b]] = base[q][f]
        return carry

    lax.fori_loop(0, strips, inside, 0)

    def differences(t, carry):
        r = pl.multiple_of(EIGHT * t, EIGHT)
        radius = (start + r + row).astype(jnp.float32) + 0.5
        half_inv = 0.5 / radius
        half_arc = half_inv * (1.0 / dtheta)
        beyond = [edge(r)] + [pltpu.roll(edge(r), LANES - 4 * f, 1) for f in range(1, FIELDS)]
        beyond = flux_along(beyond, 3)
        for q in range(PLANES):
            for f in range(FIELDS):
                ends = [pltpu.roll(beyond[f], s, 1) if q else beyond[f] for s in (LANES - 1, 1)]
                here = [azimuthal[q, f, b, pl.ds(r, EIGHT), :] for b in range(pieces)]
                left = [ends[0]] + [pltpu.roll(x, 1, 1) for x in here]
                right = [pltpu.roll(x, LANES - 1, 1) for x in here] + [ends[1]]
                out = place(f, q, r)
                for b in range(pieces):
                    behind = jnp.where(lane == 0, left[b], left[b + 1])
                    ahead = jnp.where(lane == LANES - 1, right[b + 1], right[b])
                    up = radial[q, f, b, pl.ds(r + EIGHT - 1, EIGHT), :]
                    down = radial[q, f, b, pl.ds(r + EIGHT + 1, EIGHT), :]
                    change = (behind - ahead) * half_arc + (up - down) * half_inv
                    out[:, at[b]] = out[:, at[b]] + change
        return carry

    lax.fori_loop(0, strips, differences, 0)


def bulk_kernel(
    dtheta, rows, first, total_rows, flags, state, before, after, low, high, inner, edge, outer, token, held, out, *scratch
):
    odd = flags[ODD]
    step = pl.program_id(0)
    first_row = first + step * rows
    at_end = first_row + rows == total_rows
    sub = lax.broadcasted_iota(jnp.int32, (EIGHT, LANES), 0)

    def load(f, q, r, at):
        return state[f, plane_of(odd, q), pl.ds(r, EIGHT), at]

    def next_rows(f, q, at):
        p, k = plane_of(odd, q), f * PLANES + q
        under = jnp.where(at_end, high[k : k + 1, at], after[f, p, :, at])
        return jnp.where(sub >= EIGHT // 2, before[f, p, :, at], under)

    stencil(
        flags,
        first_row,
        rows,
        total_rows,
        dtheta,
        load,
        next_rows,
        lambda r: edge[pl.ds(r, EIGHT), :],
        lambda f, r, at: inner[f, pl.ds(r, EIGHT), at],
        lambda f, r, at: outer[f, pl.ds(r, EIGHT), at],
        lambda f, q, r: out.at[f, plane_of(odd, q), pl.ds(r, EIGHT), :],
        *scratch,
    )


def near_kernel(
    dtheta,
    total_rows,
    part_first,
    flags,
    state,
    after,
    low,
    high,
    inner,
    outer,
    edge,
    factor,
    table,
    solve,
    token,
    hbm,
    rhs,
    local,
    carry,
    *rest,
):
    cells = state.shape[-1]
    odd = flags[ODD]
    part = rest[0] if len(rest) > 2 else None
    scratch = rest[-2:] if part is None else rest[-3:-1]
    if part is not None:
        source = hbm.at[:, lax.axis_index("ax") % 2, part_first : part_first + part.shape[1], :]
        copy = pltpu.make_async_copy(source, part, rest[-1])
        copy.start()

    sub = lax.broadcasted_iota(jnp.int32, (EIGHT, LANES), 0)

    def next_rows(f, q, at):
        k = f * PLANES + q
        under = high[k : k + 1, at] if total_rows == R_NEAR else after[f, plane_of(odd, q), :, at]
        return jnp.where(sub >= EIGHT // 2, low[k : k + 1, at], under)

    stencil(
        flags,
        0,
        R_NEAR,
        total_rows,
        dtheta,
        lambda f, q, r, at: state[f, plane_of(odd, q), pl.ds(r, EIGHT), at],
        next_rows,
        lambda r: edge[pl.ds(r, EIGHT), :],
        lambda f, r, at: inner[f, pl.ds(r, EIGHT), at],
        lambda f, r, at: outer[f, pl.ds(r, EIGHT), at],
        lambda f, q, r: rhs.at[f * PLANES + q, pl.ds(r, EIGHT), :],
        *scratch,
    )

    pieces = cells // LANES
    lane = lax.broadcasted_iota(jnp.int32, (R_NEAR, LANES), 1)
    width = factor[...]
    log_ratio = table[:, COL_LOG : COL_LOG + 1]
    block = jnp.floor((lane.astype(jnp.float32) + 0.5) / width)
    ahead_entry = jnp.exp(log_ratio * (block + 1.0))
    behind_entry = jnp.exp(log_ratio * (LANES / width - block))
    across = jnp.exp(log_ratio * (LANES / width))

    def line(k, ends):
        rows = jnp.concatenate([rhs[k, :, b * LANES : (b + 1) * LANES] for b in range(pieces)], axis=0)
        solved = jnp.dot(
            rows, solve[...], precision=lax.Precision.HIGHEST, preferred_element_type=jnp.float32
        )
        inside = []
        for b in range(pieces):
            mine = solved[b * R_NEAR : (b + 1) * R_NEAR]
            value = mine[:, :LANES]
            for level in range(1, FMAX.bit_length()):
                chosen = mine[:, level * LANES : (level + 1) * LANES]
                value = jnp.where(width == (1 << level), chosen, value)
            inside.append(value)
        total = list(inside)
        enter = jnp.zeros((R_NEAR, LANES), jnp.float32)
        for b in range(pieces):
            leave = jnp.broadcast_to(inside[b][:, LANES - 1 : LANES], (R_NEAR, LANES))
            total[b] = total[b] + ahead_entry * enter
            enter = leave + across * enter
        ends = jnp.where(lane == k, enter, ends)
        enter = jnp.zeros((R_NEAR, LANES), jnp.float32)
        for b in reversed(range(pieces)):
            leave = jnp.broadcast_to(inside[b][:, 0:1], (R_NEAR, LANES))
            total[b] = total[b] + behind_entry * enter
            enter = leave + across * enter
        for b in range(pieces):
            local[k, :, b * LANES : (b + 1) * LANES] = total[b]
        return jnp.where(lane == k + LINES, enter, ends)

    carry[...] = lax.fori_loop(
        0, LINES, line, jnp.zeros((R_NEAR, LANES), jnp.float32)
    )
    if part is not None:
        copy.wait()


def finish_kernel(flags, factor, rhs, local, carry, table, held, out):
    cells = out.shape[-1]
    lane = lax.broadcasted_iota(jnp.int32, (R_NEAR, cells), 1).astype(jnp.float32)
    width = factor[:, 0:1]
    block = jnp.floor((lane + 0.5) / width)
    count = cells / width
    log_ratio = table[:, COL_LOG : COL_LOG + 1]
    gain = table[:, COL_GAIN : COL_GAIN + 1]
    from_left = jnp.exp(log_ratio * (block + 1.0))
    from_right = jnp.exp(log_ratio * (count - block))
    near = flags[FIRST] == 1
    for f in range(FIELDS):
        for q in range(PLANES):
            k = f * PLANES + q
            j = k + LINES
            smooth = gain * (
                local[k] + from_left * carry[:, k : k + 1] + from_right * carry[:, j : j + 1]
            )
            out[f, plane_of(flags[ODD], q)] = jnp.where(near, smooth, rhs[k])


def pack_first_kernel(count, state, part, low, high, top, bottom, sems):
    _, _, rows, _ = state.shape
    odd = lax.axis_index("ax") % 2
    copies = [
        pltpu.make_async_copy(state.at[:, odd, 0:count, :], part, sems.at[0]),
        pltpu.make_async_copy(state.at[:, :, rows - EIGHT : rows, :], top, sems.at[1]),
        pltpu.make_async_copy(state.at[:, :, 0:EIGHT, :], bottom, sems.at[2]),
    ]
    for copy in copies:
        copy.start()
    for copy in copies[1:]:
        copy.wait()
    for f in range(FIELDS):
        for q in range(PLANES):
            k = f * PLANES + q
            p = plane_of(odd, q)
            low[k : k + 1, :] = top[f, p, EIGHT - 1 : EIGHT, :]
            high[k : k + 1, :] = bottom[f, p, 0:1, :]
    copies[0].wait()


def pack_edges_kernel(state, token, edge, side, left, right, sems):
    _, _, rows, cells = state.shape
    odd = lax.axis_index("ax") % 2
    copies = [
        pltpu.make_async_copy(state.at[:, :, :, cells - LANES : cells], left, sems.at[0]),
        pltpu.make_async_copy(state.at[:, :, :, 0:LANES], right, sems.at[1]),
        pltpu.make_async_copy(state.at[:, 1 - odd, 0:R_NEAR, :], side, sems.at[2]),
    ]
    for copy in copies:
        copy.start()
    for copy in copies[:2]:
        copy.wait()
    lane = lax.broadcasted_iota(jnp.int32, (rows, LANES), 1)
    columns = jnp.ones((rows, LANES), jnp.float32)
    for f in range(FIELDS):
        for q in range(PLANES):
            p = plane_of(odd, q)
            columns = jnp.where(lane == 4 * f + q, left[f, p, :, LANES - 1 : LANES], columns)
            columns = jnp.where(lane == (4 * f - 1 - q) % LANES, right[f, p, :, 0:1], columns)
    edge[...] = columns
    copies[2].wait()


def pack_rest_kernel(parts, tokens, state, *rest):
    rest = rest[tokens:]
    odd = lax.axis_index("ax") % 2
    sems = rest[-1]
    copies = []
    for k, (q, first, last) in enumerate(parts):
        source = state.at[:, plane_of(odd, q), first:last, :]
        copies.append(pltpu.make_async_copy(source, rest[k], sems.at[k]))
    for copy in copies:
        copy.start()
    for copy in copies:
        copy.wait()


ANY = pl.BlockSpec(memory_space=pl.ANY)
PARAMS = pltpu.CompilerParams(vmem_limit_bytes=VMEM_LIMIT)


def whole(*shape):
    return pl.BlockSpec(shape, lambda i, s: (0,) * len(shape))


def rows_from(shape, axis, first, step):
    def place(i, s):
        row = (first // EIGHT + i * (step // EIGHT)) * EIGHT
        return tuple(row if d == axis else 0 for d in range(len(shape)))

    return pl.BlockSpec(tuple(pl.Element(n) for n in shape), place)


def in_hbm(value):
    return pltpu.with_memory_space_constraint(value, pltpu.HBM)


def cost(flops, nbytes):
    return pl.CostEstimate(flops=flops, bytes_accessed=nbytes, transcendentals=0)


def pack_first(state, count):
    fields, planes, _, cells = state.shape
    vmem = pl.BlockSpec(memory_space=pltpu.VMEM)
    row = jax.ShapeDtypeStruct((LINES, cells), jnp.float32)
    rows = pltpu.VMEM((fields, planes, EIGHT, cells), jnp.float32)
    return pl.pallas_call(
        functools.partial(pack_first_kernel, count),
        in_specs=[ANY],
        out_specs=[vmem, vmem, vmem],
        out_shape=[jax.ShapeDtypeStruct((fields, count, cells), jnp.float32), row, row],
        scratch_shapes=[rows, rows, pltpu.SemaphoreType.DMA((3,))],
        compiler_params=PARAMS,
        cost_estimate=cost(0, fields * count * cells * 8),
        name="pack_first",
    )(in_hbm(state))


def pack_edges(state, token):
    fields, planes, rows, cells = state.shape
    vmem = pl.BlockSpec(memory_space=pltpu.VMEM)
    tiles = pltpu.VMEM((fields, planes, rows, LANES), jnp.float32)
    return pl.pallas_call(
        pack_edges_kernel,
        in_specs=[ANY, ANY],
        out_specs=[vmem, vmem],
        out_shape=[
            jax.ShapeDtypeStruct((rows, LANES), jnp.float32),
            jax.ShapeDtypeStruct((fields, R_NEAR, cells), jnp.float32),
        ],
        scratch_shapes=[tiles, tiles, pltpu.SemaphoreType.DMA((3,))],
        compiler_params=PARAMS,
        cost_estimate=cost(0, fields * planes * rows * LANES * 16),
        name="pack_edges",
    )(in_hbm(state), token)


def pack_rest(state, parts, *tokens):
    fields, _, _, cells = state.shape
    shapes = [jax.ShapeDtypeStruct((fields, last - first, cells), jnp.float32) for _, first, last in parts]
    return pl.pallas_call(
        functools.partial(pack_rest_kernel, parts, len(tokens)),
        in_specs=[ANY] * (1 + len(tokens)),
        out_specs=[pl.BlockSpec(memory_space=pltpu.VMEM)] * len(shapes),
        out_shape=shapes,
        scratch_shapes=[pltpu.SemaphoreType.DMA((len(parts),))],
        compiler_params=PARAMS,
        cost_estimate=cost(0, sum(math.prod(x.shape) for x in shapes) * 8),
        name="pack_rest",
    )(in_hbm(state), *tokens)


def flux_scratch(rows, cells):
    shape = (PLANES, FIELDS, cells // LANES)
    return [pltpu.VMEM((*shape, n, LANES), jnp.float32) for n in (rows + 2 * EIGHT, rows)]


def bulk(flags, state, low, high, inner, edge, dtheta, outer, span, first, rows, token, held):
    fields, planes, total_rows, cells = state.shape
    end = span[1]
    tail = total_rows // EIGHT - 1
    eights = rows // EIGHT
    at = first // EIGHT
    row_block = (fields, planes, EIGHT, cells)
    in_specs = [
        rows_from((fields, planes, rows, cells), 2, first, rows),
        pl.BlockSpec(row_block, lambda i, s: (0, 0, at + i * eights - 1, 0)),
        pl.BlockSpec(row_block, lambda i, s: (0, 0, jnp.minimum(at + (i + 1) * eights, tail), 0)),
        whole(LINES, cells),
        whole(LINES, cells),
        rows_from((fields, rows, cells), 1, 0, rows),
        rows_from((rows, LANES), 0, first, rows),
        rows_from((fields, rows, cells), 1, first - span[0], rows),
        ANY,
        ANY,
    ]
    state = in_hbm(state)
    operands = [state, state, state, low, high, inner, edge, outer]
    operands += [token, state if held is None else held]
    size = fields * planes * (end - first) * cells
    return pl.pallas_call(
        functools.partial(bulk_kernel, dtheta, rows, first, total_rows),
        grid_spec=pltpu.PrefetchScalarGridSpec(
            num_scalar_prefetch=1,
            grid=((end - first) // rows,),
            in_specs=in_specs,
            out_specs=rows_from((fields, planes, rows, cells), 2, first, rows),
            scratch_shapes=flux_scratch(rows, cells),
        ),
        out_shape=pltpu.HBM(state.shape, jnp.float32),
        input_output_aliases={} if held is None else {len(operands): 0},
        compiler_params=PARAMS,
        cost_estimate=cost(size * 60, size * 60),
        name="bulk",
    )(flags, *operands)


def near(flags, state, low, high, inner, edge, dtheta, outer, factor, table, solve, token, part=None):
    fields, planes, rows, cells = state.shape
    out = jax.ShapeDtypeStruct((LINES, R_NEAR, cells), jnp.float32)
    tail = min(R_NEAR // EIGHT, rows // EIGHT - 1)
    state = in_hbm(state)
    out_specs = [whole(LINES, R_NEAR, cells), whole(LINES, R_NEAR, cells), whole(R_NEAR, LANES)]
    out_shape = [out, out, jax.ShapeDtypeStruct((R_NEAR, LANES), jnp.float32)]
    scratch = flux_scratch(R_NEAR, cells)
    if part is not None:
        out_specs.append(whole(fields, part[1] - part[0], cells))
        out_shape.append(jax.ShapeDtypeStruct((fields, part[1] - part[0], cells), jnp.float32))
        scratch.append(pltpu.SemaphoreType.DMA)
    result = pl.pallas_call(
        functools.partial(near_kernel, dtheta, rows, part[0] if part else 0),
        grid_spec=pltpu.PrefetchScalarGridSpec(
            num_scalar_prefetch=1,
            grid=(1,),
            in_specs=[
                whole(fields, planes, R_NEAR, cells),
                pl.BlockSpec((fields, planes, EIGHT, cells), lambda i, s: (0, 0, tail, 0)),
                whole(LINES, cells),
                whole(LINES, cells),
                whole(fields, R_NEAR, cells),
                whole(fields, R_NEAR, cells),
                whole(R_NEAR, LANES),
                whole(R_NEAR, LANES),
                whole(R_NEAR, LANES),
                whole(*solve.shape),
                ANY,
                ANY,
            ],
            out_specs=out_specs,
            scratch_shapes=scratch,
        ),
        out_shape=out_shape,
        compiler_params=PARAMS,
        cost_estimate=cost(LINES * R_NEAR * cells * 200, LINES * R_NEAR * cells * 250),
        name="near",
    )(flags, state, state, low, high, inner, outer, edge, factor, table, solve, token, state)
    return result if part is not None else (*result, None)


def finish(flags, factor, rhs, local, carry, table, held):
    _, _, cells = rhs.shape
    return pl.pallas_call(
        finish_kernel,
        grid_spec=pltpu.PrefetchScalarGridSpec(
            num_scalar_prefetch=1,
            grid=(1,),
            in_specs=[
                whole(R_NEAR, LANES),
                whole(LINES, R_NEAR, cells),
                whole(LINES, R_NEAR, cells),
                whole(R_NEAR, LANES),
                whole(R_NEAR, LANES),
                ANY,
            ],
            out_specs=whole(FIELDS, PLANES, R_NEAR, cells),
        ),
        out_shape=pltpu.HBM(held.shape, jnp.float32),
        input_output_aliases={6: 0},
        compiler_params=PARAMS,
        cost_estimate=cost(LINES * R_NEAR * cells * 10, LINES * R_NEAR * cells * 20),
        name="finish",
    )(flags, factor, rhs, local, carry, table, held)


def chunks(rows):
    size = 24 if (rows - R_NEAR) % 48 == 0 else EIGHT
    pairs = (rows - R_NEAR) // (2 * size)
    cuts = sorted({-(-2 * pairs // 5), -(-4 * pairs // 5), pairs})
    ends = [R_NEAR + 2 * size * c for c in cuts]
    return size, list(zip([0] + ends[:-1], ends))


def smoothing_table(coarsen, cells, total_cells, dtheta):
    factor = coarsen.astype(jnp.float32)[:, None]
    stiffness = KAPPA / (factor * dtheta) ** 2
    inverse_half = 0.5 / stiffness
    one_minus = jnp.sqrt(inverse_half * (2.0 + inverse_half)) - inverse_half
    log_ratio = jnp.log1p(-one_minus)
    gain = (1.0 - one_minus) / (stiffness * one_minus * (2.0 - one_minus))
    closing = 1.0 / -jnp.expm1((total_cells / factor) * log_ratio)
    across = jnp.exp((cells / factor) * log_ratio)
    column = jnp.arange(LANES, dtype=jnp.int32)[None, :]
    width = jnp.left_shift(1, jnp.minimum(column, 20)).astype(jnp.float32)
    table = jnp.where(width >= factor, jnp.exp(log_ratio * (width / factor)), 0.0)
    table = jnp.where(column == COL_LOG, log_ratio, table)
    table = jnp.where(column == COL_GAIN, gain, table)
    return table, closing, across


def piece_tables(dtheta):
    tables = []
    for level in range(FMAX.bit_length()):
        width = 1 << level
        half = 0.5 * (width * dtheta) ** 2 / KAPPA
        ratio = 1.0 - (math.sqrt(half * (2.0 + half)) - half)
        block = np.arange(LANES) // width
        tables.append(ratio ** np.abs(block[:, None] - block[None, :]) / width)
    return jnp.asarray(np.concatenate(tables, axis=1), jnp.float32)


def ring(value, axis, shift):
    size = lax.axis_size(axis)
    return lax.ppermute(value, axis, [(i, (i + shift) % size) for i in range(size)])


def body(state, coarsen):
    fields, planes, rows, cells = state.shape
    sec_count = lax.axis_size("sec")
    rad_count = lax.axis_size("rad")
    ax_count = lax.axis_size("ax")
    assert fields == FIELDS and planes == PLANES and ax_count % 2 == 0
    rad_index = lax.axis_index("rad")
    ax_index = lax.axis_index("ax")
    total_cells = cells * sec_count
    dtheta = 2.0 * math.pi / total_cells
    outer_pairs = []
    for i in range(1, ax_count - 1, 2):
        outer_pairs += [(i, i + 1), (i + 1, i)]
    inner_pairs = []
    for i in range(0, ax_count, 2):
        inner_pairs += [(i, i + 1), (i + 1, i)]
    up = [(i, i + 1) for i in range(rad_count - 1)]
    down = [(i + 1, i) for i in range(rad_count - 1)]
    flags = jnp.stack(
        [
            ax_index % 2,
            ((ax_index > 0) & (ax_index < ax_count - 1)).astype(jnp.int32),
            (rad_index == 0).astype(jnp.int32),
            (rad_index == rad_count - 1).astype(jnp.int32),
            rad_index * rows,
        ]
    ).astype(jnp.int32)
    size, spans = chunks(rows)
    count = len(spans)

    part, low, high = pack_first(state, spans[0][1])
    outer = [lax.ppermute(part, "ax", outer_pairs)]
    columns, side = pack_edges(state, high)
    low = lax.ppermute(low, "rad", up)
    high = lax.ppermute(high, "rad", down)
    inner = [lax.ppermute(side, "ax", inner_pairs)]
    wanted = [(0, R_NEAR, spans[0][1])] + [(0, *span) for span in spans[1:]]
    if count > 1:
        wanted.insert(1, (1, *spans[1]))
    parts = pack_rest(state, wanted, columns, low, high)
    for k, value in enumerate(parts):
        if wanted[k][0]:
            outer.append(lax.ppermute(value, "ax", outer_pairs))
        else:
            inner.append(lax.ppermute(value, "ax", inner_pairs))
    if sec_count == 2:
        edge = ring(columns, "sec", 1)
    else:
        from_left = jnp.arange(LANES)[None, :] % 4 < 2
        edge = jnp.where(from_left, ring(columns, "sec", 1), ring(columns, "sec", -1))

    table, closing, across = smoothing_table(coarsen, cells, total_cells, dtheta)
    factor = jnp.broadcast_to(coarsen.astype(jnp.float32)[:, None], (R_NEAR, LANES))

    solve = piece_tables(dtheta)
    given = (flags, state, low, high)
    part = spans[2] if count > 2 else None
    rhs, local, ends, part = near(
        *given, inner[0], edge, dtheta, outer[0], factor, table, solve, parts[0], part
    )
    if part is not None:
        outer.append(lax.ppermute(part, "ax", outer_pairs))
    arrived = [ends] + [ring(ends, "sec", k) for k in range(1, sec_count)] + [ends]
    from_left = jnp.arange(LANES)[None, :] < LINES
    carry = jnp.zeros_like(ends)
    for k in range(sec_count, 0, -1):
        carry = carry * across + jnp.where(from_left, arrived[k], arrived[sec_count - k])
    carry = carry * closing

    out = None
    for k in range(count):
        first = spans[k][0] if k else R_NEAR
        if k == count - 1 and k:
            out = finish(flags, factor, rhs, local, carry, table, out)
        out = bulk(*given, inner[k + 1], edge, dtheta, outer[k], spans[k], first, size, ends, out)
    return out if count > 1 else finish(flags, factor, rhs, local, carry, table, out)


def solution(mesh):
    return jax.shard_map(
        body,
        mesh=mesh,
        in_specs=(P(None, "ax", "rad", "sec"), P()),
        out_specs=P(None, "ax", "rad", "sec"),
        check_vma=False,
    )
```

```python
import functools
import math

import jax
import jax.numpy as jnp
import numpy as np
from jax import lax
from jax.experimental import pallas as pl
from jax.experimental.pallas import tpu as pltpu
from jax.sharding import PartitionSpec as P

R_NEAR = 16
FMAX = 16

GAMMA = 1.4
KAPPA = 1.44

FIELDS = 5
PLANES = 2
LINES = FIELDS * PLANES
EIGHT = 8
LANES = 128
VMEM_LIMIT = 28 * 1024 * 1024

COL_LOG = 32
COL_GAIN = 33

ODD, OUTER, FIRST, LAST, BASE = range(5)


def plane_of(odd, q):
    return odd if q else 1 - odd


def reciprocal(x):
    y = pl.reciprocal(x, approx=True)
    y = y * (2.0 - x * y)
    return y * (2.0 - x * y)


def fluxes(fields, want):
    density, energy = fields[0], fields[4]
    momentum = fields[1:4]
    inverse = reciprocal(density)
    velocity = [m * inverse for m in momentum]
    square = {}
    for i in range(3):
        for j in range(i, 3):
            if i == j or i + 1 in want or j + 1 in want or (i, j) == (1, 2):
                square[i, j] = square[j, i] = momentum[i] * velocity[j]
    pressure = (GAMMA - 1.0) * (energy - 0.5 * (square[0, 0] + square[1, 1] + square[2, 2]))
    enthalpy = energy + pressure
    out = {}
    for d in want:
        k = d - 1
        flow = [square[i, k] + pressure if i == k else square[i, k] for i in range(3)]
        out[d] = [momentum[k]] + flow + [enthalpy * velocity[k]]
    return out, (pressure, square[2, 2], square[1, 2])


def flux_along(fields, along):
    return fluxes(fields, (along,))[0][along]


def outer_flux(flags, outer):
    present = flags[OUTER] == 1
    outer = [jnp.where(present, outer[0], 1.0)] + [jnp.where(present, g, 0.0) for g in outer[1:]]
    return flux_along(outer, 1)


def stencil(
    flags, first_row, rows, total_rows, dtheta, load, next_rows, edge, inner, outer, place, radial, azimuthal
):
    strips = rows // EIGHT
    pieces = radial.shape[2]
    row = lax.broadcasted_iota(jnp.int32, (EIGHT, 1), 0)
    lane = lax.broadcasted_iota(jnp.int32, (EIGHT, LANES), 1)
    start = flags[BASE] + first_row
    axial_sign = jnp.where(flags[ODD] == 1, 0.5, -0.5)
    above = jnp.where((flags[FIRST] == 1) & (first_row == 0), 0.0, (start - 1).astype(jnp.float32) + 0.5)
    end = first_row + rows == total_rows
    below = jnp.where((flags[LAST] == 1) & end, 0.0, (start + rows).astype(jnp.float32) + 0.5)
    scale = jnp.where(row >= EIGHT // 2, above, below)
    at = [slice(b * LANES, (b + 1) * LANES) for b in range(pieces)]

    for q in range(PLANES):
        for b in range(pieces):
            values = [next_rows(f, q, at[b]) for f in range(FIELDS)]
            values[0] = jnp.where(scale > 0.0, values[0], 1.0)
            flux_next = flux_along(values, 2)
            for f in range(FIELDS):
                radial[q, f, b, 0:EIGHT, :] = flux_next[f] * scale
                radial[q, f, b, EIGHT + rows : 2 * EIGHT + rows, :] = flux_next[f] * scale

    def inside(t, carry):
        r = pl.multiple_of(EIGHT * t, EIGHT)
        radius = (start + r + row).astype(jnp.float32) + 0.5
        inv_radius = 1.0 / radius
        for b in range(pieces):
            beside = flux_along([inner(f, r, at[b]) for f in range(FIELDS)], 1)
            axial, source = [], []
            for q in range(PLANES):
                fields = [load(f, q, r, at[b]) for f in range(FIELDS)]
                flow, (pressure, twist, swirl) = fluxes(fields, (1, 2, 3))
                axial.append(flow[1])
                for f in range(FIELDS):
                    radial[q, f, b, pl.ds(r + EIGHT, EIGHT), :] = flow[2][f] * radius
                    azimuthal[q, f, b, pl.ds(r, EIGHT), :] = flow[3][f]
                source.append(((pressure + twist) * inv_radius, swirl * -inv_radius))
            base = [[axial_sign * (x - y) for x, y in zip(beside, axial[1])]]
            if outer is None:
                base.append([axial_sign * x for x in axial[0]])
            else:
                far = outer_flux(flags, [outer(f, r, at[b]) for f in range(FIELDS)])
                base.append([axial_sign * (x - y) for x, y in zip(axial[0], far)])
            for q in range(PLANES):
                base[q][2] = base[q][2] + source[q][0]
                base[q][3] = base[q][3] + source[q][1]
                for f in range(FIELDS):
                    place(f, q, r)[:, at[b]] = base[q][f]
        return carry

    lax.fori_loop(0, strips, inside, 0)

    def differences(t, carry):
        r = pl.multiple_of(EIGHT * t, EIGHT)
        radius = (start + r + row).astype(jnp.float32) + 0.5
        half_inv = 0.5 / radius
        half_arc = half_inv * (1.0 / dtheta)
        beyond = [edge(r)] + [pltpu.roll(edge(r), LANES - 4 * f, 1) for f in range(1, FIELDS)]
        beyond = flux_along(beyond, 3)
        for q in range(PLANES):
            for f in range(FIELDS):
                ends = [pltpu.roll(beyond[f], s, 1) if q else beyond[f] for s in (LANES - 1, 1)]
                here = [azimuthal[q, f, b, pl.ds(r, EIGHT), :] for b in range(pieces)]
                left = [ends[0]] + [pltpu.roll(x, 1, 1) for x in here]
                right = [pltpu.roll(x, LANES - 1, 1) for x in here] + [ends[1]]
                out = place(f, q, r)
                for b in range(pieces):
                    behind = jnp.where(lane == 0, left[b], left[b + 1])
                    ahead = jnp.where(lane == LANES - 1, right[b + 1], right[b])
                    up = radial[q, f, b, pl.ds(r + EIGHT - 1, EIGHT), :]
                    down = radial[q, f, b, pl.ds(r + EIGHT + 1, EIGHT), :]
                    change = (behind - ahead) * half_arc + (up - down) * half_inv
                    out[:, at[b]] = out[:, at[b]] + change
        return carry

    lax.fori_loop(0, strips, differences, 0)


def bulk_kernel(
    dtheta, rows, span, origin, total_rows, flags, state, low, high, inner, edge, outer, token, held, out, *scratch
):
    first, end = span
    blocks = (end - first) // rows
    state_rows, inner_rows, outer_rows, sems, *fluxes_scratch = scratch
    odd = flags[ODD]
    step = pl.program_id(0)

    def copies(k):
        a = first + k * rows + (EIGHT if k else -EIGHT)
        b = min(first + (k + 1) * rows + EIGHT, total_rows)
        at = a - first + EIGHT
        rest = pl.ds(first - origin + k * rows, rows)
        here = pl.ds(k * rows, rows)
        return [
            pltpu.make_async_copy(
                state.at[:, :, a:b, :], state_rows.at[:, :, at : at + b - a, :], sems.at[3 * k]
            ),
            pltpu.make_async_copy(inner.at[:, here, :], inner_rows.at[:, here, :], sems.at[3 * k + 1]),
            pltpu.make_async_copy(outer.at[:, rest, :], outer_rows.at[:, here, :], sems.at[3 * k + 2]),
        ]

    @pl.when(step == 0)
    def _():
        for k in range(blocks):
            for copy in copies(k):
                copy.start()

    for k in range(blocks):

        @pl.when(step == k)
        def _():
            for copy in copies(k):
                copy.wait()

    first_row = first + step * rows
    at_end = first_row + rows == total_rows
    base = pl.multiple_of(step * rows, EIGHT)
    sub = lax.broadcasted_iota(jnp.int32, (EIGHT, LANES), 0)

    def load(f, q, r, at):
        return state_rows[f, plane_of(odd, q), pl.ds(base + EIGHT + r, EIGHT), at]

    def next_rows(f, q, at):
        k = f * PLANES + q
        under = jnp.where(at_end, high[k : k + 1, at], load(f, q, rows, at))
        return jnp.where(sub >= EIGHT // 2, load(f, q, -EIGHT, at), under)

    stencil(
        flags,
        first_row,
        rows,
        total_rows,
        dtheta,
        load,
        next_rows,
        lambda r: edge[pl.ds(r, EIGHT), :],
        lambda f, r, at: inner_rows[f, pl.ds(base + r, EIGHT), at],
        lambda f, r, at: outer_rows[f, pl.ds(base + r, EIGHT), at],
        lambda f, q, r: out.at[f, plane_of(odd, q), pl.ds(r, EIGHT), :],
        *fluxes_scratch,
    )


def near_kernel(
    dtheta,
    total_rows,
    part_first,
    flags,
    state,
    after,
    low,
    high,
    inner,
    outer,
    edge,
    factor,
    table,
    solve,
    token,
    hbm,
    rhs,
    local,
    carry,
    *rest,
):
    cells = state.shape[-1]
    odd = flags[ODD]
    part = rest[0] if len(rest) > 2 else None
    scratch = rest[-2:] if part is None else rest[-3:-1]
    if part is not None:
        source = hbm.at[:, lax.axis_index("ax") % 2, part_first : part_first + part.shape[1], :]
        copy = pltpu.make_async_copy(source, part, rest[-1])
        copy.start()

    sub = lax.broadcasted_iota(jnp.int32, (EIGHT, LANES), 0)

    def next_rows(f, q, at):
        k = f * PLANES + q
        under = high[k : k + 1, at] if total_rows == R_NEAR else after[f, plane_of(odd, q), :, at]
        return jnp.where(sub >= EIGHT // 2, low[k : k + 1, at], under)

    stencil(
        flags,
        0,
        R_NEAR,
        total_rows,
        dtheta,
        lambda f, q, r, at: state[f, plane_of(odd, q), pl.ds(r, EIGHT), at],
        next_rows,
        lambda r: edge[pl.ds(r, EIGHT), :],
        lambda f, r, at: inner[f, pl.ds(r, EIGHT), at],
        lambda f, r, at: outer[f, pl.ds(r, EIGHT), at],
        lambda f, q, r: rhs.at[f * PLANES + q, pl.ds(r, EIGHT), :],
        *scratch,
    )

    pieces = cells // LANES
    lane = lax.broadcasted_iota(jnp.int32, (R_NEAR, LANES), 1)
    width = factor[...]
    log_ratio = table[:, COL_LOG : COL_LOG + 1]
    block = jnp.floor((lane.astype(jnp.float32) + 0.5) / width)
    ahead_entry = jnp.exp(log_ratio * (block + 1.0))
    behind_entry = jnp.exp(log_ratio * (LANES / width - block))
    across = jnp.exp(log_ratio * (LANES / width))

    def line(k, ends):
        rows = jnp.concatenate([rhs[k, :, b * LANES : (b + 1) * LANES] for b in range(pieces)], axis=0)
        solved = jnp.dot(
            rows, solve[...], precision=lax.Precision.HIGHEST, preferred_element_type=jnp.float32
        )
        inside = []
        for b in range(pieces):
            mine = solved[b * R_NEAR : (b + 1) * R_NEAR]
            value = mine[:, :LANES]
            for level in range(1, FMAX.bit_length()):
                chosen = mine[:, level * LANES : (level + 1) * LANES]
                value = jnp.where(width == (1 << level), chosen, value)
            inside.append(value)
        total = list(inside)
        enter = jnp.zeros((R_NEAR, LANES), jnp.float32)
        for b in range(pieces):
            leave = jnp.broadcast_to(inside[b][:, LANES - 1 : LANES], (R_NEAR, LANES))
            total[b] = total[b] + ahead_entry * enter
            enter = leave + across * enter
        ends = jnp.where(lane == k, enter, ends)
        enter = jnp.zeros((R_NEAR, LANES), jnp.float32)
        for b in reversed(range(pieces)):
            leave = jnp.broadcast_to(inside[b][:, 0:1], (R_NEAR, LANES))
            total[b] = total[b] + behind_entry * enter
            enter = leave + across * enter
        for b in range(pieces):
            local[k, :, b * LANES : (b + 1) * LANES] = total[b]
        return jnp.where(lane == k + LINES, enter, ends)

    carry[...] = lax.fori_loop(
        0, LINES, line, jnp.zeros((R_NEAR, LANES), jnp.float32)
    )
    if part is not None:
        copy.wait()


def finish_kernel(flags, factor, rhs, local, carry, table, held, out):
    cells = out.shape[-1]
    lane = lax.broadcasted_iota(jnp.int32, (R_NEAR, cells), 1).astype(jnp.float32)
    width = factor[:, 0:1]
    block = jnp.floor((lane + 0.5) / width)
    count = cells / width
    log_ratio = table[:, COL_LOG : COL_LOG + 1]
    gain = table[:, COL_GAIN : COL_GAIN + 1]
    from_left = jnp.exp(log_ratio * (block + 1.0))
    from_right = jnp.exp(log_ratio * (count - block))
    near = flags[FIRST] == 1
    for f in range(FIELDS):
        for q in range(PLANES):
            k = f * PLANES + q
            j = k + LINES
            smooth = gain * (
                local[k] + from_left * carry[:, k : k + 1] + from_right * carry[:, j : j + 1]
            )
            out[f, plane_of(flags[ODD], q)] = jnp.where(near, smooth, rhs[k])


def pack_first_kernel(count, state, part, low, high, top, bottom, sems):
    _, _, rows, _ = state.shape
    odd = lax.axis_index("ax") % 2
    copies = [
        pltpu.make_async_copy(state.at[:, odd, 0:count, :], part, sems.at[0]),
        pltpu.make_async_copy(state.at[:, :, rows - EIGHT : rows, :], top, sems.at[1]),
        pltpu.make_async_copy(state.at[:, :, 0:EIGHT, :], bottom, sems.at[2]),
    ]
    for copy in copies:
        copy.start()
    for copy in copies[1:]:
        copy.wait()
    for f in range(FIELDS):
        for q in range(PLANES):
            k = f * PLANES + q
            p = plane_of(odd, q)
            low[k : k + 1, :] = top[f, p, EIGHT - 1 : EIGHT, :]
            high[k : k + 1, :] = bottom[f, p, 0:1, :]
    copies[0].wait()


def pack_edges_kernel(state, token, edge, side, left, right, sems):
    _, _, rows, cells = state.shape
    odd = lax.axis_index("ax") % 2
    copies = [
        pltpu.make_async_copy(state.at[:, :, :, cells - LANES : cells], left, sems.at[0]),
        pltpu.make_async_copy(state.at[:, :, :, 0:LANES], right, sems.at[1]),
        pltpu.make_async_copy(state.at[:, 1 - odd, 0:R_NEAR, :], side, sems.at[2]),
    ]
    for copy in copies:
        copy.start()
    for copy in copies[:2]:
        copy.wait()
    lane = lax.broadcasted_iota(jnp.int32, (rows, LANES), 1)
    columns = jnp.ones((rows, LANES), jnp.float32)
    for f in range(FIELDS):
        for q in range(PLANES):
            p = plane_of(odd, q)
            columns = jnp.where(lane == 4 * f + q, left[f, p, :, LANES - 1 : LANES], columns)
            columns = jnp.where(lane == (4 * f - 1 - q) % LANES, right[f, p, :, 0:1], columns)
    edge[...] = columns
    copies[2].wait()


def pack_rest_kernel(parts, tokens, state, *rest):
    rest = rest[tokens:]
    odd = lax.axis_index("ax") % 2
    sems = rest[-1]
    copies = []
    for k, (q, first, last) in enumerate(parts):
        source = state.at[:, plane_of(odd, q), first:last, :]
        copies.append(pltpu.make_async_copy(source, rest[k], sems.at[k]))
    for copy in copies:
        copy.start()
    for copy in copies:
        copy.wait()


ANY = pl.BlockSpec(memory_space=pl.ANY)
PARAMS = pltpu.CompilerParams(vmem_limit_bytes=VMEM_LIMIT)


def whole(*shape):
    return pl.BlockSpec(shape, lambda i, s: (0,) * len(shape))


def rows_from(shape, axis, first, step):
    def place(i, s):
        row = (first // EIGHT + i * (step // EIGHT)) * EIGHT
        return tuple(row if d == axis else 0 for d in range(len(shape)))

    return pl.BlockSpec(tuple(pl.Element(n) for n in shape), place)


def in_hbm(value):
    return pltpu.with_memory_space_constraint(value, pltpu.HBM)


def cost(flops, nbytes):
    return pl.CostEstimate(flops=flops, bytes_accessed=nbytes, transcendentals=0)


def pack_first(state, count):
    fields, planes, _, cells = state.shape
    vmem = pl.BlockSpec(memory_space=pltpu.VMEM)
    row = jax.ShapeDtypeStruct((LINES, cells), jnp.float32)
    rows = pltpu.VMEM((fields, planes, EIGHT, cells), jnp.float32)
    return pl.pallas_call(
        functools.partial(pack_first_kernel, count),
        in_specs=[ANY],
        out_specs=[vmem, vmem, vmem],
        out_shape=[jax.ShapeDtypeStruct((fields, count, cells), jnp.float32), row, row],
        scratch_shapes=[rows, rows, pltpu.SemaphoreType.DMA((3,))],
        compiler_params=PARAMS,
        cost_estimate=cost(0, fields * count * cells * 8),
        name="pack_first",
    )(in_hbm(state))


def pack_edges(state, token):
    fields, planes, rows, cells = state.shape
    vmem = pl.BlockSpec(memory_space=pltpu.VMEM)
    tiles = pltpu.VMEM((fields, planes, rows, LANES), jnp.float32)
    return pl.pallas_call(
        pack_edges_kernel,
        in_specs=[ANY, ANY],
        out_specs=[vmem, vmem],
        out_shape=[
            jax.ShapeDtypeStruct((rows, LANES), jnp.float32),
            jax.ShapeDtypeStruct((fields, R_NEAR, cells), jnp.float32),
        ],
        scratch_shapes=[tiles, tiles, pltpu.SemaphoreType.DMA((3,))],
        compiler_params=PARAMS,
        cost_estimate=cost(0, fields * planes * rows * LANES * 16),
        name="pack_edges",
    )(in_hbm(state), token)


def pack_rest(state, parts, *tokens):
    fields, _, _, cells = state.shape
    shapes = [jax.ShapeDtypeStruct((fields, last - first, cells), jnp.float32) for _, first, last in parts]
    return pl.pallas_call(
        functools.partial(pack_rest_kernel, parts, len(tokens)),
        in_specs=[ANY] * (1 + len(tokens)),
        out_specs=[pl.BlockSpec(memory_space=pltpu.VMEM)] * len(shapes),
        out_shape=shapes,
        scratch_shapes=[pltpu.SemaphoreType.DMA((len(parts),))],
        compiler_params=PARAMS,
        cost_estimate=cost(0, sum(math.prod(x.shape) for x in shapes) * 8),
        name="pack_rest",
    )(in_hbm(state), *tokens)


def flux_scratch(rows, cells):
    shape = (PLANES, FIELDS, cells // LANES)
    return [pltpu.VMEM((*shape, n, LANES), jnp.float32) for n in (rows + 2 * EIGHT, rows)]


def bulk(flags, state, low, high, inner, edge, dtheta, outer, span, first, rows, token, held):
    fields, planes, total_rows, cells = state.shape
    origin, end = span
    count = end - first
    blocks = count // rows
    size = fields * planes * count * cells
    aliases = {} if held is None else {8: 0}
    state = in_hbm(state)
    operands = [state, low, high, inner, edge, outer, token, state if held is None else held]
    return pl.pallas_call(
        functools.partial(bulk_kernel, dtheta, rows, (first, end), origin, total_rows),
        grid_spec=pltpu.PrefetchScalarGridSpec(
            num_scalar_prefetch=1,
            grid=(blocks,),
            in_specs=[
                ANY,
                whole(LINES, cells),
                whole(LINES, cells),
                ANY,
                rows_from((rows, LANES), 0, first, rows),
                ANY,
                ANY,
                ANY,
            ],
            out_specs=rows_from((fields, planes, rows, cells), 2, first, rows),
            scratch_shapes=[
                pltpu.VMEM((fields, planes, count + 2 * EIGHT, cells), jnp.float32),
                pltpu.VMEM((fields, count, cells), jnp.float32),
                pltpu.VMEM((fields, count, cells), jnp.float32),
                pltpu.SemaphoreType.DMA((3 * blocks,)),
                *flux_scratch(rows, cells),
            ],
        ),
        out_shape=pltpu.HBM(state.shape, jnp.float32),
        input_output_aliases=aliases,
        compiler_params=PARAMS,
        cost_estimate=cost(size * 60, size * 10),
        name="bulk",
    )(flags, *operands)


def near(flags, state, low, high, inner, edge, dtheta, outer, factor, table, solve, token, part=None):
    fields, planes, rows, cells = state.shape
    out = jax.ShapeDtypeStruct((LINES, R_NEAR, cells), jnp.float32)
    tail = min(R_NEAR // EIGHT, rows // EIGHT - 1)
    state = in_hbm(state)
    out_specs = [whole(LINES, R_NEAR, cells), whole(LINES, R_NEAR, cells), whole(R_NEAR, LANES)]
    out_shape = [out, out, jax.ShapeDtypeStruct((R_NEAR, LANES), jnp.float32)]
    scratch = flux_scratch(R_NEAR, cells)
    if part is not None:
        out_specs.append(whole(fields, part[1] - part[0], cells))
        out_shape.append(jax.ShapeDtypeStruct((fields, part[1] - part[0], cells), jnp.float32))
        scratch.append(pltpu.SemaphoreType.DMA)
    result = pl.pallas_call(
        functools.partial(near_kernel, dtheta, rows, part[0] if part else 0),
        grid_spec=pltpu.PrefetchScalarGridSpec(
            num_scalar_prefetch=1,
            grid=(1,),
            in_specs=[
                whole(fields, planes, R_NEAR, cells),
                pl.BlockSpec((fields, planes, EIGHT, cells), lambda i, s: (0, 0, tail, 0)),
                whole(LINES, cells),
                whole(LINES, cells),
                whole(fields, R_NEAR, cells),
                whole(fields, R_NEAR, cells),
                whole(R_NEAR, LANES),
                whole(R_NEAR, LANES),
                whole(R_NEAR, LANES),
                whole(*solve.shape),
                ANY,
                ANY,
            ],
            out_specs=out_specs,
            scratch_shapes=scratch,
        ),
        out_shape=out_shape,
        compiler_params=PARAMS,
        cost_estimate=cost(LINES * R_NEAR * cells * 200, LINES * R_NEAR * cells * 250),
        name="near",
    )(flags, state, state, low, high, inner, outer, edge, factor, table, solve, token, state)
    return result if part is not None else (*result, None)


def finish(flags, factor, rhs, local, carry, table, held):
    _, _, cells = rhs.shape
    return pl.pallas_call(
        finish_kernel,
        grid_spec=pltpu.PrefetchScalarGridSpec(
            num_scalar_prefetch=1,
            grid=(1,),
            in_specs=[
                whole(R_NEAR, LANES),
                whole(LINES, R_NEAR, cells),
                whole(LINES, R_NEAR, cells),
                whole(R_NEAR, LANES),
                whole(R_NEAR, LANES),
                ANY,
            ],
            out_specs=whole(FIELDS, PLANES, R_NEAR, cells),
        ),
        out_shape=pltpu.HBM(held.shape, jnp.float32),
        input_output_aliases={6: 0},
        compiler_params=PARAMS,
        cost_estimate=cost(LINES * R_NEAR * cells * 10, LINES * R_NEAR * cells * 20),
        name="finish",
    )(flags, factor, rhs, local, carry, table, held)


def chunks(rows):
    size = 24 if (rows - R_NEAR) % 48 == 0 else EIGHT
    pairs = (rows - R_NEAR) // (2 * size)
    cuts = sorted({-(-2 * pairs // 5), -(-4 * pairs // 5), pairs})
    ends = [R_NEAR + 2 * size * c for c in cuts]
    return size, list(zip([0] + ends[:-1], ends))


def smoothing_table(coarsen, cells, total_cells, dtheta):
    factor = coarsen.astype(jnp.float32)[:, None]
    stiffness = KAPPA / (factor * dtheta) ** 2
    inverse_half = 0.5 / stiffness
    one_minus = jnp.sqrt(inverse_half * (2.0 + inverse_half)) - inverse_half
    log_ratio = jnp.log1p(-one_minus)
    gain = (1.0 - one_minus) / (stiffness * one_minus * (2.0 - one_minus))
    closing = 1.0 / -jnp.expm1((total_cells / factor) * log_ratio)
    across = jnp.exp((cells / factor) * log_ratio)
    column = jnp.arange(LANES, dtype=jnp.int32)[None, :]
    width = jnp.left_shift(1, jnp.minimum(column, 20)).astype(jnp.float32)
    table = jnp.where(width >= factor, jnp.exp(log_ratio * (width / factor)), 0.0)
    table = jnp.where(column == COL_LOG, log_ratio, table)
    table = jnp.where(column == COL_GAIN, gain, table)
    return table, closing, across


def piece_tables(dtheta):
    tables = []
    for level in range(FMAX.bit_length()):
        width = 1 << level
        half = 0.5 * (width * dtheta) ** 2 / KAPPA
        ratio = 1.0 - (math.sqrt(half * (2.0 + half)) - half)
        block = np.arange(LANES) // width
        tables.append(ratio ** np.abs(block[:, None] - block[None, :]) / width)
    return jnp.asarray(np.concatenate(tables, axis=1), jnp.float32)


def ring(value, axis, shift):
    size = lax.axis_size(axis)
    return lax.ppermute(value, axis, [(i, (i + shift) % size) for i in range(size)])


def body(state, coarsen):
    fields, planes, rows, cells = state.shape
    sec_count = lax.axis_size("sec")
    rad_count = lax.axis_size("rad")
    ax_count = lax.axis_size("ax")
    assert fields == FIELDS and planes == PLANES and ax_count % 2 == 0
    rad_index = lax.axis_index("rad")
    ax_index = lax.axis_index("ax")
    total_cells = cells * sec_count
    dtheta = 2.0 * math.pi / total_cells
    outer_pairs = []
    for i in range(1, ax_count - 1, 2):
        outer_pairs += [(i, i + 1), (i + 1, i)]
    inner_pairs = []
    for i in range(0, ax_count, 2):
        inner_pairs += [(i, i + 1), (i + 1, i)]
    up = [(i, i + 1) for i in range(rad_count - 1)]
    down = [(i + 1, i) for i in range(rad_count - 1)]
    flags = jnp.stack(
        [
            ax_index % 2,
            ((ax_index > 0) & (ax_index < ax_count - 1)).astype(jnp.int32),
            (rad_index == 0).astype(jnp.int32),
            (rad_index == rad_count - 1).astype(jnp.int32),
            rad_index * rows,
        ]
    ).astype(jnp.int32)
    size, spans = chunks(rows)
    count = len(spans)

    part, low, high = pack_first(state, spans[0][1])
    outer = [lax.ppermute(part, "ax", outer_pairs)]
    columns, side = pack_edges(state, high)
    low = lax.ppermute(low, "rad", up)
    high = lax.ppermute(high, "rad", down)
    inner = [lax.ppermute(side, "ax", inner_pairs)]
    wanted = [(0, R_NEAR, spans[0][1])] + [(0, *span) for span in spans[1:]]
    if count > 1:
        wanted.insert(1, (1, *spans[1]))
    parts = pack_rest(state, wanted, columns, low, high)
    for k, value in enumerate(parts):
        if wanted[k][0]:
            outer.append(lax.ppermute(value, "ax", outer_pairs))
        else:
            inner.append(lax.ppermute(value, "ax", inner_pairs))
    if sec_count == 2:
        edge = ring(columns, "sec", 1)
    else:
        from_left = jnp.arange(LANES)[None, :] % 4 < 2
        edge = jnp.where(from_left, ring(columns, "sec", 1), ring(columns, "sec", -1))

    table, closing, across = smoothing_table(coarsen, cells, total_cells, dtheta)
    factor = jnp.broadcast_to(coarsen.astype(jnp.float32)[:, None], (R_NEAR, LANES))

    solve = piece_tables(dtheta)
    given = (flags, state, low, high)
    part = spans[2] if count > 2 else None
    rhs, local, ends, part = near(
        *given, inner[0], edge, dtheta, outer[0], factor, table, solve, parts[0], part
    )
    if part is not None:
        outer.append(lax.ppermute(part, "ax", outer_pairs))
    arrived = [ends] + [ring(ends, "sec", k) for k in range(1, sec_count)] + [ends]
    from_left = jnp.arange(LANES)[None, :] < LINES
    carry = jnp.zeros_like(ends)
    for k in range(sec_count, 0, -1):
        carry = carry * across + jnp.where(from_left, arrived[k], arrived[sec_count - k])
    carry = carry * closing

    out = None
    for k in range(count):
        first = spans[k][0] if k else R_NEAR
        if k == count - 1 and k:
            out = finish(flags, factor, rhs, local, carry, table, out)
        out = bulk(*given, inner[k + 1], edge, dtheta, outer[k], spans[k], first, size, ends, out)
    return out if count > 1 else finish(flags, factor, rhs, local, carry, table, out)


def solution(mesh):
    return jax.shard_map(
        body,
        mesh=mesh,
        in_specs=(P(None, "ax", "rad", "sec"), P()),
        out_specs=P(None, "ax", "rad", "sec"),
        check_vma=False,
    )
```

```python
import functools
import math

import jax
import jax.numpy as jnp
import ml_dtypes
import numpy as np
from jax import lax
from jax.experimental import pallas as pl
from jax.experimental.pallas import tpu as pltpu
from jax.sharding import PartitionSpec as P

R_NEAR = 16
FMAX = 16

GAMMA = 1.4
KAPPA = 1.44

FIELDS = 5
PLANES = 2
LINES = FIELDS * PLANES
EIGHT = 8
LANES = 128
VMEM_LIMIT = 28 * 1024 * 1024

COL_LOG = 32
COL_GAIN = 33

ODD, OUTER, FIRST, LAST, BASE = range(5)


def plane_of(odd, q):
    return odd if q else 1 - odd


def reciprocal(x):
    y = pl.reciprocal(x, approx=True)
    y = y * (2.0 - x * y)
    return y * (2.0 - x * y)


def fluxes(fields, want):
    density, energy = fields[0], fields[4]
    momentum = fields[1:4]
    inverse = reciprocal(density)
    velocity = [m * inverse for m in momentum]
    square = {}
    for i in range(3):
        for j in range(i, 3):
            if i == j or i + 1 in want or j + 1 in want or (i, j) == (1, 2):
                square[i, j] = square[j, i] = momentum[i] * velocity[j]
    pressure = (GAMMA - 1.0) * (energy - 0.5 * (square[0, 0] + square[1, 1] + square[2, 2]))
    enthalpy = energy + pressure
    out = {}
    for d in want:
        k = d - 1
        flow = [square[i, k] + pressure if i == k else square[i, k] for i in range(3)]
        out[d] = [momentum[k]] + flow + [enthalpy * velocity[k]]
    return out, (pressure, square[2, 2], square[1, 2])


def flux_along(fields, along):
    return fluxes(fields, (along,))[0][along]


def outer_flux(flags, outer):
    present = flags[OUTER] == 1
    outer = [jnp.where(present, outer[0], 1.0)] + [jnp.where(present, g, 0.0) for g in outer[1:]]
    return flux_along(outer, 1)


def stencil(
    flags, first_row, rows, total_rows, dtheta, load, next_rows, edge, inner, outer, place, radial, azimuthal
):
    strips = rows // EIGHT
    pieces = radial.shape[2]
    row = lax.broadcasted_iota(jnp.int32, (EIGHT, 1), 0)
    lane = lax.broadcasted_iota(jnp.int32, (EIGHT, LANES), 1)
    start = flags[BASE] + first_row
    axial_sign = jnp.where(flags[ODD] == 1, 0.5, -0.5)
    above = jnp.where((flags[FIRST] == 1) & (first_row == 0), 0.0, (start - 1).astype(jnp.float32) + 0.5)
    end = first_row + rows == total_rows
    below = jnp.where((flags[LAST] == 1) & end, 0.0, (start + rows).astype(jnp.float32) + 0.5)
    scale = jnp.where(row >= EIGHT // 2, above, below)
    at = [slice(b * LANES, (b + 1) * LANES) for b in range(pieces)]

    for q in range(PLANES):
        for b in range(pieces):
            values = [next_rows(f, q, at[b]) for f in range(FIELDS)]
            values[0] = jnp.where(scale > 0.0, values[0], 1.0)
            flux_next = flux_along(values, 2)
            for f in range(FIELDS):
                radial[q, f, b, 0:EIGHT, :] = flux_next[f] * scale
                radial[q, f, b, EIGHT + rows : 2 * EIGHT + rows, :] = flux_next[f] * scale

    def inside(t, carry):
        r = pl.multiple_of(EIGHT * t, EIGHT)
        radius = (start + r + row).astype(jnp.float32) + 0.5
        inv_radius = 1.0 / radius
        for b in range(pieces):
            beside = flux_along([inner(f, r, at[b]) for f in range(FIELDS)], 1)
            axial, source = [], []
            for q in range(PLANES):
                fields = [load(f, q, r, at[b]) for f in range(FIELDS)]
                flow, (pressure, twist, swirl) = fluxes(fields, (1, 2, 3))
                axial.append(flow[1])
                for f in range(FIELDS):
                    radial[q, f, b, pl.ds(r + EIGHT, EIGHT), :] = flow[2][f] * radius
                    azimuthal[q, f, b, pl.ds(r, EIGHT), :] = flow[3][f]
                source.append(((pressure + twist) * inv_radius, swirl * -inv_radius))
            base = [[axial_sign * (x - y) for x, y in zip(beside, axial[1])]]
            if outer is None:
                base.append([axial_sign * x for x in axial[0]])
            else:
                far = outer_flux(flags, [outer(f, r, at[b]) for f in range(FIELDS)])
                base.append([axial_sign * (x - y) for x, y in zip(axial[0], far)])
            for q in range(PLANES):
                base[q][2] = base[q][2] + source[q][0]
                base[q][3] = base[q][3] + source[q][1]
                for f in range(FIELDS):
                    place(f, q, r)[:, at[b]] = base[q][f]
        return carry

    lax.fori_loop(0, strips, inside, 0)

    def differences(t, carry):
        r = pl.multiple_of(EIGHT * t, EIGHT)
        radius = (start + r + row).astype(jnp.float32) + 0.5
        half_inv = 0.5 / radius
        half_arc = half_inv * (1.0 / dtheta)
        beyond = [edge(r)] + [pltpu.roll(edge(r), LANES - 4 * f, 1) for f in range(1, FIELDS)]
        beyond = flux_along(beyond, 3)
        for q in range(PLANES):
            for f in range(FIELDS):
                ends = [pltpu.roll(beyond[f], s, 1) if q else beyond[f] for s in (LANES - 1, 1)]
                here = [azimuthal[q, f, b, pl.ds(r, EIGHT), :] for b in range(pieces)]
                left = [ends[0]] + [pltpu.roll(x, 1, 1) for x in here]
                right = [pltpu.roll(x, LANES - 1, 1) for x in here] + [ends[1]]
                out = place(f, q, r)
                for b in range(pieces):
                    behind = jnp.where(lane == 0, left[b], left[b + 1])
                    ahead = jnp.where(lane == LANES - 1, right[b + 1], right[b])
                    up = radial[q, f, b, pl.ds(r + EIGHT - 1, EIGHT), :]
                    down = radial[q, f, b, pl.ds(r + EIGHT + 1, EIGHT), :]
                    change = (behind - ahead) * half_arc + (up - down) * half_inv
                    out[:, at[b]] = out[:, at[b]] + change
        return carry

    lax.fori_loop(0, strips, differences, 0)


def bulk_kernel(
    dtheta, rows, span, total_rows, fused, flags, state, low, high, inner, edge, outer, token, held, out, *scratch
):
    first, end = span
    blocks = (end - first) // rows
    state_rows, inner_rows, sems, radial, azimuthal, *outer_rows = scratch
    outer_rows = outer_rows[0] if fused else None
    odd = flags[ODD]
    step = pl.program_id(0)

    def copies(k):
        a = first + k * rows + (EIGHT if k else -EIGHT)
        b = min(first + (k + 1) * rows + EIGHT, total_rows)
        at = a - first + EIGHT
        rest = pl.ds(outer.shape[1] - (end - first) + k * rows, rows)
        here = pl.ds(k * rows, rows)
        sets = [
            (state.at[:, :, a:b, :], state_rows.at[:, :, at : at + b - a, :]),
            (inner.at[:, here, :], inner_rows.at[:, here, :]),
        ]
        if fused:
            sets.append((outer.at[:, rest, :], outer_rows.at[:, here, :]))
        return [pltpu.make_async_copy(x, y, sems.at[3 * k + i]) for i, (x, y) in enumerate(sets)]

    @pl.when(step == 0)
    def _():
        for k in range(blocks):
            for copy in copies(k):
                copy.start()

    for k in range(blocks):

        @pl.when(step == k)
        def _():
            for copy in copies(k):
                copy.wait()

    first_row = first + step * rows
    at_end = first_row + rows == total_rows
    base = pl.multiple_of(step * rows, EIGHT)
    sub = lax.broadcasted_iota(jnp.int32, (EIGHT, LANES), 0)

    def load(f, q, r, at):
        return state_rows[f, plane_of(odd, q), pl.ds(base + EIGHT + r, EIGHT), at]

    def next_rows(f, q, at):
        k = f * PLANES + q
        under = jnp.where(at_end, high[k : k + 1, at], load(f, q, rows, at))
        return jnp.where(sub >= EIGHT // 2, load(f, q, -EIGHT, at), under)

    stencil(
        flags,
        first_row,
        rows,
        total_rows,
        dtheta,
        load,
        next_rows,
        lambda r: edge[pl.ds(r, EIGHT), :],
        lambda f, r, at: inner_rows[f, pl.ds(base + r, EIGHT), at],
        (lambda f, r, at: outer_rows[f, pl.ds(base + r, EIGHT), at]) if fused else None,
        lambda f, q, r: out.at[f, plane_of(odd, q), pl.ds(r, EIGHT), :],
        radial,
        azimuthal,
    )


def outer_kernel(rows, span, flags, outer, held, out, outer_rows, held_rows, sems):
    first, end = span
    plane = lax.axis_index("ax") % 2
    sign = jnp.where(flags[ODD] == 1, -0.5, 0.5)
    steps = []
    for k in range((end - first) // rows):
        here = pl.ds(k * rows, rows)
        there = pl.ds(first + k * rows, rows)
        ways = [
            (outer.at[:, here, :], outer_rows.at[:, here, :]),
            (held.at[:, plane, there, :], held_rows.at[:, here, :]),
            (held_rows.at[:, here, :], out.at[:, plane, there, :]),
        ]
        steps.append([pltpu.make_async_copy(x, y, sems.at[3 * k + i]) for i, (x, y) in enumerate(ways)])
        steps[-1][0].start()
        steps[-1][1].start()
    for k, (come, have, leave) in enumerate(steps):
        come.wait()
        have.wait()
        for t in range(rows // EIGHT):
            at = pl.ds(k * rows + EIGHT * t, EIGHT)
            values = outer_flux(flags, [outer_rows[f, at, :] for f in range(FIELDS)])
            for f in range(FIELDS):
                held_rows[f, at, :] = held_rows[f, at, :] + sign * values[f]
        leave.start()
    for _, _, leave in steps:
        leave.wait()


def near_kernel(
    dtheta,
    total_rows,
    part_first,
    flags,
    state,
    after,
    low,
    high,
    inner,
    outer,
    edge,
    factor,
    table,
    solve,
    token,
    hbm,
    rhs,
    local,
    carry,
    *rest,
):
    cells = state.shape[-1]
    odd = flags[ODD]
    part = rest[0] if len(rest) > 2 else None
    scratch = rest[-2:] if part is None else rest[-3:-1]
    if part is not None:
        source = hbm.at[:, lax.axis_index("ax") % 2, part_first : part_first + part.shape[1], :]
        copy = pltpu.make_async_copy(source, part, rest[-1])
        copy.start()

    sub = lax.broadcasted_iota(jnp.int32, (EIGHT, LANES), 0)

    def next_rows(f, q, at):
        k = f * PLANES + q
        under = high[k : k + 1, at] if total_rows == R_NEAR else after[f, plane_of(odd, q), :, at]
        return jnp.where(sub >= EIGHT // 2, low[k : k + 1, at], under)

    stencil(
        flags,
        0,
        R_NEAR,
        total_rows,
        dtheta,
        lambda f, q, r, at: state[f, plane_of(odd, q), pl.ds(r, EIGHT), at],
        next_rows,
        lambda r: edge[pl.ds(r, EIGHT), :],
        lambda f, r, at: inner[f, pl.ds(r, EIGHT), at],
        lambda f, r, at: outer[f, pl.ds(r, EIGHT), at],
        lambda f, q, r: rhs.at[f * PLANES + q, pl.ds(r, EIGHT), :],
        *scratch,
    )

    pieces = cells // LANES
    lane = lax.broadcasted_iota(jnp.int32, (R_NEAR, LANES), 1)
    width = factor[...]
    log_ratio = table[:, COL_LOG : COL_LOG + 1]
    block = jnp.floor((lane.astype(jnp.float32) + 0.5) / width)
    ahead_entry = jnp.exp(log_ratio * (block + 1.0))
    behind_entry = jnp.exp(log_ratio * (LANES / width - block))
    across = jnp.exp(log_ratio * (LANES / width))

    def line(k, ends):
        rows = jnp.concatenate([rhs[k, :, b * LANES : (b + 1) * LANES] for b in range(pieces)], axis=0)
        high = rows.astype(jnp.bfloat16)
        low = (rows - high.astype(jnp.float32)).astype(jnp.bfloat16)
        solved = jnp.dot(
            jnp.concatenate([high, low, high], axis=1), solve[...], preferred_element_type=jnp.float32
        )
        inside = []
        for b in range(pieces):
            mine = solved[b * R_NEAR : (b + 1) * R_NEAR]
            value = mine[:, :LANES]
            for level in range(1, FMAX.bit_length()):
                chosen = mine[:, level * LANES : (level + 1) * LANES]
                value = jnp.where(width == (1 << level), chosen, value)
            inside.append(value)
        total = list(inside)
        enter = jnp.zeros((R_NEAR, LANES), jnp.float32)
        for b in range(pieces):
            leave = jnp.broadcast_to(inside[b][:, LANES - 1 : LANES], (R_NEAR, LANES))
            total[b] = total[b] + ahead_entry * enter
            enter = leave + across * enter
        ends = jnp.where(lane == k, enter, ends)
        enter = jnp.zeros((R_NEAR, LANES), jnp.float32)
        for b in reversed(range(pieces)):
            leave = jnp.broadcast_to(inside[b][:, 0:1], (R_NEAR, LANES))
            total[b] = total[b] + behind_entry * enter
            enter = leave + across * enter
        for b in range(pieces):
            local[k, :, b * LANES : (b + 1) * LANES] = total[b]
        return jnp.where(lane == k + LINES, enter, ends)

    carry[...] = lax.fori_loop(
        0, LINES, line, jnp.zeros((R_NEAR, LANES), jnp.float32)
    )
    if part is not None:
        copy.wait()


def finish_kernel(flags, factor, rhs, local, carry, table, held, out):
    cells = out.shape[-1]
    lane = lax.broadcasted_iota(jnp.int32, (R_NEAR, cells), 1).astype(jnp.float32)
    width = factor[:, 0:1]
    block = jnp.floor((lane + 0.5) / width)
    count = cells / width
    log_ratio = table[:, COL_LOG : COL_LOG + 1]
    gain = table[:, COL_GAIN : COL_GAIN + 1]
    from_left = jnp.exp(log_ratio * (block + 1.0))
    from_right = jnp.exp(log_ratio * (count - block))
    near = flags[FIRST] == 1
    for f in range(FIELDS):
        for q in range(PLANES):
            k = f * PLANES + q
            j = k + LINES
            smooth = gain * (
                local[k] + from_left * carry[:, k : k + 1] + from_right * carry[:, j : j + 1]
            )
            out[f, plane_of(flags[ODD], q)] = jnp.where(near, smooth, rhs[k])


def stream(pieces, sems):
    steps = []
    for source, stage, target in pieces:
        for f in range(FIELDS):
            k = 2 * len(steps)
            come = pltpu.make_async_copy(source.at[f], stage.at[f], sems.at[k])
            leave = pltpu.make_async_copy(stage.at[f], target.at[f], sems.at[k + 1])
            steps.append((come, leave))
    for come, _ in steps:
        come.start()

    def finish():
        for come, leave in steps:
            come.wait()
            leave.start()
        for _, leave in steps:
            leave.wait()

    return finish


def pack_first_kernel(count, state, part, low, high, stage, top, bottom, row_sems, sems):
    _, _, rows, _ = state.shape
    odd = lax.axis_index("ax") % 2
    finish = stream([(state.at[:, odd, 0:count, :], stage, part)], sems)
    copies = [
        pltpu.make_async_copy(state.at[:, :, rows - EIGHT : rows, :], top, row_sems.at[0]),
        pltpu.make_async_copy(state.at[:, :, 0:EIGHT, :], bottom, row_sems.at[1]),
    ]
    for copy in copies:
        copy.start()
    finish()
    for copy in copies:
        copy.wait()
    for f in range(FIELDS):
        for q in range(PLANES):
            k = f * PLANES + q
            p = plane_of(odd, q)
            low[k : k + 1, :] = top[f, p, EIGHT - 1 : EIGHT, :]
            high[k : k + 1, :] = bottom[f, p, 0:1, :]


def pack_edges_kernel(state, token, edge, side, left, right, sems):
    _, _, rows, cells = state.shape
    odd = lax.axis_index("ax") % 2
    copies = [
        pltpu.make_async_copy(state.at[:, :, :, cells - LANES : cells], left, sems.at[0]),
        pltpu.make_async_copy(state.at[:, :, :, 0:LANES], right, sems.at[1]),
        pltpu.make_async_copy(state.at[:, 1 - odd, 0:R_NEAR, :], side, sems.at[2]),
    ]
    for copy in copies:
        copy.start()
    for copy in copies[:2]:
        copy.wait()
    lane = lax.broadcasted_iota(jnp.int32, (rows, LANES), 1)
    columns = jnp.ones((rows, LANES), jnp.float32)
    for f in range(FIELDS):
        for q in range(PLANES):
            p = plane_of(odd, q)
            columns = jnp.where(lane == 4 * f + q, left[f, p, :, LANES - 1 : LANES], columns)
            columns = jnp.where(lane == (4 * f - 1 - q) % LANES, right[f, p, :, 0:1], columns)
    edge[...] = columns
    copies[2].wait()


def pack_rest_kernel(parts, tokens, state, *rest):
    rest = rest[tokens:]
    odd = lax.axis_index("ax") % 2
    count = len(parts)
    pieces = []
    for k, (q, first, last) in enumerate(parts):
        pieces.append((state.at[:, plane_of(odd, q), first:last, :], rest[count + k], rest[k]))
    stream(pieces, rest[-1])()


ANY = pl.BlockSpec(memory_space=pl.ANY)
PARAMS = pltpu.CompilerParams(vmem_limit_bytes=VMEM_LIMIT)


def whole(*shape):
    return pl.BlockSpec(shape, lambda i, s: (0,) * len(shape))


def rows_from(shape, axis, first, step):
    def place(i, s):
        row = (first // EIGHT + i * (step // EIGHT)) * EIGHT
        return tuple(row if d == axis else 0 for d in range(len(shape)))

    return pl.BlockSpec(tuple(pl.Element(n) for n in shape), place)


def in_hbm(value):
    return pltpu.with_memory_space_constraint(value, pltpu.HBM)


def cost(flops, nbytes):
    return pl.CostEstimate(flops=flops, bytes_accessed=nbytes, transcendentals=0)


def pack_first(state, count):
    fields, planes, _, cells = state.shape
    vmem = pl.BlockSpec(memory_space=pltpu.VMEM)
    row = jax.ShapeDtypeStruct((LINES, cells), jnp.float32)
    rows = pltpu.VMEM((fields, planes, EIGHT, cells), jnp.float32)
    return pl.pallas_call(
        functools.partial(pack_first_kernel, count),
        in_specs=[ANY],
        out_specs=[ANY, vmem, vmem],
        out_shape=[jax.ShapeDtypeStruct((fields, count, cells), jnp.float32), row, row],
        scratch_shapes=[
            pltpu.VMEM((fields, count, cells), jnp.float32),
            rows,
            rows,
            pltpu.SemaphoreType.DMA((2,)),
            pltpu.SemaphoreType.DMA((2 * fields,)),
        ],
        compiler_params=PARAMS,
        cost_estimate=cost(0, fields * count * cells * 8),
        name="pack_first",
    )(in_hbm(state))


def pack_edges(state, token):
    fields, planes, rows, cells = state.shape
    vmem = pl.BlockSpec(memory_space=pltpu.VMEM)
    tiles = pltpu.VMEM((fields, planes, rows, LANES), jnp.float32)
    return pl.pallas_call(
        pack_edges_kernel,
        in_specs=[ANY, ANY],
        out_specs=[vmem, vmem],
        out_shape=[
            jax.ShapeDtypeStruct((rows, LANES), jnp.float32),
            jax.ShapeDtypeStruct((fields, R_NEAR, cells), jnp.float32),
        ],
        scratch_shapes=[tiles, tiles, pltpu.SemaphoreType.DMA((3,))],
        compiler_params=PARAMS,
        cost_estimate=cost(0, fields * planes * rows * LANES * 16),
        name="pack_edges",
    )(in_hbm(state), token)


def pack_rest(state, parts, *tokens):
    fields, _, _, cells = state.shape
    shapes = [jax.ShapeDtypeStruct((fields, last - first, cells), jnp.float32) for _, first, last in parts]
    return pl.pallas_call(
        functools.partial(pack_rest_kernel, parts, len(tokens)),
        in_specs=[ANY] * (1 + len(tokens)),
        out_specs=[ANY] * len(shapes),
        out_shape=shapes,
        scratch_shapes=[
            *[pltpu.VMEM(x.shape, jnp.float32) for x in shapes],
            pltpu.SemaphoreType.DMA((2 * fields * len(parts),)),
        ],
        compiler_params=PARAMS,
        cost_estimate=cost(0, sum(math.prod(x.shape) for x in shapes) * 8),
        name="pack_rest",
    )(in_hbm(state), *tokens)


def flux_scratch(rows, cells):
    shape = (PLANES, FIELDS, cells // LANES)
    return [pltpu.VMEM((*shape, n, LANES), jnp.float32) for n in (rows + 2 * EIGHT, rows)]


def bulk(flags, state, low, high, inner, edge, dtheta, outer, span, rows, token, held):
    fields, planes, total_rows, cells = state.shape
    first, end = span
    count = end - first
    blocks = count // rows
    size = fields * planes * count * cells
    aliases = {} if held is None else {8: 0}
    state = in_hbm(state)
    operands = [state, low, high, inner, edge, inner if outer is None else outer, token]
    operands.append(state if held is None else held)
    chunk = pltpu.VMEM((fields, count, cells), jnp.float32)
    return pl.pallas_call(
        functools.partial(bulk_kernel, dtheta, rows, span, total_rows, outer is not None),
        grid_spec=pltpu.PrefetchScalarGridSpec(
            num_scalar_prefetch=1,
            grid=(blocks,),
            in_specs=[
                ANY,
                whole(LINES, cells),
                whole(LINES, cells),
                ANY,
                rows_from((rows, LANES), 0, first, rows),
                ANY,
                ANY,
                ANY,
            ],
            out_specs=rows_from((fields, planes, rows, cells), 2, first, rows),
            scratch_shapes=[
                pltpu.VMEM((fields, planes, count + 2 * EIGHT, cells), jnp.float32),
                chunk,
                pltpu.SemaphoreType.DMA((3 * blocks,)),
                *flux_scratch(rows, cells),
                *([] if outer is None else [chunk]),
            ],
        ),
        out_shape=pltpu.HBM(state.shape, jnp.float32),
        input_output_aliases=aliases,
        compiler_params=PARAMS,
        cost_estimate=cost(size * 60, size * 10),
        name="bulk",
    )(flags, *operands)


def add_outer(flags, outer, span, rows, held):
    fields, count, cells = outer.shape
    chunk = pltpu.VMEM((fields, count, cells), jnp.float32)
    return pl.pallas_call(
        functools.partial(outer_kernel, rows, span),
        grid_spec=pltpu.PrefetchScalarGridSpec(
            num_scalar_prefetch=1,
            grid=(1,),
            in_specs=[ANY, ANY],
            out_specs=ANY,
            scratch_shapes=[chunk, chunk, pltpu.SemaphoreType.DMA((3 * (count // rows),))],
        ),
        out_shape=pltpu.HBM(held.shape, jnp.float32),
        input_output_aliases={2: 0},
        compiler_params=PARAMS,
        cost_estimate=cost(outer.size * 6, outer.size * 16),
        name="add_outer",
    )(flags, outer, held)


def near(flags, state, low, high, inner, edge, dtheta, outer, factor, table, solve, token, part=None):
    fields, planes, rows, cells = state.shape
    out = jax.ShapeDtypeStruct((LINES, R_NEAR, cells), jnp.float32)
    tail = min(R_NEAR // EIGHT, rows // EIGHT - 1)
    state = in_hbm(state)
    out_specs = [whole(LINES, R_NEAR, cells), whole(LINES, R_NEAR, cells), whole(R_NEAR, LANES)]
    out_shape = [out, out, jax.ShapeDtypeStruct((R_NEAR, LANES), jnp.float32)]
    scratch = flux_scratch(R_NEAR, cells)
    if part is not None:
        out_specs.append(whole(fields, part[1] - part[0], cells))
        out_shape.append(jax.ShapeDtypeStruct((fields, part[1] - part[0], cells), jnp.float32))
        scratch.append(pltpu.SemaphoreType.DMA)
    result = pl.pallas_call(
        functools.partial(near_kernel, dtheta, rows, part[0] if part else 0),
        grid_spec=pltpu.PrefetchScalarGridSpec(
            num_scalar_prefetch=1,
            grid=(1,),
            in_specs=[
                whole(fields, planes, R_NEAR, cells),
                pl.BlockSpec((fields, planes, EIGHT, cells), lambda i, s: (0, 0, tail, 0)),
                whole(LINES, cells),
                whole(LINES, cells),
                whole(fields, R_NEAR, cells),
                whole(fields, R_NEAR, cells),
                whole(R_NEAR, LANES),
                whole(R_NEAR, LANES),
                whole(R_NEAR, LANES),
                whole(*solve.shape),
                ANY,
                ANY,
            ],
            out_specs=out_specs,
            scratch_shapes=scratch,
        ),
        out_shape=out_shape,
        compiler_params=PARAMS,
        cost_estimate=cost(LINES * R_NEAR * cells * 200, LINES * R_NEAR * cells * 250),
        name="near",
    )(flags, state, state, low, high, inner, outer, edge, factor, table, solve, token, state)
    return result if part is not None else (*result, None)


def finish(flags, factor, rhs, local, carry, table, held):
    _, _, cells = rhs.shape
    return pl.pallas_call(
        finish_kernel,
        grid_spec=pltpu.PrefetchScalarGridSpec(
            num_scalar_prefetch=1,
            grid=(1,),
            in_specs=[
                whole(R_NEAR, LANES),
                whole(LINES, R_NEAR, cells),
                whole(LINES, R_NEAR, cells),
                whole(R_NEAR, LANES),
                whole(R_NEAR, LANES),
                ANY,
            ],
            out_specs=whole(FIELDS, PLANES, R_NEAR, cells),
        ),
        out_shape=pltpu.HBM(held.shape, jnp.float32),
        input_output_aliases={6: 0},
        compiler_params=PARAMS,
        cost_estimate=cost(LINES * R_NEAR * cells * 10, LINES * R_NEAR * cells * 20),
        name="finish",
    )(flags, factor, rhs, local, carry, table, held)


def chunks(rows):
    size = 16
    triples = (rows - R_NEAR) // (3 * size)
    cuts = sorted({-(-2 * triples // 5), -(-4 * triples // 5), triples})
    ends = [R_NEAR + 3 * size * c for c in cuts]
    return size, list(zip([0] + ends[:-1], ends))


def smoothing_table(coarsen, cells, total_cells, dtheta):
    factor = coarsen.astype(jnp.float32)[:, None]
    stiffness = KAPPA / (factor * dtheta) ** 2
    inverse_half = 0.5 / stiffness
    one_minus = jnp.sqrt(inverse_half * (2.0 + inverse_half)) - inverse_half
    log_ratio = jnp.log1p(-one_minus)
    gain = (1.0 - one_minus) / (stiffness * one_minus * (2.0 - one_minus))
    closing = 1.0 / -jnp.expm1((total_cells / factor) * log_ratio)
    across = jnp.exp((cells / factor) * log_ratio)
    column = jnp.arange(LANES, dtype=jnp.int32)[None, :]
    width = jnp.left_shift(1, jnp.minimum(column, 20)).astype(jnp.float32)
    table = jnp.where(width >= factor, jnp.exp(log_ratio * (width / factor)), 0.0)
    table = jnp.where(column == COL_LOG, log_ratio, table)
    table = jnp.where(column == COL_GAIN, gain, table)
    return table, closing, across


def piece_tables(dtheta):
    tables = []
    for level in range(FMAX.bit_length()):
        width = 1 << level
        half = 0.5 * (width * dtheta) ** 2 / KAPPA
        ratio = 1.0 - (math.sqrt(half * (2.0 + half)) - half)
        block = np.arange(LANES) // width
        tables.append(ratio ** np.abs(block[:, None] - block[None, :]) / width)
    table = np.concatenate(tables, axis=1)
    high = table.astype(ml_dtypes.bfloat16)
    low = (table - high.astype(np.float64)).astype(ml_dtypes.bfloat16)
    return jnp.asarray(np.concatenate([high, high, low], axis=0))


def ring(value, axis, shift):
    size = lax.axis_size(axis)
    return lax.ppermute(value, axis, [(i, (i + shift) % size) for i in range(size)])


def body(state, coarsen):
    fields, planes, rows, cells = state.shape
    sec_count = lax.axis_size("sec")
    rad_count = lax.axis_size("rad")
    ax_count = lax.axis_size("ax")
    assert fields == FIELDS and planes == PLANES and ax_count % 2 == 0
    rad_index = lax.axis_index("rad")
    ax_index = lax.axis_index("ax")
    total_cells = cells * sec_count
    dtheta = 2.0 * math.pi / total_cells
    outer_pairs = []
    for i in range(1, ax_count - 1, 2):
        outer_pairs += [(i, i + 1), (i + 1, i)]
    inner_pairs = []
    for i in range(0, ax_count, 2):
        inner_pairs += [(i, i + 1), (i + 1, i)]
    up = [(i, i + 1) for i in range(rad_count - 1)]
    down = [(i + 1, i) for i in range(rad_count - 1)]
    flags = jnp.stack(
        [
            ax_index % 2,
            ((ax_index > 0) & (ax_index < ax_count - 1)).astype(jnp.int32),
            (rad_index == 0).astype(jnp.int32),
            (rad_index == rad_count - 1).astype(jnp.int32),
            rad_index * rows,
        ]
    ).astype(jnp.int32)
    size, spans = chunks(rows)
    count = len(spans)

    part, low, high = pack_first(state, spans[0][1])
    outer = [lax.ppermute(part, "ax", outer_pairs)]
    columns, side = pack_edges(state, high)
    low = lax.ppermute(low, "rad", up)
    high = lax.ppermute(high, "rad", down)
    inner = [lax.ppermute(side, "ax", inner_pairs)]
    wanted = [(0, R_NEAR, spans[0][1])] + [(0, *span) for span in spans[1:]]
    if count > 1:
        wanted.insert(1, (1, *spans[1]))
    parts = pack_rest(state, wanted, columns, low, high)
    for k, value in enumerate(parts):
        if wanted[k][0]:
            outer.append(lax.ppermute(value, "ax", outer_pairs))
        else:
            inner.append(lax.ppermute(value, "ax", inner_pairs))
    if sec_count == 2:
        edge = ring(columns, "sec", 1)
    else:
        from_left = jnp.arange(LANES)[None, :] % 4 < 2
        edge = jnp.where(from_left, ring(columns, "sec", 1), ring(columns, "sec", -1))

    table, closing, across = smoothing_table(coarsen, cells, total_cells, dtheta)
    factor = jnp.broadcast_to(coarsen.astype(jnp.float32)[:, None], (R_NEAR, LANES))

    solve = piece_tables(dtheta)
    given = (flags, state, low, high)
    def pass_over(k, token, held, fused=True):
        span = (spans[k][0] if k else R_NEAR, spans[k][1])
        return bulk(*given, inner[k + 1], edge, dtheta, outer[k] if fused else None, span, size, token, held)

    out = pass_over(2, parts[0], None, fused=False) if count > 2 else None
    part = spans[2] if count > 2 else None
    token = parts[0] if out is None else out
    rhs, local, ends, part = near(
        *given, inner[0], edge, dtheta, outer[0], factor, table, solve, token, part
    )
    if part is not None:
        outer.append(lax.ppermute(part, "ax", outer_pairs))
    arrived = [ends] + [ring(ends, "sec", k) for k in range(1, sec_count)] + [ends]
    from_left = jnp.arange(LANES)[None, :] < LINES
    carry = jnp.zeros_like(ends)
    for k in range(sec_count, 0, -1):
        carry = carry * across + jnp.where(from_left, arrived[k], arrived[sec_count - k])
    carry = carry * closing

    for k in range(min(count, 2)):
        out = pass_over(k, ends, out)
    out = finish(flags, factor, rhs, local, carry, table, out)
    return add_outer(flags, outer[2], spans[2], size, out) if count > 2 else out


def solution(mesh):
    return jax.shard_map(
        body,
        mesh=mesh,
        in_specs=(P(None, "ax", "rad", "sec"), P()),
        out_specs=P(None, "ax", "rad", "sec"),
        check_vma=False,
    )
```

```python
import functools
import math

import jax
import jax.numpy as jnp
import ml_dtypes
import numpy as np
from jax import lax
from jax.experimental import pallas as pl
from jax.experimental.pallas import tpu as pltpu
from jax.sharding import PartitionSpec as P

R_NEAR = 16
FMAX = 16

GAMMA = 1.4
KAPPA = 1.44

FIELDS = 5
PLANES = 2
LINES = FIELDS * PLANES
EIGHT = 8
LANES = 128
VMEM_LIMIT = 28 * 1024 * 1024

COL_LOG = 32
COL_GAIN = 33

ODD, OUTER, FIRST, LAST, BASE = range(5)


def plane_of(odd, q):
    return odd if q else 1 - odd


def reciprocal(x):
    y = pl.reciprocal(x, approx=True)
    y = y * (2.0 - x * y)
    return y * (2.0 - x * y)


def fluxes(fields, want):
    density, energy = fields[0], fields[4]
    momentum = fields[1:4]
    inverse = reciprocal(density)
    velocity = [m * inverse for m in momentum]
    square = {}
    for i in range(3):
        for j in range(i, 3):
            if i == j or i + 1 in want or j + 1 in want or (i, j) == (1, 2):
                square[i, j] = square[j, i] = momentum[i] * velocity[j]
    pressure = (GAMMA - 1.0) * (energy - 0.5 * (square[0, 0] + square[1, 1] + square[2, 2]))
    enthalpy = energy + pressure
    out = {}
    for d in want:
        k = d - 1
        flow = [square[i, k] + pressure if i == k else square[i, k] for i in range(3)]
        out[d] = [momentum[k]] + flow + [enthalpy * velocity[k]]
    return out, (pressure, square[2, 2], square[1, 2])


def flux_along(fields, along):
    return fluxes(fields, (along,))[0][along]


def outer_flux(flags, outer):
    present = flags[OUTER] == 1
    outer = [jnp.where(present, outer[0], 1.0)] + [jnp.where(present, g, 0.0) for g in outer[1:]]
    return flux_along(outer, 1)


def stencil(
    flags, first_row, rows, total_rows, dtheta, load, next_rows, edge, inner, outer, place, radial, azimuthal
):
    strips = rows // EIGHT
    pieces = radial.shape[2]
    row = lax.broadcasted_iota(jnp.int32, (EIGHT, 1), 0)
    lane = lax.broadcasted_iota(jnp.int32, (EIGHT, LANES), 1)
    start = flags[BASE] + first_row
    axial_sign = jnp.where(flags[ODD] == 1, 0.5, -0.5)
    above = jnp.where((flags[FIRST] == 1) & (first_row == 0), 0.0, (start - 1).astype(jnp.float32) + 0.5)
    end = first_row + rows == total_rows
    below = jnp.where((flags[LAST] == 1) & end, 0.0, (start + rows).astype(jnp.float32) + 0.5)
    scale = jnp.where(row >= EIGHT // 2, above, below)
    at = [slice(b * LANES, (b + 1) * LANES) for b in range(pieces)]

    for q in range(PLANES):
        for b in range(pieces):
            values = [next_rows(f, q, at[b]) for f in range(FIELDS)]
            values[0] = jnp.where(scale > 0.0, values[0], 1.0)
            flux_next = flux_along(values, 2)
            for f in range(FIELDS):
                radial[q, f, b, 0:EIGHT, :] = flux_next[f] * scale
                radial[q, f, b, EIGHT + rows : 2 * EIGHT + rows, :] = flux_next[f] * scale

    def inside(t, carry):
        r = pl.multiple_of(EIGHT * t, EIGHT)
        radius = (start + r + row).astype(jnp.float32) + 0.5
        inv_radius = 1.0 / radius
        for b in range(pieces):
            beside = flux_along([inner(f, r, at[b]) for f in range(FIELDS)], 1)
            axial, source = [], []
            for q in range(PLANES):
                fields = [load(f, q, r, at[b]) for f in range(FIELDS)]
                flow, (pressure, twist, swirl) = fluxes(fields, (1, 2, 3))
                axial.append(flow[1])
                for f in range(FIELDS):
                    radial[q, f, b, pl.ds(r + EIGHT, EIGHT), :] = flow[2][f] * radius
                    azimuthal[q, f, b, pl.ds(r, EIGHT), :] = flow[3][f]
                source.append(((pressure + twist) * inv_radius, swirl * -inv_radius))
            base = [[axial_sign * (x - y) for x, y in zip(beside, axial[1])]]
            if outer is None:
                base.append([axial_sign * x for x in axial[0]])
            else:
                far = outer_flux(flags, [outer(f, r, at[b]) for f in range(FIELDS)])
                base.append([axial_sign * (x - y) for x, y in zip(axial[0], far)])
            for q in range(PLANES):
                base[q][2] = base[q][2] + source[q][0]
                base[q][3] = base[q][3] + source[q][1]
                for f in range(FIELDS):
                    place(f, q, r)[:, at[b]] = base[q][f]
        return carry

    lax.fori_loop(0, strips, inside, 0)

    def differences(t, carry):
        r = pl.multiple_of(EIGHT * t, EIGHT)
        radius = (start + r + row).astype(jnp.float32) + 0.5
        half_inv = 0.5 / radius
        half_arc = half_inv * (1.0 / dtheta)
        beyond = [edge(r)] + [pltpu.roll(edge(r), LANES - 4 * f, 1) for f in range(1, FIELDS)]
        beyond = flux_along(beyond, 3)
        for q in range(PLANES):
            for f in range(FIELDS):
                ends = [pltpu.roll(beyond[f], s, 1) if q else beyond[f] for s in (LANES - 1, 1)]
                here = [azimuthal[q, f, b, pl.ds(r, EIGHT), :] for b in range(pieces)]
                left = [ends[0]] + [pltpu.roll(x, 1, 1) for x in here]
                right = [pltpu.roll(x, LANES - 1, 1) for x in here] + [ends[1]]
                out = place(f, q, r)
                for b in range(pieces):
                    behind = jnp.where(lane == 0, left[b], left[b + 1])
                    ahead = jnp.where(lane == LANES - 1, right[b + 1], right[b])
                    up = radial[q, f, b, pl.ds(r + EIGHT - 1, EIGHT), :]
                    down = radial[q, f, b, pl.ds(r + EIGHT + 1, EIGHT), :]
                    change = (behind - ahead) * half_arc + (up - down) * half_inv
                    out[:, at[b]] = out[:, at[b]] + change
        return carry

    lax.fori_loop(0, strips, differences, 0)


def bulk_kernel(
    dtheta, rows, span, total_rows, fused, flags, state, low, high, inner, edge, outer, token, held, out, *scratch
):
    first, end = span
    blocks = (end - first) // rows
    state_rows, inner_rows, sems, radial, azimuthal, *outer_rows = scratch
    outer_rows = outer_rows[0] if fused else None
    odd = flags[ODD]
    step = pl.program_id(0)

    def copies(k):
        a = first + k * rows + (EIGHT if k else -EIGHT)
        b = min(first + (k + 1) * rows + EIGHT, total_rows)
        at = a - first + EIGHT
        rest = pl.ds(outer.shape[1] - (end - first) + k * rows, rows)
        here = pl.ds(k * rows, rows)
        sets = [
            (state.at[:, :, a:b, :], state_rows.at[:, :, at : at + b - a, :]),
            (inner.at[:, here, :], inner_rows.at[:, here, :]),
        ]
        if fused:
            sets.append((outer.at[:, rest, :], outer_rows.at[:, here, :]))
        return [pltpu.make_async_copy(x, y, sems.at[3 * k + i]) for i, (x, y) in enumerate(sets)]

    @pl.when(step == 0)
    def _():
        for k in range(blocks):
            for copy in copies(k):
                copy.start()

    for k in range(blocks):

        @pl.when(step == k)
        def _():
            for copy in copies(k):
                copy.wait()

    first_row = first + step * rows
    at_end = first_row + rows == total_rows
    base = pl.multiple_of(step * rows, EIGHT)
    sub = lax.broadcasted_iota(jnp.int32, (EIGHT, LANES), 0)

    def load(f, q, r, at):
        return state_rows[f, plane_of(odd, q), pl.ds(base + EIGHT + r, EIGHT), at]

    def next_rows(f, q, at):
        k = f * PLANES + q
        under = jnp.where(at_end, high[k : k + 1, at], load(f, q, rows, at))
        return jnp.where(sub >= EIGHT // 2, load(f, q, -EIGHT, at), under)

    stencil(
        flags,
        first_row,
        rows,
        total_rows,
        dtheta,
        load,
        next_rows,
        lambda r: edge[pl.ds(r, EIGHT), :],
        lambda f, r, at: inner_rows[f, pl.ds(base + r, EIGHT), at],
        (lambda f, r, at: outer_rows[f, pl.ds(base + r, EIGHT), at]) if fused else None,
        lambda f, q, r: out.at[f, plane_of(odd, q), pl.ds(r, EIGHT), :],
        radial,
        azimuthal,
    )


def outer_kernel(rows, span, flags, outer, held, out, outer_rows, held_rows, sems):
    first, end = span
    plane = lax.axis_index("ax") % 2
    sign = jnp.where(flags[ODD] == 1, -0.5, 0.5)
    steps = []
    for k in range((end - first) // rows):
        here = pl.ds(k * rows, rows)
        there = pl.ds(first + k * rows, rows)
        ways = [
            (outer.at[:, here, :], outer_rows.at[:, here, :]),
            (held.at[:, plane, there, :], held_rows.at[:, here, :]),
            (held_rows.at[:, here, :], out.at[:, plane, there, :]),
        ]
        steps.append([pltpu.make_async_copy(x, y, sems.at[3 * k + i]) for i, (x, y) in enumerate(ways)])
        steps[-1][0].start()
        steps[-1][1].start()
    for k, (come, have, leave) in enumerate(steps):
        come.wait()
        have.wait()
        for t in range(rows // EIGHT):
            at = pl.ds(k * rows + EIGHT * t, EIGHT)
            values = outer_flux(flags, [outer_rows[f, at, :] for f in range(FIELDS)])
            for f in range(FIELDS):
                held_rows[f, at, :] = held_rows[f, at, :] + sign * values[f]
        leave.start()
    for _, _, leave in steps:
        leave.wait()


def near_kernel(
    dtheta,
    total_rows,
    part_first,
    flags,
    state,
    after,
    low,
    high,
    inner,
    outer,
    edge,
    factor,
    table,
    solve,
    token,
    hbm,
    rhs,
    local,
    carry,
    *rest,
):
    cells = state.shape[-1]
    odd = flags[ODD]
    part = rest[0] if len(rest) > 2 else None
    scratch = rest[-2:] if part is None else rest[-3:-1]
    if part is not None:
        source = hbm.at[:, lax.axis_index("ax") % 2, part_first : part_first + part.shape[1], :]
        copy = pltpu.make_async_copy(source, part, rest[-1])
        copy.start()

    sub = lax.broadcasted_iota(jnp.int32, (EIGHT, LANES), 0)

    def next_rows(f, q, at):
        k = f * PLANES + q
        under = high[k : k + 1, at] if total_rows == R_NEAR else after[f, plane_of(odd, q), :, at]
        return jnp.where(sub >= EIGHT // 2, low[k : k + 1, at], under)

    stencil(
        flags,
        0,
        R_NEAR,
        total_rows,
        dtheta,
        lambda f, q, r, at: state[f, plane_of(odd, q), pl.ds(r, EIGHT), at],
        next_rows,
        lambda r: edge[pl.ds(r, EIGHT), :],
        lambda f, r, at: inner[f, pl.ds(r, EIGHT), at],
        lambda f, r, at: outer[f, pl.ds(r, EIGHT), at],
        lambda f, q, r: rhs.at[f * PLANES + q, pl.ds(r, EIGHT), :],
        *scratch,
    )

    pieces = cells // LANES
    lane = lax.broadcasted_iota(jnp.int32, (R_NEAR, LANES), 1)
    width = factor[...]
    log_ratio = table[:, COL_LOG : COL_LOG + 1]
    block = jnp.floor((lane.astype(jnp.float32) + 0.5) / width)
    ahead_entry = jnp.exp(log_ratio * (block + 1.0))
    behind_entry = jnp.exp(log_ratio * (LANES / width - block))
    across = jnp.exp(log_ratio * (LANES / width))

    def line(k, ends):
        rows = jnp.concatenate([rhs[k, :, b * LANES : (b + 1) * LANES] for b in range(pieces)], axis=0)
        high = rows.astype(jnp.bfloat16)
        low = (rows - high.astype(jnp.float32)).astype(jnp.bfloat16)
        solved = jnp.dot(
            jnp.concatenate([high, low, high], axis=1), solve[...], preferred_element_type=jnp.float32
        )
        inside = []
        for b in range(pieces):
            mine = solved[b * R_NEAR : (b + 1) * R_NEAR]
            value = mine[:, :LANES]
            for level in range(1, FMAX.bit_length()):
                chosen = mine[:, level * LANES : (level + 1) * LANES]
                value = jnp.where(width == (1 << level), chosen, value)
            inside.append(value)
        total = list(inside)
        enter = jnp.zeros((R_NEAR, LANES), jnp.float32)
        for b in range(pieces):
            leave = jnp.broadcast_to(inside[b][:, LANES - 1 : LANES], (R_NEAR, LANES))
            total[b] = total[b] + ahead_entry * enter
            enter = leave + across * enter
        ends = jnp.where(lane == k, enter, ends)
        enter = jnp.zeros((R_NEAR, LANES), jnp.float32)
        for b in reversed(range(pieces)):
            leave = jnp.broadcast_to(inside[b][:, 0:1], (R_NEAR, LANES))
            total[b] = total[b] + behind_entry * enter
            enter = leave + across * enter
        for b in range(pieces):
            local[k, :, b * LANES : (b + 1) * LANES] = total[b]
        return jnp.where(lane == k + LINES, enter, ends)

    carry[...] = lax.fori_loop(
        0, LINES, line, jnp.zeros((R_NEAR, LANES), jnp.float32)
    )
    if part is not None:
        copy.wait()


def finish_kernel(flags, factor, rhs, local, carry, table, held, out):
    cells = out.shape[-1]
    lane = lax.broadcasted_iota(jnp.int32, (R_NEAR, cells), 1).astype(jnp.float32)
    width = factor[:, 0:1]
    block = jnp.floor((lane + 0.5) / width)
    count = cells / width
    log_ratio = table[:, COL_LOG : COL_LOG + 1]
    gain = table[:, COL_GAIN : COL_GAIN + 1]
    from_left = jnp.exp(log_ratio * (block + 1.0))
    from_right = jnp.exp(log_ratio * (count - block))
    near = flags[FIRST] == 1
    for f in range(FIELDS):
        for q in range(PLANES):
            k = f * PLANES + q
            j = k + LINES
            smooth = gain * (
                local[k] + from_left * carry[:, k : k + 1] + from_right * carry[:, j : j + 1]
            )
            out[f, plane_of(flags[ODD], q)] = jnp.where(near, smooth, rhs[k])


def stream(pieces, sems):
    steps = []
    for source, stage, target in pieces:
        for f in range(FIELDS):
            k = 2 * len(steps)
            come = pltpu.make_async_copy(source.at[f], stage.at[f], sems.at[k])
            leave = pltpu.make_async_copy(stage.at[f], target.at[f], sems.at[k + 1])
            steps.append((come, leave))
    for come, _ in steps:
        come.start()

    def finish():
        for come, leave in steps:
            come.wait()
            leave.start()
        for _, leave in steps:
            leave.wait()

    return finish


def pack_first_kernel(count, state, part, low, high, stage, top, bottom, row_sems, sems):
    _, _, rows, _ = state.shape
    odd = lax.axis_index("ax") % 2
    finish = stream([(state.at[:, odd, 0:count, :], stage, part)], sems)
    copies = [
        pltpu.make_async_copy(state.at[:, :, rows - EIGHT : rows, :], top, row_sems.at[0]),
        pltpu.make_async_copy(state.at[:, :, 0:EIGHT, :], bottom, row_sems.at[1]),
    ]
    for copy in copies:
        copy.start()
    finish()
    for copy in copies:
        copy.wait()
    for f in range(FIELDS):
        for q in range(PLANES):
            k = f * PLANES + q
            p = plane_of(odd, q)
            low[k : k + 1, :] = top[f, p, EIGHT - 1 : EIGHT, :]
            high[k : k + 1, :] = bottom[f, p, 0:1, :]


def pack_edges_kernel(state, token, edge, side, left, right, sems):
    _, _, rows, cells = state.shape
    odd = lax.axis_index("ax") % 2
    copies = [
        pltpu.make_async_copy(state.at[:, :, :, cells - LANES : cells], left, sems.at[0]),
        pltpu.make_async_copy(state.at[:, :, :, 0:LANES], right, sems.at[1]),
        pltpu.make_async_copy(state.at[:, 1 - odd, 0:R_NEAR, :], side, sems.at[2]),
    ]
    for copy in copies:
        copy.start()
    for copy in copies[:2]:
        copy.wait()
    lane = lax.broadcasted_iota(jnp.int32, (rows, LANES), 1)
    columns = jnp.ones((rows, LANES), jnp.float32)
    for f in range(FIELDS):
        for q in range(PLANES):
            p = plane_of(odd, q)
            columns = jnp.where(lane == 4 * f + q, left[f, p, :, LANES - 1 : LANES], columns)
            columns = jnp.where(lane == (4 * f - 1 - q) % LANES, right[f, p, :, 0:1], columns)
    edge[...] = columns
    copies[2].wait()


def pack_rest_kernel(parts, tokens, state, *rest):
    rest = rest[tokens:]
    odd = lax.axis_index("ax") % 2
    count = len(parts)
    pieces = []
    for k, (q, first, last) in enumerate(parts):
        pieces.append((state.at[:, plane_of(odd, q), first:last, :], rest[count + k], rest[k]))
    stream(pieces, rest[-1])()


ANY = pl.BlockSpec(memory_space=pl.ANY)
PARAMS = pltpu.CompilerParams(vmem_limit_bytes=VMEM_LIMIT)


def whole(*shape):
    return pl.BlockSpec(shape, lambda i, s: (0,) * len(shape))


def rows_from(shape, axis, first, step):
    def place(i, s):
        row = (first // EIGHT + i * (step // EIGHT)) * EIGHT
        return tuple(row if d == axis else 0 for d in range(len(shape)))

    return pl.BlockSpec(tuple(pl.Element(n) for n in shape), place)


def in_hbm(value):
    return pltpu.with_memory_space_constraint(value, pltpu.HBM)


def cost(flops, nbytes):
    return pl.CostEstimate(flops=flops, bytes_accessed=nbytes, transcendentals=0)


def pack_first(state, count):
    fields, planes, _, cells = state.shape
    vmem = pl.BlockSpec(memory_space=pltpu.VMEM)
    row = jax.ShapeDtypeStruct((LINES, cells), jnp.float32)
    rows = pltpu.VMEM((fields, planes, EIGHT, cells), jnp.float32)
    return pl.pallas_call(
        functools.partial(pack_first_kernel, count),
        in_specs=[ANY],
        out_specs=[ANY, vmem, vmem],
        out_shape=[jax.ShapeDtypeStruct((fields, count, cells), jnp.float32), row, row],
        scratch_shapes=[
            pltpu.VMEM((fields, count, cells), jnp.float32),
            rows,
            rows,
            pltpu.SemaphoreType.DMA((2,)),
            pltpu.SemaphoreType.DMA((2 * fields,)),
        ],
        compiler_params=PARAMS,
        cost_estimate=cost(0, fields * count * cells * 8),
        name="pack_first",
    )(in_hbm(state))


def pack_edges(state, token):
    fields, planes, rows, cells = state.shape
    vmem = pl.BlockSpec(memory_space=pltpu.VMEM)
    tiles = pltpu.VMEM((fields, planes, rows, LANES), jnp.float32)
    return pl.pallas_call(
        pack_edges_kernel,
        in_specs=[ANY, ANY],
        out_specs=[vmem, vmem],
        out_shape=[
            jax.ShapeDtypeStruct((rows, LANES), jnp.float32),
            jax.ShapeDtypeStruct((fields, R_NEAR, cells), jnp.float32),
        ],
        scratch_shapes=[tiles, tiles, pltpu.SemaphoreType.DMA((3,))],
        compiler_params=PARAMS,
        cost_estimate=cost(0, fields * planes * rows * LANES * 16),
        name="pack_edges",
    )(in_hbm(state), token)


def pack_rest(state, parts, *tokens):
    fields, _, _, cells = state.shape
    shapes = [jax.ShapeDtypeStruct((fields, last - first, cells), jnp.float32) for _, first, last in parts]
    return pl.pallas_call(
        functools.partial(pack_rest_kernel, parts, len(tokens)),
        in_specs=[ANY] * (1 + len(tokens)),
        out_specs=[ANY] * len(shapes),
        out_shape=shapes,
        scratch_shapes=[
            *[pltpu.VMEM(x.shape, jnp.float32) for x in shapes],
            pltpu.SemaphoreType.DMA((2 * fields * len(parts),)),
        ],
        compiler_params=PARAMS,
        cost_estimate=cost(0, sum(math.prod(x.shape) for x in shapes) * 8),
        name="pack_rest",
    )(in_hbm(state), *tokens)


def flux_scratch(rows, cells):
    shape = (PLANES, FIELDS, cells // LANES)
    return [pltpu.VMEM((*shape, n, LANES), jnp.float32) for n in (rows + 2 * EIGHT, rows)]


def bulk(flags, state, low, high, inner, edge, dtheta, outer, span, rows, token, held):
    fields, planes, total_rows, cells = state.shape
    first, end = span
    count = end - first
    blocks = count // rows
    size = fields * planes * count * cells
    aliases = {} if held is None else {8: 0}
    state = in_hbm(state)
    operands = [state, low, high, inner, edge, inner if outer is None else outer, in_hbm(token)]
    operands.append(state if held is None else held)
    chunk = pltpu.VMEM((fields, count, cells), jnp.float32)
    return pl.pallas_call(
        functools.partial(bulk_kernel, dtheta, rows, span, total_rows, outer is not None),
        grid_spec=pltpu.PrefetchScalarGridSpec(
            num_scalar_prefetch=1,
            grid=(blocks,),
            in_specs=[
                ANY,
                whole(LINES, cells),
                whole(LINES, cells),
                ANY,
                rows_from((rows, LANES), 0, first, rows),
                ANY,
                ANY,
                ANY,
            ],
            out_specs=rows_from((fields, planes, rows, cells), 2, first, rows),
            scratch_shapes=[
                pltpu.VMEM((fields, planes, count + 2 * EIGHT, cells), jnp.float32),
                chunk,
                pltpu.SemaphoreType.DMA((3 * blocks,)),
                *flux_scratch(rows, cells),
                *([] if outer is None else [chunk]),
            ],
        ),
        out_shape=pltpu.HBM(state.shape, jnp.float32),
        input_output_aliases=aliases,
        compiler_params=PARAMS,
        cost_estimate=cost(size * 60, size * 10),
        name="bulk",
    )(flags, *operands)


def add_outer(flags, outer, span, rows, held):
    fields, count, cells = outer.shape
    chunk = pltpu.VMEM((fields, count, cells), jnp.float32)
    return pl.pallas_call(
        functools.partial(outer_kernel, rows, span),
        grid_spec=pltpu.PrefetchScalarGridSpec(
            num_scalar_prefetch=1,
            grid=(1,),
            in_specs=[ANY, ANY],
            out_specs=ANY,
            scratch_shapes=[chunk, chunk, pltpu.SemaphoreType.DMA((3 * (count // rows),))],
        ),
        out_shape=pltpu.HBM(held.shape, jnp.float32),
        input_output_aliases={2: 0},
        compiler_params=PARAMS,
        cost_estimate=cost(outer.size * 6, outer.size * 16),
        name="add_outer",
    )(flags, outer, held)


def near(flags, state, low, high, inner, edge, dtheta, outer, factor, table, solve, token, part=None):
    fields, planes, rows, cells = state.shape
    out = jax.ShapeDtypeStruct((LINES, R_NEAR, cells), jnp.float32)
    tail = min(R_NEAR // EIGHT, rows // EIGHT - 1)
    state = in_hbm(state)
    out_specs = [whole(LINES, R_NEAR, cells), whole(LINES, R_NEAR, cells), whole(R_NEAR, LANES)]
    out_shape = [out, out, jax.ShapeDtypeStruct((R_NEAR, LANES), jnp.float32)]
    scratch = flux_scratch(R_NEAR, cells)
    if part is not None:
        out_specs.append(whole(fields, part[1] - part[0], cells))
        out_shape.append(jax.ShapeDtypeStruct((fields, part[1] - part[0], cells), jnp.float32))
        scratch.append(pltpu.SemaphoreType.DMA)
    result = pl.pallas_call(
        functools.partial(near_kernel, dtheta, rows, part[0] if part else 0),
        grid_spec=pltpu.PrefetchScalarGridSpec(
            num_scalar_prefetch=1,
            grid=(1,),
            in_specs=[
                whole(fields, planes, R_NEAR, cells),
                pl.BlockSpec((fields, planes, EIGHT, cells), lambda i, s: (0, 0, tail, 0)),
                whole(LINES, cells),
                whole(LINES, cells),
                whole(fields, R_NEAR, cells),
                whole(fields, R_NEAR, cells),
                whole(R_NEAR, LANES),
                whole(R_NEAR, LANES),
                whole(R_NEAR, LANES),
                whole(*solve.shape),
                ANY,
                ANY,
            ],
            out_specs=out_specs,
            scratch_shapes=scratch,
        ),
        out_shape=out_shape,
        compiler_params=PARAMS,
        cost_estimate=cost(LINES * R_NEAR * cells * 200, LINES * R_NEAR * cells * 250),
        name="near",
    )(flags, state, state, low, high, inner, outer, edge, factor, table, solve, in_hbm(token), state)
    return result if part is not None else (*result, None)


def finish(flags, factor, rhs, local, carry, table, held):
    _, _, cells = rhs.shape
    return pl.pallas_call(
        finish_kernel,
        grid_spec=pltpu.PrefetchScalarGridSpec(
            num_scalar_prefetch=1,
            grid=(1,),
            in_specs=[
                whole(R_NEAR, LANES),
                whole(LINES, R_NEAR, cells),
                whole(LINES, R_NEAR, cells),
                whole(R_NEAR, LANES),
                whole(R_NEAR, LANES),
                ANY,
            ],
            out_specs=whole(FIELDS, PLANES, R_NEAR, cells),
        ),
        out_shape=pltpu.HBM(held.shape, jnp.float32),
        input_output_aliases={6: 0},
        compiler_params=PARAMS,
        cost_estimate=cost(LINES * R_NEAR * cells * 10, LINES * R_NEAR * cells * 20),
        name="finish",
    )(flags, factor, rhs, local, carry, table, held)


def chunks(rows):
    size = 16
    triples = (rows - R_NEAR) // (3 * size)
    cuts = sorted({-(-2 * triples // 5), -(-4 * triples // 5), triples})
    ends = [R_NEAR + 3 * size * c for c in cuts]
    return size, list(zip([0] + ends[:-1], ends))


def smoothing_table(coarsen, cells, total_cells, dtheta):
    factor = coarsen.astype(jnp.float32)[:, None]
    stiffness = KAPPA / (factor * dtheta) ** 2
    inverse_half = 0.5 / stiffness
    one_minus = jnp.sqrt(inverse_half * (2.0 + inverse_half)) - inverse_half
    log_ratio = jnp.log1p(-one_minus)
    gain = (1.0 - one_minus) / (stiffness * one_minus * (2.0 - one_minus))
    closing = 1.0 / -jnp.expm1((total_cells / factor) * log_ratio)
    across = jnp.exp((cells / factor) * log_ratio)
    column = jnp.arange(LANES, dtype=jnp.int32)[None, :]
    width = jnp.left_shift(1, jnp.minimum(column, 20)).astype(jnp.float32)
    table = jnp.where(width >= factor, jnp.exp(log_ratio * (width / factor)), 0.0)
    table = jnp.where(column == COL_LOG, log_ratio, table)
    table = jnp.where(column == COL_GAIN, gain, table)
    return table, closing, across


def piece_tables(dtheta):
    tables = []
    for level in range(FMAX.bit_length()):
        width = 1 << level
        half = 0.5 * (width * dtheta) ** 2 / KAPPA
        ratio = 1.0 - (math.sqrt(half * (2.0 + half)) - half)
        block = np.arange(LANES) // width
        tables.append(ratio ** np.abs(block[:, None] - block[None, :]) / width)
    table = np.concatenate(tables, axis=1)
    high = table.astype(ml_dtypes.bfloat16)
    low = (table - high.astype(np.float64)).astype(ml_dtypes.bfloat16)
    return jnp.asarray(np.concatenate([high, high, low], axis=0))


def ring(value, axis, shift):
    size = lax.axis_size(axis)
    return lax.ppermute(value, axis, [(i, (i + shift) % size) for i in range(size)])


def body(state, coarsen):
    fields, planes, rows, cells = state.shape
    sec_count = lax.axis_size("sec")
    rad_count = lax.axis_size("rad")
    ax_count = lax.axis_size("ax")
    assert fields == FIELDS and planes == PLANES and ax_count % 2 == 0
    rad_index = lax.axis_index("rad")
    ax_index = lax.axis_index("ax")
    total_cells = cells * sec_count
    dtheta = 2.0 * math.pi / total_cells
    outer_pairs = []
    for i in range(1, ax_count - 1, 2):
        outer_pairs += [(i, i + 1), (i + 1, i)]
    inner_pairs = []
    for i in range(0, ax_count, 2):
        inner_pairs += [(i, i + 1), (i + 1, i)]
    up = [(i, i + 1) for i in range(rad_count - 1)]
    down = [(i + 1, i) for i in range(rad_count - 1)]
    flags = jnp.stack(
        [
            ax_index % 2,
            ((ax_index > 0) & (ax_index < ax_count - 1)).astype(jnp.int32),
            (rad_index == 0).astype(jnp.int32),
            (rad_index == rad_count - 1).astype(jnp.int32),
            rad_index * rows,
        ]
    ).astype(jnp.int32)
    size, spans = chunks(rows)
    count = len(spans)

    part, low, high = pack_first(state, spans[0][1])
    outer = [lax.ppermute(part, "ax", outer_pairs)]
    columns, side = pack_edges(state, high)
    low = lax.ppermute(low, "rad", up)
    high = lax.ppermute(high, "rad", down)
    inner = [lax.ppermute(side, "ax", inner_pairs)]
    wanted = [(0, R_NEAR, spans[0][1])] + [(0, *span) for span in spans[1:]]
    if count > 1:
        wanted.insert(1, (1, *spans[1]))
    parts = pack_rest(state, wanted, columns, low, high)
    for k, value in enumerate(parts):
        if wanted[k][0]:
            outer.append(lax.ppermute(value, "ax", outer_pairs))
        else:
            inner.append(lax.ppermute(value, "ax", inner_pairs))
    if sec_count == 2:
        edge = ring(columns, "sec", 1)
    else:
        from_left = jnp.arange(LANES)[None, :] % 4 < 2
        edge = jnp.where(from_left, ring(columns, "sec", 1), ring(columns, "sec", -1))

    table, closing, across = smoothing_table(coarsen, cells, total_cells, dtheta)
    factor = jnp.broadcast_to(coarsen.astype(jnp.float32)[:, None], (R_NEAR, LANES))

    solve = piece_tables(dtheta)
    given = (flags, state, low, high)
    def pass_over(k, token, held, fused=True):
        span = (spans[k][0] if k else R_NEAR, spans[k][1])
        return bulk(*given, inner[k + 1], edge, dtheta, outer[k] if fused else None, span, size, token, held)

    out = pass_over(2, parts[0], None, fused=False) if count > 2 else None
    part = spans[2] if count > 2 else None
    token = parts[0] if out is None else out
    rhs, local, ends, part = near(
        *given, inner[0], edge, dtheta, outer[0], factor, table, solve, token, part
    )
    if part is not None:
        outer.append(lax.ppermute(part, "ax", outer_pairs))
    arrived = [ends] + [ring(ends, "sec", k) for k in range(1, sec_count)] + [ends]
    from_left = jnp.arange(LANES)[None, :] < LINES
    carry = jnp.zeros_like(ends)
    for k in range(sec_count, 0, -1):
        carry = carry * across + jnp.where(from_left, arrived[k], arrived[sec_count - k])
    carry = carry * closing

    for k in range(min(count, 2)):
        out = pass_over(k, ends, out)
    out = finish(flags, factor, rhs, local, carry, table, out)
    return add_outer(flags, outer[2], spans[2], size, out) if count > 2 else out


def solution(mesh):
    return jax.shard_map(
        body,
        mesh=mesh,
        in_specs=(P(None, "ax", "rad", "sec"), P()),
        out_specs=P(None, "ax", "rad", "sec"),
        check_vma=False,
    )
```

```python
import functools
import math

import jax
import jax.numpy as jnp
import ml_dtypes
import numpy as np
from jax import lax
from jax.experimental import pallas as pl
from jax.experimental.pallas import tpu as pltpu
from jax.sharding import PartitionSpec as P

R_NEAR = 16
FMAX = 16

GAMMA = 1.4
KAPPA = 1.44

FIELDS = 5
PLANES = 2
LINES = FIELDS * PLANES
EIGHT = 8
LANES = 128
VMEM_LIMIT = 28 * 1024 * 1024

COL_LOG = 32
COL_GAIN = 33

ODD, OUTER, FIRST, LAST, BASE = range(5)


def plane_of(odd, q):
    return odd if q else 1 - odd


def reciprocal(x):
    y = pl.reciprocal(x, approx=True)
    y = y * (2.0 - x * y)
    return y * (2.0 - x * y)


def fluxes(fields, want):
    density, energy = fields[0], fields[4]
    momentum = fields[1:4]
    inverse = reciprocal(density)
    velocity = [m * inverse for m in momentum]
    square = {}
    for i in range(3):
        for j in range(i, 3):
            if i == j or i + 1 in want or j + 1 in want or (i, j) == (1, 2):
                square[i, j] = square[j, i] = momentum[i] * velocity[j]
    pressure = (GAMMA - 1.0) * (energy - 0.5 * (square[0, 0] + square[1, 1] + square[2, 2]))
    enthalpy = energy + pressure
    out = {}
    for d in want:
        k = d - 1
        flow = [square[i, k] + pressure if i == k else square[i, k] for i in range(3)]
        out[d] = [momentum[k]] + flow + [enthalpy * velocity[k]]
    return out, (pressure, square[2, 2], square[1, 2])


def flux_along(fields, along):
    return fluxes(fields, (along,))[0][along]


def outer_flux(flags, outer):
    present = flags[OUTER] == 1
    outer = [jnp.where(present, outer[0], 1.0)] + [jnp.where(present, g, 0.0) for g in outer[1:]]
    return flux_along(outer, 1)


def stencil(
    flags, first_row, rows, total_rows, dtheta, load, next_rows, edge, inner, outer, place, radial, azimuthal
):
    strips = rows // EIGHT
    pieces = radial.shape[2]
    row = lax.broadcasted_iota(jnp.int32, (EIGHT, LANES), 0)
    lane = lax.broadcasted_iota(jnp.int32, (EIGHT, LANES), 1)
    start = flags[BASE] + first_row
    axial_sign = jnp.where(flags[ODD] == 1, 0.5, -0.5)
    above = jnp.where((flags[FIRST] == 1) & (first_row == 0), 0.0, (start - 1).astype(jnp.float32) + 0.5)
    end = first_row + rows == total_rows
    below = jnp.where((flags[LAST] == 1) & end, 0.0, (start + rows).astype(jnp.float32) + 0.5)
    scale = jnp.where(row >= EIGHT // 2, above, below)
    at = [slice(b * LANES, (b + 1) * LANES) for b in range(pieces)]

    for q in range(PLANES):
        for b in range(pieces):
            values = [next_rows(f, q, at[b]) for f in range(FIELDS)]
            values[0] = jnp.where(scale > 0.0, values[0], 1.0)
            flux_next = flux_along(values, 2)
            for f in range(FIELDS):
                radial[q, f, b, 0:EIGHT, :] = flux_next[f] * scale
                radial[q, f, b, EIGHT + rows : 2 * EIGHT + rows, :] = flux_next[f] * scale

    def inside(t, carry):
        r = pl.multiple_of(EIGHT * t, EIGHT)
        radius = (start + r + row).astype(jnp.float32) + 0.5
        inv_radius = 1.0 / radius
        for b in range(pieces):
            beside = flux_along([inner(f, r, at[b]) for f in range(FIELDS)], 1)
            axial, source = [], []
            for q in range(PLANES):
                fields = [load(f, q, r, at[b]) for f in range(FIELDS)]
                flow, (pressure, twist, swirl) = fluxes(fields, (1, 2, 3))
                axial.append(flow[1])
                for f in range(FIELDS):
                    radial[q, f, b, pl.ds(r + EIGHT, EIGHT), :] = flow[2][f] * radius
                    azimuthal[q, f, b, pl.ds(r, EIGHT), :] = flow[3][f]
                source.append(((pressure + twist) * inv_radius, swirl * -inv_radius))
            base = [[axial_sign * (x - y) for x, y in zip(beside, axial[1])]]
            if outer is None:
                base.append([axial_sign * x for x in axial[0]])
            else:
                far = outer_flux(flags, [outer(f, r, at[b]) for f in range(FIELDS)])
                base.append([axial_sign * (x - y) for x, y in zip(axial[0], far)])
            for q in range(PLANES):
                base[q][2] = base[q][2] + source[q][0]
                base[q][3] = base[q][3] + source[q][1]
                for f in range(FIELDS):
                    place(f, q, r)[:, at[b]] = base[q][f]
        return carry

    lax.fori_loop(0, strips, inside, 0)

    def differences(t, carry):
        r = pl.multiple_of(EIGHT * t, EIGHT)
        radius = (start + r + row).astype(jnp.float32) + 0.5
        half_inv = 0.5 / radius
        half_arc = half_inv * (1.0 / dtheta)
        beyond = [edge(r)] + [pltpu.roll(edge(r), LANES - 4 * f, 1) for f in range(1, FIELDS)]
        beyond = flux_along(beyond, 3)
        for q in range(PLANES):
            for f in range(FIELDS):
                ends = [pltpu.roll(beyond[f], s, 1) if q else beyond[f] for s in (LANES - 1, 1)]
                here = [azimuthal[q, f, b, pl.ds(r, EIGHT), :] for b in range(pieces)]
                left = [ends[0]] + [pltpu.roll(x, 1, 1) for x in here]
                right = [pltpu.roll(x, LANES - 1, 1) for x in here] + [ends[1]]
                out = place(f, q, r)
                for b in range(pieces):
                    behind = jnp.where(lane == 0, left[b], left[b + 1])
                    ahead = jnp.where(lane == LANES - 1, right[b + 1], right[b])
                    up = radial[q, f, b, pl.ds(r + EIGHT - 1, EIGHT), :]
                    down = radial[q, f, b, pl.ds(r + EIGHT + 1, EIGHT), :]
                    change = (behind - ahead) * half_arc + (up - down) * half_inv
                    out[:, at[b]] = out[:, at[b]] + change
        return carry

    lax.fori_loop(0, strips, differences, 0)


def bulk_kernel(
    dtheta, rows, span, total_rows, fused, flags, state, low, high, inner, edge, outer, token, held, out, *scratch
):
    first, end = span
    blocks = (end - first) // rows
    state_rows, inner_rows, sems, radial, azimuthal, *outer_rows = scratch
    outer_rows = outer_rows[0] if fused else None
    odd = flags[ODD]
    step = pl.program_id(0)

    def copies(k):
        a = first + k * rows + (EIGHT if k else -EIGHT)
        b = min(first + (k + 1) * rows + EIGHT, total_rows)
        at = a - first + EIGHT
        rest = pl.ds(outer.shape[1] - (end - first) + k * rows, rows)
        here = pl.ds(k * rows, rows)
        sets = [
            (state.at[:, :, a:b, :], state_rows.at[:, :, at : at + b - a, :]),
            (inner.at[:, here, :], inner_rows.at[:, here, :]),
        ]
        if fused:
            sets.append((outer.at[:, rest, :], outer_rows.at[:, here, :]))
        return [pltpu.make_async_copy(x, y, sems.at[3 * k + i]) for i, (x, y) in enumerate(sets)]

    @pl.when(step == 0)
    def _():
        for k in range(blocks):
            for copy in copies(k):
                copy.start()

    for k in range(blocks):

        @pl.when(step == k)
        def _():
            for copy in copies(k):
                copy.wait()

    first_row = first + step * rows
    at_end = first_row + rows == total_rows
    base = pl.multiple_of(step * rows, EIGHT)
    sub = lax.broadcasted_iota(jnp.int32, (EIGHT, LANES), 0)

    def load(f, q, r, at):
        return state_rows[f, plane_of(odd, q), pl.ds(base + EIGHT + r, EIGHT), at]

    def next_rows(f, q, at):
        k = f * PLANES + q
        under = jnp.where(at_end, high[k : k + 1, at], load(f, q, rows, at))
        return jnp.where(sub >= EIGHT // 2, load(f, q, -EIGHT, at), under)

    stencil(
        flags,
        first_row,
        rows,
        total_rows,
        dtheta,
        load,
        next_rows,
        lambda r: edge[pl.ds(r, EIGHT), :],
        lambda f, r, at: inner_rows[f, pl.ds(base + r, EIGHT), at],
        (lambda f, r, at: outer_rows[f, pl.ds(base + r, EIGHT), at]) if fused else None,
        lambda f, q, r: out.at[f, plane_of(odd, q), pl.ds(r, EIGHT), :],
        radial,
        azimuthal,
    )


def outer_kernel(rows, span, flags, outer, held, out, outer_rows, held_rows, sems):
    first, end = span
    plane = lax.axis_index("ax") % 2
    sign = jnp.where(flags[ODD] == 1, -0.5, 0.5)
    steps = []
    for k in range((end - first) // rows):
        here = pl.ds(k * rows, rows)
        there = pl.ds(first + k * rows, rows)
        ways = [
            (outer.at[:, here, :], outer_rows.at[:, here, :]),
            (held.at[:, plane, there, :], held_rows.at[:, here, :]),
            (held_rows.at[:, here, :], out.at[:, plane, there, :]),
        ]
        steps.append([pltpu.make_async_copy(x, y, sems.at[3 * k + i]) for i, (x, y) in enumerate(ways)])
        steps[-1][0].start()
        steps[-1][1].start()
    for k, (come, have, leave) in enumerate(steps):
        come.wait()
        have.wait()
        for t in range(rows // EIGHT):
            at = pl.ds(k * rows + EIGHT * t, EIGHT)
            values = outer_flux(flags, [outer_rows[f, at, :] for f in range(FIELDS)])
            for f in range(FIELDS):
                held_rows[f, at, :] = held_rows[f, at, :] + sign * values[f]
        leave.start()
    for _, _, leave in steps:
        leave.wait()


def near_kernel(
    dtheta,
    total_rows,
    part_first,
    flags,
    state,
    after,
    low,
    high,
    inner,
    outer,
    edge,
    factor,
    table,
    solve,
    token,
    hbm,
    rhs,
    local,
    carry,
    *rest,
):
    cells = state.shape[-1]
    odd = flags[ODD]
    part = rest[0] if len(rest) > 2 else None
    scratch = rest[-2:] if part is None else rest[-3:-1]
    if part is not None:
        source = hbm.at[:, lax.axis_index("ax") % 2, part_first : part_first + part.shape[1], :]
        copy = pltpu.make_async_copy(source, part, rest[-1])
        copy.start()

    sub = lax.broadcasted_iota(jnp.int32, (EIGHT, LANES), 0)

    def next_rows(f, q, at):
        k = f * PLANES + q
        under = high[k : k + 1, at] if total_rows == R_NEAR else after[f, plane_of(odd, q), :, at]
        return jnp.where(sub >= EIGHT // 2, low[k : k + 1, at], under)

    stencil(
        flags,
        0,
        R_NEAR,
        total_rows,
        dtheta,
        lambda f, q, r, at: state[f, plane_of(odd, q), pl.ds(r, EIGHT), at],
        next_rows,
        lambda r: edge[pl.ds(r, EIGHT), :],
        lambda f, r, at: inner[f, pl.ds(r, EIGHT), at],
        lambda f, r, at: outer[f, pl.ds(r, EIGHT), at],
        lambda f, q, r: rhs.at[f * PLANES + q, pl.ds(r, EIGHT), :],
        *scratch,
    )

    pieces = cells // LANES
    lane = lax.broadcasted_iota(jnp.int32, (R_NEAR, LANES), 1)
    width = factor[...]
    log_ratio = table[:, COL_LOG : COL_LOG + 1]
    block = jnp.floor((lane.astype(jnp.float32) + 0.5) / width)
    ahead_entry = jnp.exp(log_ratio * (block + 1.0))
    behind_entry = jnp.exp(log_ratio * (LANES / width - block))
    across = jnp.exp(log_ratio * (LANES / width))

    def line(k, ends):
        rows = jnp.concatenate([rhs[k, :, b * LANES : (b + 1) * LANES] for b in range(pieces)], axis=0)
        high = rows.astype(jnp.bfloat16)
        low = (rows - high.astype(jnp.float32)).astype(jnp.bfloat16)
        solved = jnp.dot(
            jnp.concatenate([high, low, high], axis=1), solve[...], preferred_element_type=jnp.float32
        )
        inside = []
        for b in range(pieces):
            mine = solved[b * R_NEAR : (b + 1) * R_NEAR]
            value = mine[:, :LANES]
            for level in range(1, FMAX.bit_length()):
                chosen = mine[:, level * LANES : (level + 1) * LANES]
                value = jnp.where(width == (1 << level), chosen, value)
            inside.append(value)
        total = list(inside)
        enter = jnp.zeros((R_NEAR, LANES), jnp.float32)
        for b in range(pieces):
            leave = jnp.broadcast_to(inside[b][:, LANES - 1 : LANES], (R_NEAR, LANES))
            total[b] = total[b] + ahead_entry * enter
            enter = leave + across * enter
        ends = jnp.where(lane == k, enter, ends)
        enter = jnp.zeros((R_NEAR, LANES), jnp.float32)
        for b in reversed(range(pieces)):
            leave = jnp.broadcast_to(inside[b][:, 0:1], (R_NEAR, LANES))
            total[b] = total[b] + behind_entry * enter
            enter = leave + across * enter
        for b in range(pieces):
            local[k, :, b * LANES : (b + 1) * LANES] = total[b]
        return jnp.where(lane == k + LINES, enter, ends)

    carry[...] = lax.fori_loop(
        0, LINES, line, jnp.zeros((R_NEAR, LANES), jnp.float32)
    )
    if part is not None:
        copy.wait()


def finish_kernel(flags, factor, rhs, local, carry, table, held, out):
    cells = out.shape[-1]
    lane = lax.broadcasted_iota(jnp.int32, (R_NEAR, cells), 1).astype(jnp.float32)
    width = factor[:, 0:1]
    block = jnp.floor((lane + 0.5) / width)
    count = cells / width
    log_ratio = table[:, COL_LOG : COL_LOG + 1]
    gain = jnp.broadcast_to(table[:, COL_GAIN : COL_GAIN + 1], (R_NEAR, cells))
    from_left = jnp.exp(log_ratio * (block + 1.0))
    from_right = jnp.exp(log_ratio * (count - block))
    near = flags[FIRST] == 1
    for f in range(FIELDS):
        for q in range(PLANES):
            k = f * PLANES + q
            j = k + LINES
            smooth = gain * (
                local[k] + from_left * carry[:, k : k + 1] + from_right * carry[:, j : j + 1]
            )
            out[f, plane_of(flags[ODD], q)] = jnp.where(near, smooth, rhs[k])


def stream(pieces, sems):
    steps = []
    for source, stage, target in pieces:
        for f in range(FIELDS):
            k = 2 * len(steps)
            come = pltpu.make_async_copy(source.at[f], stage.at[f], sems.at[k])
            leave = pltpu.make_async_copy(stage.at[f], target.at[f], sems.at[k + 1])
            steps.append((come, leave))
    for come, _ in steps:
        come.start()

    def finish():
        for come, leave in steps:
            come.wait()
            leave.start()
        for _, leave in steps:
            leave.wait()

    return finish


def pack_first_kernel(count, state, part, low, high, stage, top, bottom, row_sems, sems):
    _, _, rows, _ = state.shape
    odd = lax.axis_index("ax") % 2
    finish = stream([(state.at[:, odd, 0:count, :], stage, part)], sems)
    copies = [
        pltpu.make_async_copy(state.at[:, :, rows - EIGHT : rows, :], top, row_sems.at[0]),
        pltpu.make_async_copy(state.at[:, :, 0:EIGHT, :], bottom, row_sems.at[1]),
    ]
    for copy in copies:
        copy.start()
    finish()
    for copy in copies:
        copy.wait()
    for f in range(FIELDS):
        for q in range(PLANES):
            k = f * PLANES + q
            p = plane_of(odd, q)
            low[k : k + 1, :] = top[f, p, EIGHT - 1 : EIGHT, :]
            high[k : k + 1, :] = bottom[f, p, 0:1, :]


def pack_edges_kernel(state, token, edge, side, left, right, sems):
    _, _, rows, cells = state.shape
    odd = lax.axis_index("ax") % 2
    copies = [
        pltpu.make_async_copy(state.at[:, :, :, cells - LANES : cells], left, sems.at[0]),
        pltpu.make_async_copy(state.at[:, :, :, 0:LANES], right, sems.at[1]),
        pltpu.make_async_copy(state.at[:, 1 - odd, 0:R_NEAR, :], side, sems.at[2]),
    ]
    for copy in copies:
        copy.start()
    for copy in copies[:2]:
        copy.wait()
    lane = lax.broadcasted_iota(jnp.int32, (rows, LANES), 1)
    columns = jnp.ones((rows, LANES), jnp.float32)
    for f in range(FIELDS):
        for q in range(PLANES):
            p = plane_of(odd, q)
            columns = jnp.where(lane == 4 * f + q, left[f, p, :, LANES - 1 : LANES], columns)
            columns = jnp.where(lane == (4 * f - 1 - q) % LANES, right[f, p, :, 0:1], columns)
    edge[...] = columns
    copies[2].wait()


def pack_rest_kernel(parts, tokens, state, *rest):
    rest = rest[tokens:]
    odd = lax.axis_index("ax") % 2
    count = len(parts)
    pieces = []
    for k, (q, first, last) in enumerate(parts):
        pieces.append((state.at[:, plane_of(odd, q), first:last, :], rest[count + k], rest[k]))
    stream(pieces, rest[-1])()


ANY = pl.BlockSpec(memory_space=pl.ANY)
PARAMS = pltpu.CompilerParams(vmem_limit_bytes=VMEM_LIMIT)


def whole(*shape):
    return pl.BlockSpec(shape, lambda i, s: (0,) * len(shape))


def rows_from(shape, axis, first, step):
    def place(i, s):
        row = (first // EIGHT + i * (step // EIGHT)) * EIGHT
        return tuple(row if d == axis else 0 for d in range(len(shape)))

    return pl.BlockSpec(tuple(pl.Element(n) for n in shape), place)


def in_hbm(value):
    return pltpu.with_memory_space_constraint(value, pltpu.HBM)


def cost(flops, nbytes):
    return pl.CostEstimate(flops=flops, bytes_accessed=nbytes, transcendentals=0)


def pack_first(state, count):
    fields, planes, _, cells = state.shape
    vmem = pl.BlockSpec(memory_space=pltpu.VMEM)
    row = jax.ShapeDtypeStruct((LINES, cells), jnp.float32)
    rows = pltpu.VMEM((fields, planes, EIGHT, cells), jnp.float32)
    return pl.pallas_call(
        functools.partial(pack_first_kernel, count),
        in_specs=[ANY],
        out_specs=[ANY, vmem, vmem],
        out_shape=[jax.ShapeDtypeStruct((fields, count, cells), jnp.float32), row, row],
        scratch_shapes=[
            pltpu.VMEM((fields, count, cells), jnp.float32),
            rows,
            rows,
            pltpu.SemaphoreType.DMA((2,)),
            pltpu.SemaphoreType.DMA((2 * fields,)),
        ],
        compiler_params=PARAMS,
        cost_estimate=cost(0, fields * count * cells * 8),
        name="pack_first",
    )(in_hbm(state))


def pack_edges(state, token):
    fields, planes, rows, cells = state.shape
    vmem = pl.BlockSpec(memory_space=pltpu.VMEM)
    tiles = pltpu.VMEM((fields, planes, rows, LANES), jnp.float32)
    return pl.pallas_call(
        pack_edges_kernel,
        in_specs=[ANY, ANY],
        out_specs=[vmem, vmem],
        out_shape=[
            jax.ShapeDtypeStruct((rows, LANES), jnp.float32),
            jax.ShapeDtypeStruct((fields, R_NEAR, cells), jnp.float32),
        ],
        scratch_shapes=[tiles, tiles, pltpu.SemaphoreType.DMA((3,))],
        compiler_params=PARAMS,
        cost_estimate=cost(0, fields * planes * rows * LANES * 16),
        name="pack_edges",
    )(in_hbm(state), token)


def pack_rest(state, parts, *tokens):
    fields, _, _, cells = state.shape
    shapes = [jax.ShapeDtypeStruct((fields, last - first, cells), jnp.float32) for _, first, last in parts]
    return pl.pallas_call(
        functools.partial(pack_rest_kernel, parts, len(tokens)),
        in_specs=[ANY] * (1 + len(tokens)),
        out_specs=[ANY] * len(shapes),
        out_shape=shapes,
        scratch_shapes=[
            *[pltpu.VMEM(x.shape, jnp.float32) for x in shapes],
            pltpu.SemaphoreType.DMA((2 * fields * len(parts),)),
        ],
        compiler_params=PARAMS,
        cost_estimate=cost(0, sum(math.prod(x.shape) for x in shapes) * 8),
        name="pack_rest",
    )(in_hbm(state), *tokens)


def flux_scratch(rows, cells):
    shape = (PLANES, FIELDS, cells // LANES)
    return [pltpu.VMEM((*shape, n, LANES), jnp.float32) for n in (rows + 2 * EIGHT, rows)]


def bulk(flags, state, low, high, inner, edge, dtheta, outer, span, rows, token, held):
    fields, planes, total_rows, cells = state.shape
    first, end = span
    count = end - first
    blocks = count // rows
    size = fields * planes * count * cells
    aliases = {} if held is None else {8: 0}
    state = in_hbm(state)
    operands = [state, low, high, inner, edge, inner if outer is None else outer, in_hbm(token)]
    operands.append(state if held is None else held)
    chunk = pltpu.VMEM((fields, count, cells), jnp.float32)
    return pl.pallas_call(
        functools.partial(bulk_kernel, dtheta, rows, span, total_rows, outer is not None),
        grid_spec=pltpu.PrefetchScalarGridSpec(
            num_scalar_prefetch=1,
            grid=(blocks,),
            in_specs=[
                ANY,
                whole(LINES, cells),
                whole(LINES, cells),
                ANY,
                rows_from((rows, LANES), 0, first, rows),
                ANY,
                ANY,
                ANY,
            ],
            out_specs=rows_from((fields, planes, rows, cells), 2, first, rows),
            scratch_shapes=[
                pltpu.VMEM((fields, planes, count + 2 * EIGHT, cells), jnp.float32),
                chunk,
                pltpu.SemaphoreType.DMA((3 * blocks,)),
                *flux_scratch(rows, cells),
                *([] if outer is None else [chunk]),
            ],
        ),
        out_shape=pltpu.HBM(state.shape, jnp.float32),
        input_output_aliases=aliases,
        compiler_params=PARAMS,
        cost_estimate=cost(size * 60, size * 10),
        name="bulk",
    )(flags, *operands)


def add_outer(flags, outer, span, rows, held):
    fields, count, cells = outer.shape
    chunk = pltpu.VMEM((fields, count, cells), jnp.float32)
    return pl.pallas_call(
        functools.partial(outer_kernel, rows, span),
        grid_spec=pltpu.PrefetchScalarGridSpec(
            num_scalar_prefetch=1,
            grid=(1,),
            in_specs=[ANY, ANY],
            out_specs=ANY,
            scratch_shapes=[chunk, chunk, pltpu.SemaphoreType.DMA((3 * (count // rows),))],
        ),
        out_shape=pltpu.HBM(held.shape, jnp.float32),
        input_output_aliases={2: 0},
        compiler_params=PARAMS,
        cost_estimate=cost(outer.size * 6, outer.size * 16),
        name="add_outer",
    )(flags, outer, held)


def near(flags, state, low, high, inner, edge, dtheta, outer, factor, table, solve, token, part=None):
    fields, planes, rows, cells = state.shape
    out = jax.ShapeDtypeStruct((LINES, R_NEAR, cells), jnp.float32)
    tail = min(R_NEAR // EIGHT, rows // EIGHT - 1)
    state = in_hbm(state)
    out_specs = [whole(LINES, R_NEAR, cells), whole(LINES, R_NEAR, cells), whole(R_NEAR, LANES)]
    out_shape = [out, out, jax.ShapeDtypeStruct((R_NEAR, LANES), jnp.float32)]
    scratch = flux_scratch(R_NEAR, cells)
    if part is not None:
        out_specs.append(whole(fields, part[1] - part[0], cells))
        out_shape.append(jax.ShapeDtypeStruct((fields, part[1] - part[0], cells), jnp.float32))
        scratch.append(pltpu.SemaphoreType.DMA)
    result = pl.pallas_call(
        functools.partial(near_kernel, dtheta, rows, part[0] if part else 0),
        grid_spec=pltpu.PrefetchScalarGridSpec(
            num_scalar_prefetch=1,
            grid=(1,),
            in_specs=[
                whole(fields, planes, R_NEAR, cells),
                pl.BlockSpec((fields, planes, EIGHT, cells), lambda i, s: (0, 0, tail, 0)),
                whole(LINES, cells),
                whole(LINES, cells),
                whole(fields, R_NEAR, cells),
                whole(fields, R_NEAR, cells),
                whole(R_NEAR, LANES),
                whole(R_NEAR, LANES),
                whole(R_NEAR, LANES),
                whole(*solve.shape),
                ANY,
                ANY,
            ],
            out_specs=out_specs,
            scratch_shapes=scratch,
        ),
        out_shape=out_shape,
        compiler_params=PARAMS,
        cost_estimate=cost(LINES * R_NEAR * cells * 200, LINES * R_NEAR * cells * 250),
        name="near",
    )(flags, state, state, low, high, inner, outer, edge, factor, table, solve, in_hbm(token), state)
    return result if part is not None else (*result, None)


def finish(flags, factor, rhs, local, carry, table, held):
    _, _, cells = rhs.shape
    return pl.pallas_call(
        finish_kernel,
        grid_spec=pltpu.PrefetchScalarGridSpec(
            num_scalar_prefetch=1,
            grid=(1,),
            in_specs=[
                whole(R_NEAR, LANES),
                whole(LINES, R_NEAR, cells),
                whole(LINES, R_NEAR, cells),
                whole(R_NEAR, LANES),
                whole(R_NEAR, LANES),
                ANY,
            ],
            out_specs=whole(FIELDS, PLANES, R_NEAR, cells),
        ),
        out_shape=pltpu.HBM(held.shape, jnp.float32),
        input_output_aliases={6: 0},
        compiler_params=PARAMS,
        cost_estimate=cost(LINES * R_NEAR * cells * 10, LINES * R_NEAR * cells * 20),
        name="finish",
    )(flags, factor, rhs, local, carry, table, held)


def chunks(rows):
    size = 16
    blocks = (rows - R_NEAR) // size
    cuts = sorted({-(-2 * blocks // 5), -(-4 * blocks // 5), blocks})
    ends = [R_NEAR + size * c for c in cuts]
    return size, list(zip([0] + ends[:-1], ends))


def smoothing_table(coarsen, cells, total_cells, dtheta):
    factor = coarsen.astype(jnp.float32)[:, None]
    stiffness = KAPPA / (factor * dtheta) ** 2
    inverse_half = 0.5 / stiffness
    one_minus = jnp.sqrt(inverse_half * (2.0 + inverse_half)) - inverse_half
    log_ratio = jnp.log1p(-one_minus)
    gain = (1.0 - one_minus) / (stiffness * one_minus * (2.0 - one_minus))
    closing = 1.0 / -jnp.expm1((total_cells / factor) * log_ratio)
    across = jnp.exp((cells / factor) * log_ratio)
    column = jnp.arange(LANES, dtype=jnp.int32)[None, :]
    width = jnp.left_shift(1, jnp.minimum(column, 20)).astype(jnp.float32)
    table = jnp.where(width >= factor, jnp.exp(log_ratio * (width / factor)), 0.0)
    table = jnp.where(column == COL_LOG, log_ratio, table)
    table = jnp.where(column == COL_GAIN, gain, table)
    return table, closing, across


def piece_tables(dtheta):
    tables = []
    for level in range(FMAX.bit_length()):
        width = 1 << level
        half = 0.5 * (width * dtheta) ** 2 / KAPPA
        ratio = 1.0 - (math.sqrt(half * (2.0 + half)) - half)
        block = np.arange(LANES) // width
        tables.append(ratio ** np.abs(block[:, None] - block[None, :]) / width)
    table = np.concatenate(tables, axis=1)
    high = table.astype(ml_dtypes.bfloat16)
    low = (table - high.astype(np.float64)).astype(ml_dtypes.bfloat16)
    return jnp.asarray(np.concatenate([high, high, low], axis=0))


def ring(value, axis, shift):
    size = lax.axis_size(axis)
    return lax.ppermute(value, axis, [(i, (i + shift) % size) for i in range(size)])


def body(state, coarsen):
    fields, planes, rows, cells = state.shape
    sec_count = lax.axis_size("sec")
    rad_count = lax.axis_size("rad")
    ax_count = lax.axis_size("ax")
    assert fields == FIELDS and planes == PLANES and ax_count % 2 == 0
    rad_index = lax.axis_index("rad")
    ax_index = lax.axis_index("ax")
    total_cells = cells * sec_count
    dtheta = 2.0 * math.pi / total_cells
    outer_pairs = []
    for i in range(1, ax_count - 1, 2):
        outer_pairs += [(i, i + 1), (i + 1, i)]
    inner_pairs = []
    for i in range(0, ax_count, 2):
        inner_pairs += [(i, i + 1), (i + 1, i)]
    up = [(i, i + 1) for i in range(rad_count - 1)]
    down = [(i + 1, i) for i in range(rad_count - 1)]
    flags = jnp.stack(
        [
            ax_index % 2,
            ((ax_index > 0) & (ax_index < ax_count - 1)).astype(jnp.int32),
            (rad_index == 0).astype(jnp.int32),
            (rad_index == rad_count - 1).astype(jnp.int32),
            rad_index * rows,
        ]
    ).astype(jnp.int32)
    size, spans = chunks(rows)
    count = len(spans)

    part, low, high = pack_first(state, spans[0][1])
    outer = [lax.ppermute(part, "ax", outer_pairs)]
    columns, side = pack_edges(state, high)
    low = lax.ppermute(low, "rad", up)
    high = lax.ppermute(high, "rad", down)
    inner = [lax.ppermute(side, "ax", inner_pairs)]
    wanted = [(0, R_NEAR, spans[0][1])] + [(0, *span) for span in spans[1:]]
    if count > 1:
        wanted.insert(1, (1, *spans[1]))
    parts = pack_rest(state, wanted, columns, low, high)
    for k, value in enumerate(parts):
        if wanted[k][0]:
            outer.append(lax.ppermute(value, "ax", outer_pairs))
        else:
            inner.append(lax.ppermute(value, "ax", inner_pairs))
    if sec_count == 2:
        edge = ring(columns, "sec", 1)
    else:
        from_left = jnp.arange(LANES)[None, :] % 4 < 2
        edge = jnp.where(from_left, ring(columns, "sec", 1), ring(columns, "sec", -1))

    table, closing, across = smoothing_table(coarsen, cells, total_cells, dtheta)
    factor = jnp.broadcast_to(coarsen.astype(jnp.float32)[:, None], (R_NEAR, LANES))

    solve = piece_tables(dtheta)
    given = (flags, state, low, high)
    def pass_over(k, token, held, fused=True):
        span = (spans[k][0] if k else R_NEAR, spans[k][1])
        return bulk(*given, inner[k + 1], edge, dtheta, outer[k] if fused else None, span, size, token, held)

    out = pass_over(2, parts[0], None, fused=False) if count > 2 else None
    part = spans[2] if count > 2 else None
    token = parts[0] if out is None else out
    rhs, local, ends, part = near(
        *given, inner[0], edge, dtheta, outer[0], factor, table, solve, token, part
    )
    if part is not None:
        outer.append(lax.ppermute(part, "ax", outer_pairs))
    arrived = [ends] + [ring(ends, "sec", k) for k in range(1, sec_count)] + [ends]
    from_left = jnp.arange(LANES)[None, :] < LINES
    carry = jnp.zeros_like(ends)
    for k in range(sec_count, 0, -1):
        carry = carry * across + jnp.where(from_left, arrived[k], arrived[sec_count - k])
    carry = carry * closing

    for k in range(min(count, 2)):
        out = pass_over(k, ends, out)
    out = finish(flags, factor, rhs, local, carry, table, out)
    return add_outer(flags, outer[2], spans[2], size, out) if count > 2 else out


def solution(mesh):
    return jax.shard_map(
        body,
        mesh=mesh,
        in_specs=(P(None, "ax", "rad", "sec"), P()),
        out_specs=P(None, "ax", "rad", "sec"),
        check_vma=False,
    )
```

```python
import functools
import math

import jax
import jax.numpy as jnp
import ml_dtypes
import numpy as np
from jax import lax
from jax.experimental import pallas as pl
from jax.experimental.pallas import tpu as pltpu
from jax.sharding import PartitionSpec as P

R_NEAR = 16
FMAX = 16

GAMMA = 1.4
KAPPA = 1.44

FIELDS = 5
PLANES = 2
LINES = FIELDS * PLANES
EIGHT = 8
LANES = 128
VMEM_LIMIT = 28 * 1024 * 1024

COL_LOG = 32
COL_GAIN = 33
COL_CLOSING = 34
COL_ACROSS = 35

ODD, OUTER, FIRST, LAST, BASE = range(5)


def plane_of(odd, q):
    return odd if q else 1 - odd


def reciprocal(x):
    y = pl.reciprocal(x, approx=True)
    y = y * (2.0 - x * y)
    return y * (2.0 - x * y)


def fluxes(fields, want):
    density, energy = fields[0], fields[4]
    momentum = fields[1:4]
    inverse = reciprocal(density)
    velocity = [m * inverse for m in momentum]
    square = {}
    for i in range(3):
        for j in range(i, 3):
            if i == j or i + 1 in want or j + 1 in want or (i, j) == (1, 2):
                square[i, j] = square[j, i] = momentum[i] * velocity[j]
    pressure = (GAMMA - 1.0) * (energy - 0.5 * (square[0, 0] + square[1, 1] + square[2, 2]))
    enthalpy = energy + pressure
    out = {}
    for d in want:
        k = d - 1
        flow = [square[i, k] + pressure if i == k else square[i, k] for i in range(3)]
        out[d] = [momentum[k]] + flow + [enthalpy * velocity[k]]
    return out, (pressure, square[2, 2], square[1, 2])


def flux_along(fields, along):
    return fluxes(fields, (along,))[0][along]


def outer_flux(flags, outer):
    present = flags[OUTER] == 1
    outer = [jnp.where(present, outer[0], 1.0)] + [jnp.where(present, g, 0.0) for g in outer[1:]]
    return flux_along(outer, 1)


def stencil(
    flags, first_row, rows, total_rows, dtheta, load, next_rows, edge, inner, outer, place, radial, azimuthal
):
    strips = rows // EIGHT
    pieces = radial.shape[2]
    row = lax.broadcasted_iota(jnp.int32, (EIGHT, LANES), 0)
    lane = lax.broadcasted_iota(jnp.int32, (EIGHT, LANES), 1)
    start = flags[BASE] + first_row
    axial_sign = jnp.where(flags[ODD] == 1, 0.5, -0.5)
    above = jnp.where((flags[FIRST] == 1) & (first_row == 0), 0.0, (start - 1).astype(jnp.float32) + 0.5)
    end = first_row + rows == total_rows
    below = jnp.where((flags[LAST] == 1) & end, 0.0, (start + rows).astype(jnp.float32) + 0.5)
    scale = jnp.where(row >= EIGHT // 2, above, below)
    at = [slice(b * LANES, (b + 1) * LANES) for b in range(pieces)]

    for q in range(PLANES):
        for b in range(pieces):
            values = [next_rows(f, q, at[b]) for f in range(FIELDS)]
            values[0] = jnp.where(scale > 0.0, values[0], 1.0)
            flux_next = flux_along(values, 2)
            for f in range(FIELDS):
                radial[q, f, b, 0:EIGHT, :] = flux_next[f] * scale
                radial[q, f, b, EIGHT + rows : 2 * EIGHT + rows, :] = flux_next[f] * scale

    def inside(t, carry):
        r = pl.multiple_of(EIGHT * t, EIGHT)
        radius = (start + r + row).astype(jnp.float32) + 0.5
        inv_radius = 1.0 / radius
        for b in range(pieces):
            beside = flux_along([inner(f, r, at[b]) for f in range(FIELDS)], 1)
            axial, source = [], []
            for q in range(PLANES):
                fields = [load(f, q, r, at[b]) for f in range(FIELDS)]
                flow, (pressure, twist, swirl) = fluxes(fields, (1, 2, 3))
                axial.append(flow[1])
                for f in range(FIELDS):
                    radial[q, f, b, pl.ds(r + EIGHT, EIGHT), :] = flow[2][f] * radius
                    azimuthal[q, f, b, pl.ds(r, EIGHT), :] = flow[3][f]
                source.append(((pressure + twist) * inv_radius, swirl * -inv_radius))
            base = [[axial_sign * (x - y) for x, y in zip(beside, axial[1])]]
            if outer is None:
                base.append([axial_sign * x for x in axial[0]])
            else:
                far = outer_flux(flags, [outer(f, r, at[b]) for f in range(FIELDS)])
                base.append([axial_sign * (x - y) for x, y in zip(axial[0], far)])
            for q in range(PLANES):
                base[q][2] = base[q][2] + source[q][0]
                base[q][3] = base[q][3] + source[q][1]
                for f in range(FIELDS):
                    place(f, q, r)[:, at[b]] = base[q][f]
        return carry

    lax.fori_loop(0, strips, inside, 0)

    def differences(t, carry):
        r = pl.multiple_of(EIGHT * t, EIGHT)
        radius = (start + r + row).astype(jnp.float32) + 0.5
        half_inv = 0.5 / radius
        half_arc = half_inv * (1.0 / dtheta)
        beyond = [edge(r)] + [pltpu.roll(edge(r), LANES - 4 * f, 1) for f in range(1, FIELDS)]
        beyond = flux_along(beyond, 3)
        for q in range(PLANES):
            for f in range(FIELDS):
                ends = [pltpu.roll(beyond[f], s, 1) if q else beyond[f] for s in (LANES - 1, 1)]
                here = [azimuthal[q, f, b, pl.ds(r, EIGHT), :] for b in range(pieces)]
                left = [ends[0]] + [pltpu.roll(x, 1, 1) for x in here]
                right = [pltpu.roll(x, LANES - 1, 1) for x in here] + [ends[1]]
                out = place(f, q, r)
                for b in range(pieces):
                    behind = jnp.where(lane == 0, left[b], left[b + 1])
                    ahead = jnp.where(lane == LANES - 1, right[b + 1], right[b])
                    up = radial[q, f, b, pl.ds(r + EIGHT - 1, EIGHT), :]
                    down = radial[q, f, b, pl.ds(r + EIGHT + 1, EIGHT), :]
                    change = (behind - ahead) * half_arc + (up - down) * half_inv
                    out[:, at[b]] = out[:, at[b]] + change
        return carry

    lax.fori_loop(0, strips, differences, 0)


def bulk_kernel(
    dtheta, rows, span, total_rows, fused, pieces, flags, state, low, high, edge, outer, token, held, *rest
):
    inner, out, scratch = rest[:pieces], rest[pieces], rest[pieces + 1 :]
    inner_blocks = [(x, pl.ds(r, rows)) for x in inner for r in range(0, x.shape[1], rows)]
    first, end = span
    blocks = (end - first) // rows
    state_rows, inner_rows, sems, radial, azimuthal, *outer_rows = scratch
    outer_rows = outer_rows[0] if fused else None
    odd = flags[ODD]
    step = pl.program_id(0)

    def copies(k):
        a = first + k * rows + (EIGHT if k else -EIGHT)
        b = min(first + (k + 1) * rows + EIGHT, total_rows)
        at = a - first + EIGHT
        rest = pl.ds(outer.shape[1] - (end - first) + k * rows, rows)
        here = pl.ds(k * rows, rows)
        sets = [
            (state.at[:, :, a:b, :], state_rows.at[:, :, at : at + b - a, :]),
            (inner_blocks[k][0].at[:, inner_blocks[k][1], :], inner_rows.at[:, here, :]),
        ]
        if fused:
            sets.append((outer.at[:, rest, :], outer_rows.at[:, here, :]))
        return [pltpu.make_async_copy(x, y, sems.at[3 * k + i]) for i, (x, y) in enumerate(sets)]

    @pl.when(step == 0)
    def _():
        for k in range(blocks):
            for copy in copies(k):
                copy.start()

    for k in range(blocks):

        @pl.when(step == k)
        def _():
            for copy in copies(k):
                copy.wait()

    first_row = first + step * rows
    at_end = first_row + rows == total_rows
    base = pl.multiple_of(step * rows, EIGHT)
    sub = lax.broadcasted_iota(jnp.int32, (EIGHT, LANES), 0)

    def load(f, q, r, at):
        return state_rows[f, plane_of(odd, q), pl.ds(base + EIGHT + r, EIGHT), at]

    def next_rows(f, q, at):
        k = f * PLANES + q
        under = jnp.where(at_end, high[k : k + 1, at], load(f, q, rows, at))
        return jnp.where(sub >= EIGHT // 2, load(f, q, -EIGHT, at), under)

    stencil(
        flags,
        first_row,
        rows,
        total_rows,
        dtheta,
        load,
        next_rows,
        lambda r: edge[pl.ds(r, EIGHT), :],
        lambda f, r, at: inner_rows[f, pl.ds(base + r, EIGHT), at],
        (lambda f, r, at: outer_rows[f, pl.ds(base + r, EIGHT), at]) if fused else None,
        lambda f, q, r: out.at[f, plane_of(odd, q), pl.ds(r, EIGHT), :],
        radial,
        azimuthal,
    )


def outer_kernel(rows, span, flags, outer, held, out, outer_rows, held_rows, sems):
    first, end = span
    plane = lax.axis_index("ax") % 2
    sign = jnp.where(flags[ODD] == 1, -0.5, 0.5)
    steps = []
    for k in range((end - first) // rows):
        here = pl.ds(k * rows, rows)
        there = pl.ds(first + k * rows, rows)
        ways = [
            (outer.at[:, here, :], outer_rows.at[:, here, :]),
            (held.at[:, plane, there, :], held_rows.at[:, here, :]),
            (held_rows.at[:, here, :], out.at[:, plane, there, :]),
        ]
        steps.append([pltpu.make_async_copy(x, y, sems.at[3 * k + i]) for i, (x, y) in enumerate(ways)])
        steps[-1][0].start()
        steps[-1][1].start()
    for k, (come, have, leave) in enumerate(steps):
        come.wait()
        have.wait()
        for t in range(rows // EIGHT):
            at = pl.ds(k * rows + EIGHT * t, EIGHT)
            values = outer_flux(flags, [outer_rows[f, at, :] for f in range(FIELDS)])
            for f in range(FIELDS):
                held_rows[f, at, :] = held_rows[f, at, :] + sign * values[f]
        leave.start()
    for _, _, leave in steps:
        leave.wait()


def near_kernel(
    dtheta,
    total_rows,
    part_first,
    flags,
    state,
    after,
    low,
    high,
    inner,
    outer,
    edge,
    factor,
    table,
    solve,
    token,
    hbm,
    rhs,
    local,
    carry,
    *rest,
):
    cells = state.shape[-1]
    odd = flags[ODD]
    part = rest[0] if len(rest) > 2 else None
    scratch = rest[-2:] if part is None else rest[-3:-1]
    if part is not None:
        source = hbm.at[:, lax.axis_index("ax") % 2, part_first : part_first + part.shape[1], :]
        copy = pltpu.make_async_copy(source, part, rest[-1])
        copy.start()

    sub = lax.broadcasted_iota(jnp.int32, (EIGHT, LANES), 0)

    def next_rows(f, q, at):
        k = f * PLANES + q
        under = high[k : k + 1, at] if total_rows == R_NEAR else after[f, plane_of(odd, q), :, at]
        return jnp.where(sub >= EIGHT // 2, low[k : k + 1, at], under)

    stencil(
        flags,
        0,
        R_NEAR,
        total_rows,
        dtheta,
        lambda f, q, r, at: state[f, plane_of(odd, q), pl.ds(r, EIGHT), at],
        next_rows,
        lambda r: edge[pl.ds(r, EIGHT), :],
        lambda f, r, at: inner[f, pl.ds(r, EIGHT), at],
        lambda f, r, at: outer[f, pl.ds(r, EIGHT), at],
        lambda f, q, r: rhs.at[f * PLANES + q, pl.ds(r, EIGHT), :],
        *scratch,
    )

    pieces = cells // LANES
    lane = lax.broadcasted_iota(jnp.int32, (R_NEAR, LANES), 1)
    width = factor[...]
    log_ratio = table[:, COL_LOG : COL_LOG + 1]
    block = jnp.floor((lane.astype(jnp.float32) + 0.5) / width)
    ahead_entry = jnp.exp(log_ratio * (block + 1.0))
    behind_entry = jnp.exp(log_ratio * (LANES / width - block))
    across = jnp.exp(log_ratio * (LANES / width))

    def line(k, ends):
        rows = jnp.concatenate([rhs[k, :, b * LANES : (b + 1) * LANES] for b in range(pieces)], axis=0)
        high = rows.astype(jnp.bfloat16)
        low = (rows - high.astype(jnp.float32)).astype(jnp.bfloat16)
        solved = jnp.dot(
            jnp.concatenate([high, low, high], axis=1), solve[...], preferred_element_type=jnp.float32
        )
        inside = []
        for b in range(pieces):
            mine = solved[b * R_NEAR : (b + 1) * R_NEAR]
            value = mine[:, :LANES]
            for level in range(1, FMAX.bit_length()):
                chosen = mine[:, level * LANES : (level + 1) * LANES]
                value = jnp.where(width == (1 << level), chosen, value)
            inside.append(value)
        total = list(inside)
        enter = jnp.zeros((R_NEAR, LANES), jnp.float32)
        for b in range(pieces):
            leave = jnp.broadcast_to(inside[b][:, LANES - 1 : LANES], (R_NEAR, LANES))
            total[b] = total[b] + ahead_entry * enter
            enter = leave + across * enter
        ends = jnp.where(lane == k, enter, ends)
        enter = jnp.zeros((R_NEAR, LANES), jnp.float32)
        for b in reversed(range(pieces)):
            leave = jnp.broadcast_to(inside[b][:, 0:1], (R_NEAR, LANES))
            total[b] = total[b] + behind_entry * enter
            enter = leave + across * enter
        for b in range(pieces):
            local[k, :, b * LANES : (b + 1) * LANES] = total[b]
        return jnp.where(lane == k + LINES, enter, ends)

    carry[...] = lax.fori_loop(
        0, LINES, line, jnp.zeros((R_NEAR, LANES), jnp.float32)
    )
    if part is not None:
        copy.wait()


def finish_kernel(flags, factor, rhs, local, table, *rest):
    *ends, held, out = rest
    cells = out.shape[-1]
    column = lax.broadcasted_iota(jnp.int32, (R_NEAR, LANES), 1)
    ends = [x[...] for x in ends]
    ends.append(ends[0])
    carry = jnp.zeros((R_NEAR, LANES), jnp.float32)
    for k in range(len(ends) - 1, 0, -1):
        arrived = jnp.where(column < LINES, ends[k], ends[len(ends) - 1 - k])
        carry = carry * table[:, COL_ACROSS : COL_ACROSS + 1] + arrived
    carry = carry * table[:, COL_CLOSING : COL_CLOSING + 1]
    lane = lax.broadcasted_iota(jnp.int32, (R_NEAR, cells), 1).astype(jnp.float32)
    width = factor[:, 0:1]
    block = jnp.floor((lane + 0.5) / width)
    count = cells / width
    log_ratio = table[:, COL_LOG : COL_LOG + 1]
    gain = jnp.broadcast_to(table[:, COL_GAIN : COL_GAIN + 1], (R_NEAR, cells))
    from_left = jnp.exp(log_ratio * (block + 1.0))
    from_right = jnp.exp(log_ratio * (count - block))
    near = flags[FIRST] == 1
    for f in range(FIELDS):
        for q in range(PLANES):
            k = f * PLANES + q
            j = k + LINES
            smooth = gain * (
                local[k] + from_left * carry[:, k : k + 1] + from_right * carry[:, j : j + 1]
            )
            out[f, plane_of(flags[ODD], q)] = jnp.where(near, smooth, rhs[k])


def stream(pieces, sems):
    steps = []
    for source, stage, target in pieces:
        for f in range(FIELDS):
            k = 2 * len(steps)
            come = pltpu.make_async_copy(source.at[f], stage.at[f], sems.at[k])
            leave = pltpu.make_async_copy(stage.at[f], target.at[f], sems.at[k + 1])
            steps.append((come, leave))
    for come, _ in steps:
        come.start()

    def finish():
        for come, leave in steps:
            come.wait()
            leave.start()
        for _, leave in steps:
            leave.wait()

    return finish


def pack_first_kernel(count, state, part, low, high, stage, top, bottom, low_row, high_row, row_sems, sems):
    _, _, rows, _ = state.shape
    odd = lax.axis_index("ax") % 2
    copies = [
        pltpu.make_async_copy(state.at[:, :, rows - EIGHT : rows, :], top, row_sems.at[0]),
        pltpu.make_async_copy(state.at[:, :, 0:EIGHT, :], bottom, row_sems.at[1]),
    ]
    leave = [
        pltpu.make_async_copy(low_row, low, row_sems.at[2]),
        pltpu.make_async_copy(high_row, high, row_sems.at[3]),
    ]
    for copy in copies:
        copy.start()
    finish = stream([(state.at[:, odd, 0:count, :], stage, part)], sems)
    for copy in copies:
        copy.wait()
    for f in range(FIELDS):
        for q in range(PLANES):
            k = f * PLANES + q
            p = plane_of(odd, q)
            low_row[k : k + 1, :] = top[f, p, EIGHT - 1 : EIGHT, :]
            high_row[k : k + 1, :] = bottom[f, p, 0:1, :]
    for copy in leave:
        copy.start()
    finish()
    for copy in leave:
        copy.wait()


def pack_edges_kernel(state, token, edge, side, left, right, columns_row, stage, col_sems, sems):
    _, _, rows, cells = state.shape
    odd = lax.axis_index("ax") % 2
    copies = [
        pltpu.make_async_copy(state.at[:, :, :, cells - LANES : cells], left, col_sems.at[0]),
        pltpu.make_async_copy(state.at[:, :, :, 0:LANES], right, col_sems.at[1]),
    ]
    for copy in copies:
        copy.start()
    finish = stream([(state.at[:, 1 - odd, 0:R_NEAR, :], stage, side)], sems)
    for copy in copies:
        copy.wait()
    lane = lax.broadcasted_iota(jnp.int32, (rows, LANES), 1)
    columns = jnp.ones((rows, LANES), jnp.float32)
    for f in range(FIELDS):
        for q in range(PLANES):
            p = plane_of(odd, q)
            columns = jnp.where(lane == 4 * f + q, left[f, p, :, LANES - 1 : LANES], columns)
            columns = jnp.where(lane == (4 * f - 1 - q) % LANES, right[f, p, :, 0:1], columns)
    columns_row[...] = columns
    leave = pltpu.make_async_copy(columns_row, edge, col_sems.at[2])
    leave.start()
    finish()
    leave.wait()


def pack_rest_kernel(parts, tokens, state, *rest):
    rest = rest[tokens:]
    odd = lax.axis_index("ax") % 2
    count = len(parts)
    pieces = []
    for k, (q, first, last) in enumerate(parts):
        pieces.append((state.at[:, plane_of(odd, q), first:last, :], rest[count + k], rest[k]))
    stream(pieces, rest[-1])()


ANY = pl.BlockSpec(memory_space=pl.ANY)
PARAMS = pltpu.CompilerParams(vmem_limit_bytes=VMEM_LIMIT)


def whole(*shape):
    return pl.BlockSpec(shape, lambda i, s: (0,) * len(shape))


def rows_from(shape, axis, first, step):
    def place(i, s):
        row = (first // EIGHT + i * (step // EIGHT)) * EIGHT
        return tuple(row if d == axis else 0 for d in range(len(shape)))

    return pl.BlockSpec(tuple(pl.Element(n) for n in shape), place)


def in_hbm(value):
    return pltpu.with_memory_space_constraint(value, pltpu.HBM)


def cost(flops, nbytes):
    return pl.CostEstimate(flops=flops, bytes_accessed=nbytes, transcendentals=0)


def pack_first(state, count):
    fields, planes, _, cells = state.shape
    rows = pltpu.VMEM((fields, planes, EIGHT, cells), jnp.float32)
    row = pltpu.VMEM((LINES, cells), jnp.float32)
    return pl.pallas_call(
        functools.partial(pack_first_kernel, count),
        in_specs=[ANY],
        out_specs=[ANY] * 3,
        out_shape=[
            jax.ShapeDtypeStruct((fields, count, cells), jnp.float32),
            jax.ShapeDtypeStruct((LINES, cells), jnp.float32),
            jax.ShapeDtypeStruct((LINES, cells), jnp.float32),
        ],
        scratch_shapes=[
            pltpu.VMEM((fields, count, cells), jnp.float32),
            rows,
            rows,
            row,
            row,
            pltpu.SemaphoreType.DMA((4,)),
            pltpu.SemaphoreType.DMA((2 * fields,)),
        ],
        compiler_params=PARAMS,
        cost_estimate=cost(0, fields * count * cells * 8),
        name="pack_first",
    )(in_hbm(state))


def pack_edges(state, token):
    fields, planes, rows, cells = state.shape
    tiles = pltpu.VMEM((fields, planes, rows, LANES), jnp.float32)
    return pl.pallas_call(
        pack_edges_kernel,
        in_specs=[ANY, ANY],
        out_specs=[ANY, ANY],
        out_shape=[
            jax.ShapeDtypeStruct((rows, LANES), jnp.float32),
            pltpu.HBM((fields, R_NEAR, cells), jnp.float32),
        ],
        scratch_shapes=[
            tiles,
            tiles,
            pltpu.VMEM((rows, LANES), jnp.float32),
            pltpu.VMEM((fields, R_NEAR, cells), jnp.float32),
            pltpu.SemaphoreType.DMA((3,)),
            pltpu.SemaphoreType.DMA((2 * fields,)),
        ],
        compiler_params=PARAMS,
        cost_estimate=cost(0, fields * planes * rows * LANES * 16),
        name="pack_edges",
    )(in_hbm(state), token)


def pack_rest(state, parts, *tokens):
    fields, _, _, cells = state.shape
    shapes = [jax.ShapeDtypeStruct((fields, last - first, cells), jnp.float32) for _, first, last in parts]
    return pl.pallas_call(
        functools.partial(pack_rest_kernel, parts, len(tokens)),
        in_specs=[ANY] * (1 + len(tokens)),
        out_specs=[ANY] * len(shapes),
        out_shape=shapes,
        scratch_shapes=[
            *[pltpu.VMEM(x.shape, jnp.float32) for x in shapes],
            pltpu.SemaphoreType.DMA((2 * fields * len(parts),)),
        ],
        compiler_params=PARAMS,
        cost_estimate=cost(0, sum(math.prod(x.shape) for x in shapes) * 8),
        name="pack_rest",
    )(in_hbm(state), *tokens)


def flux_scratch(rows, cells):
    shape = (PLANES, FIELDS, cells // LANES)
    return [pltpu.VMEM((*shape, n, LANES), jnp.float32) for n in (rows + 2 * EIGHT, rows)]


def bulk(flags, state, low, high, inner, edge, dtheta, outer, span, rows, token, held):
    fields, planes, total_rows, cells = state.shape
    first, end = span
    count = end - first
    blocks = count // rows
    size = fields * planes * count * cells
    aliases = {} if held is None else {7: 0}
    state = in_hbm(state)
    operands = [state, low, high, edge, inner[0] if outer is None else outer, in_hbm(token)]
    operands += [state if held is None else held, *inner]
    chunk = pltpu.VMEM((fields, count, cells), jnp.float32)
    return pl.pallas_call(
        functools.partial(bulk_kernel, dtheta, rows, span, total_rows, outer is not None, len(inner)),
        grid_spec=pltpu.PrefetchScalarGridSpec(
            num_scalar_prefetch=1,
            grid=(blocks,),
            in_specs=[
                ANY,
                whole(LINES, cells),
                whole(LINES, cells),
                rows_from((rows, LANES), 0, first, rows),
                *[ANY] * (3 + len(inner)),
            ],
            out_specs=rows_from((fields, planes, rows, cells), 2, first, rows),
            scratch_shapes=[
                pltpu.VMEM((fields, planes, count + 2 * EIGHT, cells), jnp.float32),
                chunk,
                pltpu.SemaphoreType.DMA((3 * blocks,)),
                *flux_scratch(rows, cells),
                *([] if outer is None else [chunk]),
            ],
        ),
        out_shape=pltpu.HBM(state.shape, jnp.float32),
        input_output_aliases=aliases,
        compiler_params=PARAMS,
        cost_estimate=cost(size * 60, size * 10),
        name="bulk",
    )(flags, *operands)


def add_outer(flags, outer, span, rows, held):
    fields, count, cells = outer.shape
    chunk = pltpu.VMEM((fields, count, cells), jnp.float32)
    return pl.pallas_call(
        functools.partial(outer_kernel, rows, span),
        grid_spec=pltpu.PrefetchScalarGridSpec(
            num_scalar_prefetch=1,
            grid=(1,),
            in_specs=[ANY, ANY],
            out_specs=ANY,
            scratch_shapes=[chunk, chunk, pltpu.SemaphoreType.DMA((3 * (count // rows),))],
        ),
        out_shape=pltpu.HBM(held.shape, jnp.float32),
        input_output_aliases={2: 0},
        compiler_params=PARAMS,
        cost_estimate=cost(outer.size * 6, outer.size * 16),
        name="add_outer",
    )(flags, outer, held)


def near(flags, state, low, high, inner, edge, dtheta, outer, factor, table, solve, token, part=None):
    fields, planes, rows, cells = state.shape
    out = jax.ShapeDtypeStruct((LINES, R_NEAR, cells), jnp.float32)
    tail = min(R_NEAR // EIGHT, rows // EIGHT - 1)
    state = in_hbm(state)
    out_specs = [whole(LINES, R_NEAR, cells), whole(LINES, R_NEAR, cells), whole(R_NEAR, LANES)]
    out_shape = [out, out, jax.ShapeDtypeStruct((R_NEAR, LANES), jnp.float32)]
    scratch = flux_scratch(R_NEAR, cells)
    if part is not None:
        out_specs.append(whole(fields, part[1] - part[0], cells))
        out_shape.append(jax.ShapeDtypeStruct((fields, part[1] - part[0], cells), jnp.float32))
        scratch.append(pltpu.SemaphoreType.DMA)
    result = pl.pallas_call(
        functools.partial(near_kernel, dtheta, rows, part[0] if part else 0),
        grid_spec=pltpu.PrefetchScalarGridSpec(
            num_scalar_prefetch=1,
            grid=(1,),
            in_specs=[
                whole(fields, planes, R_NEAR, cells),
                pl.BlockSpec((fields, planes, EIGHT, cells), lambda i, s: (0, 0, tail, 0)),
                whole(LINES, cells),
                whole(LINES, cells),
                whole(fields, R_NEAR, cells),
                whole(fields, R_NEAR, cells),
                whole(R_NEAR, LANES),
                whole(R_NEAR, LANES),
                whole(R_NEAR, LANES),
                whole(*solve.shape),
                ANY,
                ANY,
            ],
            out_specs=out_specs,
            scratch_shapes=scratch,
        ),
        out_shape=out_shape,
        compiler_params=PARAMS,
        cost_estimate=cost(LINES * R_NEAR * cells * 200, LINES * R_NEAR * cells * 250),
        name="near",
    )(flags, state, state, low, high, inner, outer, edge, factor, table, solve, in_hbm(token), state)
    return result if part is not None else (*result, None)


def finish(flags, factor, rhs, local, table, ends, held):
    _, _, cells = rhs.shape
    return pl.pallas_call(
        finish_kernel,
        grid_spec=pltpu.PrefetchScalarGridSpec(
            num_scalar_prefetch=1,
            grid=(1,),
            in_specs=[
                whole(R_NEAR, LANES),
                whole(LINES, R_NEAR, cells),
                whole(LINES, R_NEAR, cells),
                whole(R_NEAR, LANES),
                *[whole(R_NEAR, LANES)] * len(ends),
                ANY,
            ],
            out_specs=whole(FIELDS, PLANES, R_NEAR, cells),
        ),
        out_shape=pltpu.HBM(held.shape, jnp.float32),
        input_output_aliases={5 + len(ends): 0},
        compiler_params=PARAMS,
        cost_estimate=cost(LINES * R_NEAR * cells * 10, LINES * R_NEAR * cells * 20),
        name="finish",
    )(flags, factor, rhs, local, table, *ends, held)


def chunks(rows):
    size = 16
    blocks = (rows - R_NEAR) // size
    cuts = sorted({-(-2 * blocks // 5), -(-11 * blocks // 15), blocks})
    ends = [R_NEAR + size * c for c in cuts]
    return size, list(zip([0] + ends[:-1], ends))


def smoothing_table(coarsen, cells, total_cells, dtheta):
    factor = coarsen.astype(jnp.float32)[:, None]
    stiffness = KAPPA / (factor * dtheta) ** 2
    inverse_half = 0.5 / stiffness
    one_minus = jnp.sqrt(inverse_half * (2.0 + inverse_half)) - inverse_half
    log_ratio = jnp.log1p(-one_minus)
    gain = (1.0 - one_minus) / (stiffness * one_minus * (2.0 - one_minus))
    closing = 1.0 / -jnp.expm1((total_cells / factor) * log_ratio)
    across = jnp.exp((cells / factor) * log_ratio)
    column = jnp.arange(LANES, dtype=jnp.int32)[None, :]
    width = jnp.left_shift(1, jnp.minimum(column, 20)).astype(jnp.float32)
    table = jnp.where(width >= factor, jnp.exp(log_ratio * (width / factor)), 0.0)
    table = jnp.where(column == COL_LOG, log_ratio, table)
    table = jnp.where(column == COL_GAIN, gain, table)
    table = jnp.where(column == COL_CLOSING, closing, table)
    return jnp.where(column == COL_ACROSS, across, table)


def piece_tables(dtheta):
    tables = []
    for level in range(FMAX.bit_length()):
        width = 1 << level
        half = 0.5 * (width * dtheta) ** 2 / KAPPA
        ratio = 1.0 - (math.sqrt(half * (2.0 + half)) - half)
        block = np.arange(LANES) // width
        tables.append(ratio ** np.abs(block[:, None] - block[None, :]) / width)
    table = np.concatenate(tables, axis=1)
    high = table.astype(ml_dtypes.bfloat16)
    low = (table - high.astype(np.float64)).astype(ml_dtypes.bfloat16)
    return jnp.asarray(np.concatenate([high, high, low], axis=0))


def ring(value, axis, shift):
    size = lax.axis_size(axis)
    return lax.ppermute(value, axis, [(i, (i + shift) % size) for i in range(size)])


def body(state, coarsen):
    fields, planes, rows, cells = state.shape
    sec_count = lax.axis_size("sec")
    rad_count = lax.axis_size("rad")
    ax_count = lax.axis_size("ax")
    assert fields == FIELDS and planes == PLANES and ax_count % 2 == 0
    rad_index = lax.axis_index("rad")
    ax_index = lax.axis_index("ax")
    total_cells = cells * sec_count
    dtheta = 2.0 * math.pi / total_cells
    outer_pairs = []
    for i in range(1, ax_count - 1, 2):
        outer_pairs += [(i, i + 1), (i + 1, i)]
    inner_pairs = []
    for i in range(0, ax_count, 2):
        inner_pairs += [(i, i + 1), (i + 1, i)]
    up = [(i, i + 1) for i in range(rad_count - 1)]
    down = [(i + 1, i) for i in range(rad_count - 1)]
    flags = jnp.stack(
        [
            ax_index % 2,
            ((ax_index > 0) & (ax_index < ax_count - 1)).astype(jnp.int32),
            (rad_index == 0).astype(jnp.int32),
            (rad_index == rad_count - 1).astype(jnp.int32),
            rad_index * rows,
        ]
    ).astype(jnp.int32)
    size, spans = chunks(rows)
    count = len(spans)

    part, low, high = pack_first(state, spans[0][1])
    outer = [lax.ppermute(part, "ax", outer_pairs)]
    columns, side = pack_edges(state, high)
    low = lax.ppermute(low, "rad", up)
    high = lax.ppermute(high, "rad", down)
    near_inner = lax.ppermute(side, "ax", inner_pairs)
    wanted = [(0, R_NEAR, spans[0][1], 0)]
    for k in range(1, count):
        first, last = spans[k]
        cut = min(first + 2 * size, last) if k == count - 1 else last
        wanted += [(0, a, b, k) for a, b in ((first, cut), (cut, last)) if a < b]
    if count > 1:
        wanted.insert(1, (1, *spans[1], 1))
    parts = pack_rest(state, [piece[:3] for piece in wanted], columns, low, high)
    inner = [[] for _ in spans]
    for (q, _, _, k), value in zip(wanted, parts):
        if q:
            outer.append(lax.ppermute(value, "ax", outer_pairs))
        else:
            inner[k].append(lax.ppermute(value, "ax", inner_pairs))
    if sec_count == 2:
        edge = ring(columns, "sec", 1)
    else:
        from_left = jnp.arange(LANES)[None, :] % 4 < 2
        edge = jnp.where(from_left, ring(columns, "sec", 1), ring(columns, "sec", -1))

    table = smoothing_table(coarsen, cells, total_cells, dtheta)
    factor = jnp.broadcast_to(coarsen.astype(jnp.float32)[:, None], (R_NEAR, LANES))

    solve = piece_tables(dtheta)
    given = (flags, state, low, high)
    def pass_over(k, token, held, fused=True):
        span = (spans[k][0] if k else R_NEAR, spans[k][1])
        far = outer[k] if fused else None
        return bulk(*given, inner[k], edge, dtheta, far, span, size, token, held)

    out = pass_over(2, parts[0], None, fused=False) if count > 2 else None
    part = spans[2] if count > 2 else None
    token = parts[0] if out is None else out
    rhs, local, ends, part = near(
        *given, near_inner, edge, dtheta, outer[0], factor, table, solve, token, part
    )
    if part is not None:
        outer.append(lax.ppermute(part, "ax", outer_pairs))
    all_ends = [ends] + [ring(ends, "sec", k) for k in range(1, sec_count)]

    for k in range(min(count, 2)):
        out = pass_over(k, ends, out)
    out = finish(flags, factor, rhs, local, table, all_ends, out)
    return add_outer(flags, outer[2], spans[2], size, out) if count > 2 else out


def solution(mesh):
    return jax.shard_map(
        body,
        mesh=mesh,
        in_specs=(P(None, "ax", "rad", "sec"), P()),
        out_specs=P(None, "ax", "rad", "sec"),
        check_vma=False,
    )
```

```python
import functools
import math

import jax
import jax.numpy as jnp
import ml_dtypes
import numpy as np
from jax import lax
from jax.experimental import pallas as pl
from jax.experimental.pallas import tpu as pltpu
from jax.sharding import PartitionSpec as P

R_NEAR = 16
FMAX = 16

GAMMA = 1.4
KAPPA = 1.44

FIELDS = 5
PLANES = 2
LINES = FIELDS * PLANES
EIGHT = 8
LANES = 128
VMEM_LIMIT = 28 * 1024 * 1024

COL_LOG = 32
COL_GAIN = 33

ODD, OUTER, FIRST, LAST, BASE = range(5)


def plane_of(odd, q):
    return odd if q else 1 - odd


def reciprocal(x):
    y = pl.reciprocal(x, approx=True)
    y = y * (2.0 - x * y)
    return y * (2.0 - x * y)


def fluxes(fields, want):
    density, energy = fields[0], fields[4]
    momentum = fields[1:4]
    inverse = reciprocal(density)
    velocity = [m * inverse for m in momentum]
    square = {}
    for i in range(3):
        for j in range(i, 3):
            if i == j or i + 1 in want or j + 1 in want or (i, j) == (1, 2):
                square[i, j] = square[j, i] = momentum[i] * velocity[j]
    pressure = (GAMMA - 1.0) * (energy - 0.5 * (square[0, 0] + square[1, 1] + square[2, 2]))
    enthalpy = energy + pressure
    out = {}
    for d in want:
        k = d - 1
        flow = [square[i, k] + pressure if i == k else square[i, k] for i in range(3)]
        out[d] = [momentum[k]] + flow + [enthalpy * velocity[k]]
    return out, (pressure, square[2, 2], square[1, 2])


def flux_along(fields, along):
    return fluxes(fields, (along,))[0][along]


def outer_flux(flags, outer):
    present = flags[OUTER] == 1
    outer = [jnp.where(present, outer[0], 1.0)] + [jnp.where(present, g, 0.0) for g in outer[1:]]
    return flux_along(outer, 1)


def stencil(
    flags, first_row, rows, total_rows, dtheta, load, next_rows, edge, inner, outer, place, radial, azimuthal
):
    strips = rows // EIGHT
    pieces = radial.shape[2]
    row = lax.broadcasted_iota(jnp.int32, (EIGHT, LANES), 0)
    lane = lax.broadcasted_iota(jnp.int32, (EIGHT, LANES), 1)
    start = flags[BASE] + first_row
    axial_sign = jnp.where(flags[ODD] == 1, 0.5, -0.5)
    above = jnp.where((flags[FIRST] == 1) & (first_row == 0), 0.0, (start - 1).astype(jnp.float32) + 0.5)
    end = first_row + rows == total_rows
    below = jnp.where((flags[LAST] == 1) & end, 0.0, (start + rows).astype(jnp.float32) + 0.5)
    scale = jnp.where(row >= EIGHT // 2, above, below)
    at = [slice(b * LANES, (b + 1) * LANES) for b in range(pieces)]

    for q in range(PLANES):
        for b in range(pieces):
            values = [next_rows(f, q, at[b]) for f in range(FIELDS)]
            values[0] = jnp.where(scale > 0.0, values[0], 1.0)
            flux_next = flux_along(values, 2)
            for f in range(FIELDS):
                radial[q, f, b, 0:EIGHT, :] = flux_next[f] * scale
                radial[q, f, b, EIGHT + rows : 2 * EIGHT + rows, :] = flux_next[f] * scale

    def inside(t, carry):
        r = pl.multiple_of(EIGHT * t, EIGHT)
        radius = (start + r + row).astype(jnp.float32) + 0.5
        inv_radius = 1.0 / radius
        for b in range(pieces):
            beside = flux_along([inner(f, r, at[b]) for f in range(FIELDS)], 1)
            axial, source = [], []
            for q in range(PLANES):
                fields = [load(f, q, r, at[b]) for f in range(FIELDS)]
                flow, (pressure, twist, swirl) = fluxes(fields, (1, 2, 3))
                axial.append(flow[1])
                for f in range(FIELDS):
                    radial[q, f, b, pl.ds(r + EIGHT, EIGHT), :] = flow[2][f] * radius
                    azimuthal[q, f, b, pl.ds(r, EIGHT), :] = flow[3][f]
                source.append(((pressure + twist) * inv_radius, swirl * -inv_radius))
            base = [[axial_sign * (x - y) for x, y in zip(beside, axial[1])]]
            if outer is None:
                base.append([axial_sign * x for x in axial[0]])
            else:
                far = outer_flux(flags, [outer(f, r, at[b]) for f in range(FIELDS)])
                base.append([axial_sign * (x - y) for x, y in zip(axial[0], far)])
            for q in range(PLANES):
                base[q][2] = base[q][2] + source[q][0]
                base[q][3] = base[q][3] + source[q][1]
                for f in range(FIELDS):
                    place(f, q, r)[:, at[b]] = base[q][f]
        return carry

    lax.fori_loop(0, strips, inside, 0)

    def differences(t, carry):
        r = pl.multiple_of(EIGHT * t, EIGHT)
        radius = (start + r + row).astype(jnp.float32) + 0.5
        half_inv = 0.5 / radius
        half_arc = half_inv * (1.0 / dtheta)
        beyond = [edge(r)] + [pltpu.roll(edge(r), LANES - 4 * f, 1) for f in range(1, FIELDS)]
        beyond = flux_along(beyond, 3)
        for q in range(PLANES):
            for f in range(FIELDS):
                ends = [pltpu.roll(beyond[f], s, 1) if q else beyond[f] for s in (LANES - 1, 1)]
                here = [azimuthal[q, f, b, pl.ds(r, EIGHT), :] for b in range(pieces)]
                left = [ends[0]] + [pltpu.roll(x, 1, 1) for x in here]
                right = [pltpu.roll(x, LANES - 1, 1) for x in here] + [ends[1]]
                out = place(f, q, r)
                for b in range(pieces):
                    behind = jnp.where(lane == 0, left[b], left[b + 1])
                    ahead = jnp.where(lane == LANES - 1, right[b + 1], right[b])
                    up = radial[q, f, b, pl.ds(r + EIGHT - 1, EIGHT), :]
                    down = radial[q, f, b, pl.ds(r + EIGHT + 1, EIGHT), :]
                    change = (behind - ahead) * half_arc + (up - down) * half_inv
                    out[:, at[b]] = out[:, at[b]] + change
        return carry

    lax.fori_loop(0, strips, differences, 0)


def bulk_kernel(
    dtheta, rows, span, total_rows, fused, near, flags, state, low, high, inner, edge, outer, token, held, *rest
):
    near_parts, out, scratch = rest[:near], rest[near], rest[near + 1 :]
    first, end = span
    blocks = (end - first) // rows
    state_rows, inner_rows, sems, radial, azimuthal, *outer_rows = scratch
    *outer_rows, near_rows, near_sem = [*outer_rows, None, None] if not near else outer_rows
    outer_rows = outer_rows[0] if fused else None
    odd = flags[ODD]
    step = pl.program_id(0)

    def copies(k):
        a = first + k * rows + (EIGHT if k else -EIGHT)
        b = min(first + (k + 1) * rows + EIGHT, total_rows)
        at = a - first + EIGHT
        rest = pl.ds(outer.shape[1] - (end - first) + k * rows, rows)
        here = pl.ds(k * rows, rows)
        sets = [
            (state.at[:, :, a:b, :], state_rows.at[:, :, at : at + b - a, :]),
            (inner.at[:, here, :], inner_rows.at[:, here, :]),
        ]
        if fused:
            sets.append((outer.at[:, rest, :], outer_rows.at[:, here, :]))
        return [pltpu.make_async_copy(x, y, sems.at[3 * k + i]) for i, (x, y) in enumerate(sets)]

    @pl.when(step == 0)
    def _():
        for k in range(blocks):
            for copy in copies(k):
                copy.start()
        if near:
            close_circle(flags, *near_parts, near_rows)
            pltpu.make_async_copy(near_rows, held.at[:, :, 0:R_NEAR, :], near_sem).start()

    for k in range(blocks):

        @pl.when(step == k)
        def _():
            for copy in copies(k):
                copy.wait()

    first_row = first + step * rows
    at_end = first_row + rows == total_rows
    base = pl.multiple_of(step * rows, EIGHT)
    sub = lax.broadcasted_iota(jnp.int32, (EIGHT, LANES), 0)

    def load(f, q, r, at):
        return state_rows[f, plane_of(odd, q), pl.ds(base + EIGHT + r, EIGHT), at]

    def next_rows(f, q, at):
        k = f * PLANES + q
        under = jnp.where(at_end, high[k : k + 1, at], load(f, q, rows, at))
        return jnp.where(sub >= EIGHT // 2, load(f, q, -EIGHT, at), under)

    stencil(
        flags,
        first_row,
        rows,
        total_rows,
        dtheta,
        load,
        next_rows,
        lambda r: edge[pl.ds(r, EIGHT), :],
        lambda f, r, at: inner_rows[f, pl.ds(base + r, EIGHT), at],
        (lambda f, r, at: outer_rows[f, pl.ds(base + r, EIGHT), at]) if fused else None,
        lambda f, q, r: out.at[f, plane_of(odd, q), pl.ds(r, EIGHT), :],
        radial,
        azimuthal,
    )
    if near:

        @pl.when(step == blocks - 1)
        def _():
            pltpu.make_async_copy(near_rows, held.at[:, :, 0:R_NEAR, :], near_sem).wait()


def outer_kernel(rows, span, flags, outer, held, out, outer_rows, held_rows, sems):
    first, end = span
    plane = lax.axis_index("ax") % 2
    sign = jnp.where(flags[ODD] == 1, -0.5, 0.5)
    steps = []
    for k in range((end - first) // rows):
        here = pl.ds(k * rows, rows)
        there = pl.ds(first + k * rows, rows)
        ways = [
            (outer.at[:, here, :], outer_rows.at[:, here, :]),
            (held.at[:, plane, there, :], held_rows.at[:, here, :]),
            (held_rows.at[:, here, :], out.at[:, plane, there, :]),
        ]
        steps.append([pltpu.make_async_copy(x, y, sems.at[3 * k + i]) for i, (x, y) in enumerate(ways)])
        steps[-1][0].start()
        steps[-1][1].start()
    for k, (come, have, leave) in enumerate(steps):
        come.wait()
        have.wait()
        for t in range(rows // EIGHT):
            at = pl.ds(k * rows + EIGHT * t, EIGHT)
            values = outer_flux(flags, [outer_rows[f, at, :] for f in range(FIELDS)])
            for f in range(FIELDS):
                held_rows[f, at, :] = held_rows[f, at, :] + sign * values[f]
        leave.start()
    for _, _, leave in steps:
        leave.wait()


def near_kernel(
    dtheta,
    total_rows,
    part_first,
    flags,
    state,
    after,
    low,
    high,
    inner,
    outer,
    edge,
    factor,
    table,
    solve,
    token,
    hbm,
    rhs,
    local,
    carry,
    *rest,
):
    cells = state.shape[-1]
    odd = flags[ODD]
    part = rest[0] if len(rest) > 2 else None
    scratch = rest[-2:] if part is None else rest[-3:-1]
    if part is not None:
        source = hbm.at[:, lax.axis_index("ax") % 2, part_first : part_first + part.shape[1], :]
        copy = pltpu.make_async_copy(source, part, rest[-1])
        copy.start()

    sub = lax.broadcasted_iota(jnp.int32, (EIGHT, LANES), 0)

    def next_rows(f, q, at):
        k = f * PLANES + q
        under = high[k : k + 1, at] if total_rows == R_NEAR else after[f, plane_of(odd, q), :, at]
        return jnp.where(sub >= EIGHT // 2, low[k : k + 1, at], under)

    stencil(
        flags,
        0,
        R_NEAR,
        total_rows,
        dtheta,
        lambda f, q, r, at: state[f, plane_of(odd, q), pl.ds(r, EIGHT), at],
        next_rows,
        lambda r: edge[pl.ds(r, EIGHT), :],
        lambda f, r, at: inner[f, pl.ds(r, EIGHT), at],
        lambda f, r, at: outer[f, pl.ds(r, EIGHT), at],
        lambda f, q, r: rhs.at[f * PLANES + q, pl.ds(r, EIGHT), :],
        *scratch,
    )

    pieces = cells // LANES
    lane = lax.broadcasted_iota(jnp.int32, (R_NEAR, LANES), 1)
    width = factor[...]
    log_ratio = table[:, COL_LOG : COL_LOG + 1]
    block = jnp.floor((lane.astype(jnp.float32) + 0.5) / width)
    ahead_entry = jnp.exp(log_ratio * (block + 1.0))
    behind_entry = jnp.exp(log_ratio * (LANES / width - block))
    across = jnp.exp(log_ratio * (LANES / width))

    def line(k, ends):
        rows = jnp.concatenate([rhs[k, :, b * LANES : (b + 1) * LANES] for b in range(pieces)], axis=0)
        high = rows.astype(jnp.bfloat16)
        low = (rows - high.astype(jnp.float32)).astype(jnp.bfloat16)
        solved = jnp.dot(
            jnp.concatenate([high, low, high], axis=1), solve[...], preferred_element_type=jnp.float32
        )
        inside = []
        for b in range(pieces):
            mine = solved[b * R_NEAR : (b + 1) * R_NEAR]
            value = mine[:, :LANES]
            for level in range(1, FMAX.bit_length()):
                chosen = mine[:, level * LANES : (level + 1) * LANES]
                value = jnp.where(width == (1 << level), chosen, value)
            inside.append(value)
        total = list(inside)
        enter = jnp.zeros((R_NEAR, LANES), jnp.float32)
        for b in range(pieces):
            leave = jnp.broadcast_to(inside[b][:, LANES - 1 : LANES], (R_NEAR, LANES))
            total[b] = total[b] + ahead_entry * enter
            enter = leave + across * enter
        ends = jnp.where(lane == k, enter, ends)
        enter = jnp.zeros((R_NEAR, LANES), jnp.float32)
        for b in reversed(range(pieces)):
            leave = jnp.broadcast_to(inside[b][:, 0:1], (R_NEAR, LANES))
            total[b] = total[b] + behind_entry * enter
            enter = leave + across * enter
        for b in range(pieces):
            local[k, :, b * LANES : (b + 1) * LANES] = total[b]
        return jnp.where(lane == k + LINES, enter, ends)

    carry[...] = lax.fori_loop(
        0, LINES, line, jnp.zeros((R_NEAR, LANES), jnp.float32)
    )
    if part is not None:
        copy.wait()


def close_circle(flags, factor, rhs, local, carry, table, out):
    cells = out.shape[-1]
    lane = lax.broadcasted_iota(jnp.int32, (R_NEAR, cells), 1).astype(jnp.float32)
    width = factor[:, 0:1]
    block = jnp.floor((lane + 0.5) / width)
    count = cells / width
    log_ratio = table[:, COL_LOG : COL_LOG + 1]
    gain = jnp.broadcast_to(table[:, COL_GAIN : COL_GAIN + 1], (R_NEAR, cells))
    from_left = jnp.exp(log_ratio * (block + 1.0))
    from_right = jnp.exp(log_ratio * (count - block))
    near = flags[FIRST] == 1
    for f in range(FIELDS):
        for q in range(PLANES):
            k = f * PLANES + q
            j = k + LINES
            smooth = gain * (
                local[k] + from_left * carry[:, k : k + 1] + from_right * carry[:, j : j + 1]
            )
            out[f, plane_of(flags[ODD], q)] = jnp.where(near, smooth, rhs[k])


def stream(pieces, sems):
    steps = []
    for source, stage, target in pieces:
        for f in range(FIELDS):
            k = 2 * len(steps)
            come = pltpu.make_async_copy(source.at[f], stage.at[f], sems.at[k])
            leave = pltpu.make_async_copy(stage.at[f], target.at[f], sems.at[k + 1])
            steps.append((come, leave))
    for come, _ in steps:
        come.start()

    def finish():
        for come, leave in steps:
            come.wait()
            leave.start()
        for _, leave in steps:
            leave.wait()

    return finish


def pack_first_kernel(count, state, part, low, high, stage, top, bottom, row_sems, sems):
    _, _, rows, _ = state.shape
    odd = lax.axis_index("ax") % 2
    finish = stream([(state.at[:, odd, 0:count, :], stage, part)], sems)
    copies = [
        pltpu.make_async_copy(state.at[:, :, rows - EIGHT : rows, :], top, row_sems.at[0]),
        pltpu.make_async_copy(state.at[:, :, 0:EIGHT, :], bottom, row_sems.at[1]),
    ]
    for copy in copies:
        copy.start()
    finish()
    for copy in copies:
        copy.wait()
    for f in range(FIELDS):
        for q in range(PLANES):
            k = f * PLANES + q
            p = plane_of(odd, q)
            low[k : k + 1, :] = top[f, p, EIGHT - 1 : EIGHT, :]
            high[k : k + 1, :] = bottom[f, p, 0:1, :]


def pack_edges_kernel(state, token, edge, side, left, right, sems):
    _, _, rows, cells = state.shape
    odd = lax.axis_index("ax") % 2
    copies = [
        pltpu.make_async_copy(state.at[:, :, :, cells - LANES : cells], left, sems.at[0]),
        pltpu.make_async_copy(state.at[:, :, :, 0:LANES], right, sems.at[1]),
        pltpu.make_async_copy(state.at[:, 1 - odd, 0:R_NEAR, :], side, sems.at[2]),
    ]
    for copy in copies:
        copy.start()
    for copy in copies[:2]:
        copy.wait()
    lane = lax.broadcasted_iota(jnp.int32, (rows, LANES), 1)
    columns = jnp.ones((rows, LANES), jnp.float32)
    for f in range(FIELDS):
        for q in range(PLANES):
            p = plane_of(odd, q)
            columns = jnp.where(lane == 4 * f + q, left[f, p, :, LANES - 1 : LANES], columns)
            columns = jnp.where(lane == (4 * f - 1 - q) % LANES, right[f, p, :, 0:1], columns)
    edge[...] = columns
    copies[2].wait()


def pack_rest_kernel(parts, tokens, state, *rest):
    rest = rest[tokens:]
    odd = lax.axis_index("ax") % 2
    count = len(parts)
    pieces = []
    for k, (q, first, last) in enumerate(parts):
        pieces.append((state.at[:, plane_of(odd, q), first:last, :], rest[count + k], rest[k]))
    stream(pieces, rest[-1])()


ANY = pl.BlockSpec(memory_space=pl.ANY)
PARAMS = pltpu.CompilerParams(vmem_limit_bytes=VMEM_LIMIT)


def whole(*shape):
    return pl.BlockSpec(shape, lambda i, s: (0,) * len(shape))


def rows_from(shape, axis, first, step):
    def place(i, s):
        row = (first // EIGHT + i * (step // EIGHT)) * EIGHT
        return tuple(row if d == axis else 0 for d in range(len(shape)))

    return pl.BlockSpec(tuple(pl.Element(n) for n in shape), place)


def in_hbm(value):
    return pltpu.with_memory_space_constraint(value, pltpu.HBM)


def cost(flops, nbytes):
    return pl.CostEstimate(flops=flops, bytes_accessed=nbytes, transcendentals=0)


def pack_first(state, count):
    fields, planes, _, cells = state.shape
    vmem = pl.BlockSpec(memory_space=pltpu.VMEM)
    row = jax.ShapeDtypeStruct((LINES, cells), jnp.float32)
    rows = pltpu.VMEM((fields, planes, EIGHT, cells), jnp.float32)
    return pl.pallas_call(
        functools.partial(pack_first_kernel, count),
        in_specs=[ANY],
        out_specs=[ANY, vmem, vmem],
        out_shape=[jax.ShapeDtypeStruct((fields, count, cells), jnp.float32), row, row],
        scratch_shapes=[
            pltpu.VMEM((fields, count, cells), jnp.float32),
            rows,
            rows,
            pltpu.SemaphoreType.DMA((2,)),
            pltpu.SemaphoreType.DMA((2 * fields,)),
        ],
        compiler_params=PARAMS,
        cost_estimate=cost(0, fields * count * cells * 8),
        name="pack_first",
    )(in_hbm(state))


def pack_edges(state, token):
    fields, planes, rows, cells = state.shape
    vmem = pl.BlockSpec(memory_space=pltpu.VMEM)
    tiles = pltpu.VMEM((fields, planes, rows, LANES), jnp.float32)
    return pl.pallas_call(
        pack_edges_kernel,
        in_specs=[ANY, ANY],
        out_specs=[vmem, vmem],
        out_shape=[
            jax.ShapeDtypeStruct((rows, LANES), jnp.float32),
            jax.ShapeDtypeStruct((fields, R_NEAR, cells), jnp.float32),
        ],
        scratch_shapes=[tiles, tiles, pltpu.SemaphoreType.DMA((3,))],
        compiler_params=PARAMS,
        cost_estimate=cost(0, fields * planes * rows * LANES * 16),
        name="pack_edges",
    )(in_hbm(state), token)


def pack_rest(state, parts, *tokens):
    fields, _, _, cells = state.shape
    shapes = [jax.ShapeDtypeStruct((fields, last - first, cells), jnp.float32) for _, first, last in parts]
    return pl.pallas_call(
        functools.partial(pack_rest_kernel, parts, len(tokens)),
        in_specs=[ANY] * (1 + len(tokens)),
        out_specs=[ANY] * len(shapes),
        out_shape=shapes,
        scratch_shapes=[
            *[pltpu.VMEM(x.shape, jnp.float32) for x in shapes],
            pltpu.SemaphoreType.DMA((2 * fields * len(parts),)),
        ],
        compiler_params=PARAMS,
        cost_estimate=cost(0, sum(math.prod(x.shape) for x in shapes) * 8),
        name="pack_rest",
    )(in_hbm(state), *tokens)


def flux_scratch(rows, cells):
    shape = (PLANES, FIELDS, cells // LANES)
    return [pltpu.VMEM((*shape, n, LANES), jnp.float32) for n in (rows + 2 * EIGHT, rows)]


def bulk(flags, state, low, high, inner, edge, dtheta, outer, span, token, held, near_parts=()):
    fields, planes, total_rows, cells = state.shape
    first, end = span
    count = end - first
    rows = 32 if count % 32 == 0 else 24 if count % 24 == 0 else 16
    blocks = count // rows
    size = fields * planes * count * cells
    aliases = {} if held is None else {8: 0}
    state = in_hbm(state)
    operands = [state, low, high, inner, edge, inner if outer is None else outer, token]
    operands += [state if held is None else held, *near_parts]
    chunk = pltpu.VMEM((fields, count, cells), jnp.float32)
    near_scratch = [pltpu.VMEM((fields, planes, R_NEAR, cells), jnp.float32), pltpu.SemaphoreType.DMA]
    return pl.pallas_call(
        functools.partial(bulk_kernel, dtheta, rows, span, total_rows, outer is not None, len(near_parts)),
        grid_spec=pltpu.PrefetchScalarGridSpec(
            num_scalar_prefetch=1,
            grid=(blocks,),
            in_specs=[
                ANY,
                whole(LINES, cells),
                whole(LINES, cells),
                ANY,
                rows_from((rows, LANES), 0, first, rows),
                ANY,
                ANY,
                ANY,
                *[whole(*x.shape) for x in near_parts],
            ],
            out_specs=rows_from((fields, planes, rows, cells), 2, first, rows),
            scratch_shapes=[
                pltpu.VMEM((fields, planes, count + 2 * EIGHT, cells), jnp.float32),
                chunk,
                pltpu.SemaphoreType.DMA((3 * blocks,)),
                *flux_scratch(rows, cells),
                *([] if outer is None else [chunk]),
                *(near_scratch if near_parts else []),
            ],
        ),
        out_shape=pltpu.HBM(state.shape, jnp.float32),
        input_output_aliases=aliases,
        compiler_params=PARAMS,
        cost_estimate=cost(size * 60, size * 10),
        name="bulk",
    )(flags, *operands)


def add_outer(flags, outer, span, rows, held):
    fields, count, cells = outer.shape
    chunk = pltpu.VMEM((fields, count, cells), jnp.float32)
    return pl.pallas_call(
        functools.partial(outer_kernel, rows, span),
        grid_spec=pltpu.PrefetchScalarGridSpec(
            num_scalar_prefetch=1,
            grid=(1,),
            in_specs=[ANY, ANY],
            out_specs=ANY,
            scratch_shapes=[chunk, chunk, pltpu.SemaphoreType.DMA((3 * (count // rows),))],
        ),
        out_shape=pltpu.HBM(held.shape, jnp.float32),
        input_output_aliases={2: 0},
        compiler_params=PARAMS,
        cost_estimate=cost(outer.size * 6, outer.size * 16),
        name="add_outer",
    )(flags, outer, held)


def near(flags, state, low, high, inner, edge, dtheta, outer, factor, table, solve, token, part=None):
    fields, planes, rows, cells = state.shape
    out = jax.ShapeDtypeStruct((LINES, R_NEAR, cells), jnp.float32)
    tail = min(R_NEAR // EIGHT, rows // EIGHT - 1)
    state = in_hbm(state)
    out_specs = [whole(LINES, R_NEAR, cells), whole(LINES, R_NEAR, cells), whole(R_NEAR, LANES)]
    out_shape = [out, out, jax.ShapeDtypeStruct((R_NEAR, LANES), jnp.float32)]
    scratch = flux_scratch(R_NEAR, cells)
    if part is not None:
        out_specs.append(whole(fields, part[1] - part[0], cells))
        out_shape.append(jax.ShapeDtypeStruct((fields, part[1] - part[0], cells), jnp.float32))
        scratch.append(pltpu.SemaphoreType.DMA)
    result = pl.pallas_call(
        functools.partial(near_kernel, dtheta, rows, part[0] if part else 0),
        grid_spec=pltpu.PrefetchScalarGridSpec(
            num_scalar_prefetch=1,
            grid=(1,),
            in_specs=[
                whole(fields, planes, R_NEAR, cells),
                pl.BlockSpec((fields, planes, EIGHT, cells), lambda i, s: (0, 0, tail, 0)),
                whole(LINES, cells),
                whole(LINES, cells),
                whole(fields, R_NEAR, cells),
                whole(fields, R_NEAR, cells),
                whole(R_NEAR, LANES),
                whole(R_NEAR, LANES),
                whole(R_NEAR, LANES),
                whole(*solve.shape),
                ANY,
                ANY,
            ],
            out_specs=out_specs,
            scratch_shapes=scratch,
        ),
        out_shape=out_shape,
        compiler_params=PARAMS,
        cost_estimate=cost(LINES * R_NEAR * cells * 200, LINES * R_NEAR * cells * 250),
        name="near",
    )(flags, state, state, low, high, inner, outer, edge, factor, table, solve, in_hbm(token), state)
    return result if part is not None else (*result, None)


def chunks(rows):
    size = 16
    blocks = (rows - R_NEAR) // size
    cuts = sorted({-(-2 * blocks // 5), -(-4 * blocks // 5), blocks})
    ends = [R_NEAR + size * c for c in cuts]
    return size, list(zip([0] + ends[:-1], ends))


def smoothing_table(coarsen, cells, total_cells, dtheta):
    factor = coarsen.astype(jnp.float32)[:, None]
    stiffness = KAPPA / (factor * dtheta) ** 2
    inverse_half = 0.5 / stiffness
    one_minus = jnp.sqrt(inverse_half * (2.0 + inverse_half)) - inverse_half
    log_ratio = jnp.log1p(-one_minus)
    gain = (1.0 - one_minus) / (stiffness * one_minus * (2.0 - one_minus))
    closing = 1.0 / -jnp.expm1((total_cells / factor) * log_ratio)
    across = jnp.exp((cells / factor) * log_ratio)
    column = jnp.arange(LANES, dtype=jnp.int32)[None, :]
    width = jnp.left_shift(1, jnp.minimum(column, 20)).astype(jnp.float32)
    table = jnp.where(width >= factor, jnp.exp(log_ratio * (width / factor)), 0.0)
    table = jnp.where(column == COL_LOG, log_ratio, table)
    table = jnp.where(column == COL_GAIN, gain, table)
    return table, closing, across


def piece_tables(dtheta):
    tables = []
    for level in range(FMAX.bit_length()):
        width = 1 << level
        half = 0.5 * (width * dtheta) ** 2 / KAPPA
        ratio = 1.0 - (math.sqrt(half * (2.0 + half)) - half)
        block = np.arange(LANES) // width
        tables.append(ratio ** np.abs(block[:, None] - block[None, :]) / width)
    table = np.concatenate(tables, axis=1)
    high = table.astype(ml_dtypes.bfloat16)
    low = (table - high.astype(np.float64)).astype(ml_dtypes.bfloat16)
    return jnp.asarray(np.concatenate([high, high, low], axis=0))


def ring(value, axis, shift):
    size = lax.axis_size(axis)
    return lax.ppermute(value, axis, [(i, (i + shift) % size) for i in range(size)])


def body(state, coarsen):
    fields, planes, rows, cells = state.shape
    sec_count = lax.axis_size("sec")
    rad_count = lax.axis_size("rad")
    ax_count = lax.axis_size("ax")
    assert fields == FIELDS and planes == PLANES and ax_count % 2 == 0
    rad_index = lax.axis_index("rad")
    ax_index = lax.axis_index("ax")
    total_cells = cells * sec_count
    dtheta = 2.0 * math.pi / total_cells
    outer_pairs = []
    for i in range(1, ax_count - 1, 2):
        outer_pairs += [(i, i + 1), (i + 1, i)]
    inner_pairs = []
    for i in range(0, ax_count, 2):
        inner_pairs += [(i, i + 1), (i + 1, i)]
    up = [(i, i + 1) for i in range(rad_count - 1)]
    down = [(i + 1, i) for i in range(rad_count - 1)]
    flags = jnp.stack(
        [
            ax_index % 2,
            ((ax_index > 0) & (ax_index < ax_count - 1)).astype(jnp.int32),
            (rad_index == 0).astype(jnp.int32),
            (rad_index == rad_count - 1).astype(jnp.int32),
            rad_index * rows,
        ]
    ).astype(jnp.int32)
    size, spans = chunks(rows)
    count = len(spans)

    part, low, high = pack_first(state, spans[0][1])
    outer = [lax.ppermute(part, "ax", outer_pairs)]
    columns, side = pack_edges(state, high)
    low = lax.ppermute(low, "rad", up)
    high = lax.ppermute(high, "rad", down)
    inner = [lax.ppermute(side, "ax", inner_pairs)]
    wanted = [(0, R_NEAR, spans[0][1])] + [(0, *span) for span in spans[1:]]
    if count > 1:
        wanted.insert(1, (1, *spans[1]))
    parts = pack_rest(state, wanted, columns, low, high)
    for k, value in enumerate(parts):
        if wanted[k][0]:
            outer.append(lax.ppermute(value, "ax", outer_pairs))
        else:
            inner.append(lax.ppermute(value, "ax", inner_pairs))
    if sec_count == 2:
        edge = ring(columns, "sec", 1)
    else:
        from_left = jnp.arange(LANES)[None, :] % 4 < 2
        edge = jnp.where(from_left, ring(columns, "sec", 1), ring(columns, "sec", -1))

    table, closing, across = smoothing_table(coarsen, cells, total_cells, dtheta)
    factor = jnp.broadcast_to(coarsen.astype(jnp.float32)[:, None], (R_NEAR, LANES))

    solve = piece_tables(dtheta)
    given = (flags, state, low, high)

    def pass_over(k, token, held, fused=True, near_parts=()):
        span = (spans[k][0] if k else R_NEAR, spans[k][1])
        far = outer[k] if fused else None
        return bulk(*given, inner[k + 1], edge, dtheta, far, span, token, held, near_parts)

    out = pass_over(2, in_hbm(parts[0]), None, fused=False) if count > 2 else None
    part = spans[2] if count > 2 else None
    token = parts[0] if out is None else out
    rhs, local, ends, part = near(
        *given, inner[0], edge, dtheta, outer[0], factor, table, solve, token, part
    )
    if part is not None:
        outer.append(lax.ppermute(part, "ax", outer_pairs))
    arrived = [ends] + [ring(ends, "sec", k) for k in range(1, sec_count)] + [ends]
    from_left = jnp.arange(LANES)[None, :] < LINES
    carry = jnp.zeros_like(ends)
    for k in range(sec_count, 0, -1):
        carry = carry * across + jnp.where(from_left, arrived[k], arrived[sec_count - k])
    carry = carry * closing
    passes = min(count, 2)
    for k in range(passes):
        near_parts = (factor, rhs, local, carry, table) if k == passes - 1 else ()
        out = pass_over(k, ends, out, near_parts=near_parts)
    return add_outer(flags, outer[2], spans[2], size, out) if count > 2 else out


def solution(mesh):
    return jax.shard_map(
        body,
        mesh=mesh,
        in_specs=(P(None, "ax", "rad", "sec"), P()),
        out_specs=P(None, "ax", "rad", "sec"),
        check_vma=False,
    )
```

```python
import functools
import math

import jax
import jax.numpy as jnp
import ml_dtypes
import numpy as np
from jax import lax
from jax.experimental import pallas as pl
from jax.experimental.pallas import tpu as pltpu
from jax.sharding import PartitionSpec as P

R_NEAR = 16
FMAX = 16

GAMMA = 1.4
KAPPA = 1.44

FIELDS = 5
PLANES = 2
LINES = FIELDS * PLANES
EIGHT = 8
LANES = 128
VMEM_LIMIT = 28 * 1024 * 1024

COL_LOG = 32
COL_GAIN = 33

ODD, OUTER, FIRST, LAST, BASE = range(5)


def plane_of(odd, q):
    return odd if q else 1 - odd


def reciprocal(x):
    y = pl.reciprocal(x, approx=True)
    y = y * (2.0 - x * y)
    return y * (2.0 - x * y)


def fluxes(fields, want):
    density, energy = fields[0], fields[4]
    momentum = fields[1:4]
    inverse = reciprocal(density)
    velocity = [m * inverse for m in momentum]
    square = {}
    for i in range(3):
        for j in range(i, 3):
            if i == j or i + 1 in want or j + 1 in want or (i, j) == (1, 2):
                square[i, j] = square[j, i] = momentum[i] * velocity[j]
    pressure = (GAMMA - 1.0) * (energy - 0.5 * (square[0, 0] + square[1, 1] + square[2, 2]))
    enthalpy = energy + pressure
    out = {}
    for d in want:
        k = d - 1
        flow = [square[i, k] + pressure if i == k else square[i, k] for i in range(3)]
        out[d] = [momentum[k]] + flow + [enthalpy * velocity[k]]
    return out, (pressure, square[2, 2], square[1, 2])


def flux_along(fields, along):
    return fluxes(fields, (along,))[0][along]


def outer_flux(flags, outer):
    present = flags[OUTER] == 1
    outer = [jnp.where(present, outer[0], 1.0)] + [jnp.where(present, g, 0.0) for g in outer[1:]]
    return flux_along(outer, 1)


def stencil(
    flags, first_row, rows, total_rows, dtheta, load, next_rows, edge, inner, outer, place, radial, azimuthal
):
    strips = rows // EIGHT
    pieces = radial.shape[2]
    row = lax.broadcasted_iota(jnp.int32, (EIGHT, LANES), 0)
    lane = lax.broadcasted_iota(jnp.int32, (EIGHT, LANES), 1)
    start = flags[BASE] + first_row
    axial_sign = jnp.where(flags[ODD] == 1, 0.5, -0.5)
    above = jnp.where((flags[FIRST] == 1) & (first_row == 0), 0.0, (start - 1).astype(jnp.float32) + 0.5)
    end = first_row + rows == total_rows
    below = jnp.where((flags[LAST] == 1) & end, 0.0, (start + rows).astype(jnp.float32) + 0.5)
    scale = jnp.where(row >= EIGHT // 2, above, below)
    at = [slice(b * LANES, (b + 1) * LANES) for b in range(pieces)]

    for q in range(PLANES):
        for b in range(pieces):
            values = [next_rows(f, q, at[b]) for f in range(FIELDS)]
            values[0] = jnp.where(scale > 0.0, values[0], 1.0)
            flux_next = flux_along(values, 2)
            for f in range(FIELDS):
                radial[q, f, b, 0:EIGHT, :] = flux_next[f] * scale
                radial[q, f, b, EIGHT + rows : 2 * EIGHT + rows, :] = flux_next[f] * scale

    def inside(t, carry):
        r = pl.multiple_of(EIGHT * t, EIGHT)
        radius = (start + r + row).astype(jnp.float32) + 0.5
        inv_radius = 1.0 / radius
        for b in range(pieces):
            beside = flux_along([inner(f, r, at[b]) for f in range(FIELDS)], 1)
            axial, source = [], []
            for q in range(PLANES):
                fields = [load(f, q, r, at[b]) for f in range(FIELDS)]
                flow, (pressure, twist, swirl) = fluxes(fields, (1, 2, 3))
                axial.append(flow[1])
                for f in range(FIELDS):
                    radial[q, f, b, pl.ds(r + EIGHT, EIGHT), :] = flow[2][f] * radius
                    azimuthal[q, f, b, pl.ds(r, EIGHT), :] = flow[3][f]
                source.append(((pressure + twist) * inv_radius, swirl * -inv_radius))
            base = [[axial_sign * (x - y) for x, y in zip(beside, axial[1])]]
            if outer is None:
                base.append([axial_sign * x for x in axial[0]])
            else:
                far = outer_flux(flags, [outer(f, r, at[b]) for f in range(FIELDS)])
                base.append([axial_sign * (x - y) for x, y in zip(axial[0], far)])
            for q in range(PLANES):
                base[q][2] = base[q][2] + source[q][0]
                base[q][3] = base[q][3] + source[q][1]
                for f in range(FIELDS):
                    place(f, q, r)[:, at[b]] = base[q][f]
        return carry

    lax.fori_loop(0, strips, inside, 0)

    def differences(t, carry):
        r = pl.multiple_of(EIGHT * t, EIGHT)
        radius = (start + r + row).astype(jnp.float32) + 0.5
        half_inv = 0.5 / radius
        half_arc = half_inv * (1.0 / dtheta)
        beyond = [edge(r)] + [pltpu.roll(edge(r), LANES - 4 * f, 1) for f in range(1, FIELDS)]
        beyond = flux_along(beyond, 3)
        for q in range(PLANES):
            for f in range(FIELDS):
                ends = [pltpu.roll(beyond[f], s, 1) if q else beyond[f] for s in (LANES - 1, 1)]
                here = [azimuthal[q, f, b, pl.ds(r, EIGHT), :] for b in range(pieces)]
                left = [ends[0]] + [pltpu.roll(x, 1, 1) for x in here]
                right = [pltpu.roll(x, LANES - 1, 1) for x in here] + [ends[1]]
                out = place(f, q, r)
                for b in range(pieces):
                    behind = jnp.where(lane == 0, left[b], left[b + 1])
                    ahead = jnp.where(lane == LANES - 1, right[b + 1], right[b])
                    up = radial[q, f, b, pl.ds(r + EIGHT - 1, EIGHT), :]
                    down = radial[q, f, b, pl.ds(r + EIGHT + 1, EIGHT), :]
                    change = (behind - ahead) * half_arc + (up - down) * half_inv
                    out[:, at[b]] = out[:, at[b]] + change
        return carry

    lax.fori_loop(0, strips, differences, 0)


def bulk_kernel(
    dtheta, rows, span, total_rows, fused, near, flags, state, low, high, inner, edge, outer, token, held, *rest
):
    near_parts, out, scratch = rest[:near], rest[near], rest[near + 1 :]
    first, end = span
    blocks = (end - first) // rows
    state_rows, inner_rows, sems, radial, azimuthal, *outer_rows = scratch
    *outer_rows, near_rows, near_sem = [*outer_rows, None, None] if not near else outer_rows
    outer_rows = outer_rows[0] if fused else None
    odd = flags[ODD]
    step = pl.program_id(0)

    def copies(k):
        a = first + k * rows + (EIGHT if k else -EIGHT)
        b = min(first + (k + 1) * rows + EIGHT, total_rows)
        at = a - first + EIGHT
        rest = pl.ds(outer.shape[1] - (end - first) + k * rows, rows)
        here = pl.ds(k * rows, rows)
        sets = [
            (state.at[:, :, a:b, :], state_rows.at[:, :, at : at + b - a, :]),
            (inner.at[:, here, :], inner_rows.at[:, here, :]),
        ]
        if fused:
            sets.append((outer.at[:, rest, :], outer_rows.at[:, here, :]))
        return [pltpu.make_async_copy(x, y, sems.at[3 * k + i]) for i, (x, y) in enumerate(sets)]

    @pl.when(step == 0)
    def _():
        for k in range(blocks):
            for copy in copies(k):
                copy.start()
        if near:
            close_circle(flags, *near_parts, near_rows)
            pltpu.make_async_copy(near_rows, held.at[:, :, 0:R_NEAR, :], near_sem).start()

    for k in range(blocks):

        @pl.when(step == k)
        def _():
            for copy in copies(k):
                copy.wait()

    first_row = first + step * rows
    at_end = first_row + rows == total_rows
    base = pl.multiple_of(step * rows, EIGHT)
    sub = lax.broadcasted_iota(jnp.int32, (EIGHT, LANES), 0)

    def load(f, q, r, at):
        return state_rows[f, plane_of(odd, q), pl.ds(base + EIGHT + r, EIGHT), at]

    def next_rows(f, q, at):
        k = f * PLANES + q
        under = jnp.where(at_end, high[k : k + 1, at], load(f, q, rows, at))
        return jnp.where(sub >= EIGHT // 2, load(f, q, -EIGHT, at), under)

    stencil(
        flags,
        first_row,
        rows,
        total_rows,
        dtheta,
        load,
        next_rows,
        lambda r: edge[pl.ds(r, EIGHT), :],
        lambda f, r, at: inner_rows[f, pl.ds(base + r, EIGHT), at],
        (lambda f, r, at: outer_rows[f, pl.ds(base + r, EIGHT), at]) if fused else None,
        lambda f, q, r: out.at[f, plane_of(odd, q), pl.ds(r, EIGHT), :],
        radial,
        azimuthal,
    )
    if near:

        @pl.when(step == blocks - 1)
        def _():
            pltpu.make_async_copy(near_rows, held.at[:, :, 0:R_NEAR, :], near_sem).wait()


def outer_kernel(rows, span, flags, outer, held, out, outer_rows, held_rows, sems):
    first, end = span
    plane = lax.axis_index("ax") % 2
    sign = jnp.where(flags[ODD] == 1, -0.5, 0.5)
    steps = []
    for k in range((end - first) // rows):
        here = pl.ds(k * rows, rows)
        there = pl.ds(first + k * rows, rows)
        ways = [
            (outer.at[:, here, :], outer_rows.at[:, here, :]),
            (held.at[:, plane, there, :], held_rows.at[:, here, :]),
            (held_rows.at[:, here, :], out.at[:, plane, there, :]),
        ]
        steps.append([pltpu.make_async_copy(x, y, sems.at[3 * k + i]) for i, (x, y) in enumerate(ways)])
        steps[-1][0].start()
        steps[-1][1].start()
    for k, (come, have, leave) in enumerate(steps):
        come.wait()
        have.wait()
        for t in range(rows // EIGHT):
            at = pl.ds(k * rows + EIGHT * t, EIGHT)
            values = outer_flux(flags, [outer_rows[f, at, :] for f in range(FIELDS)])
            for f in range(FIELDS):
                held_rows[f, at, :] = held_rows[f, at, :] + sign * values[f]
        leave.start()
    for _, _, leave in steps:
        leave.wait()


def near_kernel(
    dtheta,
    total_rows,
    part_first,
    flags,
    state,
    after,
    low,
    high,
    inner,
    outer,
    edge,
    factor,
    table,
    solve,
    token,
    hbm,
    rhs,
    local,
    carry,
    *rest,
):
    cells = state.shape[-1]
    odd = flags[ODD]
    part = rest[0] if len(rest) > 2 else None
    scratch = rest[-2:] if part is None else rest[-3:-1]
    if part is not None:
        source = hbm.at[:, lax.axis_index("ax") % 2, part_first : part_first + part.shape[1], :]
        copy = pltpu.make_async_copy(source, part, rest[-1])
        copy.start()

    sub = lax.broadcasted_iota(jnp.int32, (EIGHT, LANES), 0)

    def next_rows(f, q, at):
        k = f * PLANES + q
        under = high[k : k + 1, at] if total_rows == R_NEAR else after[f, plane_of(odd, q), :, at]
        return jnp.where(sub >= EIGHT // 2, low[k : k + 1, at], under)

    stencil(
        flags,
        0,
        R_NEAR,
        total_rows,
        dtheta,
        lambda f, q, r, at: state[f, plane_of(odd, q), pl.ds(r, EIGHT), at],
        next_rows,
        lambda r: edge[pl.ds(r, EIGHT), :],
        lambda f, r, at: inner[f, pl.ds(r, EIGHT), at],
        lambda f, r, at: outer[f, pl.ds(r, EIGHT), at],
        lambda f, q, r: rhs.at[f * PLANES + q, pl.ds(r, EIGHT), :],
        *scratch,
    )

    pieces = cells // LANES
    lane = lax.broadcasted_iota(jnp.int32, (R_NEAR, LANES), 1)
    width = factor[...]
    log_ratio = table[:, COL_LOG : COL_LOG + 1]
    block = jnp.floor((lane.astype(jnp.float32) + 0.5) / width)
    ahead_entry = jnp.exp(log_ratio * (block + 1.0))
    behind_entry = jnp.exp(log_ratio * (LANES / width - block))
    across = jnp.exp(log_ratio * (LANES / width))

    def line(k, ends):
        rows = jnp.concatenate([rhs[k, :, b * LANES : (b + 1) * LANES] for b in range(pieces)], axis=0)
        high = rows.astype(jnp.bfloat16)
        low = (rows - high.astype(jnp.float32)).astype(jnp.bfloat16)
        solved = jnp.dot(
            jnp.concatenate([high, low, high], axis=1), solve[...], preferred_element_type=jnp.float32
        )
        inside = []
        for b in range(pieces):
            mine = solved[b * R_NEAR : (b + 1) * R_NEAR]
            value = mine[:, :LANES]
            for level in range(1, FMAX.bit_length()):
                chosen = mine[:, level * LANES : (level + 1) * LANES]
                value = jnp.where(width == (1 << level), chosen, value)
            inside.append(value)
        total = list(inside)
        enter = jnp.zeros((R_NEAR, LANES), jnp.float32)
        for b in range(pieces):
            leave = jnp.broadcast_to(inside[b][:, LANES - 1 : LANES], (R_NEAR, LANES))
            total[b] = total[b] + ahead_entry * enter
            enter = leave + across * enter
        ends = jnp.where(lane == k, enter, ends)
        enter = jnp.zeros((R_NEAR, LANES), jnp.float32)
        for b in reversed(range(pieces)):
            leave = jnp.broadcast_to(inside[b][:, 0:1], (R_NEAR, LANES))
            total[b] = total[b] + behind_entry * enter
            enter = leave + across * enter
        for b in range(pieces):
            local[k, :, b * LANES : (b + 1) * LANES] = total[b]
        return jnp.where(lane == k + LINES, enter, ends)

    carry[...] = lax.fori_loop(
        0, LINES, line, jnp.zeros((R_NEAR, LANES), jnp.float32)
    )
    if part is not None:
        copy.wait()


def close_circle(flags, factor, rhs, local, carry, table, out):
    cells = out.shape[-1]
    lane = lax.broadcasted_iota(jnp.int32, (R_NEAR, cells), 1).astype(jnp.float32)
    width = factor[:, 0:1]
    block = jnp.floor((lane + 0.5) / width)
    count = cells / width
    log_ratio = table[:, COL_LOG : COL_LOG + 1]
    gain = jnp.broadcast_to(table[:, COL_GAIN : COL_GAIN + 1], (R_NEAR, cells))
    from_left = jnp.exp(log_ratio * (block + 1.0))
    from_right = jnp.exp(log_ratio * (count - block))
    near = flags[FIRST] == 1
    for f in range(FIELDS):
        for q in range(PLANES):
            k = f * PLANES + q
            j = k + LINES
            smooth = gain * (
                local[k] + from_left * carry[:, k : k + 1] + from_right * carry[:, j : j + 1]
            )
            out[f, plane_of(flags[ODD], q)] = jnp.where(near, smooth, rhs[k])


def stream(pieces, sems):
    steps = []
    for source, stage, target in pieces:
        for f in range(FIELDS):
            k = 2 * len(steps)
            come = pltpu.make_async_copy(source.at[f], stage.at[f], sems.at[k])
            leave = pltpu.make_async_copy(stage.at[f], target.at[f], sems.at[k + 1])
            steps.append((come, leave))
    for come, _ in steps:
        come.start()

    def finish():
        for come, leave in steps:
            come.wait()
            leave.start()
        for _, leave in steps:
            leave.wait()

    return finish


def pack_first_kernel(count, state, part, low, high, stage, top, bottom, row_sems, sems):
    _, _, rows, _ = state.shape
    odd = lax.axis_index("ax") % 2
    finish = stream([(state.at[:, odd, 0:count, :], stage, part)], sems)
    copies = [
        pltpu.make_async_copy(state.at[:, :, rows - EIGHT : rows, :], top, row_sems.at[0]),
        pltpu.make_async_copy(state.at[:, :, 0:EIGHT, :], bottom, row_sems.at[1]),
    ]
    for copy in copies:
        copy.start()
    finish()
    for copy in copies:
        copy.wait()
    for f in range(FIELDS):
        for q in range(PLANES):
            k = f * PLANES + q
            p = plane_of(odd, q)
            low[k : k + 1, :] = top[f, p, EIGHT - 1 : EIGHT, :]
            high[k : k + 1, :] = bottom[f, p, 0:1, :]


def pack_edges_kernel(state, token, edge, side, left, right, sems):
    _, _, rows, cells = state.shape
    odd = lax.axis_index("ax") % 2
    copies = [
        pltpu.make_async_copy(state.at[:, :, :, cells - LANES : cells], left, sems.at[0]),
        pltpu.make_async_copy(state.at[:, :, :, 0:LANES], right, sems.at[1]),
        pltpu.make_async_copy(state.at[:, 1 - odd, 0:R_NEAR, :], side, sems.at[2]),
    ]
    for copy in copies:
        copy.start()
    for copy in copies[:2]:
        copy.wait()
    lane = lax.broadcasted_iota(jnp.int32, (rows, LANES), 1)
    columns = jnp.ones((rows, LANES), jnp.float32)
    for f in range(FIELDS):
        for q in range(PLANES):
            p = plane_of(odd, q)
            columns = jnp.where(lane == 4 * f + q, left[f, p, :, LANES - 1 : LANES], columns)
            columns = jnp.where(lane == (4 * f - 1 - q) % LANES, right[f, p, :, 0:1], columns)
    edge[...] = columns
    copies[2].wait()


def pack_rest_kernel(parts, tokens, state, *rest):
    rest = rest[tokens:]
    odd = lax.axis_index("ax") % 2
    count = len(parts)
    pieces = []
    for k, (q, first, last) in enumerate(parts):
        pieces.append((state.at[:, plane_of(odd, q), first:last, :], rest[count + k], rest[k]))
    stream(pieces, rest[-1])()


ANY = pl.BlockSpec(memory_space=pl.ANY)
PARAMS = pltpu.CompilerParams(vmem_limit_bytes=VMEM_LIMIT)


def whole(*shape):
    return pl.BlockSpec(shape, lambda i, s: (0,) * len(shape))


def rows_from(shape, axis, first, step):
    def place(i, s):
        row = (first // EIGHT + i * (step // EIGHT)) * EIGHT
        return tuple(row if d == axis else 0 for d in range(len(shape)))

    return pl.BlockSpec(tuple(pl.Element(n) for n in shape), place)


def in_hbm(value):
    return pltpu.with_memory_space_constraint(value, pltpu.HBM)


def cost(flops, nbytes):
    return pl.CostEstimate(flops=flops, bytes_accessed=nbytes, transcendentals=0)


def pack_first(state, count):
    fields, planes, _, cells = state.shape
    vmem = pl.BlockSpec(memory_space=pltpu.VMEM)
    row = jax.ShapeDtypeStruct((LINES, cells), jnp.float32)
    rows = pltpu.VMEM((fields, planes, EIGHT, cells), jnp.float32)
    return pl.pallas_call(
        functools.partial(pack_first_kernel, count),
        in_specs=[ANY],
        out_specs=[ANY, vmem, vmem],
        out_shape=[jax.ShapeDtypeStruct((fields, count, cells), jnp.float32), row, row],
        scratch_shapes=[
            pltpu.VMEM((fields, count, cells), jnp.float32),
            rows,
            rows,
            pltpu.SemaphoreType.DMA((2,)),
            pltpu.SemaphoreType.DMA((2 * fields,)),
        ],
        compiler_params=PARAMS,
        cost_estimate=cost(0, fields * count * cells * 8),
        name="pack_first",
    )(in_hbm(state))


def pack_edges(state, token):
    fields, planes, rows, cells = state.shape
    vmem = pl.BlockSpec(memory_space=pltpu.VMEM)
    tiles = pltpu.VMEM((fields, planes, rows, LANES), jnp.float32)
    return pl.pallas_call(
        pack_edges_kernel,
        in_specs=[ANY, ANY],
        out_specs=[vmem, vmem],
        out_shape=[
            jax.ShapeDtypeStruct((rows, LANES), jnp.float32),
            jax.ShapeDtypeStruct((fields, R_NEAR, cells), jnp.float32),
        ],
        scratch_shapes=[tiles, tiles, pltpu.SemaphoreType.DMA((3,))],
        compiler_params=PARAMS,
        cost_estimate=cost(0, fields * planes * rows * LANES * 16),
        name="pack_edges",
    )(in_hbm(state), token)


def pack_rest(state, parts, *tokens):
    fields, _, _, cells = state.shape
    shapes = [jax.ShapeDtypeStruct((fields, last - first, cells), jnp.float32) for _, first, last in parts]
    return pl.pallas_call(
        functools.partial(pack_rest_kernel, parts, len(tokens)),
        in_specs=[ANY] * (1 + len(tokens)),
        out_specs=[ANY] * len(shapes),
        out_shape=shapes,
        scratch_shapes=[
            *[pltpu.VMEM(x.shape, jnp.float32) for x in shapes],
            pltpu.SemaphoreType.DMA((2 * fields * len(parts),)),
        ],
        compiler_params=PARAMS,
        cost_estimate=cost(0, sum(math.prod(x.shape) for x in shapes) * 8),
        name="pack_rest",
    )(in_hbm(state), *tokens)


def flux_scratch(rows, cells):
    shape = (PLANES, FIELDS, cells // LANES)
    return [pltpu.VMEM((*shape, n, LANES), jnp.float32) for n in (rows + 2 * EIGHT, rows)]


def bulk(flags, state, low, high, inner, edge, dtheta, outer, span, token, held, near_parts=()):
    fields, planes, total_rows, cells = state.shape
    first, end = span
    count = end - first
    rows = 32 if count % 32 == 0 else 24 if count % 24 == 0 else 16
    blocks = count // rows
    size = fields * planes * count * cells
    aliases = {} if held is None else {8: 0}
    state = in_hbm(state)
    operands = [state, low, high, inner, edge, inner if outer is None else outer, token]
    operands += [state if held is None else held, *near_parts]
    chunk = pltpu.VMEM((fields, count, cells), jnp.float32)
    near_scratch = [pltpu.VMEM((fields, planes, R_NEAR, cells), jnp.float32), pltpu.SemaphoreType.DMA]
    return pl.pallas_call(
        functools.partial(bulk_kernel, dtheta, rows, span, total_rows, outer is not None, len(near_parts)),
        grid_spec=pltpu.PrefetchScalarGridSpec(
            num_scalar_prefetch=1,
            grid=(blocks,),
            in_specs=[
                ANY,
                whole(LINES, cells),
                whole(LINES, cells),
                ANY,
                rows_from((rows, LANES), 0, first, rows),
                ANY,
                ANY,
                ANY,
                *[whole(*x.shape) for x in near_parts],
            ],
            out_specs=rows_from((fields, planes, rows, cells), 2, first, rows),
            scratch_shapes=[
                pltpu.VMEM((fields, planes, count + 2 * EIGHT, cells), jnp.float32),
                chunk,
                pltpu.SemaphoreType.DMA((3 * blocks,)),
                *flux_scratch(rows, cells),
                *([] if outer is None else [chunk]),
                *(near_scratch if near_parts else []),
            ],
        ),
        out_shape=pltpu.HBM(state.shape, jnp.float32),
        input_output_aliases=aliases,
        compiler_params=PARAMS,
        cost_estimate=cost(size * 60, size * 10),
        name="bulk",
    )(flags, *operands)


def add_outer(flags, outer, span, rows, held):
    fields, count, cells = outer.shape
    chunk = pltpu.VMEM((fields, count, cells), jnp.float32)
    return pl.pallas_call(
        functools.partial(outer_kernel, rows, span),
        grid_spec=pltpu.PrefetchScalarGridSpec(
            num_scalar_prefetch=1,
            grid=(1,),
            in_specs=[ANY, ANY],
            out_specs=ANY,
            scratch_shapes=[chunk, chunk, pltpu.SemaphoreType.DMA((3 * (count // rows),))],
        ),
        out_shape=pltpu.HBM(held.shape, jnp.float32),
        input_output_aliases={2: 0},
        compiler_params=PARAMS,
        cost_estimate=cost(outer.size * 6, outer.size * 16),
        name="add_outer",
    )(flags, outer, held)


def near(flags, state, low, high, inner, edge, dtheta, outer, factor, table, solve, token, part=None):
    fields, planes, rows, cells = state.shape
    out = jax.ShapeDtypeStruct((LINES, R_NEAR, cells), jnp.float32)
    tail = min(R_NEAR // EIGHT, rows // EIGHT - 1)
    state = in_hbm(state)
    out_specs = [whole(LINES, R_NEAR, cells), whole(LINES, R_NEAR, cells), whole(R_NEAR, LANES)]
    out_shape = [out, out, jax.ShapeDtypeStruct((R_NEAR, LANES), jnp.float32)]
    scratch = flux_scratch(R_NEAR, cells)
    if part is not None:
        out_specs.append(whole(fields, part[1] - part[0], cells))
        out_shape.append(jax.ShapeDtypeStruct((fields, part[1] - part[0], cells), jnp.float32))
        scratch.append(pltpu.SemaphoreType.DMA)
    result = pl.pallas_call(
        functools.partial(near_kernel, dtheta, rows, part[0] if part else 0),
        grid_spec=pltpu.PrefetchScalarGridSpec(
            num_scalar_prefetch=1,
            grid=(1,),
            in_specs=[
                whole(fields, planes, R_NEAR, cells),
                pl.BlockSpec((fields, planes, EIGHT, cells), lambda i, s: (0, 0, tail, 0)),
                whole(LINES, cells),
                whole(LINES, cells),
                whole(fields, R_NEAR, cells),
                whole(fields, R_NEAR, cells),
                whole(R_NEAR, LANES),
                whole(R_NEAR, LANES),
                whole(R_NEAR, LANES),
                whole(*solve.shape),
                ANY,
                ANY,
            ],
            out_specs=out_specs,
            scratch_shapes=scratch,
        ),
        out_shape=out_shape,
        compiler_params=PARAMS,
        cost_estimate=cost(LINES * R_NEAR * cells * 200, LINES * R_NEAR * cells * 250),
        name="near",
    )(flags, state, state, low, high, inner, outer, edge, factor, table, solve, in_hbm(token), state)
    return result if part is not None else (*result, None)


def chunks(rows):
    size = 16
    blocks = (rows - R_NEAR) // size
    cuts = sorted({-(-2 * blocks // 5), -(-4 * blocks // 5), blocks})
    ends = [R_NEAR + size * c for c in cuts]
    return size, list(zip([0] + ends[:-1], ends))


def smoothing_table(coarsen, cells, total_cells, dtheta):
    factor = coarsen.astype(jnp.float32)[:, None]
    stiffness = KAPPA / (factor * dtheta) ** 2
    inverse_half = 0.5 / stiffness
    one_minus = jnp.sqrt(inverse_half * (2.0 + inverse_half)) - inverse_half
    log_ratio = jnp.log1p(-one_minus)
    gain = (1.0 - one_minus) / (stiffness * one_minus * (2.0 - one_minus))
    closing = 1.0 / -jnp.expm1((total_cells / factor) * log_ratio)
    across = jnp.exp((cells / factor) * log_ratio)
    column = jnp.arange(LANES, dtype=jnp.int32)[None, :]
    width = jnp.left_shift(1, jnp.minimum(column, 20)).astype(jnp.float32)
    table = jnp.where(width >= factor, jnp.exp(log_ratio * (width / factor)), 0.0)
    table = jnp.where(column == COL_LOG, log_ratio, table)
    table = jnp.where(column == COL_GAIN, gain, table)
    return table, closing, across


def piece_tables(dtheta):
    tables = []
    for level in range(FMAX.bit_length()):
        width = 1 << level
        half = 0.5 * (width * dtheta) ** 2 / KAPPA
        ratio = 1.0 - (math.sqrt(half * (2.0 + half)) - half)
        block = np.arange(LANES) // width
        tables.append(ratio ** np.abs(block[:, None] - block[None, :]) / width)
    table = np.concatenate(tables, axis=1)
    high = table.astype(ml_dtypes.bfloat16)
    low = (table - high.astype(np.float64)).astype(ml_dtypes.bfloat16)
    return jnp.asarray(np.concatenate([high, high, low], axis=0))


def ring(value, axis, shift):
    size = lax.axis_size(axis)
    return lax.ppermute(value, axis, [(i, (i + shift) % size) for i in range(size)])


def body(state, coarsen):
    fields, planes, rows, cells = state.shape
    sec_count = lax.axis_size("sec")
    rad_count = lax.axis_size("rad")
    ax_count = lax.axis_size("ax")
    assert fields == FIELDS and planes == PLANES and ax_count % 2 == 0
    rad_index = lax.axis_index("rad")
    ax_index = lax.axis_index("ax")
    total_cells = cells * sec_count
    dtheta = 2.0 * math.pi / total_cells
    outer_pairs = []
    for i in range(1, ax_count - 1, 2):
        outer_pairs += [(i, i + 1), (i + 1, i)]
    inner_pairs = []
    for i in range(0, ax_count, 2):
        inner_pairs += [(i, i + 1), (i + 1, i)]
    up = [(i, i + 1) for i in range(rad_count - 1)]
    down = [(i + 1, i) for i in range(rad_count - 1)]
    flags = jnp.stack(
        [
            ax_index % 2,
            ((ax_index > 0) & (ax_index < ax_count - 1)).astype(jnp.int32),
            (rad_index == 0).astype(jnp.int32),
            (rad_index == rad_count - 1).astype(jnp.int32),
            rad_index * rows,
        ]
    ).astype(jnp.int32)
    size, spans = chunks(rows)
    count = len(spans)

    part, low, high = pack_first(state, spans[0][1])
    outer = [lax.ppermute(part, "ax", outer_pairs)]
    columns, side = pack_edges(state, high)
    low = lax.ppermute(low, "rad", up)
    high = lax.ppermute(high, "rad", down)
    near_inner = lax.ppermute(side, "ax", inner_pairs)
    if sec_count == 2:
        edge = ring(columns, "sec", 1)
    else:
        from_left = jnp.arange(LANES)[None, :] % 4 < 2
        edge = jnp.where(from_left, ring(columns, "sec", 1), ring(columns, "sec", -1))
    early = [(0, *span) for span in spans[2:]] + [(1, *span) for span in spans[1:2]]
    late = [(0, R_NEAR, spans[0][1])] + [(0, *span) for span in spans[1:2]]
    parts = pack_rest(state, early, columns, low, high) if early else []
    order = in_hbm(parts[0]) if early else columns
    parts = list(parts) + list(pack_rest(state, late, order, edge))
    inner = {}
    for (q, first, last), value in zip(early + late, parts):
        if q:
            outer.append(lax.ppermute(value, "ax", outer_pairs))
        else:
            inner[first, last] = lax.ppermute(value, "ax", inner_pairs)
    order = in_hbm(parts[-1])

    table, closing, across = smoothing_table(coarsen, cells, total_cells, dtheta)
    factor = jnp.broadcast_to(coarsen.astype(jnp.float32)[:, None], (R_NEAR, LANES))

    solve = piece_tables(dtheta)
    given = (flags, state, low, high)

    def pass_over(k, token, held, fused=True, near_parts=()):
        span = (spans[k][0] if k else R_NEAR, spans[k][1])
        far = outer[k] if fused else None
        return bulk(*given, inner[span], edge, dtheta, far, span, token, held, near_parts)

    out = pass_over(2, order, None, fused=False) if count > 2 else None
    part = spans[2] if count > 2 else None
    token = order if out is None else out
    rhs, local, ends, part = near(
        *given, near_inner, edge, dtheta, outer[0], factor, table, solve, token, part
    )
    if part is not None:
        outer.append(lax.ppermute(part, "ax", outer_pairs))
    arrived = [ends] + [ring(ends, "sec", k) for k in range(1, sec_count)] + [ends]
    from_left = jnp.arange(LANES)[None, :] < LINES
    carry = jnp.zeros_like(ends)
    for k in range(sec_count, 0, -1):
        carry = carry * across + jnp.where(from_left, arrived[k], arrived[sec_count - k])
    carry = carry * closing
    passes = min(count, 2)
    for k in range(passes):
        near_parts = (factor, rhs, local, carry, table) if k == passes - 1 else ()
        out = pass_over(k, ends, out, near_parts=near_parts)
    return add_outer(flags, outer[2], spans[2], size, out) if count > 2 else out


def solution(mesh):
    return jax.shard_map(
        body,
        mesh=mesh,
        in_specs=(P(None, "ax", "rad", "sec"), P()),
        out_specs=P(None, "ax", "rad", "sec"),
        check_vma=False,
    )
```

```python
import functools
import math

import jax
import jax.numpy as jnp
import ml_dtypes
import numpy as np
from jax import lax
from jax.experimental import pallas as pl
from jax.experimental.pallas import tpu as pltpu
from jax.sharding import PartitionSpec as P

R_NEAR = 16
FMAX = 16

GAMMA = 1.4
KAPPA = 1.44

FIELDS = 5
PLANES = 2
LINES = FIELDS * PLANES
EIGHT = 8
LANES = 128
VMEM_LIMIT = 28 * 1024 * 1024

COL_LOG = 32
COL_GAIN = 33

ODD, OUTER, FIRST, LAST, BASE = range(5)


def place_flags(counts, rows):
    ax_count, rad_count = counts
    ax = lax.axis_index("ax")
    rad = lax.axis_index("rad")
    beside = (ax > 0) & (ax < ax_count - 1)
    flags = [ax % 2, beside, rad == 0, rad == rad_count - 1, rad * rows]
    return [x.astype(jnp.int32) for x in flags]


def plane_of(odd, q):
    return odd if q else 1 - odd


def reciprocal(x):
    y = pl.reciprocal(x, approx=True)
    y = y * (2.0 - x * y)
    return y * (2.0 - x * y)


def fluxes(fields, want):
    density, energy = fields[0], fields[4]
    momentum = fields[1:4]
    inverse = reciprocal(density)
    velocity = [m * inverse for m in momentum]
    square = {}
    for i in range(3):
        for j in range(i, 3):
            if i == j or i + 1 in want or j + 1 in want or (i, j) == (1, 2):
                square[i, j] = square[j, i] = momentum[i] * velocity[j]
    pressure = (GAMMA - 1.0) * (energy - 0.5 * (square[0, 0] + square[1, 1] + square[2, 2]))
    enthalpy = energy + pressure
    out = {}
    for d in want:
        k = d - 1
        flow = [square[i, k] + pressure if i == k else square[i, k] for i in range(3)]
        out[d] = [momentum[k]] + flow + [enthalpy * velocity[k]]
    return out, (pressure, square[2, 2], square[1, 2])


def flux_along(fields, along):
    return fluxes(fields, (along,))[0][along]


def outer_flux(flags, outer):
    present = flags[OUTER] == 1
    outer = [jnp.where(present, outer[0], 1.0)] + [jnp.where(present, g, 0.0) for g in outer[1:]]
    return flux_along(outer, 1)


def stencil(
    flags, first_row, rows, total_rows, dtheta, load, next_rows, edge, inner, outer, place, radial, azimuthal
):
    strips = rows // EIGHT
    pieces = radial.shape[2]
    row = lax.broadcasted_iota(jnp.int32, (EIGHT, LANES), 0)
    lane = lax.broadcasted_iota(jnp.int32, (EIGHT, LANES), 1)
    start = flags[BASE] + first_row
    axial_sign = jnp.where(flags[ODD] == 1, 0.5, -0.5)
    above = jnp.where((flags[FIRST] == 1) & (first_row == 0), 0.0, (start - 1).astype(jnp.float32) + 0.5)
    end = first_row + rows == total_rows
    below = jnp.where((flags[LAST] == 1) & end, 0.0, (start + rows).astype(jnp.float32) + 0.5)
    scale = jnp.where(row >= EIGHT // 2, above, below)
    at = [slice(b * LANES, (b + 1) * LANES) for b in range(pieces)]

    for q in range(PLANES):
        for b in range(pieces):
            values = [next_rows(f, q, at[b]) for f in range(FIELDS)]
            values[0] = jnp.where(scale > 0.0, values[0], 1.0)
            flux_next = flux_along(values, 2)
            for f in range(FIELDS):
                radial[q, f, b, 0:EIGHT, :] = flux_next[f] * scale
                radial[q, f, b, EIGHT + rows : 2 * EIGHT + rows, :] = flux_next[f] * scale

    def inside(t, carry):
        r = pl.multiple_of(EIGHT * t, EIGHT)
        radius = (start + r + row).astype(jnp.float32) + 0.5
        inv_radius = 1.0 / radius
        for b in range(pieces):
            beside = flux_along([inner(f, r, at[b]) for f in range(FIELDS)], 1)
            axial, source = [], []
            for q in range(PLANES):
                fields = [load(f, q, r, at[b]) for f in range(FIELDS)]
                flow, (pressure, twist, swirl) = fluxes(fields, (1, 2, 3))
                axial.append(flow[1])
                for f in range(FIELDS):
                    radial[q, f, b, pl.ds(r + EIGHT, EIGHT), :] = flow[2][f] * radius
                    azimuthal[q, f, b, pl.ds(r, EIGHT), :] = flow[3][f]
                source.append(((pressure + twist) * inv_radius, swirl * -inv_radius))
            base = [[axial_sign * (x - y) for x, y in zip(beside, axial[1])]]
            if outer is None:
                base.append([axial_sign * x for x in axial[0]])
            else:
                far = outer_flux(flags, [outer(f, r, at[b]) for f in range(FIELDS)])
                base.append([axial_sign * (x - y) for x, y in zip(axial[0], far)])
            for q in range(PLANES):
                base[q][2] = base[q][2] + source[q][0]
                base[q][3] = base[q][3] + source[q][1]
                for f in range(FIELDS):
                    place(f, q, r)[:, at[b]] = base[q][f]
        return carry

    lax.fori_loop(0, strips, inside, 0)

    def differences(t, carry):
        r = pl.multiple_of(EIGHT * t, EIGHT)
        radius = (start + r + row).astype(jnp.float32) + 0.5
        half_inv = 0.5 / radius
        half_arc = half_inv * (1.0 / dtheta)
        beyond = [edge(r)] + [pltpu.roll(edge(r), LANES - 4 * f, 1) for f in range(1, FIELDS)]
        beyond = flux_along(beyond, 3)
        for q in range(PLANES):
            for f in range(FIELDS):
                ends = [pltpu.roll(beyond[f], s, 1) if q else beyond[f] for s in (LANES - 1, 1)]
                here = [azimuthal[q, f, b, pl.ds(r, EIGHT), :] for b in range(pieces)]
                left = [ends[0]] + [pltpu.roll(x, 1, 1) for x in here]
                right = [pltpu.roll(x, LANES - 1, 1) for x in here] + [ends[1]]
                out = place(f, q, r)
                for b in range(pieces):
                    behind = jnp.where(lane == 0, left[b], left[b + 1])
                    ahead = jnp.where(lane == LANES - 1, right[b + 1], right[b])
                    up = radial[q, f, b, pl.ds(r + EIGHT - 1, EIGHT), :]
                    down = radial[q, f, b, pl.ds(r + EIGHT + 1, EIGHT), :]
                    change = (behind - ahead) * half_arc + (up - down) * half_inv
                    out[:, at[b]] = out[:, at[b]] + change
        return carry

    lax.fori_loop(0, strips, differences, 0)


def bulk_kernel(
    dtheta, rows, span, total_rows, fused, near, counts, state, low, high, inner, edge, outer, token, held, *rest
):
    flags = place_flags(counts, total_rows)
    near_parts, out, scratch = rest[:near], rest[near], rest[near + 1 :]
    first, end = span
    blocks = (end - first) // rows
    state_rows, inner_rows, sems, radial, azimuthal, *outer_rows = scratch
    *outer_rows, near_rows, near_sem = [*outer_rows, None, None] if not near else outer_rows
    outer_rows = outer_rows[0] if fused else None
    odd = flags[ODD]
    step = pl.program_id(0)

    def copies(k):
        a = first + k * rows + (EIGHT if k else -EIGHT)
        b = min(first + (k + 1) * rows + EIGHT, total_rows)
        at = a - first + EIGHT
        rest = pl.ds(outer.shape[1] - (end - first) + k * rows, rows)
        here = pl.ds(k * rows, rows)
        sets = [
            (state.at[:, :, a:b, :], state_rows.at[:, :, at : at + b - a, :]),
            (inner.at[:, here, :], inner_rows.at[:, here, :]),
        ]
        if fused:
            sets.append((outer.at[:, rest, :], outer_rows.at[:, here, :]))
        return [pltpu.make_async_copy(x, y, sems.at[3 * k + i]) for i, (x, y) in enumerate(sets)]

    @pl.when(step == 0)
    def _():
        for k in range(blocks):
            for copy in copies(k):
                copy.start()
        if near:
            close_circle(flags, *near_parts, near_rows)
            pltpu.make_async_copy(near_rows, held.at[:, :, 0:R_NEAR, :], near_sem).start()

    for k in range(blocks):

        @pl.when(step == k)
        def _():
            for copy in copies(k):
                copy.wait()

    first_row = first + step * rows
    at_end = first_row + rows == total_rows
    base = pl.multiple_of(step * rows, EIGHT)
    sub = lax.broadcasted_iota(jnp.int32, (EIGHT, LANES), 0)

    def load(f, q, r, at):
        return state_rows[f, plane_of(odd, q), pl.ds(base + EIGHT + r, EIGHT), at]

    def next_rows(f, q, at):
        k = f * PLANES + q
        under = jnp.where(at_end, high[k : k + 1, at], load(f, q, rows, at))
        return jnp.where(sub >= EIGHT // 2, load(f, q, -EIGHT, at), under)

    stencil(
        flags,
        first_row,
        rows,
        total_rows,
        dtheta,
        load,
        next_rows,
        lambda r: edge[pl.ds(r, EIGHT), :],
        lambda f, r, at: inner_rows[f, pl.ds(base + r, EIGHT), at],
        (lambda f, r, at: outer_rows[f, pl.ds(base + r, EIGHT), at]) if fused else None,
        lambda f, q, r: out.at[f, plane_of(odd, q), pl.ds(r, EIGHT), :],
        radial,
        azimuthal,
    )
    if near:

        @pl.when(step == blocks - 1)
        def _():
            pltpu.make_async_copy(near_rows, held.at[:, :, 0:R_NEAR, :], near_sem).wait()


def outer_kernel(rows, span, counts, outer, held, out, outer_rows, held_rows, sems):
    flags = place_flags(counts, 0)
    first, end = span
    plane = lax.axis_index("ax") % 2
    sign = jnp.where(flags[ODD] == 1, -0.5, 0.5)
    steps = []
    for k in range((end - first) // rows):
        here = pl.ds(k * rows, rows)
        there = pl.ds(first + k * rows, rows)
        ways = [
            (outer.at[:, here, :], outer_rows.at[:, here, :]),
            (held.at[:, plane, there, :], held_rows.at[:, here, :]),
            (held_rows.at[:, here, :], out.at[:, plane, there, :]),
        ]
        steps.append([pltpu.make_async_copy(x, y, sems.at[3 * k + i]) for i, (x, y) in enumerate(ways)])
        steps[-1][0].start()
        steps[-1][1].start()
    for k, (come, have, leave) in enumerate(steps):
        come.wait()
        have.wait()
        for t in range(rows // EIGHT):
            at = pl.ds(k * rows + EIGHT * t, EIGHT)
            values = outer_flux(flags, [outer_rows[f, at, :] for f in range(FIELDS)])
            for f in range(FIELDS):
                held_rows[f, at, :] = held_rows[f, at, :] + sign * values[f]
        leave.start()
    for _, _, leave in steps:
        leave.wait()


def near_kernel(
    dtheta,
    total_rows,
    part_first,
    counts,
    state,
    after,
    low,
    high,
    inner,
    outer,
    edge,
    factor,
    table,
    solve,
    token,
    hbm,
    rhs,
    local,
    carry,
    *rest,
):
    flags = place_flags(counts, total_rows)
    cells = state.shape[-1]
    odd = flags[ODD]
    part = rest[0] if len(rest) > 2 else None
    scratch = rest[-2:] if part is None else rest[-3:-1]
    if part is not None:
        source = hbm.at[:, lax.axis_index("ax") % 2, part_first : part_first + part.shape[1], :]
        copy = pltpu.make_async_copy(source, part, rest[-1])
        copy.start()

    sub = lax.broadcasted_iota(jnp.int32, (EIGHT, LANES), 0)

    def next_rows(f, q, at):
        k = f * PLANES + q
        under = high[k : k + 1, at] if total_rows == R_NEAR else after[f, plane_of(odd, q), :, at]
        return jnp.where(sub >= EIGHT // 2, low[k : k + 1, at], under)

    stencil(
        flags,
        0,
        R_NEAR,
        total_rows,
        dtheta,
        lambda f, q, r, at: state[f, plane_of(odd, q), pl.ds(r, EIGHT), at],
        next_rows,
        lambda r: edge[pl.ds(r, EIGHT), :],
        lambda f, r, at: inner[f, pl.ds(r, EIGHT), at],
        lambda f, r, at: outer[f, pl.ds(r, EIGHT), at],
        lambda f, q, r: rhs.at[f * PLANES + q, pl.ds(r, EIGHT), :],
        *scratch,
    )

    pieces = cells // LANES
    lane = lax.broadcasted_iota(jnp.int32, (R_NEAR, LANES), 1)
    width = factor[...]
    log_ratio = table[:, COL_LOG : COL_LOG + 1]
    block = jnp.floor((lane.astype(jnp.float32) + 0.5) / width)
    ahead_entry = jnp.exp(log_ratio * (block + 1.0))
    behind_entry = jnp.exp(log_ratio * (LANES / width - block))
    across = jnp.exp(log_ratio * (LANES / width))

    def line(k, ends):
        rows = jnp.concatenate([rhs[k, :, b * LANES : (b + 1) * LANES] for b in range(pieces)], axis=0)
        high = rows.astype(jnp.bfloat16)
        low = (rows - high.astype(jnp.float32)).astype(jnp.bfloat16)
        solved = jnp.dot(
            jnp.concatenate([high, low, high], axis=1), solve[...], preferred_element_type=jnp.float32
        )
        inside = []
        for b in range(pieces):
            mine = solved[b * R_NEAR : (b + 1) * R_NEAR]
            value = mine[:, :LANES]
            for level in range(1, FMAX.bit_length()):
                chosen = mine[:, level * LANES : (level + 1) * LANES]
                value = jnp.where(width == (1 << level), chosen, value)
            inside.append(value)
        total = list(inside)
        enter = jnp.zeros((R_NEAR, LANES), jnp.float32)
        for b in range(pieces):
            leave = jnp.broadcast_to(inside[b][:, LANES - 1 : LANES], (R_NEAR, LANES))
            total[b] = total[b] + ahead_entry * enter
            enter = leave + across * enter
        ends = jnp.where(lane == k, enter, ends)
        enter = jnp.zeros((R_NEAR, LANES), jnp.float32)
        for b in reversed(range(pieces)):
            leave = jnp.broadcast_to(inside[b][:, 0:1], (R_NEAR, LANES))
            total[b] = total[b] + behind_entry * enter
            enter = leave + across * enter
        for b in range(pieces):
            local[k, :, b * LANES : (b + 1) * LANES] = total[b]
        return jnp.where(lane == k + LINES, enter, ends)

    carry[...] = lax.fori_loop(
        0, LINES, line, jnp.zeros((R_NEAR, LANES), jnp.float32)
    )
    if part is not None:
        copy.wait()


def close_circle(flags, factor, rhs, local, carry, table, out):
    cells = out.shape[-1]
    lane = lax.broadcasted_iota(jnp.int32, (R_NEAR, cells), 1).astype(jnp.float32)
    width = factor[:, 0:1]
    block = jnp.floor((lane + 0.5) / width)
    count = cells / width
    log_ratio = table[:, COL_LOG : COL_LOG + 1]
    gain = jnp.broadcast_to(table[:, COL_GAIN : COL_GAIN + 1], (R_NEAR, cells))
    from_left = jnp.exp(log_ratio * (block + 1.0))
    from_right = jnp.exp(log_ratio * (count - block))
    near = flags[FIRST] == 1
    for f in range(FIELDS):
        for q in range(PLANES):
            k = f * PLANES + q
            j = k + LINES
            smooth = gain * (
                local[k] + from_left * carry[:, k : k + 1] + from_right * carry[:, j : j + 1]
            )
            out[f, plane_of(flags[ODD], q)] = jnp.where(near, smooth, rhs[k])


def stream(pieces, sems):
    steps = []
    for source, stage, target in pieces:
        for f in range(FIELDS):
            k = 2 * len(steps)
            come = pltpu.make_async_copy(source.at[f], stage.at[f], sems.at[k])
            leave = pltpu.make_async_copy(stage.at[f], target.at[f], sems.at[k + 1])
            steps.append((come, leave))
    for come, _ in steps:
        come.start()

    def forward():
        for come, leave in steps:
            come.wait()
            leave.start()

    def finish():
        for _, leave in steps:
            leave.wait()

    return forward, finish


def pack_first_kernel(count, state, part, low, high, stage, top, bottom, row_sems, sems):
    _, _, rows, _ = state.shape
    odd = lax.axis_index("ax") % 2
    forward, finish = stream([(state.at[:, odd, 0:count, :], stage, part)], sems)
    copies = [
        pltpu.make_async_copy(state.at[:, :, rows - EIGHT : rows, :], top, row_sems.at[0]),
        pltpu.make_async_copy(state.at[:, :, 0:EIGHT, :], bottom, row_sems.at[1]),
    ]
    for copy in copies:
        copy.start()
    forward()
    for copy in copies:
        copy.wait()
    for f in range(FIELDS):
        for q in range(PLANES):
            k = f * PLANES + q
            p = plane_of(odd, q)
            low[k : k + 1, :] = top[f, p, EIGHT - 1 : EIGHT, :]
            high[k : k + 1, :] = bottom[f, p, 0:1, :]
    finish()


def pack_edges_kernel(state, token, edge, side, left, right, sems):
    _, _, rows, cells = state.shape
    odd = lax.axis_index("ax") % 2
    copies = [
        pltpu.make_async_copy(state.at[:, :, :, cells - LANES : cells], left, sems.at[0]),
        pltpu.make_async_copy(state.at[:, :, :, 0:LANES], right, sems.at[1]),
        pltpu.make_async_copy(state.at[:, 1 - odd, 0:R_NEAR, :], side, sems.at[2]),
    ]
    for copy in copies:
        copy.start()
    for copy in copies[:2]:
        copy.wait()
    lane = lax.broadcasted_iota(jnp.int32, (rows, LANES), 1)
    columns = jnp.ones((rows, LANES), jnp.float32)
    for f in range(FIELDS):
        for q in range(PLANES):
            p = plane_of(odd, q)
            columns = jnp.where(lane == 4 * f + q, left[f, p, :, LANES - 1 : LANES], columns)
            columns = jnp.where(lane == (4 * f - 1 - q) % LANES, right[f, p, :, 0:1], columns)
    edge[...] = columns
    copies[2].wait()


def pack_rest_kernel(parts, tokens, state, *rest):
    rest = rest[tokens:]
    odd = lax.axis_index("ax") % 2
    count = len(parts)
    pieces = []
    for k, (q, first, last) in enumerate(parts):
        pieces.append((state.at[:, plane_of(odd, q), first:last, :], rest[count + k], rest[k]))
    for step in stream(pieces, rest[-1]):
        step()


ANY = pl.BlockSpec(memory_space=pl.ANY)
PARAMS = pltpu.CompilerParams(vmem_limit_bytes=VMEM_LIMIT)


def whole(*shape):
    return pl.BlockSpec(shape, lambda i: (0,) * len(shape))


def rows_from(shape, axis, first, step):
    def place(i):
        row = (first // EIGHT + i * (step // EIGHT)) * EIGHT
        return tuple(row if d == axis else 0 for d in range(len(shape)))

    return pl.BlockSpec(tuple(pl.Element(n) for n in shape), place)


def in_hbm(value):
    return pltpu.with_memory_space_constraint(value, pltpu.HBM)


def cost(flops, nbytes):
    return pl.CostEstimate(flops=flops, bytes_accessed=nbytes, transcendentals=0)


def pack_first(state, count):
    fields, planes, _, cells = state.shape
    vmem = pl.BlockSpec(memory_space=pltpu.VMEM)
    row = jax.ShapeDtypeStruct((LINES, cells), jnp.float32)
    rows = pltpu.VMEM((fields, planes, EIGHT, cells), jnp.float32)
    return pl.pallas_call(
        functools.partial(pack_first_kernel, count),
        in_specs=[ANY],
        out_specs=[ANY, vmem, vmem],
        out_shape=[jax.ShapeDtypeStruct((fields, count, cells), jnp.float32), row, row],
        scratch_shapes=[
            pltpu.VMEM((fields, count, cells), jnp.float32),
            rows,
            rows,
            pltpu.SemaphoreType.DMA((2,)),
            pltpu.SemaphoreType.DMA((2 * fields,)),
        ],
        compiler_params=PARAMS,
        cost_estimate=cost(0, fields * count * cells * 8),
        name="pack_first",
    )(in_hbm(state))


def pack_edges(state, token):
    fields, planes, rows, cells = state.shape
    vmem = pl.BlockSpec(memory_space=pltpu.VMEM)
    tiles = pltpu.VMEM((fields, planes, rows, LANES), jnp.float32)
    return pl.pallas_call(
        pack_edges_kernel,
        in_specs=[ANY, ANY],
        out_specs=[vmem, vmem],
        out_shape=[
            jax.ShapeDtypeStruct((rows, LANES), jnp.float32),
            jax.ShapeDtypeStruct((fields, R_NEAR, cells), jnp.float32),
        ],
        scratch_shapes=[tiles, tiles, pltpu.SemaphoreType.DMA((3,))],
        compiler_params=PARAMS,
        cost_estimate=cost(0, fields * planes * rows * LANES * 16),
        name="pack_edges",
    )(in_hbm(state), token)


def pack_rest(state, parts, *tokens):
    fields, _, _, cells = state.shape
    shapes = [jax.ShapeDtypeStruct((fields, last - first, cells), jnp.float32) for _, first, last in parts]
    return pl.pallas_call(
        functools.partial(pack_rest_kernel, parts, len(tokens)),
        in_specs=[ANY] * (1 + len(tokens)),
        out_specs=[ANY] * len(shapes),
        out_shape=shapes,
        scratch_shapes=[
            *[pltpu.VMEM(x.shape, jnp.float32) for x in shapes],
            pltpu.SemaphoreType.DMA((2 * fields * len(parts),)),
        ],
        compiler_params=PARAMS,
        cost_estimate=cost(0, sum(math.prod(x.shape) for x in shapes) * 8),
        name="pack_rest",
    )(in_hbm(state), *tokens)


def flux_scratch(rows, cells):
    shape = (PLANES, FIELDS, cells // LANES)
    return [pltpu.VMEM((*shape, n, LANES), jnp.float32) for n in (rows + 2 * EIGHT, rows)]


def bulk(counts, state, low, high, inner, edge, dtheta, outer, span, token, held, near_parts=()):
    fields, planes, total_rows, cells = state.shape
    first, end = span
    count = end - first
    rows = 32 if count % 32 == 0 else 24 if count % 24 == 0 else 16
    blocks = count // rows
    size = fields * planes * count * cells
    aliases = {} if held is None else {7: 0}
    state = in_hbm(state)
    operands = [state, low, high, inner, edge, inner if outer is None else outer, token]
    operands += [state if held is None else held, *near_parts]
    chunk = pltpu.VMEM((fields, count, cells), jnp.float32)
    near_scratch = [pltpu.VMEM((fields, planes, R_NEAR, cells), jnp.float32), pltpu.SemaphoreType.DMA]
    return pl.pallas_call(
        functools.partial(bulk_kernel, dtheta, rows, span, total_rows, outer is not None, len(near_parts), counts),
        grid_spec=pltpu.PrefetchScalarGridSpec(
            num_scalar_prefetch=0,
            grid=(blocks,),
            in_specs=[
                ANY,
                whole(LINES, cells),
                whole(LINES, cells),
                ANY,
                rows_from((rows, LANES), 0, first, rows),
                ANY,
                ANY,
                ANY,
                *[whole(*x.shape) for x in near_parts],
            ],
            out_specs=rows_from((fields, planes, rows, cells), 2, first, rows),
            scratch_shapes=[
                pltpu.VMEM((fields, planes, count + 2 * EIGHT, cells), jnp.float32),
                chunk,
                pltpu.SemaphoreType.DMA((3 * blocks,)),
                *flux_scratch(rows, cells),
                *([] if outer is None else [chunk]),
                *(near_scratch if near_parts else []),
            ],
        ),
        out_shape=pltpu.HBM(state.shape, jnp.float32),
        input_output_aliases=aliases,
        compiler_params=PARAMS,
        cost_estimate=cost(size * 60, size * 10),
        name="bulk",
    )(*operands)


def add_outer(counts, outer, span, rows, held):
    fields, count, cells = outer.shape
    chunk = pltpu.VMEM((fields, count, cells), jnp.float32)
    return pl.pallas_call(
        functools.partial(outer_kernel, rows, span, counts),
        grid_spec=pltpu.PrefetchScalarGridSpec(
            num_scalar_prefetch=0,
            grid=(1,),
            in_specs=[ANY, ANY],
            out_specs=ANY,
            scratch_shapes=[chunk, chunk, pltpu.SemaphoreType.DMA((3 * (count // rows),))],
        ),
        out_shape=pltpu.HBM(held.shape, jnp.float32),
        input_output_aliases={1: 0},
        compiler_params=PARAMS,
        cost_estimate=cost(outer.size * 6, outer.size * 16),
        name="add_outer",
    )(outer, held)


def near(counts, state, low, high, inner, edge, dtheta, outer, factor, table, solve, token, part=None):
    fields, planes, rows, cells = state.shape
    out = jax.ShapeDtypeStruct((LINES, R_NEAR, cells), jnp.float32)
    tail = min(R_NEAR // EIGHT, rows // EIGHT - 1)
    state = in_hbm(state)
    out_specs = [whole(LINES, R_NEAR, cells), whole(LINES, R_NEAR, cells), whole(R_NEAR, LANES)]
    out_shape = [out, out, jax.ShapeDtypeStruct((R_NEAR, LANES), jnp.float32)]
    scratch = flux_scratch(R_NEAR, cells)
    if part is not None:
        out_specs.append(whole(fields, part[1] - part[0], cells))
        out_shape.append(jax.ShapeDtypeStruct((fields, part[1] - part[0], cells), jnp.float32))
        scratch.append(pltpu.SemaphoreType.DMA)
    result = pl.pallas_call(
        functools.partial(near_kernel, dtheta, rows, part[0] if part else 0, counts),
        grid_spec=pltpu.PrefetchScalarGridSpec(
            num_scalar_prefetch=0,
            grid=(1,),
            in_specs=[
                whole(fields, planes, R_NEAR, cells),
                pl.BlockSpec((fields, planes, EIGHT, cells), lambda i: (0, 0, tail, 0)),
                whole(LINES, cells),
                whole(LINES, cells),
                whole(fields, R_NEAR, cells),
                whole(fields, R_NEAR, cells),
                whole(R_NEAR, LANES),
                whole(R_NEAR, LANES),
                whole(R_NEAR, LANES),
                whole(*solve.shape),
                ANY,
                ANY,
            ],
            out_specs=out_specs,
            scratch_shapes=scratch,
        ),
        out_shape=out_shape,
        compiler_params=PARAMS,
        cost_estimate=cost(LINES * R_NEAR * cells * 200, LINES * R_NEAR * cells * 250),
        name="near",
    )(state, state, low, high, inner, outer, edge, factor, table, solve, in_hbm(token), state)
    return result if part is not None else (*result, None)


def chunks(rows):
    size = 16
    blocks = (rows - R_NEAR) // size
    cuts = sorted({-(-2 * blocks // 5), -(-4 * blocks // 5), blocks})
    ends = [R_NEAR + size * c for c in cuts]
    return size, list(zip([0] + ends[:-1], ends))


def smoothing_table(coarsen, cells, total_cells, dtheta):
    factor = coarsen.astype(jnp.float32)[:, None]
    stiffness = KAPPA / (factor * dtheta) ** 2
    inverse_half = 0.5 / stiffness
    one_minus = jnp.sqrt(inverse_half * (2.0 + inverse_half)) - inverse_half
    log_ratio = jnp.log1p(-one_minus)
    gain = (1.0 - one_minus) / (stiffness * one_minus * (2.0 - one_minus))
    closing = 1.0 / -jnp.expm1((total_cells / factor) * log_ratio)
    across = jnp.exp((cells / factor) * log_ratio)
    column = jnp.arange(LANES, dtype=jnp.int32)[None, :]
    width = jnp.left_shift(1, jnp.minimum(column, 20)).astype(jnp.float32)
    table = jnp.where(width >= factor, jnp.exp(log_ratio * (width / factor)), 0.0)
    table = jnp.where(column == COL_LOG, log_ratio, table)
    table = jnp.where(column == COL_GAIN, gain, table)
    return table, closing, across


def piece_tables(dtheta):
    tables = []
    for level in range(FMAX.bit_length()):
        width = 1 << level
        half = 0.5 * (width * dtheta) ** 2 / KAPPA
        ratio = 1.0 - (math.sqrt(half * (2.0 + half)) - half)
        block = np.arange(LANES) // width
        tables.append(ratio ** np.abs(block[:, None] - block[None, :]) / width)
    table = np.concatenate(tables, axis=1)
    high = table.astype(ml_dtypes.bfloat16)
    low = (table - high.astype(np.float64)).astype(ml_dtypes.bfloat16)
    return jnp.asarray(np.concatenate([high, high, low], axis=0))


def ring(value, axis, shift):
    size = lax.axis_size(axis)
    return lax.ppermute(value, axis, [(i, (i + shift) % size) for i in range(size)])


def body(state, coarsen):
    fields, planes, rows, cells = state.shape
    sec_count = lax.axis_size("sec")
    rad_count = lax.axis_size("rad")
    ax_count = lax.axis_size("ax")
    assert fields == FIELDS and planes == PLANES and ax_count % 2 == 0
    total_cells = cells * sec_count
    dtheta = 2.0 * math.pi / total_cells
    outer_pairs = []
    for i in range(1, ax_count - 1, 2):
        outer_pairs += [(i, i + 1), (i + 1, i)]
    inner_pairs = []
    for i in range(0, ax_count, 2):
        inner_pairs += [(i, i + 1), (i + 1, i)]
    up = [(i, i + 1) for i in range(rad_count - 1)]
    down = [(i + 1, i) for i in range(rad_count - 1)]
    counts = (ax_count, rad_count)
    size, spans = chunks(rows)
    count = len(spans)

    part, low, high = pack_first(state, spans[0][1])
    outer = [lax.ppermute(part, "ax", outer_pairs)]
    columns, side = pack_edges(state, high)
    low = lax.ppermute(low, "rad", up)
    high = lax.ppermute(high, "rad", down)
    near_inner = lax.ppermute(side, "ax", inner_pairs)
    if sec_count == 2:
        edge = ring(columns, "sec", 1)
    else:
        from_left = jnp.arange(LANES)[None, :] % 4 < 2
        edge = jnp.where(from_left, ring(columns, "sec", 1), ring(columns, "sec", -1))
    early = [(0, *span) for span in spans[2:]] + [(1, *span) for span in spans[1:2]]
    late = [(0, R_NEAR, spans[0][1])] + [(0, *span) for span in spans[1:2]]
    parts = pack_rest(state, early, columns, low, high) if early else []
    order = in_hbm(parts[0]) if early else columns
    parts = list(parts) + list(pack_rest(state, late, order, edge))
    inner = {}
    for (q, first, last), value in zip(early + late, parts):
        if q:
            outer.append(lax.ppermute(value, "ax", outer_pairs))
        else:
            inner[first, last] = lax.ppermute(value, "ax", inner_pairs)
    order = in_hbm(parts[-1])

    table, closing, across = smoothing_table(coarsen, cells, total_cells, dtheta)
    factor = jnp.broadcast_to(coarsen.astype(jnp.float32)[:, None], (R_NEAR, LANES))

    solve = piece_tables(dtheta)
    given = (counts, state, low, high)

    def pass_over(k, token, held, fused=True, near_parts=()):
        span = (spans[k][0] if k else R_NEAR, spans[k][1])
        far = outer[k] if fused else None
        return bulk(*given, inner[span], edge, dtheta, far, span, token, held, near_parts)

    out = pass_over(2, order, None, fused=False) if count > 2 else None
    part = spans[2] if count > 2 else None
    token = order if out is None else out
    rhs, local, ends, part = near(
        *given, near_inner, edge, dtheta, outer[0], factor, table, solve, token, part
    )
    if part is not None:
        outer.append(lax.ppermute(part, "ax", outer_pairs))
    arrived = [ends] + [ring(ends, "sec", k) for k in range(1, sec_count)] + [ends]
    from_left = jnp.arange(LANES)[None, :] < LINES
    carry = jnp.zeros_like(ends)
    for k in range(sec_count, 0, -1):
        carry = carry * across + jnp.where(from_left, arrived[k], arrived[sec_count - k])
    carry = carry * closing
    passes = min(count, 2)
    for k in range(passes):
        near_parts = (factor, rhs, local, carry, table) if k == passes - 1 else ()
        out = pass_over(k, ends, out, near_parts=near_parts)
    return add_outer(counts, outer[2], spans[2], size, out) if count > 2 else out


def solution(mesh):
    return jax.shard_map(
        body,
        mesh=mesh,
        in_specs=(P(None, "ax", "rad", "sec"), P()),
        out_specs=P(None, "ax", "rad", "sec"),
        check_vma=False,
    )
```

```python
import functools
import math

import jax
import jax.numpy as jnp
import ml_dtypes
import numpy as np
from jax import lax
from jax.experimental import pallas as pl
from jax.experimental.pallas import tpu as pltpu
from jax.sharding import PartitionSpec as P

R_NEAR = 16
FMAX = 16

GAMMA = 1.4
KAPPA = 1.44

FIELDS = 5
PLANES = 2
LINES = FIELDS * PLANES
EIGHT = 8
LANES = 128
VMEM_LIMIT = 28 * 1024 * 1024

COL_LOG = 32
COL_GAIN = 33

ODD, OUTER, FIRST, LAST, BASE = range(5)


def place_flags(counts, rows):
    ax_count, rad_count = counts
    ax = lax.axis_index("ax")
    rad = lax.axis_index("rad")
    beside = (ax > 0) & (ax < ax_count - 1)
    flags = [ax % 2, beside, rad == 0, rad == rad_count - 1, rad * rows]
    return [x.astype(jnp.int32) for x in flags]


def plane_of(odd, q):
    return odd if q else 1 - odd


def reciprocal(x):
    y = pl.reciprocal(x, approx=True)
    y = y * (2.0 - x * y)
    return y * (2.0 - x * y)


def fluxes(fields, want):
    density, energy = fields[0], fields[4]
    momentum = fields[1:4]
    inverse = reciprocal(density)
    velocity = [m * inverse for m in momentum]
    square = {}
    for i in range(3):
        for j in range(i, 3):
            if i == j or i + 1 in want or j + 1 in want or (i, j) == (1, 2):
                square[i, j] = square[j, i] = momentum[i] * velocity[j]
    pressure = (GAMMA - 1.0) * (energy - 0.5 * (square[0, 0] + square[1, 1] + square[2, 2]))
    enthalpy = energy + pressure
    out = {}
    for d in want:
        k = d - 1
        flow = [square[i, k] + pressure if i == k else square[i, k] for i in range(3)]
        out[d] = [momentum[k]] + flow + [enthalpy * velocity[k]]
    return out, (pressure, square[2, 2], square[1, 2])


def flux_along(fields, along):
    return fluxes(fields, (along,))[0][along]


def outer_flux(flags, outer):
    present = flags[OUTER] == 1
    outer = [jnp.where(present, outer[0], 1.0)] + [jnp.where(present, g, 0.0) for g in outer[1:]]
    return flux_along(outer, 1)


def stencil(
    flags, first_row, rows, total_rows, dtheta, load, next_rows, edge, inner, outer, place, radial, azimuthal
):
    strips = rows // EIGHT
    pieces = radial.shape[2]
    row = lax.broadcasted_iota(jnp.int32, (EIGHT, LANES), 0)
    lane = lax.broadcasted_iota(jnp.int32, (EIGHT, LANES), 1)
    start = flags[BASE] + first_row
    axial_sign = jnp.where(flags[ODD] == 1, 0.5, -0.5)
    above = jnp.where((flags[FIRST] == 1) & (first_row == 0), 0.0, (start - 1).astype(jnp.float32) + 0.5)
    end = first_row + rows == total_rows
    below = jnp.where((flags[LAST] == 1) & end, 0.0, (start + rows).astype(jnp.float32) + 0.5)
    scale = jnp.where(row >= EIGHT // 2, above, below)
    at = [slice(b * LANES, (b + 1) * LANES) for b in range(pieces)]

    for q in range(PLANES):
        for b in range(pieces):
            values = [next_rows(f, q, at[b]) for f in range(FIELDS)]
            values[0] = jnp.where(scale > 0.0, values[0], 1.0)
            flux_next = flux_along(values, 2)
            for f in range(FIELDS):
                radial[q, f, b, 0:EIGHT, :] = flux_next[f] * scale
                radial[q, f, b, EIGHT + rows : 2 * EIGHT + rows, :] = flux_next[f] * scale

    def inside(t, carry):
        r = pl.multiple_of(EIGHT * t, EIGHT)
        radius = (start + r + row).astype(jnp.float32) + 0.5
        inv_radius = 1.0 / radius
        for b in range(pieces):
            beside = flux_along([inner(f, r, at[b]) for f in range(FIELDS)], 1)
            axial, source = [], []
            for q in range(PLANES):
                fields = [load(f, q, r, at[b]) for f in range(FIELDS)]
                flow, (pressure, twist, swirl) = fluxes(fields, (1, 2, 3))
                axial.append(flow[1])
                for f in range(FIELDS):
                    radial[q, f, b, pl.ds(r + EIGHT, EIGHT), :] = flow[2][f] * radius
                    azimuthal[q, f, b, pl.ds(r, EIGHT), :] = flow[3][f]
                source.append(((pressure + twist) * inv_radius, swirl * -inv_radius))
            base = [[axial_sign * (x - y) for x, y in zip(beside, axial[1])]]
            if outer is None:
                base.append([axial_sign * x for x in axial[0]])
            else:
                far = outer_flux(flags, [outer(f, r, at[b]) for f in range(FIELDS)])
                base.append([axial_sign * (x - y) for x, y in zip(axial[0], far)])
            for q in range(PLANES):
                base[q][2] = base[q][2] + source[q][0]
                base[q][3] = base[q][3] + source[q][1]
                for f in range(FIELDS):
                    place(f, q, r)[:, at[b]] = base[q][f]
        return carry

    lax.fori_loop(0, strips, inside, 0)

    def differences(t, carry):
        r = pl.multiple_of(EIGHT * t, EIGHT)
        radius = (start + r + row).astype(jnp.float32) + 0.5
        half_inv = 0.5 / radius
        half_arc = half_inv * (1.0 / dtheta)
        beyond = [edge(r)] + [pltpu.roll(edge(r), LANES - 4 * f, 1) for f in range(1, FIELDS)]
        beyond = flux_along(beyond, 3)
        for q in range(PLANES):
            for f in range(FIELDS):
                ends = [pltpu.roll(beyond[f], s, 1) if q else beyond[f] for s in (LANES - 1, 1)]
                here = [azimuthal[q, f, b, pl.ds(r, EIGHT), :] for b in range(pieces)]
                left = [ends[0]] + [pltpu.roll(x, 1, 1) for x in here]
                right = [pltpu.roll(x, LANES - 1, 1) for x in here] + [ends[1]]
                out = place(f, q, r)
                for b in range(pieces):
                    behind = jnp.where(lane == 0, left[b], left[b + 1])
                    ahead = jnp.where(lane == LANES - 1, right[b + 1], right[b])
                    up = radial[q, f, b, pl.ds(r + EIGHT - 1, EIGHT), :]
                    down = radial[q, f, b, pl.ds(r + EIGHT + 1, EIGHT), :]
                    change = (behind - ahead) * half_arc + (up - down) * half_inv
                    out[:, at[b]] = out[:, at[b]] + change
        return carry

    lax.fori_loop(0, strips, differences, 0)


def bulk_kernel(
    dtheta, rows, span, total_rows, fused, near, counts, state, low, high, inner, edge, outer, token, held, *rest
):
    flags = place_flags(counts, total_rows)
    near_parts, out, scratch = rest[:near], rest[near], rest[near + 1 :]
    first, end = span
    blocks = (end - first) // rows
    state_rows, inner_rows, sems, radial, azimuthal, *outer_rows = scratch
    *outer_rows, near_rows, near_sem = [*outer_rows, None, None] if not near else outer_rows
    outer_rows = outer_rows[0] if fused else None
    odd = flags[ODD]
    step = pl.program_id(0)

    def copies(k):
        a = first + k * rows + (EIGHT if k else -EIGHT)
        b = min(first + (k + 1) * rows + EIGHT, total_rows)
        at = a - first + EIGHT
        rest = pl.ds(outer.shape[1] - (end - first) + k * rows, rows)
        here = pl.ds(k * rows, rows)
        sets = [
            (state.at[:, :, a:b, :], state_rows.at[:, :, at : at + b - a, :]),
            (inner.at[:, here, :], inner_rows.at[:, here, :]),
        ]
        if fused:
            sets.append((outer.at[:, rest, :], outer_rows.at[:, here, :]))
        return [pltpu.make_async_copy(x, y, sems.at[3 * k + i]) for i, (x, y) in enumerate(sets)]

    @pl.when(step == 0)
    def _():
        for k in range(blocks):
            for copy in copies(k):
                copy.start()
        if near:
            close_circle(flags, *near_parts, near_rows)
            pltpu.make_async_copy(near_rows, held.at[:, :, 0:R_NEAR, :], near_sem).start()

    for k in range(blocks):

        @pl.when(step == k)
        def _():
            for copy in copies(k):
                copy.wait()

    first_row = first + step * rows
    at_end = first_row + rows == total_rows
    base = pl.multiple_of(step * rows, EIGHT)
    sub = lax.broadcasted_iota(jnp.int32, (EIGHT, LANES), 0)

    def load(f, q, r, at):
        return state_rows[f, plane_of(odd, q), pl.ds(base + EIGHT + r, EIGHT), at]

    def next_rows(f, q, at):
        k = f * PLANES + q
        under = jnp.where(at_end, high[k : k + 1, at], load(f, q, rows, at))
        return jnp.where(sub >= EIGHT // 2, load(f, q, -EIGHT, at), under)

    stencil(
        flags,
        first_row,
        rows,
        total_rows,
        dtheta,
        load,
        next_rows,
        lambda r: edge[pl.ds(r, EIGHT), :],
        lambda f, r, at: inner_rows[f, pl.ds(base + r, EIGHT), at],
        (lambda f, r, at: outer_rows[f, pl.ds(base + r, EIGHT), at]) if fused else None,
        lambda f, q, r: out.at[f, plane_of(odd, q), pl.ds(r, EIGHT), :],
        radial,
        azimuthal,
    )
    if near:

        @pl.when(step == blocks - 1)
        def _():
            pltpu.make_async_copy(near_rows, held.at[:, :, 0:R_NEAR, :], near_sem).wait()


def outer_kernel(rows, span, counts, outer, held, out, outer_rows, held_rows, sems):
    flags = place_flags(counts, 0)
    first, end = span
    plane = lax.axis_index("ax") % 2
    sign = jnp.where(flags[ODD] == 1, -0.5, 0.5)
    steps = []
    for k in range((end - first) // rows):
        here = pl.ds(k * rows, rows)
        there = pl.ds(first + k * rows, rows)
        ways = [
            (outer.at[:, here, :], outer_rows.at[:, here, :]),
            (held.at[:, plane, there, :], held_rows.at[:, here, :]),
            (held_rows.at[:, here, :], out.at[:, plane, there, :]),
        ]
        steps.append([pltpu.make_async_copy(x, y, sems.at[3 * k + i]) for i, (x, y) in enumerate(ways)])
        steps[-1][0].start()
        steps[-1][1].start()
    for k, (come, have, leave) in enumerate(steps):
        come.wait()
        have.wait()
        for t in range(rows // EIGHT):
            at = pl.ds(k * rows + EIGHT * t, EIGHT)
            values = outer_flux(flags, [outer_rows[f, at, :] for f in range(FIELDS)])
            for f in range(FIELDS):
                held_rows[f, at, :] = held_rows[f, at, :] + sign * values[f]
        leave.start()
    for _, _, leave in steps:
        leave.wait()


def near_kernel(
    dtheta,
    total_rows,
    part_first,
    counts,
    state,
    after,
    low,
    high,
    inner,
    outer,
    edge,
    factor,
    table,
    solve,
    token,
    hbm,
    rhs,
    local,
    carry,
    *rest,
):
    flags = place_flags(counts, total_rows)
    cells = state.shape[-1]
    odd = flags[ODD]
    part = rest[0] if len(rest) > 2 else None
    scratch = rest[-2:] if part is None else rest[-3:-1]
    if part is not None:
        source = hbm.at[:, lax.axis_index("ax") % 2, part_first : part_first + part.shape[1], :]
        copy = pltpu.make_async_copy(source, part, rest[-1])
        copy.start()

    sub = lax.broadcasted_iota(jnp.int32, (EIGHT, LANES), 0)

    def next_rows(f, q, at):
        k = f * PLANES + q
        under = high[k : k + 1, at] if total_rows == R_NEAR else after[f, plane_of(odd, q), :, at]
        return jnp.where(sub >= EIGHT // 2, low[k : k + 1, at], under)

    stencil(
        flags,
        0,
        R_NEAR,
        total_rows,
        dtheta,
        lambda f, q, r, at: state[f, plane_of(odd, q), pl.ds(r, EIGHT), at],
        next_rows,
        lambda r: edge[pl.ds(r, EIGHT), :],
        lambda f, r, at: inner[f, pl.ds(r, EIGHT), at],
        lambda f, r, at: outer[f, pl.ds(r, EIGHT), at],
        lambda f, q, r: rhs.at[f * PLANES + q, pl.ds(r, EIGHT), :],
        *scratch,
    )

    pieces = cells // LANES
    lane = lax.broadcasted_iota(jnp.int32, (R_NEAR, LANES), 1)
    width = factor[...]
    log_ratio = table[:, COL_LOG : COL_LOG + 1]
    block = jnp.floor((lane.astype(jnp.float32) + 0.5) / width)
    ahead_entry = jnp.exp(log_ratio * (block + 1.0))
    behind_entry = jnp.exp(log_ratio * (LANES / width - block))
    across = jnp.exp(log_ratio * (LANES / width))

    def line(k, ends):
        rows = jnp.concatenate([rhs[k, :, b * LANES : (b + 1) * LANES] for b in range(pieces)], axis=0)
        high = rows.astype(jnp.bfloat16)
        low = (rows - high.astype(jnp.float32)).astype(jnp.bfloat16)
        solved = jnp.dot(
            jnp.concatenate([high, low, high], axis=1), solve[...], preferred_element_type=jnp.float32
        )
        inside = []
        for b in range(pieces):
            mine = solved[b * R_NEAR : (b + 1) * R_NEAR]
            value = mine[:, :LANES]
            for level in range(1, FMAX.bit_length()):
                chosen = mine[:, level * LANES : (level + 1) * LANES]
                value = jnp.where(width == (1 << level), chosen, value)
            inside.append(value)
        total = list(inside)
        enter = jnp.zeros((R_NEAR, LANES), jnp.float32)
        for b in range(pieces):
            leave = jnp.broadcast_to(inside[b][:, LANES - 1 : LANES], (R_NEAR, LANES))
            total[b] = total[b] + ahead_entry * enter
            enter = leave + across * enter
        ends = jnp.where(lane == k, enter, ends)
        enter = jnp.zeros((R_NEAR, LANES), jnp.float32)
        for b in reversed(range(pieces)):
            leave = jnp.broadcast_to(inside[b][:, 0:1], (R_NEAR, LANES))
            total[b] = total[b] + behind_entry * enter
            enter = leave + across * enter
        for b in range(pieces):
            local[k, :, b * LANES : (b + 1) * LANES] = total[b]
        return jnp.where(lane == k + LINES, enter, ends)

    carry[...] = lax.fori_loop(
        0, LINES, line, jnp.zeros((R_NEAR, LANES), jnp.float32)
    )
    if part is not None:
        copy.wait()


def close_circle(flags, factor, rhs, local, carry, table, out):
    cells = out.shape[-1]
    lane = lax.broadcasted_iota(jnp.int32, (R_NEAR, cells), 1).astype(jnp.float32)
    width = factor[:, 0:1]
    block = jnp.floor((lane + 0.5) / width)
    count = cells / width
    log_ratio = table[:, COL_LOG : COL_LOG + 1]
    gain = jnp.broadcast_to(table[:, COL_GAIN : COL_GAIN + 1], (R_NEAR, cells))
    from_left = jnp.exp(log_ratio * (block + 1.0))
    from_right = jnp.exp(log_ratio * (count - block))
    near = flags[FIRST] == 1
    for f in range(FIELDS):
        for q in range(PLANES):
            k = f * PLANES + q
            j = k + LINES
            smooth = gain * (
                local[k] + from_left * carry[:, k : k + 1] + from_right * carry[:, j : j + 1]
            )
            out[f, plane_of(flags[ODD], q)] = jnp.where(near, smooth, rhs[k])


def stream(pieces, sems):
    steps = []
    for source, stage, target in pieces:
        for f in range(FIELDS):
            k = 2 * len(steps)
            come = pltpu.make_async_copy(source.at[f], stage.at[f], sems.at[k])
            leave = pltpu.make_async_copy(stage.at[f], target.at[f], sems.at[k + 1])
            steps.append((come, leave))
    for come, _ in steps:
        come.start()

    def forward():
        for come, leave in steps:
            come.wait()
            leave.start()

    def finish():
        for _, leave in steps:
            leave.wait()

    return forward, finish


def pack_first_kernel(count, state, part, low, high, stage, top, bottom, row_sems, sems):
    _, _, rows, _ = state.shape
    odd = lax.axis_index("ax") % 2
    pieces = []
    for a, b in ((0, count // 16 * EIGHT), (count // 16 * EIGHT, count)):
        pieces.append((state.at[:, odd, a:b, :], stage.at[:, a:b, :], part.at[:, a:b, :]))
    forward, finish = stream(pieces, sems)
    copies = [
        pltpu.make_async_copy(state.at[:, :, rows - EIGHT : rows, :], top, row_sems.at[0]),
        pltpu.make_async_copy(state.at[:, :, 0:EIGHT, :], bottom, row_sems.at[1]),
    ]
    for copy in copies:
        copy.start()
    forward()
    for copy in copies:
        copy.wait()
    for f in range(FIELDS):
        for q in range(PLANES):
            k = f * PLANES + q
            p = plane_of(odd, q)
            low[k : k + 1, :] = top[f, p, EIGHT - 1 : EIGHT, :]
            high[k : k + 1, :] = bottom[f, p, 0:1, :]
    finish()


def pack_edges_kernel(state, token, edge, side, left, right, sems):
    _, _, rows, cells = state.shape
    odd = lax.axis_index("ax") % 2
    copies = [
        pltpu.make_async_copy(state.at[:, :, :, cells - LANES : cells], left, sems.at[0]),
        pltpu.make_async_copy(state.at[:, :, :, 0:LANES], right, sems.at[1]),
        pltpu.make_async_copy(state.at[:, 1 - odd, 0:R_NEAR, :], side, sems.at[2]),
    ]
    for copy in copies:
        copy.start()
    for copy in copies[:2]:
        copy.wait()
    lane = lax.broadcasted_iota(jnp.int32, (rows, LANES), 1)
    columns = jnp.ones((rows, LANES), jnp.float32)
    for f in range(FIELDS):
        for q in range(PLANES):
            p = plane_of(odd, q)
            columns = jnp.where(lane == 4 * f + q, left[f, p, :, LANES - 1 : LANES], columns)
            columns = jnp.where(lane == (4 * f - 1 - q) % LANES, right[f, p, :, 0:1], columns)
    edge[...] = columns
    copies[2].wait()


def pack_rest_kernel(parts, tokens, state, *rest):
    rest = rest[tokens:]
    odd = lax.axis_index("ax") % 2
    count = len(parts)
    pieces = []
    for k, (q, first, last) in enumerate(parts):
        pieces.append((state.at[:, plane_of(odd, q), first:last, :], rest[count + k], rest[k]))
    for step in stream(pieces, rest[-1]):
        step()


ANY = pl.BlockSpec(memory_space=pl.ANY)
PARAMS = pltpu.CompilerParams(vmem_limit_bytes=VMEM_LIMIT)


def whole(*shape):
    return pl.BlockSpec(shape, lambda i: (0,) * len(shape))


def rows_from(shape, axis, first, step):
    def place(i):
        row = (first // EIGHT + i * (step // EIGHT)) * EIGHT
        return tuple(row if d == axis else 0 for d in range(len(shape)))

    return pl.BlockSpec(tuple(pl.Element(n) for n in shape), place)


def in_hbm(value):
    return pltpu.with_memory_space_constraint(value, pltpu.HBM)


def cost(flops, nbytes):
    return pl.CostEstimate(flops=flops, bytes_accessed=nbytes, transcendentals=0)


def pack_first(state, count):
    fields, planes, _, cells = state.shape
    vmem = pl.BlockSpec(memory_space=pltpu.VMEM)
    row = jax.ShapeDtypeStruct((LINES, cells), jnp.float32)
    rows = pltpu.VMEM((fields, planes, EIGHT, cells), jnp.float32)
    return pl.pallas_call(
        functools.partial(pack_first_kernel, count),
        in_specs=[ANY],
        out_specs=[ANY, vmem, vmem],
        out_shape=[jax.ShapeDtypeStruct((fields, count, cells), jnp.float32), row, row],
        scratch_shapes=[
            pltpu.VMEM((fields, count, cells), jnp.float32),
            rows,
            rows,
            pltpu.SemaphoreType.DMA((2,)),
            pltpu.SemaphoreType.DMA((4 * fields,)),
        ],
        compiler_params=PARAMS,
        cost_estimate=cost(0, fields * count * cells * 8),
        name="pack_first",
    )(in_hbm(state))


def pack_edges(state, token):
    fields, planes, rows, cells = state.shape
    vmem = pl.BlockSpec(memory_space=pltpu.VMEM)
    tiles = pltpu.VMEM((fields, planes, rows, LANES), jnp.float32)
    return pl.pallas_call(
        pack_edges_kernel,
        in_specs=[ANY, ANY],
        out_specs=[vmem, vmem],
        out_shape=[
            jax.ShapeDtypeStruct((rows, LANES), jnp.float32),
            jax.ShapeDtypeStruct((fields, R_NEAR, cells), jnp.float32),
        ],
        scratch_shapes=[tiles, tiles, pltpu.SemaphoreType.DMA((3,))],
        compiler_params=PARAMS,
        cost_estimate=cost(0, fields * planes * rows * LANES * 16),
        name="pack_edges",
    )(in_hbm(state), token)


def pack_rest(state, parts, *tokens):
    fields, _, _, cells = state.shape
    shapes = [jax.ShapeDtypeStruct((fields, last - first, cells), jnp.float32) for _, first, last in parts]
    return pl.pallas_call(
        functools.partial(pack_rest_kernel, parts, len(tokens)),
        in_specs=[ANY] * (1 + len(tokens)),
        out_specs=[ANY] * len(shapes),
        out_shape=shapes,
        scratch_shapes=[
            *[pltpu.VMEM(x.shape, jnp.float32) for x in shapes],
            pltpu.SemaphoreType.DMA((2 * fields * len(parts),)),
        ],
        compiler_params=PARAMS,
        cost_estimate=cost(0, sum(math.prod(x.shape) for x in shapes) * 8),
        name="pack_rest",
    )(in_hbm(state), *tokens)


def flux_scratch(rows, cells):
    shape = (PLANES, FIELDS, cells // LANES)
    return [pltpu.VMEM((*shape, n, LANES), jnp.float32) for n in (rows + 2 * EIGHT, rows)]


def bulk(counts, state, low, high, inner, edge, dtheta, outer, span, token, held, near_parts=()):
    fields, planes, total_rows, cells = state.shape
    first, end = span
    count = end - first
    rows = 32 if count % 32 == 0 else 24 if count % 24 == 0 else 16
    blocks = count // rows
    size = fields * planes * count * cells
    aliases = {} if held is None else {7: 0}
    state = in_hbm(state)
    operands = [state, low, high, inner, edge, inner if outer is None else outer, token]
    operands += [state if held is None else held, *near_parts]
    chunk = pltpu.VMEM((fields, count, cells), jnp.float32)
    near_scratch = [pltpu.VMEM((fields, planes, R_NEAR, cells), jnp.float32), pltpu.SemaphoreType.DMA]
    return pl.pallas_call(
        functools.partial(bulk_kernel, dtheta, rows, span, total_rows, outer is not None, len(near_parts), counts),
        grid_spec=pltpu.PrefetchScalarGridSpec(
            num_scalar_prefetch=0,
            grid=(blocks,),
            in_specs=[
                ANY,
                whole(LINES, cells),
                whole(LINES, cells),
                ANY,
                rows_from((rows, LANES), 0, first, rows),
                ANY,
                ANY,
                ANY,
                *[whole(*x.shape) for x in near_parts],
            ],
            out_specs=rows_from((fields, planes, rows, cells), 2, first, rows),
            scratch_shapes=[
                pltpu.VMEM((fields, planes, count + 2 * EIGHT, cells), jnp.float32),
                chunk,
                pltpu.SemaphoreType.DMA((3 * blocks,)),
                *flux_scratch(rows, cells),
                *([] if outer is None else [chunk]),
                *(near_scratch if near_parts else []),
            ],
        ),
        out_shape=pltpu.HBM(state.shape, jnp.float32),
        input_output_aliases=aliases,
        compiler_params=PARAMS,
        cost_estimate=cost(size * 60, size * 10),
        name="bulk",
    )(*operands)


def add_outer(counts, outer, span, rows, held):
    fields, count, cells = outer.shape
    chunk = pltpu.VMEM((fields, count, cells), jnp.float32)
    return pl.pallas_call(
        functools.partial(outer_kernel, rows, span, counts),
        grid_spec=pltpu.PrefetchScalarGridSpec(
            num_scalar_prefetch=0,
            grid=(1,),
            in_specs=[ANY, ANY],
            out_specs=ANY,
            scratch_shapes=[chunk, chunk, pltpu.SemaphoreType.DMA((3 * (count // rows),))],
        ),
        out_shape=pltpu.HBM(held.shape, jnp.float32),
        input_output_aliases={1: 0},
        compiler_params=PARAMS,
        cost_estimate=cost(outer.size * 6, outer.size * 16),
        name="add_outer",
    )(outer, held)


def near(counts, state, low, high, inner, edge, dtheta, outer, factor, table, solve, token, part=None):
    fields, planes, rows, cells = state.shape
    out = jax.ShapeDtypeStruct((LINES, R_NEAR, cells), jnp.float32)
    tail = min(R_NEAR // EIGHT, rows // EIGHT - 1)
    state = in_hbm(state)
    out_specs = [whole(LINES, R_NEAR, cells), whole(LINES, R_NEAR, cells), whole(R_NEAR, LANES)]
    out_shape = [out, out, jax.ShapeDtypeStruct((R_NEAR, LANES), jnp.float32)]
    scratch = flux_scratch(R_NEAR, cells)
    if part is not None:
        out_specs.append(whole(fields, part[1] - part[0], cells))
        out_shape.append(jax.ShapeDtypeStruct((fields, part[1] - part[0], cells), jnp.float32))
        scratch.append(pltpu.SemaphoreType.DMA)
    result = pl.pallas_call(
        functools.partial(near_kernel, dtheta, rows, part[0] if part else 0, counts),
        grid_spec=pltpu.PrefetchScalarGridSpec(
            num_scalar_prefetch=0,
            grid=(1,),
            in_specs=[
                whole(fields, planes, R_NEAR, cells),
                pl.BlockSpec((fields, planes, EIGHT, cells), lambda i: (0, 0, tail, 0)),
                whole(LINES, cells),
                whole(LINES, cells),
                whole(fields, R_NEAR, cells),
                whole(fields, R_NEAR, cells),
                whole(R_NEAR, LANES),
                whole(R_NEAR, LANES),
                whole(R_NEAR, LANES),
                whole(*solve.shape),
                ANY,
                ANY,
            ],
            out_specs=out_specs,
            scratch_shapes=scratch,
        ),
        out_shape=out_shape,
        compiler_params=PARAMS,
        cost_estimate=cost(LINES * R_NEAR * cells * 200, LINES * R_NEAR * cells * 250),
        name="near",
    )(state, state, low, high, inner, outer, edge, factor, table, solve, in_hbm(token), state)
    return result if part is not None else (*result, None)


def chunks(rows):
    size = 16
    blocks = (rows - R_NEAR) // size
    cuts = sorted({-(-2 * blocks // 5), -(-4 * blocks // 5), blocks})
    ends = [R_NEAR + size * c for c in cuts]
    return size, list(zip([0] + ends[:-1], ends))


def smoothing_table(coarsen, cells, total_cells, dtheta):
    factor = coarsen.astype(jnp.float32)[:, None]
    stiffness = KAPPA / (factor * dtheta) ** 2
    inverse_half = 0.5 / stiffness
    one_minus = jnp.sqrt(inverse_half * (2.0 + inverse_half)) - inverse_half
    log_ratio = jnp.log1p(-one_minus)
    gain = (1.0 - one_minus) / (stiffness * one_minus * (2.0 - one_minus))
    closing = 1.0 / -jnp.expm1((total_cells / factor) * log_ratio)
    across = jnp.exp((cells / factor) * log_ratio)
    column = jnp.arange(LANES, dtype=jnp.int32)[None, :]
    width = jnp.left_shift(1, jnp.minimum(column, 20)).astype(jnp.float32)
    table = jnp.where(width >= factor, jnp.exp(log_ratio * (width / factor)), 0.0)
    table = jnp.where(column == COL_LOG, log_ratio, table)
    table = jnp.where(column == COL_GAIN, gain, table)
    return table, closing, across


def piece_tables(dtheta):
    tables = []
    for level in range(FMAX.bit_length()):
        width = 1 << level
        half = 0.5 * (width * dtheta) ** 2 / KAPPA
        ratio = 1.0 - (math.sqrt(half * (2.0 + half)) - half)
        block = np.arange(LANES) // width
        tables.append(ratio ** np.abs(block[:, None] - block[None, :]) / width)
    table = np.concatenate(tables, axis=1)
    high = table.astype(ml_dtypes.bfloat16)
    low = (table - high.astype(np.float64)).astype(ml_dtypes.bfloat16)
    return jnp.asarray(np.concatenate([high, high, low], axis=0))


def ring(value, axis, shift):
    size = lax.axis_size(axis)
    return lax.ppermute(value, axis, [(i, (i + shift) % size) for i in range(size)])


def body(state, coarsen):
    fields, planes, rows, cells = state.shape
    sec_count = lax.axis_size("sec")
    rad_count = lax.axis_size("rad")
    ax_count = lax.axis_size("ax")
    assert fields == FIELDS and planes == PLANES and ax_count % 2 == 0
    total_cells = cells * sec_count
    dtheta = 2.0 * math.pi / total_cells
    outer_pairs = []
    for i in range(1, ax_count - 1, 2):
        outer_pairs += [(i, i + 1), (i + 1, i)]
    inner_pairs = []
    for i in range(0, ax_count, 2):
        inner_pairs += [(i, i + 1), (i + 1, i)]
    up = [(i, i + 1) for i in range(rad_count - 1)]
    down = [(i + 1, i) for i in range(rad_count - 1)]
    counts = (ax_count, rad_count)
    size, spans = chunks(rows)
    count = len(spans)

    part, low, high = pack_first(state, spans[0][1])
    outer = [lax.ppermute(part, "ax", outer_pairs)]
    columns, side = pack_edges(state, high)
    low = lax.ppermute(low, "rad", up)
    high = lax.ppermute(high, "rad", down)
    near_inner = lax.ppermute(side, "ax", inner_pairs)
    if sec_count == 2:
        edge = ring(columns, "sec", 1)
    else:
        from_left = jnp.arange(LANES)[None, :] % 4 < 2
        edge = jnp.where(from_left, ring(columns, "sec", 1), ring(columns, "sec", -1))
    early = [(0, *span) for span in spans[2:]] + [(1, *span) for span in spans[1:2]]
    late = [(0, R_NEAR, spans[0][1])] + [(0, *span) for span in spans[1:2]]
    parts = pack_rest(state, early, columns, low, high) if early else []
    order = in_hbm(parts[0]) if early else columns
    parts = list(parts) + list(pack_rest(state, late, order, edge))
    inner = {}
    for (q, first, last), value in zip(early + late, parts):
        if q:
            outer.append(lax.ppermute(value, "ax", outer_pairs))
        else:
            inner[first, last] = lax.ppermute(value, "ax", inner_pairs)
    order = in_hbm(parts[-1])

    table, closing, across = smoothing_table(coarsen, cells, total_cells, dtheta)
    factor = jnp.broadcast_to(coarsen.astype(jnp.float32)[:, None], (R_NEAR, LANES))

    solve = piece_tables(dtheta)
    given = (counts, state, low, high)

    def pass_over(k, token, held, fused=True, near_parts=()):
        span = (spans[k][0] if k else R_NEAR, spans[k][1])
        far = outer[k] if fused else None
        return bulk(*given, inner[span], edge, dtheta, far, span, token, held, near_parts)

    out = pass_over(2, order, None, fused=False) if count > 2 else None
    part = spans[2] if count > 2 else None
    token = order if out is None else out
    rhs, local, ends, part = near(
        *given, near_inner, edge, dtheta, outer[0], factor, table, solve, token, part
    )
    if part is not None:
        outer.append(lax.ppermute(part, "ax", outer_pairs))
    arrived = [ends] + [ring(ends, "sec", k) for k in range(1, sec_count)] + [ends]
    from_left = jnp.arange(LANES)[None, :] < LINES
    carry = jnp.zeros_like(ends)
    for k in range(sec_count, 0, -1):
        carry = carry * across + jnp.where(from_left, arrived[k], arrived[sec_count - k])
    carry = carry * closing
    passes = min(count, 2)
    for k in range(passes):
        near_parts = (factor, rhs, local, carry, table) if k == passes - 1 else ()
        out = pass_over(k, ends, out, near_parts=near_parts)
    return add_outer(counts, outer[2], spans[2], size, out) if count > 2 else out


def solution(mesh):
    return jax.shard_map(
        body,
        mesh=mesh,
        in_specs=(P(None, "ax", "rad", "sec"), P()),
        out_specs=P(None, "ax", "rad", "sec"),
        check_vma=False,
    )
```

```python
import functools
import math

import jax
import jax.numpy as jnp
import ml_dtypes
import numpy as np
from jax import lax
from jax.experimental import pallas as pl
from jax.experimental.pallas import tpu as pltpu
from jax.sharding import PartitionSpec as P

R_NEAR = 16
FMAX = 16

GAMMA = 1.4
KAPPA = 1.44

FIELDS = 5
PLANES = 2
LINES = FIELDS * PLANES
GROUPS = (slice(0, 3), slice(3, FIELDS))
EIGHT = 8
LANES = 128
VMEM_LIMIT = 28 * 1024 * 1024

COL_LOG = 32
COL_GAIN = 33

ODD, OUTER, FIRST, LAST, BASE = range(5)


def place_flags(counts, rows):
    ax_count, rad_count = counts
    ax = lax.axis_index("ax")
    rad = lax.axis_index("rad")
    beside = (ax > 0) & (ax < ax_count - 1)
    flags = [ax % 2, beside, rad == 0, rad == rad_count - 1, rad * rows]
    return [x.astype(jnp.int32) for x in flags]


def plane_of(odd, q):
    return odd if q else 1 - odd


def reciprocal(x):
    y = pl.reciprocal(x, approx=True)
    y = y * (2.0 - x * y)
    return y * (2.0 - x * y)


def fluxes(fields, want):
    density, energy = fields[0], fields[4]
    momentum = fields[1:4]
    inverse = reciprocal(density)
    velocity = [m * inverse for m in momentum]
    square = {}
    for i in range(3):
        for j in range(i, 3):
            if i == j or i + 1 in want or j + 1 in want or (i, j) == (1, 2):
                square[i, j] = square[j, i] = momentum[i] * velocity[j]
    pressure = (GAMMA - 1.0) * (energy - 0.5 * (square[0, 0] + square[1, 1] + square[2, 2]))
    enthalpy = energy + pressure
    out = {}
    for d in want:
        k = d - 1
        flow = [square[i, k] + pressure if i == k else square[i, k] for i in range(3)]
        out[d] = [momentum[k]] + flow + [enthalpy * velocity[k]]
    return out, (pressure, square[2, 2], square[1, 2])


def flux_along(fields, along):
    return fluxes(fields, (along,))[0][along]


def outer_flux(flags, outer):
    present = flags[OUTER] == 1
    outer = [jnp.where(present, outer[0], 1.0)] + [jnp.where(present, g, 0.0) for g in outer[1:]]
    return flux_along(outer, 1)


def stencil(
    flags, first_row, rows, total_rows, dtheta, load, next_rows, edge, inner, outer, place, radial, azimuthal
):
    strips = rows // EIGHT
    pieces = radial.shape[2]
    row = lax.broadcasted_iota(jnp.int32, (EIGHT, LANES), 0)
    lane = lax.broadcasted_iota(jnp.int32, (EIGHT, LANES), 1)
    start = flags[BASE] + first_row
    axial_sign = jnp.where(flags[ODD] == 1, 0.5, -0.5)
    above = jnp.where((flags[FIRST] == 1) & (first_row == 0), 0.0, (start - 1).astype(jnp.float32) + 0.5)
    end = first_row + rows == total_rows
    below = jnp.where((flags[LAST] == 1) & end, 0.0, (start + rows).astype(jnp.float32) + 0.5)
    scale = jnp.where(row >= EIGHT // 2, above, below)
    at = [slice(b * LANES, (b + 1) * LANES) for b in range(pieces)]

    for q in range(PLANES):
        for b in range(pieces):
            values = [next_rows(f, q, at[b]) for f in range(FIELDS)]
            values[0] = jnp.where(scale > 0.0, values[0], 1.0)
            flux_next = flux_along(values, 2)
            for f in range(FIELDS):
                radial[q, f, b, 0:EIGHT, :] = flux_next[f] * scale
                radial[q, f, b, EIGHT + rows : 2 * EIGHT + rows, :] = flux_next[f] * scale

    def inside(t, carry):
        r = pl.multiple_of(EIGHT * t, EIGHT)
        radius = (start + r + row).astype(jnp.float32) + 0.5
        inv_radius = 1.0 / radius
        for b in range(pieces):
            beside = flux_along([inner(f, r, at[b]) for f in range(FIELDS)], 1)
            axial, source = [], []
            for q in range(PLANES):
                fields = [load(f, q, r, at[b]) for f in range(FIELDS)]
                flow, (pressure, twist, swirl) = fluxes(fields, (1, 2, 3))
                axial.append(flow[1])
                for f in range(FIELDS):
                    radial[q, f, b, pl.ds(r + EIGHT, EIGHT), :] = flow[2][f] * radius
                    azimuthal[q, f, b, pl.ds(r, EIGHT), :] = flow[3][f]
                source.append(((pressure + twist) * inv_radius, swirl * -inv_radius))
            base = [[axial_sign * (x - y) for x, y in zip(beside, axial[1])]]
            if outer is None:
                base.append([axial_sign * x for x in axial[0]])
            else:
                far = outer_flux(flags, [outer(f, r, at[b]) for f in range(FIELDS)])
                base.append([axial_sign * (x - y) for x, y in zip(axial[0], far)])
            for q in range(PLANES):
                base[q][2] = base[q][2] + source[q][0]
                base[q][3] = base[q][3] + source[q][1]
                for f in range(FIELDS):
                    place(f, q, r)[:, at[b]] = base[q][f]
        return carry

    lax.fori_loop(0, strips, inside, 0)

    def differences(t, carry):
        r = pl.multiple_of(EIGHT * t, EIGHT)
        radius = (start + r + row).astype(jnp.float32) + 0.5
        half_inv = 0.5 / radius
        half_arc = half_inv * (1.0 / dtheta)
        beyond = [edge(r)] + [pltpu.roll(edge(r), LANES - 4 * f, 1) for f in range(1, FIELDS)]
        beyond = flux_along(beyond, 3)
        for q in range(PLANES):
            for f in range(FIELDS):
                ends = [pltpu.roll(beyond[f], s, 1) if q else beyond[f] for s in (LANES - 1, 1)]
                here = [azimuthal[q, f, b, pl.ds(r, EIGHT), :] for b in range(pieces)]
                left = [ends[0]] + [pltpu.roll(x, 1, 1) for x in here]
                right = [pltpu.roll(x, LANES - 1, 1) for x in here] + [ends[1]]
                out = place(f, q, r)
                for b in range(pieces):
                    behind = jnp.where(lane == 0, left[b], left[b + 1])
                    ahead = jnp.where(lane == LANES - 1, right[b + 1], right[b])
                    up = radial[q, f, b, pl.ds(r + EIGHT - 1, EIGHT), :]
                    down = radial[q, f, b, pl.ds(r + EIGHT + 1, EIGHT), :]
                    change = (behind - ahead) * half_arc + (up - down) * half_inv
                    out[:, at[b]] = out[:, at[b]] + change
        return carry

    lax.fori_loop(0, strips, differences, 0)


def bulk_kernel(
    dtheta, rows, span, total_rows, fused, near, counts, state, low, high, inner, edge, outer, token, held, *rest
):
    flags = place_flags(counts, total_rows)
    near_parts, out, scratch = rest[:near], rest[near], rest[near + 1 :]
    first, end = span
    blocks = (end - first) // rows
    state_rows, inner_rows, sems, radial, azimuthal, *outer_rows = scratch
    *outer_rows, near_rows, near_sem = [*outer_rows, None, None] if not near else outer_rows
    outer_rows = outer_rows[0] if fused else None
    odd = flags[ODD]
    step = pl.program_id(0)

    def copies(k):
        a = first + k * rows + (EIGHT if k else -EIGHT)
        b = min(first + (k + 1) * rows + EIGHT, total_rows)
        at = a - first + EIGHT
        rest = pl.ds(outer.shape[1] - (end - first) + k * rows, rows)
        here = pl.ds(k * rows, rows)
        sets = [
            (state.at[:, :, a:b, :], state_rows.at[:, :, at : at + b - a, :]),
            (inner.at[:, here, :], inner_rows.at[:, here, :]),
        ]
        if fused:
            sets.append((outer.at[:, rest, :], outer_rows.at[:, here, :]))
        return [pltpu.make_async_copy(x, y, sems.at[3 * k + i]) for i, (x, y) in enumerate(sets)]

    @pl.when(step == 0)
    def _():
        for k in range(blocks):
            for copy in copies(k):
                copy.start()
        if near:
            close_circle(flags, *near_parts, near_rows)
            pltpu.make_async_copy(near_rows, held.at[:, :, 0:R_NEAR, :], near_sem).start()

    for k in range(blocks):

        @pl.when(step == k)
        def _():
            for copy in copies(k):
                copy.wait()

    first_row = first + step * rows
    at_end = first_row + rows == total_rows
    base = pl.multiple_of(step * rows, EIGHT)
    sub = lax.broadcasted_iota(jnp.int32, (EIGHT, LANES), 0)

    def load(f, q, r, at):
        return state_rows[f, plane_of(odd, q), pl.ds(base + EIGHT + r, EIGHT), at]

    def next_rows(f, q, at):
        k = f * PLANES + q
        under = jnp.where(at_end, high[k : k + 1, at], load(f, q, rows, at))
        return jnp.where(sub >= EIGHT // 2, load(f, q, -EIGHT, at), under)

    stencil(
        flags,
        first_row,
        rows,
        total_rows,
        dtheta,
        load,
        next_rows,
        lambda r: edge[pl.ds(r, EIGHT), :],
        lambda f, r, at: inner_rows[f, pl.ds(base + r, EIGHT), at],
        (lambda f, r, at: outer_rows[f, pl.ds(base + r, EIGHT), at]) if fused else None,
        lambda f, q, r: out.at[f, plane_of(odd, q), pl.ds(r, EIGHT), :],
        radial,
        azimuthal,
    )
    if near:

        @pl.when(step == blocks - 1)
        def _():
            pltpu.make_async_copy(near_rows, held.at[:, :, 0:R_NEAR, :], near_sem).wait()


def outer_kernel(rows, span, counts, outer, held, out, outer_rows, held_rows, sems):
    flags = place_flags(counts, 0)
    first, end = span
    plane = lax.axis_index("ax") % 2
    sign = jnp.where(flags[ODD] == 1, -0.5, 0.5)
    steps = []
    for k in range((end - first) // rows):
        here = pl.ds(k * rows, rows)
        there = pl.ds(first + k * rows, rows)
        ways = [
            (outer.at[:, here, :], outer_rows.at[:, here, :]),
            (held.at[:, plane, there, :], held_rows.at[:, here, :]),
            (held_rows.at[:, here, :], out.at[:, plane, there, :]),
        ]
        steps.append([pltpu.make_async_copy(x, y, sems.at[3 * k + i]) for i, (x, y) in enumerate(ways)])
        steps[-1][0].start()
        steps[-1][1].start()
    for k, (come, have, leave) in enumerate(steps):
        come.wait()
        have.wait()
        for t in range(rows // EIGHT):
            at = pl.ds(k * rows + EIGHT * t, EIGHT)
            values = outer_flux(flags, [outer_rows[f, at, :] for f in range(FIELDS)])
            for f in range(FIELDS):
                held_rows[f, at, :] = held_rows[f, at, :] + sign * values[f]
        leave.start()
    for _, _, leave in steps:
        leave.wait()


def near_kernel(
    dtheta,
    total_rows,
    part_first,
    counts,
    state,
    after,
    low,
    high,
    inner,
    outer,
    edge,
    factor,
    table,
    solve,
    token,
    hbm,
    rhs,
    local,
    carry,
    *rest,
):
    flags = place_flags(counts, total_rows)
    cells = state.shape[-1]
    odd = flags[ODD]
    part = rest[0] if len(rest) > 2 else None
    scratch = rest[-2:] if part is None else rest[-3:-1]
    if part is not None:
        source = hbm.at[:, lax.axis_index("ax") % 2, part_first : part_first + part.shape[1], :]
        copy = pltpu.make_async_copy(source, part, rest[-1])
        copy.start()

    sub = lax.broadcasted_iota(jnp.int32, (EIGHT, LANES), 0)

    def next_rows(f, q, at):
        k = f * PLANES + q
        under = high[k : k + 1, at] if total_rows == R_NEAR else after[f, plane_of(odd, q), :, at]
        return jnp.where(sub >= EIGHT // 2, low[k : k + 1, at], under)

    stencil(
        flags,
        0,
        R_NEAR,
        total_rows,
        dtheta,
        lambda f, q, r, at: state[f, plane_of(odd, q), pl.ds(r, EIGHT), at],
        next_rows,
        lambda r: edge[pl.ds(r, EIGHT), :],
        lambda f, r, at: inner[f, pl.ds(r, EIGHT), at],
        lambda f, r, at: outer[f, pl.ds(r, EIGHT), at],
        lambda f, q, r: rhs.at[f * PLANES + q, pl.ds(r, EIGHT), :],
        *scratch,
    )

    pieces = cells // LANES
    lane = lax.broadcasted_iota(jnp.int32, (R_NEAR, LANES), 1)
    width = factor[...]
    log_ratio = table[:, COL_LOG : COL_LOG + 1]
    block = jnp.floor((lane.astype(jnp.float32) + 0.5) / width)
    ahead_entry = jnp.exp(log_ratio * (block + 1.0))
    behind_entry = jnp.exp(log_ratio * (LANES / width - block))
    across = jnp.exp(log_ratio * (LANES / width))

    def line(k, ends):
        rows = jnp.concatenate([rhs[k, :, b * LANES : (b + 1) * LANES] for b in range(pieces)], axis=0)
        high = rows.astype(jnp.bfloat16)
        low = (rows - high.astype(jnp.float32)).astype(jnp.bfloat16)
        solved = jnp.dot(
            jnp.concatenate([high, low, high], axis=1), solve[...], preferred_element_type=jnp.float32
        )
        inside = []
        for b in range(pieces):
            mine = solved[b * R_NEAR : (b + 1) * R_NEAR]
            value = mine[:, :LANES]
            for level in range(1, FMAX.bit_length()):
                chosen = mine[:, level * LANES : (level + 1) * LANES]
                value = jnp.where(width == (1 << level), chosen, value)
            inside.append(value)
        total = list(inside)
        enter = jnp.zeros((R_NEAR, LANES), jnp.float32)
        for b in range(pieces):
            leave = jnp.broadcast_to(inside[b][:, LANES - 1 : LANES], (R_NEAR, LANES))
            total[b] = total[b] + ahead_entry * enter
            enter = leave + across * enter
        ends = jnp.where(lane == k, enter, ends)
        enter = jnp.zeros((R_NEAR, LANES), jnp.float32)
        for b in reversed(range(pieces)):
            leave = jnp.broadcast_to(inside[b][:, 0:1], (R_NEAR, LANES))
            total[b] = total[b] + behind_entry * enter
            enter = leave + across * enter
        for b in range(pieces):
            local[k, :, b * LANES : (b + 1) * LANES] = total[b]
        return jnp.where(lane == k + LINES, enter, ends)

    carry[...] = lax.fori_loop(
        0, LINES, line, jnp.zeros((R_NEAR, LANES), jnp.float32)
    )
    if part is not None:
        copy.wait()


def close_circle(flags, factor, rhs, local, carry, table, out):
    cells = out.shape[-1]
    lane = lax.broadcasted_iota(jnp.int32, (R_NEAR, cells), 1).astype(jnp.float32)
    width = factor[:, 0:1]
    block = jnp.floor((lane + 0.5) / width)
    count = cells / width
    log_ratio = table[:, COL_LOG : COL_LOG + 1]
    gain = jnp.broadcast_to(table[:, COL_GAIN : COL_GAIN + 1], (R_NEAR, cells))
    from_left = jnp.exp(log_ratio * (block + 1.0))
    from_right = jnp.exp(log_ratio * (count - block))
    near = flags[FIRST] == 1
    for f in range(FIELDS):
        for q in range(PLANES):
            k = f * PLANES + q
            j = k + LINES
            smooth = gain * (
                local[k] + from_left * carry[:, k : k + 1] + from_right * carry[:, j : j + 1]
            )
            out[f, plane_of(flags[ODD], q)] = jnp.where(near, smooth, rhs[k])


def stream(pieces, sems):
    steps = []
    for source, stage, target in pieces:
        for f in GROUPS:
            k = 2 * len(steps)
            come = pltpu.make_async_copy(source.at[f], stage.at[f], sems.at[k])
            leave = pltpu.make_async_copy(stage.at[f], target.at[f], sems.at[k + 1])
            steps.append((come, leave))
    for come, _ in steps:
        come.start()

    def forward():
        for come, leave in steps:
            come.wait()
            leave.start()

    def finish():
        for _, leave in steps:
            leave.wait()

    return forward, finish


def pack_first_kernel(count, state, part, low, high, stage, top, bottom, row_sems, sems):
    _, _, rows, _ = state.shape
    odd = lax.axis_index("ax") % 2
    forward, finish = stream([(state.at[:, odd, 0:count, :], stage, part)], sems)
    copies = [
        pltpu.make_async_copy(state.at[:, :, rows - EIGHT : rows, :], top, row_sems.at[0]),
        pltpu.make_async_copy(state.at[:, :, 0:EIGHT, :], bottom, row_sems.at[1]),
    ]
    for copy in copies:
        copy.start()
    forward()
    for copy in copies:
        copy.wait()
    for f in range(FIELDS):
        for q in range(PLANES):
            k = f * PLANES + q
            p = plane_of(odd, q)
            low[k : k + 1, :] = top[f, p, EIGHT - 1 : EIGHT, :]
            high[k : k + 1, :] = bottom[f, p, 0:1, :]
    finish()


def pack_edges_kernel(state, token, edge, side, left, right, sems):
    _, _, rows, cells = state.shape
    odd = lax.axis_index("ax") % 2
    copies = [
        pltpu.make_async_copy(state.at[:, :, :, cells - LANES : cells], left, sems.at[0]),
        pltpu.make_async_copy(state.at[:, :, :, 0:LANES], right, sems.at[1]),
        pltpu.make_async_copy(state.at[:, 1 - odd, 0:R_NEAR, :], side, sems.at[2]),
    ]
    for copy in copies:
        copy.start()
    for copy in copies[:2]:
        copy.wait()
    lane = lax.broadcasted_iota(jnp.int32, (rows, LANES), 1)
    columns = jnp.ones((rows, LANES), jnp.float32)
    for f in range(FIELDS):
        for q in range(PLANES):
            p = plane_of(odd, q)
            columns = jnp.where(lane == 4 * f + q, left[f, p, :, LANES - 1 : LANES], columns)
            columns = jnp.where(lane == (4 * f - 1 - q) % LANES, right[f, p, :, 0:1], columns)
    edge[...] = columns
    copies[2].wait()


def pack_rest_kernel(parts, tokens, state, *rest):
    rest = rest[tokens:]
    odd = lax.axis_index("ax") % 2
    count = len(parts)
    pieces = []
    for k, (q, first, last) in enumerate(parts):
        pieces.append((state.at[:, plane_of(odd, q), first:last, :], rest[count + k], rest[k]))
    for step in stream(pieces, rest[-1]):
        step()


ANY = pl.BlockSpec(memory_space=pl.ANY)
PARAMS = pltpu.CompilerParams(vmem_limit_bytes=VMEM_LIMIT)


def whole(*shape):
    return pl.BlockSpec(shape, lambda i: (0,) * len(shape))


def rows_from(shape, axis, first, step):
    def place(i):
        row = (first // EIGHT + i * (step // EIGHT)) * EIGHT
        return tuple(row if d == axis else 0 for d in range(len(shape)))

    return pl.BlockSpec(tuple(pl.Element(n) for n in shape), place)


def in_hbm(value):
    return pltpu.with_memory_space_constraint(value, pltpu.HBM)


def cost(flops, nbytes):
    return pl.CostEstimate(flops=flops, bytes_accessed=nbytes, transcendentals=0)


def pack_first(state, count):
    fields, planes, _, cells = state.shape
    vmem = pl.BlockSpec(memory_space=pltpu.VMEM)
    row = jax.ShapeDtypeStruct((LINES, cells), jnp.float32)
    rows = pltpu.VMEM((fields, planes, EIGHT, cells), jnp.float32)
    return pl.pallas_call(
        functools.partial(pack_first_kernel, count),
        in_specs=[ANY],
        out_specs=[ANY, vmem, vmem],
        out_shape=[jax.ShapeDtypeStruct((fields, count, cells), jnp.float32), row, row],
        scratch_shapes=[
            pltpu.VMEM((fields, count, cells), jnp.float32),
            rows,
            rows,
            pltpu.SemaphoreType.DMA((2,)),
            pltpu.SemaphoreType.DMA((2 * len(GROUPS),)),
        ],
        compiler_params=PARAMS,
        cost_estimate=cost(0, fields * count * cells * 8),
        name="pack_first",
    )(in_hbm(state))


def pack_edges(state, token):
    fields, planes, rows, cells = state.shape
    vmem = pl.BlockSpec(memory_space=pltpu.VMEM)
    tiles = pltpu.VMEM((fields, planes, rows, LANES), jnp.float32)
    return pl.pallas_call(
        pack_edges_kernel,
        in_specs=[ANY, ANY],
        out_specs=[vmem, vmem],
        out_shape=[
            jax.ShapeDtypeStruct((rows, LANES), jnp.float32),
            jax.ShapeDtypeStruct((fields, R_NEAR, cells), jnp.float32),
        ],
        scratch_shapes=[tiles, tiles, pltpu.SemaphoreType.DMA((3,))],
        compiler_params=PARAMS,
        cost_estimate=cost(0, fields * planes * rows * LANES * 16),
        name="pack_edges",
    )(in_hbm(state), token)


def pack_rest(state, parts, *tokens):
    fields, _, _, cells = state.shape
    shapes = [jax.ShapeDtypeStruct((fields, last - first, cells), jnp.float32) for _, first, last in parts]
    return pl.pallas_call(
        functools.partial(pack_rest_kernel, parts, len(tokens)),
        in_specs=[ANY] * (1 + len(tokens)),
        out_specs=[ANY] * len(shapes),
        out_shape=shapes,
        scratch_shapes=[
            *[pltpu.VMEM(x.shape, jnp.float32) for x in shapes],
            pltpu.SemaphoreType.DMA((2 * len(GROUPS) * len(parts),)),
        ],
        compiler_params=PARAMS,
        cost_estimate=cost(0, sum(math.prod(x.shape) for x in shapes) * 8),
        name="pack_rest",
    )(in_hbm(state), *tokens)


def flux_scratch(rows, cells):
    shape = (PLANES, FIELDS, cells // LANES)
    return [pltpu.VMEM((*shape, n, LANES), jnp.float32) for n in (rows + 2 * EIGHT, rows)]


def block_rows(span):
    count = span[1] - span[0]
    return 32 if count % 32 == 0 else 24 if count % 24 == 0 else 16


def bulk(counts, state, low, high, inner, edge, dtheta, outer, span, token, held, near_parts=()):
    fields, planes, total_rows, cells = state.shape
    first, end = span
    count = end - first
    rows = block_rows(span)
    blocks = count // rows
    size = fields * planes * count * cells
    aliases = {} if held is None else {7: 0}
    state = in_hbm(state)
    operands = [state, low, high, inner, edge, inner if outer is None else outer, token]
    operands += [state if held is None else held, *near_parts]
    chunk = pltpu.VMEM((fields, count, cells), jnp.float32)
    near_scratch = [pltpu.VMEM((fields, planes, R_NEAR, cells), jnp.float32), pltpu.SemaphoreType.DMA]
    return pl.pallas_call(
        functools.partial(bulk_kernel, dtheta, rows, span, total_rows, outer is not None, len(near_parts), counts),
        grid_spec=pltpu.PrefetchScalarGridSpec(
            num_scalar_prefetch=0,
            grid=(blocks,),
            in_specs=[
                ANY,
                whole(LINES, cells),
                whole(LINES, cells),
                ANY,
                rows_from((rows, LANES), 0, first, rows),
                ANY,
                ANY,
                ANY,
                *[whole(*x.shape) for x in near_parts],
            ],
            out_specs=rows_from((fields, planes, rows, cells), 2, first, rows),
            scratch_shapes=[
                pltpu.VMEM((fields, planes, count + 2 * EIGHT, cells), jnp.float32),
                chunk,
                pltpu.SemaphoreType.DMA((3 * blocks,)),
                *flux_scratch(rows, cells),
                *([] if outer is None else [chunk]),
                *(near_scratch if near_parts else []),
            ],
        ),
        out_shape=pltpu.HBM(state.shape, jnp.float32),
        input_output_aliases=aliases,
        compiler_params=PARAMS,
        cost_estimate=cost(size * 60, size * 10),
        name="bulk",
    )(*operands)


def add_outer(counts, outer, span, rows, held):
    fields, count, cells = outer.shape
    chunk = pltpu.VMEM((fields, count, cells), jnp.float32)
    return pl.pallas_call(
        functools.partial(outer_kernel, rows, span, counts),
        grid_spec=pltpu.PrefetchScalarGridSpec(
            num_scalar_prefetch=0,
            grid=(1,),
            in_specs=[ANY, ANY],
            out_specs=ANY,
            scratch_shapes=[chunk, chunk, pltpu.SemaphoreType.DMA((3 * (count // rows),))],
        ),
        out_shape=pltpu.HBM(held.shape, jnp.float32),
        input_output_aliases={1: 0},
        compiler_params=PARAMS,
        cost_estimate=cost(outer.size * 6, outer.size * 16),
        name="add_outer",
    )(outer, held)


def near(counts, state, low, high, inner, edge, dtheta, outer, factor, table, solve, token, part=None):
    fields, planes, rows, cells = state.shape
    out = jax.ShapeDtypeStruct((LINES, R_NEAR, cells), jnp.float32)
    tail = min(R_NEAR // EIGHT, rows // EIGHT - 1)
    state = in_hbm(state)
    out_specs = [whole(LINES, R_NEAR, cells), whole(LINES, R_NEAR, cells), whole(R_NEAR, LANES)]
    out_shape = [out, out, jax.ShapeDtypeStruct((R_NEAR, LANES), jnp.float32)]
    scratch = flux_scratch(R_NEAR, cells)
    if part is not None:
        out_specs.append(whole(fields, part[1] - part[0], cells))
        out_shape.append(jax.ShapeDtypeStruct((fields, part[1] - part[0], cells), jnp.float32))
        scratch.append(pltpu.SemaphoreType.DMA)
    result = pl.pallas_call(
        functools.partial(near_kernel, dtheta, rows, part[0] if part else 0, counts),
        grid_spec=pltpu.PrefetchScalarGridSpec(
            num_scalar_prefetch=0,
            grid=(1,),
            in_specs=[
                whole(fields, planes, R_NEAR, cells),
                pl.BlockSpec((fields, planes, EIGHT, cells), lambda i: (0, 0, tail, 0)),
                whole(LINES, cells),
                whole(LINES, cells),
                whole(fields, R_NEAR, cells),
                whole(fields, R_NEAR, cells),
                whole(R_NEAR, LANES),
                whole(R_NEAR, LANES),
                whole(R_NEAR, LANES),
                whole(*solve.shape),
                ANY,
                ANY,
            ],
            out_specs=out_specs,
            scratch_shapes=scratch,
        ),
        out_shape=out_shape,
        compiler_params=PARAMS,
        cost_estimate=cost(LINES * R_NEAR * cells * 200, LINES * R_NEAR * cells * 250),
        name="near",
    )(state, state, low, high, inner, outer, edge, factor, table, solve, in_hbm(token), state)
    return result if part is not None else (*result, None)


def chunks(rows):
    size = 16
    blocks = (rows - R_NEAR) // size
    cuts = sorted({-(-2 * blocks // 5), -(-4 * blocks // 5), blocks})
    ends = [R_NEAR + size * c for c in cuts]
    return size, list(zip([0] + ends[:-1], ends))


def smoothing_table(coarsen, cells, total_cells, dtheta):
    factor = coarsen.astype(jnp.float32)[:, None]
    stiffness = KAPPA / (factor * dtheta) ** 2
    inverse_half = 0.5 / stiffness
    one_minus = jnp.sqrt(inverse_half * (2.0 + inverse_half)) - inverse_half
    log_ratio = jnp.log1p(-one_minus)
    gain = (1.0 - one_minus) / (stiffness * one_minus * (2.0 - one_minus))
    closing = 1.0 / -jnp.expm1((total_cells / factor) * log_ratio)
    across = jnp.exp((cells / factor) * log_ratio)
    column = jnp.arange(LANES, dtype=jnp.int32)[None, :]
    width = jnp.left_shift(1, jnp.minimum(column, 20)).astype(jnp.float32)
    table = jnp.where(width >= factor, jnp.exp(log_ratio * (width / factor)), 0.0)
    table = jnp.where(column == COL_LOG, log_ratio, table)
    table = jnp.where(column == COL_GAIN, gain, table)
    return table, closing, across


def piece_tables(dtheta):
    tables = []
    for level in range(FMAX.bit_length()):
        width = 1 << level
        half = 0.5 * (width * dtheta) ** 2 / KAPPA
        ratio = 1.0 - (math.sqrt(half * (2.0 + half)) - half)
        block = np.arange(LANES) // width
        tables.append(ratio ** np.abs(block[:, None] - block[None, :]) / width)
    table = np.concatenate(tables, axis=1)
    high = table.astype(ml_dtypes.bfloat16)
    low = (table - high.astype(np.float64)).astype(ml_dtypes.bfloat16)
    return jnp.asarray(np.concatenate([high, high, low], axis=0))


def ring(value, axis, shift):
    size = lax.axis_size(axis)
    return lax.ppermute(value, axis, [(i, (i + shift) % size) for i in range(size)])


def body(state, coarsen):
    fields, planes, rows, cells = state.shape
    sec_count = lax.axis_size("sec")
    rad_count = lax.axis_size("rad")
    ax_count = lax.axis_size("ax")
    assert fields == FIELDS and planes == PLANES and ax_count % 2 == 0
    total_cells = cells * sec_count
    dtheta = 2.0 * math.pi / total_cells
    outer_pairs = []
    for i in range(1, ax_count - 1, 2):
        outer_pairs += [(i, i + 1), (i + 1, i)]
    inner_pairs = []
    for i in range(0, ax_count, 2):
        inner_pairs += [(i, i + 1), (i + 1, i)]
    up = [(i, i + 1) for i in range(rad_count - 1)]
    down = [(i + 1, i) for i in range(rad_count - 1)]
    counts = (ax_count, rad_count)
    size, spans = chunks(rows)
    count = len(spans)

    part, low, high = pack_first(state, spans[0][1])
    outer = [lax.ppermute(part, "ax", outer_pairs)]
    columns, side = pack_edges(state, high)
    low = lax.ppermute(low, "rad", up)
    high = lax.ppermute(high, "rad", down)
    near_inner = lax.ppermute(side, "ax", inner_pairs)
    if sec_count == 2:
        edge = ring(columns, "sec", 1)
    else:
        from_left = jnp.arange(LANES)[None, :] % 4 < 2
        edge = jnp.where(from_left, ring(columns, "sec", 1), ring(columns, "sec", -1))
    early = [(0, *span) for span in spans[2:]] + [(1, *span) for span in spans[1:2]]
    late = [(0, R_NEAR, spans[0][1])] + [(0, *span) for span in spans[1:2]]
    parts = pack_rest(state, early, columns, low, high) if early else []
    order = in_hbm(parts[0]) if early else columns
    parts = list(parts) + list(pack_rest(state, late, order, edge))
    inner = {}
    for (q, first, last), value in zip(early + late, parts):
        if q:
            outer.append(lax.ppermute(value, "ax", outer_pairs))
        else:
            inner[first, last] = lax.ppermute(value, "ax", inner_pairs)
    order = in_hbm(parts[-1])

    table, closing, across = smoothing_table(coarsen, cells, total_cells, dtheta)
    factor = jnp.broadcast_to(coarsen.astype(jnp.float32)[:, None], (R_NEAR, LANES))

    solve = piece_tables(dtheta)
    given = (counts, state, low, high)

    def pass_over(k, token, held, fused=True, near_parts=()):
        span = (spans[k][0] if k else R_NEAR, spans[k][1])
        far = outer[k] if fused else None
        return bulk(*given, inner[span], edge, dtheta, far, span, token, held, near_parts)

    out = pass_over(2, order, None, fused=False) if count > 2 else None
    part = spans[2] if count > 2 else None
    token = order if out is None else out
    rhs, local, ends, part = near(
        *given, near_inner, edge, dtheta, outer[0], factor, table, solve, token, part
    )
    if part is not None:
        outer.append(lax.ppermute(part, "ax", outer_pairs))
    arrived = [ends] + [ring(ends, "sec", k) for k in range(1, sec_count)] + [ends]
    from_left = jnp.arange(LANES)[None, :] < LINES
    carry = jnp.zeros_like(ends)
    for k in range(sec_count, 0, -1):
        carry = carry * across + jnp.where(from_left, arrived[k], arrived[sec_count - k])
    carry = carry * closing
    passes = min(count, 2)
    for k in range(passes):
        near_parts = (factor, rhs, local, carry, table) if k == passes - 1 else ()
        out = pass_over(k, ends, out, near_parts=near_parts)
    return add_outer(counts, outer[2], spans[2], block_rows(spans[2]), out) if count > 2 else out


def solution(mesh):
    return jax.shard_map(
        body,
        mesh=mesh,
        in_specs=(P(None, "ax", "rad", "sec"), P()),
        out_specs=P(None, "ax", "rad", "sec"),
        check_vma=False,
    )
```

```python
import functools
import math

import jax
import jax.numpy as jnp
import ml_dtypes
import numpy as np
from jax import lax
from jax.experimental import pallas as pl
from jax.experimental.pallas import tpu as pltpu
from jax.sharding import PartitionSpec as P

R_NEAR = 16
FMAX = 16

GAMMA = 1.4
KAPPA = 1.44

FIELDS = 5
PLANES = 2
LINES = FIELDS * PLANES
GROUPS = (slice(0, 3), slice(3, FIELDS))
EIGHT = 8
LANES = 128
VMEM_LIMIT = 28 * 1024 * 1024

COL_LOG = 32
COL_GAIN = 33

ODD, OUTER, FIRST, LAST, BASE = range(5)


def place_flags(counts, rows):
    ax_count, rad_count = counts
    ax = lax.axis_index("ax")
    rad = lax.axis_index("rad")
    beside = (ax > 0) & (ax < ax_count - 1)
    flags = [ax % 2, beside, rad == 0, rad == rad_count - 1, rad * rows]
    return [x.astype(jnp.int32) for x in flags]


def plane_of(odd, q):
    return odd if q else 1 - odd


def reciprocal(x):
    y = pl.reciprocal(x, approx=True)
    y = y * (2.0 - x * y)
    return y * (2.0 - x * y)


def fluxes(fields, want):
    density, energy = fields[0], fields[4]
    momentum = fields[1:4]
    inverse = reciprocal(density)
    velocity = [m * inverse for m in momentum]
    square = {}
    for i in range(3):
        for j in range(i, 3):
            if i == j or i + 1 in want or j + 1 in want or (i, j) == (1, 2):
                square[i, j] = square[j, i] = momentum[i] * velocity[j]
    pressure = (GAMMA - 1.0) * (energy - 0.5 * (square[0, 0] + square[1, 1] + square[2, 2]))
    enthalpy = energy + pressure
    out = {}
    for d in want:
        k = d - 1
        flow = [square[i, k] + pressure if i == k else square[i, k] for i in range(3)]
        out[d] = [momentum[k]] + flow + [enthalpy * velocity[k]]
    return out, (pressure, square[2, 2], square[1, 2])


def flux_along(fields, along):
    return fluxes(fields, (along,))[0][along]


def outer_flux(flags, outer):
    present = flags[OUTER] == 1
    outer = [jnp.where(present, outer[0], 1.0)] + [jnp.where(present, g, 0.0) for g in outer[1:]]
    return flux_along(outer, 1)


def stencil(
    flags, first_row, rows, total_rows, dtheta, load, next_rows, edge, inner, outer, place, radial, azimuthal
):
    strips = rows // EIGHT
    pieces = radial.shape[2]
    row = lax.broadcasted_iota(jnp.int32, (EIGHT, LANES), 0)
    lane = lax.broadcasted_iota(jnp.int32, (EIGHT, LANES), 1)
    start = flags[BASE] + first_row
    axial_sign = jnp.where(flags[ODD] == 1, 0.5, -0.5)
    above = jnp.where((flags[FIRST] == 1) & (first_row == 0), 0.0, (start - 1).astype(jnp.float32) + 0.5)
    end = first_row + rows == total_rows
    below = jnp.where((flags[LAST] == 1) & end, 0.0, (start + rows).astype(jnp.float32) + 0.5)
    scale = jnp.where(row >= EIGHT // 2, above, below)
    at = [slice(b * LANES, (b + 1) * LANES) for b in range(pieces)]

    for q in range(PLANES):
        for b in range(pieces):
            values = [next_rows(f, q, at[b]) for f in range(FIELDS)]
            values[0] = jnp.where(scale > 0.0, values[0], 1.0)
            flux_next = flux_along(values, 2)
            for f in range(FIELDS):
                radial[q, f, b, 0:EIGHT, :] = flux_next[f] * scale
                radial[q, f, b, EIGHT + rows : 2 * EIGHT + rows, :] = flux_next[f] * scale

    def inside(t, carry):
        r = pl.multiple_of(EIGHT * t, EIGHT)
        radius = (start + r + row).astype(jnp.float32) + 0.5
        inv_radius = 1.0 / radius
        for b in range(pieces):
            beside = flux_along([inner(f, r, at[b]) for f in range(FIELDS)], 1)
            axial, source = [], []
            for q in range(PLANES):
                fields = [load(f, q, r, at[b]) for f in range(FIELDS)]
                flow, (pressure, twist, swirl) = fluxes(fields, (1, 2, 3))
                axial.append(flow[1])
                for f in range(FIELDS):
                    radial[q, f, b, pl.ds(r + EIGHT, EIGHT), :] = flow[2][f] * radius
                    azimuthal[q, f, b, pl.ds(r, EIGHT), :] = flow[3][f]
                source.append(((pressure + twist) * inv_radius, swirl * -inv_radius))
            base = [[axial_sign * (x - y) for x, y in zip(beside, axial[1])]]
            if outer is None:
                base.append([axial_sign * x for x in axial[0]])
            else:
                far = outer_flux(flags, [outer(f, r, at[b]) for f in range(FIELDS)])
                base.append([axial_sign * (x - y) for x, y in zip(axial[0], far)])
            for q in range(PLANES):
                base[q][2] = base[q][2] + source[q][0]
                base[q][3] = base[q][3] + source[q][1]
                for f in range(FIELDS):
                    place(f, q, r)[:, at[b]] = base[q][f]
        return carry

    lax.fori_loop(0, strips, inside, 0)

    def differences(t, carry):
        r = pl.multiple_of(EIGHT * t, EIGHT)
        radius = (start + r + row).astype(jnp.float32) + 0.5
        half_inv = 0.5 / radius
        half_arc = half_inv * (1.0 / dtheta)
        beyond = [edge(r)] + [pltpu.roll(edge(r), LANES - 4 * f, 1) for f in range(1, FIELDS)]
        beyond = flux_along(beyond, 3)
        for q in range(PLANES):
            for f in range(FIELDS):
                ends = [pltpu.roll(beyond[f], s, 1) if q else beyond[f] for s in (LANES - 1, 1)]
                here = [azimuthal[q, f, b, pl.ds(r, EIGHT), :] for b in range(pieces)]
                left = [ends[0]] + [pltpu.roll(x, 1, 1) for x in here]
                right = [pltpu.roll(x, LANES - 1, 1) for x in here] + [ends[1]]
                out = place(f, q, r)
                for b in range(pieces):
                    behind = jnp.where(lane == 0, left[b], left[b + 1])
                    ahead = jnp.where(lane == LANES - 1, right[b + 1], right[b])
                    up = radial[q, f, b, pl.ds(r + EIGHT - 1, EIGHT), :]
                    down = radial[q, f, b, pl.ds(r + EIGHT + 1, EIGHT), :]
                    change = (behind - ahead) * half_arc + (up - down) * half_inv
                    out[:, at[b]] = out[:, at[b]] + change
        return carry

    lax.fori_loop(0, strips, differences, 0)


def bulk_kernel(
    dtheta, rows, span, total_rows, fused, near, counts, state, low, high, inner, edge, outer, token, held, *rest
):
    flags = place_flags(counts, total_rows)
    near_parts, out, scratch = rest[:near], rest[near], rest[near + 1 :]
    first, end = span
    blocks = (end - first) // rows
    state_rows, inner_rows, sems, radial, azimuthal, *outer_rows = scratch
    *outer_rows, near_rows, near_sem = [*outer_rows, None, None] if not near else outer_rows
    outer_rows = outer_rows[0] if fused else None
    odd = flags[ODD]
    step = pl.program_id(0)

    def copies(k):
        a = first + k * rows + (EIGHT if k else -EIGHT)
        b = min(first + (k + 1) * rows + EIGHT, total_rows)
        at = a - first + EIGHT
        rest = pl.ds(outer.shape[1] - (end - first) + k * rows, rows)
        here = pl.ds(k * rows, rows)
        sets = [
            (state.at[:, :, a:b, :], state_rows.at[:, :, at : at + b - a, :]),
            (inner.at[:, here, :], inner_rows.at[:, here, :]),
        ]
        if fused:
            sets.append((outer.at[:, rest, :], outer_rows.at[:, here, :]))
        return [pltpu.make_async_copy(x, y, sems.at[3 * k + i]) for i, (x, y) in enumerate(sets)]

    @pl.when(step == 0)
    def _():
        for k in range(blocks):
            for copy in copies(k):
                copy.start()
        if near:
            close_circle(flags, *near_parts, near_rows)
            pltpu.make_async_copy(near_rows, held.at[:, :, 0:R_NEAR, :], near_sem).start()

    for k in range(blocks):

        @pl.when(step == k)
        def _():
            for copy in copies(k):
                copy.wait()

    first_row = first + step * rows
    at_end = first_row + rows == total_rows
    base = pl.multiple_of(step * rows, EIGHT)
    sub = lax.broadcasted_iota(jnp.int32, (EIGHT, LANES), 0)

    def load(f, q, r, at):
        return state_rows[f, plane_of(odd, q), pl.ds(base + EIGHT + r, EIGHT), at]

    def next_rows(f, q, at):
        k = f * PLANES + q
        under = jnp.where(at_end, high[k : k + 1, at], load(f, q, rows, at))
        return jnp.where(sub >= EIGHT // 2, load(f, q, -EIGHT, at), under)

    stencil(
        flags,
        first_row,
        rows,
        total_rows,
        dtheta,
        load,
        next_rows,
        lambda r: edge[pl.ds(r, EIGHT), :],
        lambda f, r, at: inner_rows[f, pl.ds(base + r, EIGHT), at],
        (lambda f, r, at: outer_rows[f, pl.ds(base + r, EIGHT), at]) if fused else None,
        lambda f, q, r: out.at[f, plane_of(odd, q), pl.ds(r, EIGHT), :],
        radial,
        azimuthal,
    )
    if near:

        @pl.when(step == blocks - 1)
        def _():
            pltpu.make_async_copy(near_rows, held.at[:, :, 0:R_NEAR, :], near_sem).wait()


def outer_kernel(rows, span, counts, outer, held, out, outer_rows, held_rows, sems):
    flags = place_flags(counts, 0)
    first, end = span
    plane = lax.axis_index("ax") % 2
    sign = jnp.where(flags[ODD] == 1, -0.5, 0.5)
    steps = []
    for k in range((end - first) // rows):
        here = pl.ds(k * rows, rows)
        there = pl.ds(first + k * rows, rows)
        ways = [
            (outer.at[:, here, :], outer_rows.at[:, here, :]),
            (held.at[:, plane, there, :], held_rows.at[:, here, :]),
            (held_rows.at[:, here, :], out.at[:, plane, there, :]),
        ]
        steps.append([pltpu.make_async_copy(x, y, sems.at[3 * k + i]) for i, (x, y) in enumerate(ways)])
        steps[-1][0].start()
        steps[-1][1].start()
    for k, (come, have, leave) in enumerate(steps):
        come.wait()
        have.wait()
        for t in range(rows // EIGHT):
            at = pl.ds(k * rows + EIGHT * t, EIGHT)
            values = outer_flux(flags, [outer_rows[f, at, :] for f in range(FIELDS)])
            for f in range(FIELDS):
                held_rows[f, at, :] = held_rows[f, at, :] + sign * values[f]
        leave.start()
    for _, _, leave in steps:
        leave.wait()


def near_kernel(
    dtheta,
    total_rows,
    part_first,
    counts,
    state,
    after,
    low,
    high,
    inner,
    outer,
    edge,
    factor,
    table,
    solve,
    token,
    hbm,
    rhs,
    local,
    carry,
    *rest,
):
    flags = place_flags(counts, total_rows)
    cells = state.shape[-1]
    odd = flags[ODD]
    part = rest[0] if len(rest) > 2 else None
    scratch = rest[-2:] if part is None else rest[-3:-1]
    if part is not None:
        source = hbm.at[:, lax.axis_index("ax") % 2, part_first : part_first + part.shape[1], :]
        copy = pltpu.make_async_copy(source, part, rest[-1])
        copy.start()

    sub = lax.broadcasted_iota(jnp.int32, (EIGHT, LANES), 0)

    def next_rows(f, q, at):
        k = f * PLANES + q
        under = high[k : k + 1, at] if total_rows == R_NEAR else after[f, plane_of(odd, q), :, at]
        return jnp.where(sub >= EIGHT // 2, low[k : k + 1, at], under)

    stencil(
        flags,
        0,
        R_NEAR,
        total_rows,
        dtheta,
        lambda f, q, r, at: state[f, plane_of(odd, q), pl.ds(r, EIGHT), at],
        next_rows,
        lambda r: edge[pl.ds(r, EIGHT), :],
        lambda f, r, at: inner[f, pl.ds(r, EIGHT), at],
        lambda f, r, at: outer[f, pl.ds(r, EIGHT), at],
        lambda f, q, r: rhs.at[f * PLANES + q, pl.ds(r, EIGHT), :],
        *scratch,
    )

    pieces = cells // LANES
    lane = lax.broadcasted_iota(jnp.int32, (R_NEAR, LANES), 1)
    width = factor[...]
    log_ratio = table[:, COL_LOG : COL_LOG + 1]
    block = jnp.floor((lane.astype(jnp.float32) + 0.5) / width)
    ahead_entry = jnp.exp(log_ratio * (block + 1.0))
    behind_entry = jnp.exp(log_ratio * (LANES / width - block))
    across = jnp.exp(log_ratio * (LANES / width))

    def line(k, ends):
        rows = jnp.concatenate([rhs[k, :, b * LANES : (b + 1) * LANES] for b in range(pieces)], axis=0)
        high = rows.astype(jnp.bfloat16)
        low = (rows - high.astype(jnp.float32)).astype(jnp.bfloat16)
        solved = jnp.dot(
            jnp.concatenate([high, low, high], axis=1), solve[...], preferred_element_type=jnp.float32
        )
        inside = []
        for b in range(pieces):
            mine = solved[b * R_NEAR : (b + 1) * R_NEAR]
            value = mine[:, :LANES]
            for level in range(1, FMAX.bit_length()):
                chosen = mine[:, level * LANES : (level + 1) * LANES]
                value = jnp.where(width == (1 << level), chosen, value)
            inside.append(value)
        total = list(inside)
        enter = jnp.zeros((R_NEAR, LANES), jnp.float32)
        for b in range(pieces):
            leave = jnp.broadcast_to(inside[b][:, LANES - 1 : LANES], (R_NEAR, LANES))
            total[b] = total[b] + ahead_entry * enter
            enter = leave + across * enter
        ends = jnp.where(lane == k, enter, ends)
        enter = jnp.zeros((R_NEAR, LANES), jnp.float32)
        for b in reversed(range(pieces)):
            leave = jnp.broadcast_to(inside[b][:, 0:1], (R_NEAR, LANES))
            total[b] = total[b] + behind_entry * enter
            enter = leave + across * enter
        for b in range(pieces):
            local[k, :, b * LANES : (b + 1) * LANES] = total[b]
        return jnp.where(lane == k + LINES, enter, ends)

    carry[...] = lax.fori_loop(
        0, LINES, line, jnp.zeros((R_NEAR, LANES), jnp.float32)
    )
    if part is not None:
        copy.wait()


def close_circle(flags, factor, rhs, local, carry, table, out):
    cells = out.shape[-1]
    lane = lax.broadcasted_iota(jnp.int32, (R_NEAR, cells), 1).astype(jnp.float32)
    width = factor[:, 0:1]
    block = jnp.floor((lane + 0.5) / width)
    count = cells / width
    log_ratio = table[:, COL_LOG : COL_LOG + 1]
    gain = jnp.broadcast_to(table[:, COL_GAIN : COL_GAIN + 1], (R_NEAR, cells))
    from_left = jnp.exp(log_ratio * (block + 1.0))
    from_right = jnp.exp(log_ratio * (count - block))
    near = flags[FIRST] == 1
    for f in range(FIELDS):
        for q in range(PLANES):
            k = f * PLANES + q
            j = k + LINES
            smooth = gain * (
                local[k] + from_left * carry[:, k : k + 1] + from_right * carry[:, j : j + 1]
            )
            out[f, plane_of(flags[ODD], q)] = jnp.where(near, smooth, rhs[k])


def stream(pieces, sems):
    steps = []
    for source, stage, target in pieces:
        for f in GROUPS:
            k = 2 * len(steps)
            come = pltpu.make_async_copy(source.at[f], stage.at[f], sems.at[k])
            leave = pltpu.make_async_copy(stage.at[f], target.at[f], sems.at[k + 1])
            steps.append((come, leave))
    for come, _ in steps:
        come.start()

    def forward():
        for come, leave in steps:
            come.wait()
            leave.start()

    def finish():
        for _, leave in steps:
            leave.wait()

    return forward, finish


def pack_first_kernel(count, state, part, stage, sems):
    odd = lax.axis_index("ax") % 2
    for step in stream([(state.at[:, odd, 0:count, :], stage, part)], sems):
        step()


def pack_edges_kernel(state, token, edge, side, low, high, left, right, top, bottom, sems):
    _, _, rows, cells = state.shape
    odd = lax.axis_index("ax") % 2
    copies = [
        pltpu.make_async_copy(state.at[:, :, rows - EIGHT : rows, :], top, sems.at[0]),
        pltpu.make_async_copy(state.at[:, :, 0:EIGHT, :], bottom, sems.at[1]),
        pltpu.make_async_copy(state.at[:, :, :, cells - LANES : cells], left, sems.at[2]),
        pltpu.make_async_copy(state.at[:, :, :, 0:LANES], right, sems.at[3]),
        pltpu.make_async_copy(state.at[:, 1 - odd, 0:R_NEAR, :], side, sems.at[4]),
    ]
    for copy in copies:
        copy.start()
    for copy in copies[:2]:
        copy.wait()
    for f in range(FIELDS):
        for q in range(PLANES):
            k = f * PLANES + q
            p = plane_of(odd, q)
            low[k : k + 1, :] = top[f, p, EIGHT - 1 : EIGHT, :]
            high[k : k + 1, :] = bottom[f, p, 0:1, :]
    for copy in copies[2:4]:
        copy.wait()
    lane = lax.broadcasted_iota(jnp.int32, (rows, LANES), 1)
    columns = jnp.ones((rows, LANES), jnp.float32)
    for f in range(FIELDS):
        for q in range(PLANES):
            p = plane_of(odd, q)
            columns = jnp.where(lane == 4 * f + q, left[f, p, :, LANES - 1 : LANES], columns)
            columns = jnp.where(lane == (4 * f - 1 - q) % LANES, right[f, p, :, 0:1], columns)
    edge[...] = columns
    copies[4].wait()


def pack_rest_kernel(parts, tokens, state, *rest):
    rest = rest[tokens:]
    odd = lax.axis_index("ax") % 2
    count = len(parts)
    pieces = []
    for k, (q, first, last) in enumerate(parts):
        pieces.append((state.at[:, plane_of(odd, q), first:last, :], rest[count + k], rest[k]))
    for step in stream(pieces, rest[-1]):
        step()


ANY = pl.BlockSpec(memory_space=pl.ANY)
PARAMS = pltpu.CompilerParams(vmem_limit_bytes=VMEM_LIMIT)


def whole(*shape):
    return pl.BlockSpec(shape, lambda i: (0,) * len(shape))


def rows_from(shape, axis, first, step):
    def place(i):
        row = (first // EIGHT + i * (step // EIGHT)) * EIGHT
        return tuple(row if d == axis else 0 for d in range(len(shape)))

    return pl.BlockSpec(tuple(pl.Element(n) for n in shape), place)


def in_hbm(value):
    return pltpu.with_memory_space_constraint(value, pltpu.HBM)


def cost(flops, nbytes):
    return pl.CostEstimate(flops=flops, bytes_accessed=nbytes, transcendentals=0)


def pack_first(state, count):
    fields, _, _, cells = state.shape
    return pl.pallas_call(
        functools.partial(pack_first_kernel, count),
        in_specs=[ANY],
        out_specs=ANY,
        out_shape=jax.ShapeDtypeStruct((fields, count, cells), jnp.float32),
        scratch_shapes=[
            pltpu.VMEM((fields, count, cells), jnp.float32),
            pltpu.SemaphoreType.DMA((2 * len(GROUPS),)),
        ],
        compiler_params=PARAMS,
        cost_estimate=cost(0, fields * count * cells * 8),
        name="pack_first",
    )(in_hbm(state))


def pack_edges(state, token):
    fields, planes, rows, cells = state.shape
    vmem = pl.BlockSpec(memory_space=pltpu.VMEM)
    tiles = pltpu.VMEM((fields, planes, rows, LANES), jnp.float32)
    eight = pltpu.VMEM((fields, planes, EIGHT, cells), jnp.float32)
    row = jax.ShapeDtypeStruct((LINES, cells), jnp.float32)
    return pl.pallas_call(
        pack_edges_kernel,
        in_specs=[ANY, ANY],
        out_specs=[vmem] * 4,
        out_shape=[
            jax.ShapeDtypeStruct((rows, LANES), jnp.float32),
            jax.ShapeDtypeStruct((fields, R_NEAR, cells), jnp.float32),
            row,
            row,
        ],
        scratch_shapes=[tiles, tiles, eight, eight, pltpu.SemaphoreType.DMA((5,))],
        compiler_params=PARAMS,
        cost_estimate=cost(0, fields * planes * rows * LANES * 16),
        name="pack_edges",
    )(in_hbm(state), in_hbm(token))


def pack_rest(state, parts, *tokens):
    fields, _, _, cells = state.shape
    shapes = [jax.ShapeDtypeStruct((fields, last - first, cells), jnp.float32) for _, first, last in parts]
    return pl.pallas_call(
        functools.partial(pack_rest_kernel, parts, len(tokens)),
        in_specs=[ANY] * (1 + len(tokens)),
        out_specs=[ANY] * len(shapes),
        out_shape=shapes,
        scratch_shapes=[
            *[pltpu.VMEM(x.shape, jnp.float32) for x in shapes],
            pltpu.SemaphoreType.DMA((2 * len(GROUPS) * len(parts),)),
        ],
        compiler_params=PARAMS,
        cost_estimate=cost(0, sum(math.prod(x.shape) for x in shapes) * 8),
        name="pack_rest",
    )(in_hbm(state), *tokens)


def flux_scratch(rows, cells):
    shape = (PLANES, FIELDS, cells // LANES)
    return [pltpu.VMEM((*shape, n, LANES), jnp.float32) for n in (rows + 2 * EIGHT, rows)]


def block_rows(span):
    count = span[1] - span[0]
    return 32 if count % 32 == 0 else 24 if count % 24 == 0 else 16


def bulk(counts, state, low, high, inner, edge, dtheta, outer, span, token, held, near_parts=()):
    fields, planes, total_rows, cells = state.shape
    first, end = span
    count = end - first
    rows = block_rows(span)
    blocks = count // rows
    size = fields * planes * count * cells
    aliases = {} if held is None else {7: 0}
    state = in_hbm(state)
    operands = [state, low, high, inner, edge, inner if outer is None else outer, token]
    operands += [state if held is None else held, *near_parts]
    chunk = pltpu.VMEM((fields, count, cells), jnp.float32)
    near_scratch = [pltpu.VMEM((fields, planes, R_NEAR, cells), jnp.float32), pltpu.SemaphoreType.DMA]
    return pl.pallas_call(
        functools.partial(bulk_kernel, dtheta, rows, span, total_rows, outer is not None, len(near_parts), counts),
        grid_spec=pltpu.PrefetchScalarGridSpec(
            num_scalar_prefetch=0,
            grid=(blocks,),
            in_specs=[
                ANY,
                whole(LINES, cells),
                whole(LINES, cells),
                ANY,
                rows_from((rows, LANES), 0, first, rows),
                ANY,
                ANY,
                ANY,
                *[whole(*x.shape) for x in near_parts],
            ],
            out_specs=rows_from((fields, planes, rows, cells), 2, first, rows),
            scratch_shapes=[
                pltpu.VMEM((fields, planes, count + 2 * EIGHT, cells), jnp.float32),
                chunk,
                pltpu.SemaphoreType.DMA((3 * blocks,)),
                *flux_scratch(rows, cells),
                *([] if outer is None else [chunk]),
                *(near_scratch if near_parts else []),
            ],
        ),
        out_shape=pltpu.HBM(state.shape, jnp.float32),
        input_output_aliases=aliases,
        compiler_params=PARAMS,
        cost_estimate=cost(size * 60, size * 10),
        name="bulk",
    )(*operands)


def add_outer(counts, outer, span, rows, held):
    fields, count, cells = outer.shape
    chunk = pltpu.VMEM((fields, count, cells), jnp.float32)
    return pl.pallas_call(
        functools.partial(outer_kernel, rows, span, counts),
        grid_spec=pltpu.PrefetchScalarGridSpec(
            num_scalar_prefetch=0,
            grid=(1,),
            in_specs=[ANY, ANY],
            out_specs=ANY,
            scratch_shapes=[chunk, chunk, pltpu.SemaphoreType.DMA((3 * (count // rows),))],
        ),
        out_shape=pltpu.HBM(held.shape, jnp.float32),
        input_output_aliases={1: 0},
        compiler_params=PARAMS,
        cost_estimate=cost(outer.size * 6, outer.size * 16),
        name="add_outer",
    )(outer, held)


def near(counts, state, low, high, inner, edge, dtheta, outer, factor, table, solve, token, part=None):
    fields, planes, rows, cells = state.shape
    out = jax.ShapeDtypeStruct((LINES, R_NEAR, cells), jnp.float32)
    tail = min(R_NEAR // EIGHT, rows // EIGHT - 1)
    state = in_hbm(state)
    out_specs = [whole(LINES, R_NEAR, cells), whole(LINES, R_NEAR, cells), whole(R_NEAR, LANES)]
    out_shape = [out, out, jax.ShapeDtypeStruct((R_NEAR, LANES), jnp.float32)]
    scratch = flux_scratch(R_NEAR, cells)
    if part is not None:
        out_specs.append(whole(fields, part[1] - part[0], cells))
        out_shape.append(jax.ShapeDtypeStruct((fields, part[1] - part[0], cells), jnp.float32))
        scratch.append(pltpu.SemaphoreType.DMA)
    result = pl.pallas_call(
        functools.partial(near_kernel, dtheta, rows, part[0] if part else 0, counts),
        grid_spec=pltpu.PrefetchScalarGridSpec(
            num_scalar_prefetch=0,
            grid=(1,),
            in_specs=[
                whole(fields, planes, R_NEAR, cells),
                pl.BlockSpec((fields, planes, EIGHT, cells), lambda i: (0, 0, tail, 0)),
                whole(LINES, cells),
                whole(LINES, cells),
                whole(fields, R_NEAR, cells),
                whole(fields, R_NEAR, cells),
                whole(R_NEAR, LANES),
                whole(R_NEAR, LANES),
                whole(R_NEAR, LANES),
                whole(*solve.shape),
                ANY,
                ANY,
            ],
            out_specs=out_specs,
            scratch_shapes=scratch,
        ),
        out_shape=out_shape,
        compiler_params=PARAMS,
        cost_estimate=cost(LINES * R_NEAR * cells * 200, LINES * R_NEAR * cells * 250),
        name="near",
    )(state, state, low, high, inner, outer, edge, factor, table, solve, in_hbm(token), state)
    return result if part is not None else (*result, None)


def chunks(rows):
    size = 16
    blocks = (rows - R_NEAR) // size
    cuts = sorted({-(-2 * blocks // 5), -(-4 * blocks // 5), blocks})
    ends = [R_NEAR + size * c for c in cuts]
    return size, list(zip([0] + ends[:-1], ends))


def smoothing_table(coarsen, cells, total_cells, dtheta):
    factor = coarsen.astype(jnp.float32)[:, None]
    stiffness = KAPPA / (factor * dtheta) ** 2
    inverse_half = 0.5 / stiffness
    one_minus = jnp.sqrt(inverse_half * (2.0 + inverse_half)) - inverse_half
    log_ratio = jnp.log1p(-one_minus)
    gain = (1.0 - one_minus) / (stiffness * one_minus * (2.0 - one_minus))
    closing = 1.0 / -jnp.expm1((total_cells / factor) * log_ratio)
    across = jnp.exp((cells / factor) * log_ratio)
    column = jnp.arange(LANES, dtype=jnp.int32)[None, :]
    width = jnp.left_shift(1, jnp.minimum(column, 20)).astype(jnp.float32)
    table = jnp.where(width >= factor, jnp.exp(log_ratio * (width / factor)), 0.0)
    table = jnp.where(column == COL_LOG, log_ratio, table)
    table = jnp.where(column == COL_GAIN, gain, table)
    return table, closing, across


def piece_tables(dtheta):
    tables = []
    for level in range(FMAX.bit_length()):
        width = 1 << level
        half = 0.5 * (width * dtheta) ** 2 / KAPPA
        ratio = 1.0 - (math.sqrt(half * (2.0 + half)) - half)
        block = np.arange(LANES) // width
        tables.append(ratio ** np.abs(block[:, None] - block[None, :]) / width)
    table = np.concatenate(tables, axis=1)
    high = table.astype(ml_dtypes.bfloat16)
    low = (table - high.astype(np.float64)).astype(ml_dtypes.bfloat16)
    return jnp.asarray(np.concatenate([high, high, low], axis=0))


def ring(value, axis, shift):
    size = lax.axis_size(axis)
    return lax.ppermute(value, axis, [(i, (i + shift) % size) for i in range(size)])


def body(state, coarsen):
    fields, planes, rows, cells = state.shape
    sec_count = lax.axis_size("sec")
    rad_count = lax.axis_size("rad")
    ax_count = lax.axis_size("ax")
    assert fields == FIELDS and planes == PLANES and ax_count % 2 == 0
    total_cells = cells * sec_count
    dtheta = 2.0 * math.pi / total_cells
    outer_pairs = []
    for i in range(1, ax_count - 1, 2):
        outer_pairs += [(i, i + 1), (i + 1, i)]
    inner_pairs = []
    for i in range(0, ax_count, 2):
        inner_pairs += [(i, i + 1), (i + 1, i)]
    up = [(i, i + 1) for i in range(rad_count - 1)]
    down = [(i + 1, i) for i in range(rad_count - 1)]
    counts = (ax_count, rad_count)
    size, spans = chunks(rows)
    count = len(spans)

    part = pack_first(state, spans[0][1])
    outer = [lax.ppermute(part, "ax", outer_pairs)]
    columns, side, low, high = pack_edges(state, part)
    low = lax.ppermute(low, "rad", up)
    high = lax.ppermute(high, "rad", down)
    near_inner = lax.ppermute(side, "ax", inner_pairs)
    if sec_count == 2:
        edge = ring(columns, "sec", 1)
    else:
        from_left = jnp.arange(LANES)[None, :] % 4 < 2
        edge = jnp.where(from_left, ring(columns, "sec", 1), ring(columns, "sec", -1))
    early = [(0, *span) for span in spans[2:]] + [(1, *span) for span in spans[1:2]]
    late = [(0, R_NEAR, spans[0][1])] + [(0, *span) for span in spans[1:2]]
    parts = pack_rest(state, early, columns, low, high) if early else []
    order = in_hbm(parts[0]) if early else columns
    parts = list(parts) + list(pack_rest(state, late, order, edge))
    inner = {}
    for (q, first, last), value in zip(early + late, parts):
        if q:
            outer.append(lax.ppermute(value, "ax", outer_pairs))
        else:
            inner[first, last] = lax.ppermute(value, "ax", inner_pairs)
    order = in_hbm(parts[-1])

    table, closing, across = smoothing_table(coarsen, cells, total_cells, dtheta)
    factor = jnp.broadcast_to(coarsen.astype(jnp.float32)[:, None], (R_NEAR, LANES))

    solve = piece_tables(dtheta)
    given = (counts, state, low, high)

    def pass_over(k, token, held, fused=True, near_parts=()):
        span = (spans[k][0] if k else R_NEAR, spans[k][1])
        far = outer[k] if fused else None
        return bulk(*given, inner[span], edge, dtheta, far, span, token, held, near_parts)

    out = pass_over(2, order, None, fused=False) if count > 2 else None
    part = spans[2] if count > 2 else None
    token = order if out is None else out
    rhs, local, ends, part = near(
        *given, near_inner, edge, dtheta, outer[0], factor, table, solve, token, part
    )
    if part is not None:
        outer.append(lax.ppermute(part, "ax", outer_pairs))
    arrived = [ends] + [ring(ends, "sec", k) for k in range(1, sec_count)] + [ends]
    from_left = jnp.arange(LANES)[None, :] < LINES
    carry = jnp.zeros_like(ends)
    for k in range(sec_count, 0, -1):
        carry = carry * across + jnp.where(from_left, arrived[k], arrived[sec_count - k])
    carry = carry * closing
    passes = min(count, 2)
    for k in range(passes):
        near_parts = (factor, rhs, local, carry, table) if k == passes - 1 else ()
        out = pass_over(k, ends, out, near_parts=near_parts)
    return add_outer(counts, outer[2], spans[2], size, out) if count > 2 else out


def solution(mesh):
    return jax.shard_map(
        body,
        mesh=mesh,
        in_specs=(P(None, "ax", "rad", "sec"), P()),
        out_specs=P(None, "ax", "rad", "sec"),
        check_vma=False,
    )
```

```python
import functools
import math

import jax
import jax.numpy as jnp
import ml_dtypes
import numpy as np
from jax import lax
from jax.experimental import pallas as pl
from jax.experimental.pallas import tpu as pltpu
from jax.sharding import PartitionSpec as P

R_NEAR = 16
FMAX = 16

GAMMA = 1.4
KAPPA = 1.44

FIELDS = 5
PLANES = 2
LINES = FIELDS * PLANES
GROUPS = (slice(0, 3), slice(3, FIELDS))
EIGHT = 8
LANES = 128
VMEM_LIMIT = 28 * 1024 * 1024

COL_LOG = 32
COL_GAIN = 33

ODD, OUTER, FIRST, LAST, BASE = range(5)


def place_flags(counts, rows):
    ax_count, rad_count = counts
    ax = lax.axis_index("ax")
    rad = lax.axis_index("rad")
    beside = (ax > 0) & (ax < ax_count - 1)
    flags = [ax % 2, beside, rad == 0, rad == rad_count - 1, rad * rows]
    return [x.astype(jnp.int32) for x in flags]


def plane_of(odd, q):
    return odd if q else 1 - odd


def reciprocal(x):
    y = pl.reciprocal(x, approx=True)
    y = y * (2.0 - x * y)
    return y * (2.0 - x * y)


def fluxes(fields, want):
    density, energy = fields[0], fields[4]
    momentum = fields[1:4]
    inverse = reciprocal(density)
    velocity = [m * inverse for m in momentum]
    square = {}
    for i in range(3):
        for j in range(i, 3):
            if i == j or i + 1 in want or j + 1 in want or (i, j) == (1, 2):
                square[i, j] = square[j, i] = momentum[i] * velocity[j]
    pressure = (GAMMA - 1.0) * (energy - 0.5 * (square[0, 0] + square[1, 1] + square[2, 2]))
    enthalpy = energy + pressure
    out = {}
    for d in want:
        k = d - 1
        flow = [square[i, k] + pressure if i == k else square[i, k] for i in range(3)]
        out[d] = [momentum[k]] + flow + [enthalpy * velocity[k]]
    return out, (pressure, square[2, 2], square[1, 2])


def flux_along(fields, along):
    return fluxes(fields, (along,))[0][along]


def outer_flux(flags, outer):
    present = flags[OUTER] == 1
    outer = [jnp.where(present, outer[0], 1.0)] + [jnp.where(present, g, 0.0) for g in outer[1:]]
    return flux_along(outer, 1)


def stencil(
    flags, first_row, rows, total_rows, dtheta, load, next_rows, edge, inner, outer, place, radial, azimuthal
):
    strips = rows // EIGHT
    pieces = radial.shape[2]
    row = lax.broadcasted_iota(jnp.int32, (EIGHT, LANES), 0)
    lane = lax.broadcasted_iota(jnp.int32, (EIGHT, LANES), 1)
    start = flags[BASE] + first_row
    axial_sign = jnp.where(flags[ODD] == 1, 0.5, -0.5)
    above = jnp.where((flags[FIRST] == 1) & (first_row == 0), 0.0, (start - 1).astype(jnp.float32) + 0.5)
    end = first_row + rows == total_rows
    below = jnp.where((flags[LAST] == 1) & end, 0.0, (start + rows).astype(jnp.float32) + 0.5)
    scale = jnp.where(row >= EIGHT // 2, above, below)
    at = [slice(b * LANES, (b + 1) * LANES) for b in range(pieces)]

    for q in range(PLANES):
        for b in range(pieces):
            values = [next_rows(f, q, at[b]) for f in range(FIELDS)]
            values[0] = jnp.where(scale > 0.0, values[0], 1.0)
            flux_next = flux_along(values, 2)
            for f in range(FIELDS):
                radial[q, f, b, 0:EIGHT, :] = flux_next[f] * scale
                radial[q, f, b, EIGHT + rows : 2 * EIGHT + rows, :] = flux_next[f] * scale

    def inside(t, carry):
        r = pl.multiple_of(EIGHT * t, EIGHT)
        radius = (start + r + row).astype(jnp.float32) + 0.5
        inv_radius = 1.0 / radius
        for b in range(pieces):
            beside = flux_along([inner(f, r, at[b]) for f in range(FIELDS)], 1)
            axial, source = [], []
            for q in range(PLANES):
                fields = [load(f, q, r, at[b]) for f in range(FIELDS)]
                flow, (pressure, twist, swirl) = fluxes(fields, (1, 2, 3))
                axial.append(flow[1])
                for f in range(FIELDS):
                    radial[q, f, b, pl.ds(r + EIGHT, EIGHT), :] = flow[2][f] * radius
                    azimuthal[q, f, b, pl.ds(r, EIGHT), :] = flow[3][f]
                source.append(((pressure + twist) * inv_radius, swirl * -inv_radius))
            base = [[axial_sign * (x - y) for x, y in zip(beside, axial[1])]]
            if outer is None:
                base.append([axial_sign * x for x in axial[0]])
            else:
                far = outer_flux(flags, [outer(f, r, at[b]) for f in range(FIELDS)])
                base.append([axial_sign * (x - y) for x, y in zip(axial[0], far)])
            for q in range(PLANES):
                base[q][2] = base[q][2] + source[q][0]
                base[q][3] = base[q][3] + source[q][1]
                for f in range(FIELDS):
                    place(f, q, r)[:, at[b]] = base[q][f]
        return carry

    lax.fori_loop(0, strips, inside, 0)

    def differences(t, carry):
        r = pl.multiple_of(EIGHT * t, EIGHT)
        radius = (start + r + row).astype(jnp.float32) + 0.5
        half_inv = 0.5 / radius
        half_arc = half_inv * (1.0 / dtheta)
        beyond = [edge(r)] + [pltpu.roll(edge(r), LANES - 4 * f, 1) for f in range(1, FIELDS)]
        beyond = flux_along(beyond, 3)
        for q in range(PLANES):
            for f in range(FIELDS):
                ends = [pltpu.roll(beyond[f], s, 1) if q else beyond[f] for s in (LANES - 1, 1)]
                here = [azimuthal[q, f, b, pl.ds(r, EIGHT), :] for b in range(pieces)]
                left = [ends[0]] + [pltpu.roll(x, 1, 1) for x in here]
                right = [pltpu.roll(x, LANES - 1, 1) for x in here] + [ends[1]]
                out = place(f, q, r)
                for b in range(pieces):
                    behind = jnp.where(lane == 0, left[b], left[b + 1])
                    ahead = jnp.where(lane == LANES - 1, right[b + 1], right[b])
                    up = radial[q, f, b, pl.ds(r + EIGHT - 1, EIGHT), :]
                    down = radial[q, f, b, pl.ds(r + EIGHT + 1, EIGHT), :]
                    change = (behind - ahead) * half_arc + (up - down) * half_inv
                    out[:, at[b]] = out[:, at[b]] + change
        return carry

    lax.fori_loop(0, strips, differences, 0)


def bulk_kernel(
    dtheta, rows, span, total_rows, fused, near, counts, state, low, high, inner, edge, outer, token, held, *rest
):
    flags = place_flags(counts, total_rows)
    near_parts, out, scratch = rest[:near], rest[near], rest[near + 1 :]
    first, end = span
    blocks = (end - first) // rows
    state_rows, inner_rows, sems, radial, azimuthal, *outer_rows = scratch
    *outer_rows, near_rows, near_sem = [*outer_rows, None, None] if not near else outer_rows
    outer_rows = outer_rows[0] if fused else None
    odd = flags[ODD]
    step = pl.program_id(0)

    def copies(k):
        a = first + k * rows + (EIGHT if k else -EIGHT)
        b = min(first + (k + 1) * rows + EIGHT, total_rows)
        at = a - first + EIGHT
        rest = pl.ds(outer.shape[1] - (end - first) + k * rows, rows)
        here = pl.ds(k * rows, rows)
        sets = [
            (state.at[:, :, a:b, :], state_rows.at[:, :, at : at + b - a, :]),
            (inner.at[:, here, :], inner_rows.at[:, here, :]),
        ]
        if fused:
            sets.append((outer.at[:, rest, :], outer_rows.at[:, here, :]))
        return [pltpu.make_async_copy(x, y, sems.at[3 * k + i]) for i, (x, y) in enumerate(sets)]

    @pl.when(step == 0)
    def _():
        for k in range(blocks):
            for copy in copies(k):
                copy.start()
        if near:
            close_circle(flags, *near_parts, near_rows)
            pltpu.make_async_copy(near_rows, held.at[:, :, 0:R_NEAR, :], near_sem).start()

    for k in range(blocks):

        @pl.when(step == k)
        def _():
            for copy in copies(k):
                copy.wait()

    first_row = first + step * rows
    at_end = first_row + rows == total_rows
    base = pl.multiple_of(step * rows, EIGHT)
    sub = lax.broadcasted_iota(jnp.int32, (EIGHT, LANES), 0)

    def load(f, q, r, at):
        return state_rows[f, plane_of(odd, q), pl.ds(base + EIGHT + r, EIGHT), at]

    def next_rows(f, q, at):
        k = f * PLANES + q
        under = jnp.where(at_end, high[k : k + 1, at], load(f, q, rows, at))
        return jnp.where(sub >= EIGHT // 2, load(f, q, -EIGHT, at), under)

    stencil(
        flags,
        first_row,
        rows,
        total_rows,
        dtheta,
        load,
        next_rows,
        lambda r: edge[pl.ds(r, EIGHT), :],
        lambda f, r, at: inner_rows[f, pl.ds(base + r, EIGHT), at],
        (lambda f, r, at: outer_rows[f, pl.ds(base + r, EIGHT), at]) if fused else None,
        lambda f, q, r: out.at[f, plane_of(odd, q), pl.ds(r, EIGHT), :],
        radial,
        azimuthal,
    )
    if near:

        @pl.when(step == blocks - 1)
        def _():
            pltpu.make_async_copy(near_rows, held.at[:, :, 0:R_NEAR, :], near_sem).wait()


def outer_kernel(rows, span, counts, outer, held, out, held_rows, sems):
    flags = place_flags(counts, 0)
    first, end = span
    plane = lax.axis_index("ax") % 2
    sign = jnp.where(flags[ODD] == 1, -0.5, 0.5)
    steps = []
    for k in range((end - first) // rows):
        here = pl.ds(k * rows, rows)
        there = pl.ds(first + k * rows, rows)
        ways = [
            (held.at[:, plane, there, :], held_rows.at[:, here, :]),
            (held_rows.at[:, here, :], out.at[:, plane, there, :]),
        ]
        steps.append([pltpu.make_async_copy(x, y, sems.at[2 * k + i]) for i, (x, y) in enumerate(ways)])
        steps[-1][0].start()
    for k, (have, leave) in enumerate(steps):
        have.wait()
        for t in range(rows // EIGHT):
            at = pl.ds(k * rows + EIGHT * t, EIGHT)
            values = outer_flux(flags, [outer[f, at, :] for f in range(FIELDS)])
            for f in range(FIELDS):
                held_rows[f, at, :] = held_rows[f, at, :] + sign * values[f]
        leave.start()
    for _, leave in steps:
        leave.wait()


def near_kernel(
    dtheta,
    total_rows,
    part_first,
    counts,
    state,
    after,
    low,
    high,
    inner,
    outer,
    edge,
    factor,
    table,
    solve,
    token,
    hbm,
    rhs,
    local,
    carry,
    *rest,
):
    flags = place_flags(counts, total_rows)
    cells = state.shape[-1]
    odd = flags[ODD]
    part = rest[0] if len(rest) > 2 else None
    scratch = rest[-2:] if part is None else rest[-3:-1]
    if part is not None:
        source = hbm.at[:, lax.axis_index("ax") % 2, part_first : part_first + part.shape[1], :]
        copy = pltpu.make_async_copy(source, part, rest[-1])
        copy.start()

    sub = lax.broadcasted_iota(jnp.int32, (EIGHT, LANES), 0)

    def next_rows(f, q, at):
        k = f * PLANES + q
        under = high[k : k + 1, at] if total_rows == R_NEAR else after[f, plane_of(odd, q), :, at]
        return jnp.where(sub >= EIGHT // 2, low[k : k + 1, at], under)

    stencil(
        flags,
        0,
        R_NEAR,
        total_rows,
        dtheta,
        lambda f, q, r, at: state[f, plane_of(odd, q), pl.ds(r, EIGHT), at],
        next_rows,
        lambda r: edge[pl.ds(r, EIGHT), :],
        lambda f, r, at: inner[f, pl.ds(r, EIGHT), at],
        lambda f, r, at: outer[f, pl.ds(r, EIGHT), at],
        lambda f, q, r: rhs.at[f * PLANES + q, pl.ds(r, EIGHT), :],
        *scratch,
    )

    pieces = cells // LANES
    lane = lax.broadcasted_iota(jnp.int32, (R_NEAR, LANES), 1)
    width = factor[...]
    log_ratio = table[:, COL_LOG : COL_LOG + 1]
    block = jnp.floor((lane.astype(jnp.float32) + 0.5) / width)
    ahead_entry = jnp.exp(log_ratio * (block + 1.0))
    behind_entry = jnp.exp(log_ratio * (LANES / width - block))
    across = jnp.exp(log_ratio * (LANES / width))

    def line(k, ends):
        rows = jnp.concatenate([rhs[k, :, b * LANES : (b + 1) * LANES] for b in range(pieces)], axis=0)
        high = rows.astype(jnp.bfloat16)
        low = (rows - high.astype(jnp.float32)).astype(jnp.bfloat16)
        solved = jnp.dot(
            jnp.concatenate([high, low, high], axis=1), solve[...], preferred_element_type=jnp.float32
        )
        inside = []
        for b in range(pieces):
            mine = solved[b * R_NEAR : (b + 1) * R_NEAR]
            value = mine[:, :LANES]
            for level in range(1, FMAX.bit_length()):
                chosen = mine[:, level * LANES : (level + 1) * LANES]
                value = jnp.where(width == (1 << level), chosen, value)
            inside.append(value)
        total = list(inside)
        enter = jnp.zeros((R_NEAR, LANES), jnp.float32)
        for b in range(pieces):
            leave = jnp.broadcast_to(inside[b][:, LANES - 1 : LANES], (R_NEAR, LANES))
            total[b] = total[b] + ahead_entry * enter
            enter = leave + across * enter
        ends = jnp.where(lane == k, enter, ends)
        enter = jnp.zeros((R_NEAR, LANES), jnp.float32)
        for b in reversed(range(pieces)):
            leave = jnp.broadcast_to(inside[b][:, 0:1], (R_NEAR, LANES))
            total[b] = total[b] + behind_entry * enter
            enter = leave + across * enter
        for b in range(pieces):
            local[k, :, b * LANES : (b + 1) * LANES] = total[b]
        return jnp.where(lane == k + LINES, enter, ends)

    carry[...] = lax.fori_loop(
        0, LINES, line, jnp.zeros((R_NEAR, LANES), jnp.float32)
    )
    if part is not None:
        copy.wait()


def close_circle(flags, factor, rhs, local, carry, table, out):
    cells = out.shape[-1]
    lane = lax.broadcasted_iota(jnp.int32, (R_NEAR, cells), 1).astype(jnp.float32)
    width = factor[:, 0:1]
    block = jnp.floor((lane + 0.5) / width)
    count = cells / width
    log_ratio = table[:, COL_LOG : COL_LOG + 1]
    gain = jnp.broadcast_to(table[:, COL_GAIN : COL_GAIN + 1], (R_NEAR, cells))
    from_left = jnp.exp(log_ratio * (block + 1.0))
    from_right = jnp.exp(log_ratio * (count - block))
    near = flags[FIRST] == 1
    for f in range(FIELDS):
        for q in range(PLANES):
            k = f * PLANES + q
            j = k + LINES
            smooth = gain * (
                local[k] + from_left * carry[:, k : k + 1] + from_right * carry[:, j : j + 1]
            )
            out[f, plane_of(flags[ODD], q)] = jnp.where(near, smooth, rhs[k])


def stream(pieces, sems):
    steps = []
    for source, stage, target in pieces:
        for f in GROUPS:
            k = 2 * len(steps)
            come = pltpu.make_async_copy(source.at[f], stage.at[f], sems.at[k])
            leave = pltpu.make_async_copy(stage.at[f], target.at[f], sems.at[k + 1])
            steps.append((come, leave))
    for come, _ in steps:
        come.start()

    def forward():
        for come, leave in steps:
            come.wait()
            leave.start()

    def finish():
        for _, leave in steps:
            leave.wait()

    return forward, finish


def pack_first_kernel(count, state, part, stage, sems):
    odd = lax.axis_index("ax") % 2
    for step in stream([(state.at[:, odd, 0:count, :], stage, part)], sems):
        step()


def pack_edges_kernel(state, token, edge, side, low, high, left, right, top, bottom, sems):
    _, _, rows, cells = state.shape
    odd = lax.axis_index("ax") % 2
    copies = [
        pltpu.make_async_copy(state.at[:, :, rows - EIGHT : rows, :], top, sems.at[0]),
        pltpu.make_async_copy(state.at[:, :, 0:EIGHT, :], bottom, sems.at[1]),
        pltpu.make_async_copy(state.at[:, :, :, cells - LANES : cells], left, sems.at[2]),
        pltpu.make_async_copy(state.at[:, :, :, 0:LANES], right, sems.at[3]),
        pltpu.make_async_copy(state.at[:, 1 - odd, 0:R_NEAR, :], side, sems.at[4]),
    ]
    for copy in copies:
        copy.start()
    for copy in copies[:2]:
        copy.wait()
    for f in range(FIELDS):
        for q in range(PLANES):
            k = f * PLANES + q
            p = plane_of(odd, q)
            low[k : k + 1, :] = top[f, p, EIGHT - 1 : EIGHT, :]
            high[k : k + 1, :] = bottom[f, p, 0:1, :]
    for copy in copies[2:4]:
        copy.wait()
    lane = lax.broadcasted_iota(jnp.int32, (rows, LANES), 1)
    columns = jnp.ones((rows, LANES), jnp.float32)
    for f in range(FIELDS):
        for q in range(PLANES):
            p = plane_of(odd, q)
            columns = jnp.where(lane == 4 * f + q, left[f, p, :, LANES - 1 : LANES], columns)
            columns = jnp.where(lane == (4 * f - 1 - q) % LANES, right[f, p, :, 0:1], columns)
    edge[...] = columns
    copies[4].wait()


def pack_rest_kernel(parts, tokens, state, *rest):
    rest = rest[tokens:]
    odd = lax.axis_index("ax") % 2
    count = len(parts)
    pieces = []
    for k, (q, first, last) in enumerate(parts):
        pieces.append((state.at[:, plane_of(odd, q), first:last, :], rest[count + k], rest[k]))
    for step in stream(pieces, rest[-1]):
        step()


ANY = pl.BlockSpec(memory_space=pl.ANY)
PARAMS = pltpu.CompilerParams(vmem_limit_bytes=VMEM_LIMIT)


def whole(*shape):
    return pl.BlockSpec(shape, lambda i: (0,) * len(shape))


def rows_from(shape, axis, first, step):
    def place(i):
        row = (first // EIGHT + i * (step // EIGHT)) * EIGHT
        return tuple(row if d == axis else 0 for d in range(len(shape)))

    return pl.BlockSpec(tuple(pl.Element(n) for n in shape), place)


def in_hbm(value):
    return pltpu.with_memory_space_constraint(value, pltpu.HBM)


def cost(flops, nbytes):
    return pl.CostEstimate(flops=flops, bytes_accessed=nbytes, transcendentals=0)


def pack_first(state, count):
    fields, _, _, cells = state.shape
    return pl.pallas_call(
        functools.partial(pack_first_kernel, count),
        in_specs=[ANY],
        out_specs=ANY,
        out_shape=jax.ShapeDtypeStruct((fields, count, cells), jnp.float32),
        scratch_shapes=[
            pltpu.VMEM((fields, count, cells), jnp.float32),
            pltpu.SemaphoreType.DMA((2 * len(GROUPS),)),
        ],
        compiler_params=PARAMS,
        cost_estimate=cost(0, fields * count * cells * 8),
        name="pack_first",
    )(in_hbm(state))


def pack_edges(state, token):
    fields, planes, rows, cells = state.shape
    vmem = pl.BlockSpec(memory_space=pltpu.VMEM)
    tiles = pltpu.VMEM((fields, planes, rows, LANES), jnp.float32)
    eight = pltpu.VMEM((fields, planes, EIGHT, cells), jnp.float32)
    row = jax.ShapeDtypeStruct((LINES, cells), jnp.float32)
    return pl.pallas_call(
        pack_edges_kernel,
        in_specs=[ANY, ANY],
        out_specs=[vmem] * 4,
        out_shape=[
            jax.ShapeDtypeStruct((rows, LANES), jnp.float32),
            jax.ShapeDtypeStruct((fields, R_NEAR, cells), jnp.float32),
            row,
            row,
        ],
        scratch_shapes=[tiles, tiles, eight, eight, pltpu.SemaphoreType.DMA((5,))],
        compiler_params=PARAMS,
        cost_estimate=cost(0, fields * planes * rows * LANES * 16),
        name="pack_edges",
    )(in_hbm(state), in_hbm(token))


def pack_rest(state, parts, *tokens):
    fields, _, _, cells = state.shape
    shapes = [jax.ShapeDtypeStruct((fields, last - first, cells), jnp.float32) for _, first, last in parts]
    return pl.pallas_call(
        functools.partial(pack_rest_kernel, parts, len(tokens)),
        in_specs=[ANY] * (1 + len(tokens)),
        out_specs=[ANY] * len(shapes),
        out_shape=shapes,
        scratch_shapes=[
            *[pltpu.VMEM(x.shape, jnp.float32) for x in shapes],
            pltpu.SemaphoreType.DMA((2 * len(GROUPS) * len(parts),)),
        ],
        compiler_params=PARAMS,
        cost_estimate=cost(0, sum(math.prod(x.shape) for x in shapes) * 8),
        name="pack_rest",
    )(in_hbm(state), *tokens)


def flux_scratch(rows, cells):
    shape = (PLANES, FIELDS, cells // LANES)
    return [pltpu.VMEM((*shape, n, LANES), jnp.float32) for n in (rows + 2 * EIGHT, rows)]


def block_rows(span):
    count = span[1] - span[0]
    return 32 if count % 32 == 0 else 24 if count % 24 == 0 else 16


def bulk(counts, state, low, high, inner, edge, dtheta, outer, span, token, held, near_parts=()):
    fields, planes, total_rows, cells = state.shape
    first, end = span
    count = end - first
    rows = block_rows(span)
    blocks = count // rows
    size = fields * planes * count * cells
    aliases = {} if held is None else {7: 0}
    state = in_hbm(state)
    operands = [state, low, high, inner, edge, inner if outer is None else outer, token]
    operands += [state if held is None else held, *near_parts]
    chunk = pltpu.VMEM((fields, count, cells), jnp.float32)
    near_scratch = [pltpu.VMEM((fields, planes, R_NEAR, cells), jnp.float32), pltpu.SemaphoreType.DMA]
    return pl.pallas_call(
        functools.partial(bulk_kernel, dtheta, rows, span, total_rows, outer is not None, len(near_parts), counts),
        grid_spec=pltpu.PrefetchScalarGridSpec(
            num_scalar_prefetch=0,
            grid=(blocks,),
            in_specs=[
                ANY,
                whole(LINES, cells),
                whole(LINES, cells),
                ANY,
                rows_from((rows, LANES), 0, first, rows),
                ANY,
                ANY,
                ANY,
                *[whole(*x.shape) for x in near_parts],
            ],
            out_specs=rows_from((fields, planes, rows, cells), 2, first, rows),
            scratch_shapes=[
                pltpu.VMEM((fields, planes, count + 2 * EIGHT, cells), jnp.float32),
                chunk,
                pltpu.SemaphoreType.DMA((3 * blocks,)),
                *flux_scratch(rows, cells),
                *([] if outer is None else [chunk]),
                *(near_scratch if near_parts else []),
            ],
        ),
        out_shape=pltpu.HBM(state.shape, jnp.float32),
        input_output_aliases=aliases,
        compiler_params=PARAMS,
        cost_estimate=cost(size * 60, size * 10),
        name="bulk",
    )(*operands)


def add_outer(counts, outer, span, rows, held):
    fields, count, cells = outer.shape
    chunk = pltpu.VMEM((fields, count, cells), jnp.float32)
    return pl.pallas_call(
        functools.partial(outer_kernel, rows, span, counts),
        grid_spec=pltpu.PrefetchScalarGridSpec(
            num_scalar_prefetch=0,
            grid=(1,),
            in_specs=[pl.BlockSpec(memory_space=pltpu.VMEM), ANY],
            out_specs=ANY,
            scratch_shapes=[chunk, pltpu.SemaphoreType.DMA((2 * (count // rows),))],
        ),
        out_shape=pltpu.HBM(held.shape, jnp.float32),
        input_output_aliases={1: 0},
        compiler_params=PARAMS,
        cost_estimate=cost(outer.size * 6, outer.size * 16),
        name="add_outer",
    )(outer, held)


def near(counts, state, low, high, inner, edge, dtheta, outer, factor, table, solve, token, part=None):
    fields, planes, rows, cells = state.shape
    out = jax.ShapeDtypeStruct((LINES, R_NEAR, cells), jnp.float32)
    tail = min(R_NEAR // EIGHT, rows // EIGHT - 1)
    state = in_hbm(state)
    out_specs = [whole(LINES, R_NEAR, cells), whole(LINES, R_NEAR, cells), whole(R_NEAR, LANES)]
    out_shape = [out, out, jax.ShapeDtypeStruct((R_NEAR, LANES), jnp.float32)]
    scratch = flux_scratch(R_NEAR, cells)
    if part is not None:
        out_specs.append(whole(fields, part[1] - part[0], cells))
        out_shape.append(jax.ShapeDtypeStruct((fields, part[1] - part[0], cells), jnp.float32))
        scratch.append(pltpu.SemaphoreType.DMA)
    result = pl.pallas_call(
        functools.partial(near_kernel, dtheta, rows, part[0] if part else 0, counts),
        grid_spec=pltpu.PrefetchScalarGridSpec(
            num_scalar_prefetch=0,
            grid=(1,),
            in_specs=[
                whole(fields, planes, R_NEAR, cells),
                pl.BlockSpec((fields, planes, EIGHT, cells), lambda i: (0, 0, tail, 0)),
                whole(LINES, cells),
                whole(LINES, cells),
                whole(fields, R_NEAR, cells),
                whole(fields, R_NEAR, cells),
                whole(R_NEAR, LANES),
                whole(R_NEAR, LANES),
                whole(R_NEAR, LANES),
                whole(*solve.shape),
                ANY,
                ANY,
            ],
            out_specs=out_specs,
            scratch_shapes=scratch,
        ),
        out_shape=out_shape,
        compiler_params=PARAMS,
        cost_estimate=cost(LINES * R_NEAR * cells * 200, LINES * R_NEAR * cells * 250),
        name="near",
    )(state, state, low, high, inner, outer, edge, factor, table, solve, in_hbm(token), state)
    return result if part is not None else (*result, None)


def chunks(rows):
    size = 16
    blocks = (rows - R_NEAR) // size
    cuts = sorted({-(-2 * blocks // 5), -(-4 * blocks // 5), blocks})
    ends = [R_NEAR + size * c for c in cuts]
    return size, list(zip([0] + ends[:-1], ends))


def smoothing_table(coarsen, cells, total_cells, dtheta):
    factor = coarsen.astype(jnp.float32)[:, None]
    stiffness = KAPPA / (factor * dtheta) ** 2
    inverse_half = 0.5 / stiffness
    one_minus = jnp.sqrt(inverse_half * (2.0 + inverse_half)) - inverse_half
    log_ratio = jnp.log1p(-one_minus)
    gain = (1.0 - one_minus) / (stiffness * one_minus * (2.0 - one_minus))
    closing = 1.0 / -jnp.expm1((total_cells / factor) * log_ratio)
    across = jnp.exp((cells / factor) * log_ratio)
    column = jnp.arange(LANES, dtype=jnp.int32)[None, :]
    width = jnp.left_shift(1, jnp.minimum(column, 20)).astype(jnp.float32)
    table = jnp.where(width >= factor, jnp.exp(log_ratio * (width / factor)), 0.0)
    table = jnp.where(column == COL_LOG, log_ratio, table)
    table = jnp.where(column == COL_GAIN, gain, table)
    return table, closing, across


def piece_tables(dtheta):
    tables = []
    for level in range(FMAX.bit_length()):
        width = 1 << level
        half = 0.5 * (width * dtheta) ** 2 / KAPPA
        ratio = 1.0 - (math.sqrt(half * (2.0 + half)) - half)
        block = np.arange(LANES) // width
        tables.append(ratio ** np.abs(block[:, None] - block[None, :]) / width)
    table = np.concatenate(tables, axis=1)
    high = table.astype(ml_dtypes.bfloat16)
    low = (table - high.astype(np.float64)).astype(ml_dtypes.bfloat16)
    return jnp.asarray(np.concatenate([high, high, low], axis=0))


def ring(value, axis, shift):
    size = lax.axis_size(axis)
    return lax.ppermute(value, axis, [(i, (i + shift) % size) for i in range(size)])


def body(state, coarsen):
    fields, planes, rows, cells = state.shape
    sec_count = lax.axis_size("sec")
    rad_count = lax.axis_size("rad")
    ax_count = lax.axis_size("ax")
    assert fields == FIELDS and planes == PLANES and ax_count % 2 == 0
    total_cells = cells * sec_count
    dtheta = 2.0 * math.pi / total_cells
    outer_pairs = []
    for i in range(1, ax_count - 1, 2):
        outer_pairs += [(i, i + 1), (i + 1, i)]
    inner_pairs = []
    for i in range(0, ax_count, 2):
        inner_pairs += [(i, i + 1), (i + 1, i)]
    up = [(i, i + 1) for i in range(rad_count - 1)]
    down = [(i + 1, i) for i in range(rad_count - 1)]
    counts = (ax_count, rad_count)
    size, spans = chunks(rows)
    count = len(spans)

    part = pack_first(state, spans[0][1])
    outer = [lax.ppermute(part, "ax", outer_pairs)]
    columns, side, low, high = pack_edges(state, part)
    low = lax.ppermute(low, "rad", up)
    high = lax.ppermute(high, "rad", down)
    near_inner = lax.ppermute(side, "ax", inner_pairs)
    if sec_count == 2:
        edge = ring(columns, "sec", 1)
    else:
        from_left = jnp.arange(LANES)[None, :] % 4 < 2
        edge = jnp.where(from_left, ring(columns, "sec", 1), ring(columns, "sec", -1))
    early = [(0, *span) for span in spans[2:]] + [(1, *span) for span in spans[1:2]]
    late = [(0, R_NEAR, spans[0][1])] + [(0, *span) for span in spans[1:2]]
    parts = pack_rest(state, early, columns, low, high) if early else []
    order = in_hbm(parts[0]) if early else columns
    parts = list(parts) + list(pack_rest(state, late, order, edge))
    inner = {}
    for (q, first, last), value in zip(early + late, parts):
        if q:
            outer.append(lax.ppermute(value, "ax", outer_pairs))
        else:
            inner[first, last] = lax.ppermute(value, "ax", inner_pairs)
    order = in_hbm(parts[-1])

    table, closing, across = smoothing_table(coarsen, cells, total_cells, dtheta)
    factor = jnp.broadcast_to(coarsen.astype(jnp.float32)[:, None], (R_NEAR, LANES))

    solve = piece_tables(dtheta)
    given = (counts, state, low, high)

    def pass_over(k, token, held, fused=True, near_parts=()):
        span = (spans[k][0] if k else R_NEAR, spans[k][1])
        far = outer[k] if fused else None
        return bulk(*given, inner[span], edge, dtheta, far, span, token, held, near_parts)

    out = pass_over(2, order, None, fused=False) if count > 2 else None
    part = spans[2] if count > 2 else None
    token = order if out is None else out
    rhs, local, ends, part = near(
        *given, near_inner, edge, dtheta, outer[0], factor, table, solve, token, part
    )
    if part is not None:
        outer.append(lax.ppermute(part, "ax", outer_pairs))
    arrived = [ends] + [ring(ends, "sec", k) for k in range(1, sec_count)] + [ends]
    from_left = jnp.arange(LANES)[None, :] < LINES
    carry = jnp.zeros_like(ends)
    for k in range(sec_count, 0, -1):
        carry = carry * across + jnp.where(from_left, arrived[k], arrived[sec_count - k])
    carry = carry * closing
    passes = min(count, 2)
    for k in range(passes):
        near_parts = (factor, rhs, local, carry, table) if k == passes - 1 else ()
        out = pass_over(k, ends, out, near_parts=near_parts)
    return add_outer(counts, outer[2], spans[2], size, out) if count > 2 else out


def solution(mesh):
    return jax.shard_map(
        body,
        mesh=mesh,
        in_specs=(P(None, "ax", "rad", "sec"), P()),
        out_specs=P(None, "ax", "rad", "sec"),
        check_vma=False,
    )
```
